32 devices in a mesh: groups: 2 (over x), seq: 8 (over z, y), head: 2 (over core).
Axes of the slice: x: 2, y: 2, z: 4, core: 2. Of those that a mesh axis runs over, the one named last changes fastest.
Arguments:
- patches: bfloat16 [2, 320, 4, 1024], P('groups', 'seq'), parts along dimension 0, may hold values from -6 to 6
- keep_list: int32 [2, 64], P('groups'), parts along dimension 0, may hold values from 0 to 319, as said below
- qkv_weight: bfloat16 [1024, 16, 192], P('seq', 'head')
- out_weight: bfloat16 [1024, 1024], P('head', 'seq'), may hold values from -0.1875 to 0.1875
- up_weight: bfloat16 [1024, 4096], P('seq', 'head'), may hold values from -0.1875 to 0.1875
- down_weight: bfloat16 [4096, 1024], P('head', 'seq'), may hold values from -0.09375 to 0.09375
Outputs:
- encoded: bfloat16 [2, 64, 8, 1024], P('groups', None, 'seq', 'head'), parts along dimension 0
The draws below stay inside these ranges and needn't reach their ends.
There are 2 independent parts, one for each index of `groups`. The reference program is written for one: setup_inputs(seed, part) draws one part's arguments, and reference() takes and returns one part's arrays. A program takes and returns all parts, laid end to end along the dimension named above; an argument that names none is the same for every part. Nothing has to cross between parts.
Inputs may be any that keep to these rules, and one draw needn't show every extreme that they name: `keep_list`: each row lists 64 different superpatch indices of one image in increasing order; in every image the first and the last superpatch are listed, and all 40 superpatches of one aligned block (indices b * 40 to b * 40 + 39) are listed.
All inputs are finite; a program needn't handle non-finite values.
Results may differ from the reference program's by a relative error of at most 0.0055.
Values may be sent and summed in bfloat16 or wider, within the bound.
No kernel may reach another device: no remote copies, remote signals or barrier semaphores. Data moves between devices by JAX's collectives and lax.ppermute only.
A program may use at most 64 MiB of HBM per device.

```python
import math
import jax
import jax.numpy as jnp
from jax import lax

D = 1024
HEADS = 16
HD = 64
FF = 4096
PIECE = 64
IMAGES = 1
SEQ_LEN = 512
SUPER = 320
KEEP = 64
SUP_DEV = 40
N_SEQ = 8


def draw_keep_list(key, part):
    key = jax.random.fold_in(key, 5)
    key_level, key_busy, key_noise = jax.random.split(key, 3)
    regions = SUPER // SUP_DEV
    levels = jax.random.randint(key_level, (IMAGES, regions), 0, 5)
    busiest = jax.random.randint(key_busy, (IMAGES,), 0, regions)
    noise = jax.random.randint(key_noise, (IMAGES, SUPER), 0, 1024)
    super_ids = jnp.arange(SUPER, dtype=jnp.int32)
    region_of = super_ids // SUP_DEV
    level_of = jnp.take_along_axis(levels, jnp.broadcast_to(region_of[None, :], (IMAGES, SUPER)), axis=1)
    level_of = jnp.where(region_of[None, :] == busiest[:, None], 8, level_of)
    ends = jnp.logical_or(super_ids == 0, super_ids == SUPER - 1)
    level_of = jnp.where(ends[None, :], 9, level_of)
    scores = (level_of * 1024 + noise) * SUPER + super_ids[None, :]
    chosen = lax.top_k(scores.astype(jnp.int32), KEEP)[1]
    return jnp.sort(chosen, axis=1).astype(jnp.int32)


def draw_qkv_weight(key, part):
    key = jax.random.fold_in(key, 11)
    key_base = jax.random.fold_in(key, 0)
    base = jax.random.normal(key_base, (D, HEADS, 3 * HD), jnp.float32) * D ** (-0.5)
    return base.astype(jnp.bfloat16)


def block_levels(own_key, shape, shards, least, largest):
    def one(axis_at, blocks):
        heights = jax.random.uniform(jax.random.fold_in(jax.random.fold_in(own_key, 6), axis_at), (blocks,), jnp.float32, least / len(shards), largest / len(shards))
        return jnp.repeat(jnp.exp(heights), shape[axis_at] // blocks).reshape((-1,) + (1,) * (len(shape) - axis_at - 1))

    factor_of = one(*shards[0])
    for cut in shards[1:]:
        factor_of = factor_of * one(*cut)
    return factor_of


def normal_values(stream_key, shape, width, most, cuts=(), kind=jnp.bfloat16):
    drawn = jax.random.normal(stream_key, shape, jnp.float32) * width
    if len(cuts) > 0:
        drawn = block_levels(stream_key, shape, cuts, -0.22, 0.18) * drawn
    return jnp.clip(drawn, min=-most, max=most).astype(kind)


def setup_inputs(seed: int = 0, part: int = 0) -> dict:
    seeds = jax.random.split(jax.random.key(seed), 7)
    part_splits = jax.random.split(jax.random.fold_in(seeds[6], part), 7)
    return {
        "patches": normal_values(part_splits[0], (IMAGES, SUPER, 4, D), 1.0, 6.0, ((1, 8),)),
        "keep_list": draw_keep_list(jax.random.fold_in(jax.random.fold_in(seeds[6], part), 71), part),
        "qkv_weight": draw_qkv_weight(jax.random.fold_in(seeds[6], 71), part),
        "out_weight": normal_values(seeds[3], (D, D), D ** -0.5, 0.1875, ((0, 2), (1, 8))),
        "up_weight": normal_values(seeds[4], (D, FF), D ** -0.5, 0.1875, ((0, 8), (1, 2))),
        "down_weight": normal_values(seeds[5], (FF, D), FF ** -0.5, 0.09375, ((0, 2), (1, 8))),
    }


def layer_norm(matrix):
    average = lax.optimization_barrier(jnp.mean(matrix, axis=-1, keepdims=True))
    power = lax.optimization_barrier(jnp.mean(matrix * matrix, axis=-1, keepdims=True))
    return (matrix - average) * lax.rsqrt(power - average * average + 1e-06)

def attend(queries, keys, values):
    length = queries.shape[0]
    block = math.gcd(length, 512)
    scale = 1.0 / math.sqrt(queries.shape[1])

    def one_block(query_rows):
        scores = lax.dot_general(query_rows, keys, (((1,), (1,)), ((), ())), preferred_element_type=jnp.float32) * scale
        top = lax.optimization_barrier(jnp.max(scores, axis=1, keepdims=True))
        powers = jnp.exp(scores - top)
        probs = (powers / lax.optimization_barrier(jnp.sum(powers, axis=1, keepdims=True))).astype(jnp.bfloat16)
        return jnp.dot(probs, values, preferred_element_type=jnp.float32).astype(jnp.bfloat16)
    blocks = lax.map(one_block, queries.reshape(length // block, block, queries.shape[1]))
    return blocks.reshape(length, values.shape[1])

def build_tokens(patch_rows, keep_row):
    kept_flag = jnp.zeros((SUPER,), jnp.int32).at[keep_row].set(1)
    offsets = (jnp.arange(SUPER, dtype=jnp.int32) + 3 * (jnp.cumsum(kept_flag) - kept_flag)).astype(jnp.int32)
    positions = jnp.arange(SEQ_LEN, dtype=jnp.int32)
    owner_patch = (jnp.searchsorted(offsets, positions, side='right') - 1).astype(jnp.int32)
    sub_index = jnp.minimum(positions - offsets[owner_patch], 3).astype(jnp.int32)
    kept_of = kept_flag[owner_patch]
    fine_rows = patch_rows[owner_patch, jnp.where(kept_of == 1, sub_index, 0)]
    shared_rows = lax.optimization_barrier(jnp.mean(patch_rows.astype(jnp.float32), axis=1)).astype(jnp.bfloat16)[owner_patch]
    return jnp.where((kept_of == 1)[:, None], fine_rows, shared_rows)

def reference(patches, keep_list, qkv_weight, out_weight, up_weight, down_weight):
    tokens = jax.vmap(build_tokens)(patches, keep_list).reshape(IMAGES * SEQ_LEN, D)
    start_rows = tokens.astype(jnp.float32)
    normed = layer_norm(start_rows).astype(jnp.bfloat16)
    projected = jnp.dot(normed, qkv_weight.reshape(D, HEADS * 3 * HD), preferred_element_type=jnp.float32).astype(jnp.bfloat16)
    by_head = projected.reshape(IMAGES, SEQ_LEN, HEADS, 3 * HD).transpose(0, 2, 1, 3).reshape(IMAGES * HEADS, SEQ_LEN, 3 * HD)

    def one_head(stacked):
        return attend(stacked[:, :HD], stacked[:, HD:2 * HD], stacked[:, 2 * HD:])
    attended = lax.map(one_head, by_head)
    attended = attended.reshape(IMAGES, HEADS, SEQ_LEN, HD).transpose(0, 2, 1, 3).reshape(IMAGES * SEQ_LEN, HEADS * HD)
    residual = start_rows + jnp.dot(attended, out_weight, preferred_element_type=jnp.float32)
    normed_two = layer_norm(residual).astype(jnp.bfloat16)
    hidden = jax.nn.gelu(jnp.dot(normed_two, up_weight, preferred_element_type=jnp.float32), approximate=False).astype(jnp.bfloat16)
    encoded = (residual + jnp.dot(hidden, down_weight, preferred_element_type=jnp.float32)).astype(jnp.bfloat16)
    return encoded.reshape(IMAGES, PIECE, N_SEQ, D)
```

```python
import functools
import math

import jax
import jax.numpy as jnp
from jax import lax
from jax.experimental import pallas as pl
from jax.experimental.pallas import tpu as pltpu
from jax.sharding import PartitionSpec as P

F32 = jnp.float32
BF16 = jnp.bfloat16
VMEM = pltpu.VMEM
SLOT = 32
LIMIT = 48 * 1024 * 1024

def layer_norm(matrix):
    average = jnp.mean(matrix, axis=-1, keepdims=True)
    power = jnp.mean(matrix * matrix, axis=-1, keepdims=True)
    return (matrix - average) * lax.rsqrt(power - average * average + 1e-06)


def attend(queries, keys, values):
    length = queries.shape[0]
    block = math.gcd(length, 512)
    scale = 1.0 / math.sqrt(queries.shape[1])

    def one_block(query_rows):
        scores = (
            lax.dot_general(
                query_rows, keys, (((1,), (1,)), ((), ())), preferred_element_type=jnp.float32
            )
            * scale
        )
        top = jnp.max(scores, axis=1, keepdims=True)
        powers = jnp.exp(scores - top)
        probs = (powers / jnp.sum(powers, axis=1, keepdims=True)).astype(jnp.bfloat16)
        return jnp.dot(probs, values, preferred_element_type=jnp.float32).astype(jnp.bfloat16)

    blocks = lax.map(one_block, queries.reshape(length // block, block, queries.shape[1]))
    return blocks.reshape(length, values.shape[1])


def local_general(patches, keep_list, qkv_weight, out_weight, up_weight, down_weight):
    seq_count = lax.axis_size("seq")
    seq_rank = lax.axis_index("seq")
    head_rank = lax.axis_index("head")
    images = patches.shape[0]
    sup_local = patches.shape[1]
    depth = patches.shape[3]
    half_width = depth // lax.axis_size("head")
    head_count = qkv_weight.shape[1]
    seq_length = sup_local * seq_count * 8 // 5
    per_owner = seq_length // seq_count
    capacity = (4 * sup_local + seq_count - 1) // seq_count
    slot_count = 4 * sup_local
    image_index = jnp.arange(images, dtype=jnp.int32)
    bounds = jnp.arange(seq_count + 1, dtype=jnp.int32) * sup_local
    before = jnp.sum((keep_list[:, :, None] < bounds[None, None, :]).astype(jnp.int32), axis=1)
    starts = bounds[None, :seq_count] + 3 * before[:, :seq_count]
    lengths = sup_local + 3 * (before[:, 1:] - before[:, :seq_count])
    my_start = lax.dynamic_index_in_dim(starts, seq_rank, 1, keepdims=False)
    my_length = lax.dynamic_index_in_dim(lengths, seq_rank, 1, keepdims=False)
    local_ids = seq_rank * sup_local + jnp.arange(sup_local, dtype=jnp.int32)
    kept_flag = jnp.any(keep_list[:, None, :] == local_ids[None, :, None], axis=2).astype(jnp.int32)
    offsets = jnp.arange(sup_local, dtype=jnp.int32)[None, :] + 3 * (
        jnp.cumsum(kept_flag, axis=1) - kept_flag
    )
    slot_ids = jnp.arange(slot_count, dtype=jnp.int32)
    owner_patch = (
        jnp.sum((offsets[:, None, :] <= slot_ids[None, :, None]).astype(jnp.int32), axis=2) - 1
    )
    start_of = jnp.take_along_axis(offsets, owner_patch, axis=1)
    sub_index = jnp.minimum(slot_ids[None, :] - start_of, 3)
    kept_of = jnp.take_along_axis(kept_flag, owner_patch, axis=1)
    flat_patches = patches.reshape(images, sup_local * 4, depth)
    fine_rows = flat_patches[
        image_index[:, None], owner_patch * 4 + jnp.where(kept_of == 1, sub_index, 0)
    ]
    mean_rows = jnp.mean(patches.astype(jnp.float32), axis=2).astype(jnp.bfloat16)
    shared_rows = mean_rows[image_index[:, None], owner_patch]
    local_tokens = jnp.where((kept_of == 1)[:, :, None], fine_rows, shared_rows)
    destinations = jnp.arange(seq_count, dtype=jnp.int32)[:, None, None]
    depth_slots = jnp.arange(capacity, dtype=jnp.int32)[None, None, :]
    positions = (destinations - my_start[None, :, None]) % seq_count + depth_slots * seq_count
    valid = positions < my_length[None, :, None]
    outgoing = local_tokens[image_index[None, :, None], jnp.minimum(positions, slot_count - 1)]
    outgoing = jnp.where(valid[:, :, :, None], outgoing, jnp.zeros((), jnp.bfloat16))
    incoming = lax.all_to_all(outgoing, "seq", split_axis=0, concat_axis=0, tiled=True)
    owned = jnp.arange(per_owner, dtype=jnp.int32) * seq_count + seq_rank
    source = jnp.sum((starts[:, None, :] <= owned[None, :, None]).astype(jnp.int32), axis=2) - 1
    first_of = jnp.take_along_axis(starts, source, axis=1)
    depth_of = (owned[None, :] - first_of) // seq_count
    resident = incoming[source, image_index[:, None], depth_of]
    start_rows = resident.reshape(images * per_owner, depth)
    start_float = start_rows.astype(jnp.float32)
    qkv_full, out_full, up_full, down_full = (
        lax.all_gather(qkv_weight, "seq", axis=0, tiled=True),
        lax.all_gather(out_weight, "seq", axis=1, tiled=True),
        lax.all_gather(up_weight, "seq", axis=0, tiled=True),
        lax.all_gather(down_weight, "seq", axis=1, tiled=True),
    )
    normed = layer_norm(start_float).astype(jnp.bfloat16).reshape(images, per_owner, depth)
    projected = jnp.einsum("ipd,dhc->ihpc", normed, qkv_full, preferred_element_type=jnp.float32)
    head_size = qkv_weight.shape[2] // 3
    sending = projected.astype(jnp.bfloat16).reshape(seq_count, per_owner, 3 * head_size)
    gathered = lax.all_to_all(sending, "seq", split_axis=0, concat_axis=0, tiled=True).reshape(
        seq_length, 3 * head_size
    )
    attended = attend(
        gathered[:, :head_size],
        gathered[:, head_size : 2 * head_size],
        gathered[:, 2 * head_size :],
    )
    returned = lax.all_to_all(
        attended.reshape(seq_count, per_owner, head_size),
        "seq",
        split_axis=0,
        concat_axis=0,
        tiled=True,
    )
    returned = returned.reshape(images, head_count, per_owner, head_size)
    partial_sum = jnp.einsum(
        "ihpc,hcd->ipd",
        returned,
        out_full.reshape(head_count, head_size, depth),
        preferred_element_type=jnp.float32,
    ).reshape(images * per_owner, depth)
    attn_total = lax.psum(partial_sum, "head")
    residual = start_float + attn_total
    residual_half = lax.dynamic_slice_in_dim(residual, head_rank * half_width, half_width, 1)
    normed_two = layer_norm(residual).astype(jnp.bfloat16)
    hidden = jax.nn.gelu(
        jnp.dot(normed_two, up_full, preferred_element_type=jnp.float32), approximate=False
    ).astype(jnp.bfloat16)
    mlp_terms = jnp.dot(hidden, down_full, preferred_element_type=jnp.float32)
    mlp_part = lax.psum_scatter(mlp_terms, "head", scatter_dimension=1, tiled=True)
    encoded = (residual_half + mlp_part).astype(jnp.bfloat16)
    return encoded.reshape(images, per_owner, 1, half_width)


def vspec():
    return pl.BlockSpec(memory_space=VMEM)


def aspec():
    return pl.BlockSpec(memory_space=pl.ANY)


def sspec():
    return pl.BlockSpec(memory_space=pltpu.SMEM)


def params():
    return pltpu.CompilerParams(vmem_limit_bytes=LIMIT)


def struct(shape, dtype=BF16):
    return jax.ShapeDtypeStruct(shape, dtype)


def pack_kernel(n, rank_ref, qkv_ref, up_ref, down_ref, *refs):
    qkv_outs, mlp_outs, sem = refs[:n], refs[n : 2 * n], refs[2 * n]
    rank = rank_ref[0]
    rows = up_ref.shape[0]
    wide = up_ref.shape[1] // n
    copies = []
    for j in range(n):
        dest = rank ^ j
        copies.append((qkv_ref.at[dest], qkv_outs[j]))
        for c in range(wide // 128):
            copies.append(
                (
                    up_ref.at[:, pl.ds(pl.multiple_of(dest * wide + c * 128, 128), 128)],
                    mlp_outs[j].at[pl.ds(c * rows, rows)],
                )
            )
        copies.append(
            (
                down_ref.at[pl.ds(pl.multiple_of(dest * wide, 128), wide)],
                mlp_outs[j].at[pl.ds(rows * wide // 128, wide)],
            )
        )
    started = []
    for i, (src, dst) in enumerate(copies):
        copy = pltpu.make_async_copy(src, dst, sem.at[i])
        copy.start()
        started.append(copy)
    for copy in started:
        copy.wait()


def pack(rank, qkv_t, up, down, n):
    wide = up.shape[1] // n
    rows = up.shape[0] * wide // 128 + wide
    copies = n * (2 + wide // 128)
    outs = pl.pallas_call(
        functools.partial(pack_kernel, n),
        in_specs=[sspec(), aspec(), aspec(), aspec()],
        out_specs=[aspec()] * (2 * n),
        out_shape=[struct(qkv_t.shape[1:])] * n + [struct((rows, 128))] * n,
        scratch_shapes=[pltpu.SemaphoreType.DMA((copies,))],
        compiler_params=params(),
    )(rank, qkv_t, up, down)
    return list(outs[:n]), list(outs[n:])


def prep_kernel(n, sup, rank_ref, keep_ref, patches_ref, *outs):
    rank = rank_ref[0]
    first = rank * sup
    keep = keep_ref[...]
    rows = 4 * sup
    count = keep.shape[0]
    lane = lax.broadcasted_iota(jnp.int32, (count, rows), 1)
    ids = first + (lane >> 2)
    kept = jnp.sum((keep == ids).astype(jnp.int32), axis=0, keepdims=True)
    below = jnp.sum(
        jnp.logical_and(keep >= first, keep < ids).astype(jnp.int32), axis=0, keepdims=True
    )
    lane_row = lax.broadcasted_iota(jnp.int32, (1, rows), 1)
    fine_pos = jnp.where(kept == 1, (lane_row >> 2) + 3 * below + (lane_row & 3), -1)
    lane_s = lax.broadcasted_iota(jnp.int32, (count, sup), 1)
    ids_s = first + lane_s
    kept_s = jnp.sum((keep == ids_s).astype(jnp.int32), axis=0, keepdims=True)
    below_s = jnp.sum(
        jnp.logical_and(keep >= first, keep < ids_s).astype(jnp.int32), axis=0, keepdims=True
    )
    lane_row_s = lax.broadcasted_iota(jnp.int32, (1, sup), 1)
    mean_pos = jnp.where(kept_s == 1, -1, lane_row_s + 3 * below_s)
    start = first + 3 * jnp.sum((keep < first).astype(jnp.int32), axis=0, keepdims=True)
    flat = patches_ref[...]
    sup_col = lax.broadcasted_iota(jnp.int32, (sup, rows), 0)
    sup_lane = lax.broadcasted_iota(jnp.int32, (sup, rows), 1) >> 2
    averaging = jnp.where(sup_col == sup_lane, 0.25, 0.0).astype(BF16)
    means = jnp.dot(averaging, flat, preferred_element_type=F32).astype(BF16)
    slot = lax.broadcasted_iota(jnp.int32, (SLOT, 1), 0)
    for j in range(n):
        pos = ((rank ^ j) - start) % n + slot * n
        fine = (pos == fine_pos).astype(F32).astype(BF16)
        mean = (pos == mean_pos).astype(F32).astype(BF16)
        outs[j][...] = (
            jnp.dot(fine, flat, preferred_element_type=F32)
            + jnp.dot(mean, means, preferred_element_type=F32)
        ).astype(BF16)


def prep(rank, keep_col, flat, half, n, sup):
    width = flat.shape[1] // 2
    return pl.pallas_call(
        functools.partial(prep_kernel_half, n, sup),
        grid_spec=pltpu.PrefetchScalarGridSpec(
            num_scalar_prefetch=1,
            grid=(1,),
            in_specs=[
                pl.BlockSpec(keep_col.shape, lambda i, ref: (0, 0)),
                pl.BlockSpec((flat.shape[0], width), lambda i, ref: (0, ref[1])),
            ],
            out_specs=[pl.BlockSpec((SLOT, width), lambda i, ref: (0, 0))] * n,
        ),
        out_shape=[struct((SLOT, width))] * n,
        compiler_params=params(),
    )(jnp.stack([rank, half]).astype(jnp.int32), keep_col, flat)


def prep_kernel_half(n, sup, scalars, keep_ref, patches_ref, *outs):
    prep_kernel(n, sup, scalars, keep_ref, patches_ref, *outs)


def pick_kernel(n, sup, per_owner, rank_ref, keep_ref, *refs):
    ins, out = refs[:n], refs[n]
    rank = rank_ref[0]
    keep = keep_ref[...]
    count = keep.shape[0]
    lanes = n * SLOT
    shift = SLOT.bit_length() - 1
    source = (lax.broadcasted_iota(jnp.int32, (count, lanes), 1) >> shift) ^ rank
    low = jnp.sum((keep < source * sup).astype(jnp.int32), axis=0, keepdims=True)
    high = jnp.sum((keep < source * sup + sup).astype(jnp.int32), axis=0, keepdims=True)
    lane = lax.broadcasted_iota(jnp.int32, (1, lanes), 1)
    source_row = (lane >> shift) ^ rank
    start = source_row * sup + 3 * low
    stop = source_row * sup + sup + 3 * high
    token = start + ((rank - start) & (n - 1)) + (lane & (SLOT - 1)) * n
    row = jnp.where(token < stop, token >> (n.bit_length() - 1), -1)
    own = lax.broadcasted_iota(jnp.int32, (per_owner, lanes), 0)
    choose = (own == row).astype(F32).astype(BF16)
    stacked = jnp.concatenate([ref[...] for ref in ins], axis=0)
    out[...] = jnp.dot(choose, stacked, preferred_element_type=F32).astype(BF16)


def pick(rank, keep_col, pieces, n, sup, per_owner):
    return pl.pallas_call(
        functools.partial(pick_kernel, n, sup, per_owner),
        in_specs=[sspec()] + [vspec()] * (n + 1),
        out_specs=vspec(),
        out_shape=struct((per_owner, pieces[0].shape[1])),
        compiler_params=params(),
    )(rank, keep_col, *pieces)


def norm_rows(x):
    average = jnp.mean(x, axis=-1, keepdims=True)
    power = jnp.mean(x * x, axis=-1, keepdims=True)
    return (x - average) * lax.rsqrt(power - average * average + 1e-06)


def attend_kernel(n, rank_ref, mine_ref, other_ref, *refs):
    weights = refs[:n]
    tokens_ref, out_ref, weight_ref = refs[n], refs[n + 1], refs[n + 2]
    rank, half = rank_ref[0], rank_ref[1]
    rows = mine_ref.shape[1]
    width = mine_ref.shape[2]
    depth = weights[0].shape[1]
    for j in range(n):
        source = rank ^ j
        at = pl.ds(pl.multiple_of(source * rows, rows), rows)
        tokens_ref[at, pl.ds(pl.multiple_of(half * width, width), width)] = mine_ref[j]
        tokens_ref[at, pl.ds(pl.multiple_of((1 - half) * width, width), width)] = other_ref[j]
        weight_ref[:, pl.ds(pl.multiple_of(source * depth, depth), depth)] = weights[j][...]
    normed = norm_rows(tokens_ref[...].astype(F32)).astype(BF16)
    projected = lax.dot_general(
        normed, weight_ref[...], (((1,), (1,)), ((), ())), preferred_element_type=F32
    ).astype(BF16)
    size = projected.shape[1] // 3
    queries = projected[:, :size]
    keys = projected[:, size : 2 * size]
    values = projected[:, 2 * size :]
    scores = lax.dot_general(
        queries, keys, (((1,), (1,)), ((), ())), preferred_element_type=F32
    ) * (1.0 / math.sqrt(size))
    powers = jnp.exp(scores - jnp.max(scores, axis=1, keepdims=True))
    probs = (powers / jnp.sum(powers, axis=1, keepdims=True)).astype(BF16)
    out_ref[...] = lax.dot_general(
        values, probs, (((0,), (1,)), ((), ())), preferred_element_type=F32
    ).astype(BF16)


def attend_fast(scalars, mine, other, weights, n):
    rows = mine.shape[0] * mine.shape[1]
    size = weights[0].shape[0] // 3
    return pl.pallas_call(
        functools.partial(attend_kernel, n),
        in_specs=[sspec()] + [vspec()] * (n + 2),
        out_specs=[vspec()] * 2,
        out_shape=[struct((rows, 2 * mine.shape[2])), struct((size, rows))],
        scratch_shapes=[VMEM((weights[0].shape[0], n * weights[0].shape[1]), BF16)],
        compiler_params=params(),
    )(scalars, mine, other, *weights)


def mlp_kernel(n, rank_ref, tokens_ref, mine_ref, other_ref, out_mine_ref, out_other_ref, *refs):
    weights = refs[:n]
    residual_ref, keep_ref, send_ref, up_ref, down_ref, row_ref, joined_ref = refs[n:]
    rank, half = rank_ref[0], rank_ref[1]
    wide, depth = down_ref.shape
    block = up_ref.shape[0] // n
    for j in range(n):
        source = rank ^ j
        for c in range(wide // 128):
            up_ref[pl.ds(pl.multiple_of(source * block, block), block), c * 128 : (c + 1) * 128] = (
                weights[j][c * block : (c + 1) * block]
            )
        down_ref[:, pl.ds(pl.multiple_of(source * 128, 128), 128)] = weights[j][
            block * wide // 128 :
        ]
    size = mine_ref.shape[1]
    for j in range(n):
        at = pl.ds(pl.multiple_of((rank ^ j) * size, size), size)
        joined_ref[0, at] = mine_ref[j]
        joined_ref[1, at] = other_ref[j]
    dims = (((0,), (0,)), ((), ()))
    row_ref[...] = (
        tokens_ref[...].astype(F32)
        + lax.dot_general(joined_ref[0], out_mine_ref[...], dims, preferred_element_type=F32)
        + lax.dot_general(joined_ref[1], out_other_ref[...], dims, preferred_element_type=F32)
    )
    part = residual_ref.shape[0]
    width = residual_ref.shape[1]
    my_cols = pl.ds(pl.multiple_of(half * width, width), width)
    other_cols = pl.ds(pl.multiple_of((1 - half) * width, width), width)
    residual_ref[...] = row_ref[pl.ds(pl.multiple_of(rank * part, part), part), my_cols]
    normed = norm_rows(row_ref[...]).astype(BF16)
    raw = jnp.dot(normed, up_ref[...], preferred_element_type=F32)
    hidden = (0.5 * raw * (1.0 + lax.erf(raw * math.sqrt(0.5)))).astype(BF16)
    keep_ref[...] = jnp.dot(hidden, down_ref[:, my_cols], preferred_element_type=F32)
    send_ref[...] = jnp.dot(hidden, down_ref[:, other_cols], preferred_element_type=F32).astype(BF16)


def mlp(scalars, tokens, mine, other, out_mine, out_other, weights, n, wide):
    length, depth = tokens.shape
    width = depth // 2
    return pl.pallas_call(
        functools.partial(mlp_kernel, n),
        in_specs=[sspec()] + [vspec()] * (n + 5),
        out_specs=[vspec()] * 3,
        out_shape=[
            struct((length // n, width), F32),
            struct((length, width), F32),
            struct((length, width)),
        ],
        scratch_shapes=[
            VMEM((depth, wide), BF16),
            VMEM((wide, depth), BF16),
            VMEM((length, depth), F32),
            VMEM((2, mine.shape[0] * mine.shape[1], length), BF16),
        ],
        compiler_params=params(),
    )(scalars, tokens, mine, other, out_mine, out_other, *weights)


def join_kernel(n, rank_ref, keep_ref, got_ref, residual_ref, base_ref, *outs):
    rank = rank_ref[0]
    part = residual_ref.shape[0]
    for j in range(n):
        at = pl.ds(pl.multiple_of((rank ^ j) * part, part), part)
        total = keep_ref[at] + got_ref[at].astype(F32)
        if j == 0:
            base_ref[...] = total + residual_ref[...]
        else:
            outs[j - 1][...] = total.astype(BF16)


def join(scalars, keep, got, residual, n):
    part, width = residual.shape
    outs = pl.pallas_call(
        functools.partial(join_kernel, n),
        in_specs=[sspec()] + [vspec()] * 3,
        out_specs=[vspec()] * n,
        out_shape=[struct((part, width), F32)] + [struct((part, width))] * (n - 1),
        compiler_params=params(),
    )(scalars, keep, got, residual)
    return outs[0], list(outs[1:])


def last_kernel(base_ref, *refs):
    total = base_ref[...]
    for ref in refs[:-1]:
        total = total + ref[...].astype(F32)
    refs[-1][...] = total.astype(BF16)


def last(base, terms):
    return pl.pallas_call(
        last_kernel,
        in_specs=[vspec()] * (1 + len(terms)),
        out_specs=vspec(),
        out_shape=struct(base.shape),
        compiler_params=params(),
    )(base, *terms)


def swap(value, axis, j):
    n = lax.axis_size(axis)
    return lax.ppermute(value, axis, [(i, i ^ j) for i in range(n)])


def local_fast(patches, keep_list, qkv_weight, out_weight, up_weight, down_weight):
    n = lax.axis_size("seq")
    rank = lax.axis_index("seq").astype(jnp.int32)
    half = lax.axis_index("head").astype(jnp.int32)
    sup, depth = patches.shape[1], patches.shape[3]
    length = sup * n * 8 // 5
    per_owner = length // n
    wide = up_weight.shape[1] // n
    scalars = jnp.stack([rank, half])
    keep_col = keep_list.reshape(-1, 1)
    flat = patches.reshape(4 * sup, depth)
    out_mine = lax.all_gather(out_weight, "seq", axis=1, tiled=True)
    out_other = swap(out_mine, "head", 1)
    slots = prep(rank, keep_col, flat, half, n, sup)
    qkv_blocks, mlp_blocks = pack(scalars, qkv_weight.transpose(1, 2, 0), up_weight, down_weight, n)
    dealt = [slots[0]] + [swap(slots[j], "seq", j) for j in range(1, n)]
    qkv_got = [qkv_blocks[0]] + [swap(qkv_blocks[j], "seq", j) for j in range(1, n)]
    owned = pick(scalars, keep_col, dealt, n, sup, per_owner)
    pieces = jnp.stack([owned] + [swap(owned, "seq", j) for j in range(1, n)])
    pieces_other = swap(pieces, "head", 1)
    mlp_got = [mlp_blocks[0]] + [swap(mlp_blocks[j], "seq", j) for j in range(1, n)]
    tokens, attended = attend_fast(scalars, pieces, pieces_other, qkv_got, n)
    pair = jnp.stack([attended, swap(attended, "seq", n // 2)])
    quads = [pair] + [swap(pair, "seq", j) for j in range(1, n // 2)]
    gathered = jnp.stack([quad[k] for k in range(2) for quad in quads])
    gathered_other = swap(gathered, "head", 1)
    residual, keep, send = mlp(
        scalars, tokens, gathered, gathered_other, out_mine, out_other, mlp_got, n, wide
    )
    got = swap(send, "head", 1)
    base, terms = join(scalars, keep, got, residual, n)
    terms = [swap(terms[j - 1], "seq", j) for j in range(1, n)]
    encoded = last(base, terms)
    return encoded.reshape(1, per_owner, 1, depth // 2)


def local(patches, keep_list, qkv_weight, out_weight, up_weight, down_weight):
    n = lax.axis_size("seq")
    one_image = patches.shape[0] == 1 and qkv_weight.shape[1] == n and n & (n - 1) == 0
    plan = local_fast if one_image else local_general
    return plan(patches, keep_list, qkv_weight, out_weight, up_weight, down_weight)


def solution(mesh):
    return jax.shard_map(
        local,
        mesh=mesh,
        in_specs=(
            P("groups", "seq", None, None),
            P("groups", None),
            P("seq", "head", None),
            P("head", "seq"),
            P("seq", "head"),
            P("head", "seq"),
        ),
        out_specs=P("groups", None, "seq", "head"),
        check_vma=False,
    )
```

```python
import functools
import math

import jax
import jax.numpy as jnp
from jax import lax
from jax.experimental import pallas as pl
from jax.experimental.pallas import tpu as pltpu
from jax.sharding import PartitionSpec as P

F32 = jnp.float32
BF16 = jnp.bfloat16
VMEM = pltpu.VMEM
SLOT = 32
LIMIT = 48 * 1024 * 1024

def layer_norm(matrix):
    average = jnp.mean(matrix, axis=-1, keepdims=True)
    power = jnp.mean(matrix * matrix, axis=-1, keepdims=True)
    return (matrix - average) * lax.rsqrt(power - average * average + 1e-06)


def attend(queries, keys, values):
    length = queries.shape[0]
    block = math.gcd(length, 512)
    scale = 1.0 / math.sqrt(queries.shape[1])

    def one_block(query_rows):
        scores = (
            lax.dot_general(
                query_rows, keys, (((1,), (1,)), ((), ())), preferred_element_type=jnp.float32
            )
            * scale
        )
        top = jnp.max(scores, axis=1, keepdims=True)
        powers = jnp.exp(scores - top)
        probs = (powers / jnp.sum(powers, axis=1, keepdims=True)).astype(jnp.bfloat16)
        return jnp.dot(probs, values, preferred_element_type=jnp.float32).astype(jnp.bfloat16)

    blocks = lax.map(one_block, queries.reshape(length // block, block, queries.shape[1]))
    return blocks.reshape(length, values.shape[1])


def local_general(patches, keep_list, qkv_weight, out_weight, up_weight, down_weight):
    seq_count = lax.axis_size("seq")
    seq_rank = lax.axis_index("seq")
    head_rank = lax.axis_index("head")
    images = patches.shape[0]
    sup_local = patches.shape[1]
    depth = patches.shape[3]
    half_width = depth // lax.axis_size("head")
    head_count = qkv_weight.shape[1]
    seq_length = sup_local * seq_count * 8 // 5
    per_owner = seq_length // seq_count
    capacity = (4 * sup_local + seq_count - 1) // seq_count
    slot_count = 4 * sup_local
    image_index = jnp.arange(images, dtype=jnp.int32)
    bounds = jnp.arange(seq_count + 1, dtype=jnp.int32) * sup_local
    before = jnp.sum((keep_list[:, :, None] < bounds[None, None, :]).astype(jnp.int32), axis=1)
    starts = bounds[None, :seq_count] + 3 * before[:, :seq_count]
    lengths = sup_local + 3 * (before[:, 1:] - before[:, :seq_count])
    my_start = lax.dynamic_index_in_dim(starts, seq_rank, 1, keepdims=False)
    my_length = lax.dynamic_index_in_dim(lengths, seq_rank, 1, keepdims=False)
    local_ids = seq_rank * sup_local + jnp.arange(sup_local, dtype=jnp.int32)
    kept_flag = jnp.any(keep_list[:, None, :] == local_ids[None, :, None], axis=2).astype(jnp.int32)
    offsets = jnp.arange(sup_local, dtype=jnp.int32)[None, :] + 3 * (
        jnp.cumsum(kept_flag, axis=1) - kept_flag
    )
    slot_ids = jnp.arange(slot_count, dtype=jnp.int32)
    owner_patch = (
        jnp.sum((offsets[:, None, :] <= slot_ids[None, :, None]).astype(jnp.int32), axis=2) - 1
    )
    start_of = jnp.take_along_axis(offsets, owner_patch, axis=1)
    sub_index = jnp.minimum(slot_ids[None, :] - start_of, 3)
    kept_of = jnp.take_along_axis(kept_flag, owner_patch, axis=1)
    flat_patches = patches.reshape(images, sup_local * 4, depth)
    fine_rows = flat_patches[
        image_index[:, None], owner_patch * 4 + jnp.where(kept_of == 1, sub_index, 0)
    ]
    mean_rows = jnp.mean(patches.astype(jnp.float32), axis=2).astype(jnp.bfloat16)
    shared_rows = mean_rows[image_index[:, None], owner_patch]
    local_tokens = jnp.where((kept_of == 1)[:, :, None], fine_rows, shared_rows)
    destinations = jnp.arange(seq_count, dtype=jnp.int32)[:, None, None]
    depth_slots = jnp.arange(capacity, dtype=jnp.int32)[None, None, :]
    positions = (destinations - my_start[None, :, None]) % seq_count + depth_slots * seq_count
    valid = positions < my_length[None, :, None]
    outgoing = local_tokens[image_index[None, :, None], jnp.minimum(positions, slot_count - 1)]
    outgoing = jnp.where(valid[:, :, :, None], outgoing, jnp.zeros((), jnp.bfloat16))
    incoming = lax.all_to_all(outgoing, "seq", split_axis=0, concat_axis=0, tiled=True)
    owned = jnp.arange(per_owner, dtype=jnp.int32) * seq_count + seq_rank
    source = jnp.sum((starts[:, None, :] <= owned[None, :, None]).astype(jnp.int32), axis=2) - 1
    first_of = jnp.take_along_axis(starts, source, axis=1)
    depth_of = (owned[None, :] - first_of) // seq_count
    resident = incoming[source, image_index[:, None], depth_of]
    start_rows = resident.reshape(images * per_owner, depth)
    start_float = start_rows.astype(jnp.float32)
    qkv_full, out_full, up_full, down_full = (
        lax.all_gather(qkv_weight, "seq", axis=0, tiled=True),
        lax.all_gather(out_weight, "seq", axis=1, tiled=True),
        lax.all_gather(up_weight, "seq", axis=0, tiled=True),
        lax.all_gather(down_weight, "seq", axis=1, tiled=True),
    )
    normed = layer_norm(start_float).astype(jnp.bfloat16).reshape(images, per_owner, depth)
    projected = jnp.einsum("ipd,dhc->ihpc", normed, qkv_full, preferred_element_type=jnp.float32)
    head_size = qkv_weight.shape[2] // 3
    sending = projected.astype(jnp.bfloat16).reshape(seq_count, per_owner, 3 * head_size)
    gathered = lax.all_to_all(sending, "seq", split_axis=0, concat_axis=0, tiled=True).reshape(
        seq_length, 3 * head_size
    )
    attended = attend(
        gathered[:, :head_size],
        gathered[:, head_size : 2 * head_size],
        gathered[:, 2 * head_size :],
    )
    returned = lax.all_to_all(
        attended.reshape(seq_count, per_owner, head_size),
        "seq",
        split_axis=0,
        concat_axis=0,
        tiled=True,
    )
    returned = returned.reshape(images, head_count, per_owner, head_size)
    partial_sum = jnp.einsum(
        "ihpc,hcd->ipd",
        returned,
        out_full.reshape(head_count, head_size, depth),
        preferred_element_type=jnp.float32,
    ).reshape(images * per_owner, depth)
    attn_total = lax.psum(partial_sum, "head")
    residual = start_float + attn_total
    residual_half = lax.dynamic_slice_in_dim(residual, head_rank * half_width, half_width, 1)
    normed_two = layer_norm(residual).astype(jnp.bfloat16)
    hidden = jax.nn.gelu(
        jnp.dot(normed_two, up_full, preferred_element_type=jnp.float32), approximate=False
    ).astype(jnp.bfloat16)
    mlp_terms = jnp.dot(hidden, down_full, preferred_element_type=jnp.float32)
    mlp_part = lax.psum_scatter(mlp_terms, "head", scatter_dimension=1, tiled=True)
    encoded = (residual_half + mlp_part).astype(jnp.bfloat16)
    return encoded.reshape(images, per_owner, 1, half_width)


def vspec():
    return pl.BlockSpec(memory_space=VMEM)


def aspec():
    return pl.BlockSpec(memory_space=pl.ANY)


def sspec():
    return pl.BlockSpec(memory_space=pltpu.SMEM)


def params():
    return pltpu.CompilerParams(vmem_limit_bytes=LIMIT)


def struct(shape, dtype=BF16):
    return jax.ShapeDtypeStruct(shape, dtype)


def pack_kernel(n, rank_ref, up_ref, down_ref, out_ref, sem):
    part = rank_ref[2]
    rows = up_ref.shape[0]
    wide = up_ref.shape[1] // n
    keep = wide // 2
    copies = []
    for j in range(n):
        columns = pl.ds(pl.multiple_of(j * wide + part * keep, 128), keep)
        at = pl.ds(pl.multiple_of(j * wide + part * keep, 128), keep)
        copies.append((up_ref.at[:, columns], out_ref.at[j, pl.ds(0, rows)]))
        copies.append((down_ref.at[at], out_ref.at[j, pl.ds(rows, keep)]))
    started = []
    for i, (src, dst) in enumerate(copies):
        copy = pltpu.make_async_copy(src, dst, sem.at[i])
        copy.start()
        started.append(copy)
    for copy in started:
        copy.wait()


def pack(scalars, up, down, n):
    keep = up.shape[1] // n // 2
    return pl.pallas_call(
        functools.partial(pack_kernel, n),
        in_specs=[sspec(), aspec(), aspec()],
        out_specs=aspec(),
        out_shape=struct((n, up.shape[0] + keep, keep)),
        scratch_shapes=[pltpu.SemaphoreType.DMA((2 * n,))],
        compiler_params=params(),
    )(scalars, up, down)


def prep_kernel(n, sup, rank_ref, keep_ref, patches_ref, out_ref):
    rank = rank_ref[0]
    first = rank * sup
    keep = keep_ref[...]
    rows = 4 * sup
    count = keep.shape[0]
    lane = lax.broadcasted_iota(jnp.int32, (count, rows), 1)
    ids = first + (lane >> 2)
    kept = jnp.sum((keep == ids).astype(jnp.int32), axis=0, keepdims=True)
    below = jnp.sum(
        jnp.logical_and(keep >= first, keep < ids).astype(jnp.int32), axis=0, keepdims=True
    )
    lane_row = lax.broadcasted_iota(jnp.int32, (1, rows), 1)
    fine_pos = jnp.where(kept == 1, (lane_row >> 2) + 3 * below + (lane_row & 3), -1)
    lane_s = lax.broadcasted_iota(jnp.int32, (count, sup), 1)
    ids_s = first + lane_s
    kept_s = jnp.sum((keep == ids_s).astype(jnp.int32), axis=0, keepdims=True)
    below_s = jnp.sum(
        jnp.logical_and(keep >= first, keep < ids_s).astype(jnp.int32), axis=0, keepdims=True
    )
    lane_row_s = lax.broadcasted_iota(jnp.int32, (1, sup), 1)
    mean_pos = jnp.where(kept_s == 1, -1, lane_row_s + 3 * below_s)
    start = first + 3 * jnp.sum((keep < first).astype(jnp.int32), axis=0, keepdims=True)
    flat = patches_ref[...]
    sup_col = lax.broadcasted_iota(jnp.int32, (sup, rows), 0)
    sup_lane = lax.broadcasted_iota(jnp.int32, (sup, rows), 1) >> 2
    averaging = jnp.where(sup_col == sup_lane, 0.25, 0.0).astype(BF16)
    means = jnp.dot(averaging, flat, preferred_element_type=F32).astype(BF16)
    slot = lax.broadcasted_iota(jnp.int32, (SLOT, 1), 0)
    for j in range(n):
        pos = ((j - start) & (n - 1)) + slot * n
        fine = (pos == fine_pos).astype(F32).astype(BF16)
        mean = (pos == mean_pos).astype(F32).astype(BF16)
        out_ref[j] = (
            jnp.dot(fine, flat, preferred_element_type=F32)
            + jnp.dot(mean, means, preferred_element_type=F32)
        ).astype(BF16)


def prep(scalars, keep_col, flat, n, sup):
    width = flat.shape[1] // 2
    return pl.pallas_call(
        functools.partial(prep_kernel, n, sup),
        grid_spec=pltpu.PrefetchScalarGridSpec(
            num_scalar_prefetch=1,
            grid=(1,),
            in_specs=[
                pl.BlockSpec(keep_col.shape, lambda i, ref: (0, 0)),
                pl.BlockSpec((flat.shape[0], width), lambda i, ref: (0, ref[1])),
            ],
            out_specs=pl.BlockSpec((n, SLOT, width), lambda i, ref: (0, 0, 0)),
        ),
        out_shape=struct((n, SLOT, width)),
        compiler_params=params(),
    )(scalars, keep_col, flat)


def pick_kernel(n, sup, per_owner, rank_ref, keep_ref, got_ref, out_ref):
    rank = rank_ref[0]
    keep = keep_ref[...]
    count = keep.shape[0]
    lanes = n * SLOT
    shift = SLOT.bit_length() - 1
    source = (lax.broadcasted_iota(jnp.int32, (count, lanes), 1) >> shift)
    low = jnp.sum((keep < source * sup).astype(jnp.int32), axis=0, keepdims=True)
    high = jnp.sum((keep < source * sup + sup).astype(jnp.int32), axis=0, keepdims=True)
    lane = lax.broadcasted_iota(jnp.int32, (1, lanes), 1)
    source_row = lane >> shift
    start = source_row * sup + 3 * low
    stop = source_row * sup + sup + 3 * high
    token = start + ((rank - start) & (n - 1)) + (lane & (SLOT - 1)) * n
    row = jnp.where(token < stop, token >> (n.bit_length() - 1), -1)
    own = lax.broadcasted_iota(jnp.int32, (per_owner, lanes), 0)
    choose = (own == row).astype(F32).astype(BF16)
    stacked = got_ref[...].reshape(lanes, got_ref.shape[2])
    owned = jnp.dot(choose, stacked, preferred_element_type=F32).astype(BF16)
    for j in range(n):
        out_ref[j] = owned


def pick(scalars, keep_col, got, n, sup, per_owner):
    return pl.pallas_call(
        functools.partial(pick_kernel, n, sup, per_owner),
        in_specs=[sspec(), vspec(), vspec()],
        out_specs=vspec(),
        out_shape=struct((n, per_owner, got.shape[2])),
        compiler_params=params(),
    )(scalars, keep_col, got)


def norm_rows(x):
    average = jnp.mean(x, axis=-1, keepdims=True)
    power = jnp.mean(x * x, axis=-1, keepdims=True)
    return (x - average) * lax.rsqrt(power - average * average + 1e-06)


def attend_kernel(n, rank_ref, mine_ref, other_ref, got_ref, tokens_ref, out_ref, weight_ref):
    half = rank_ref[1]
    rows, width = mine_ref.shape
    depth = got_ref.shape[2]
    tokens_ref[:, pl.ds(pl.multiple_of(half * width, width), width)] = mine_ref[...]
    tokens_ref[:, pl.ds(pl.multiple_of((1 - half) * width, width), width)] = other_ref[...]
    for j in range(n):
        weight_ref[:, j * depth : (j + 1) * depth] = got_ref[j]
    normed = norm_rows(tokens_ref[...].astype(F32)).astype(BF16)
    projected = lax.dot_general(
        normed, weight_ref[...], (((1,), (1,)), ((), ())), preferred_element_type=F32
    ).astype(BF16)
    size = projected.shape[1] // 3
    queries = projected[:, :size]
    keys = projected[:, size : 2 * size]
    values = projected[:, 2 * size :]
    scores = lax.dot_general(
        queries, keys, (((1,), (1,)), ((), ())), preferred_element_type=F32
    ) * (1.0 / math.sqrt(size))
    powers = jnp.exp(scores - jnp.max(scores, axis=1, keepdims=True))
    probs = (powers / jnp.sum(powers, axis=1, keepdims=True)).astype(BF16)
    attended = lax.dot_general(
        values, probs, (((0,), (1,)), ((), ())), preferred_element_type=F32
    ).astype(BF16)
    for j in range(n):
        out_ref[j] = attended


def attend_fast(scalars, mine, other, weights, n):
    rows, width = mine.shape
    size = weights.shape[1] // 3
    return pl.pallas_call(
        functools.partial(attend_kernel, n),
        in_specs=[sspec()] + [vspec()] * 3,
        out_specs=[vspec()] * 2,
        out_shape=[struct((rows, 2 * width)), struct((n, size, rows))],
        scratch_shapes=[VMEM((weights.shape[1], n * weights.shape[2]), BF16)],
        compiler_params=params(),
    )(scalars, mine, other, weights)


def mlp_kernel(
    n,
    rank_ref,
    tokens_ref,
    mine_ref,
    other_ref,
    out_mine_ref,
    out_other_ref,
    first_ref,
    second_ref,
    residual_ref,
    keep_ref,
    send_ref,
    up_ref,
    down_ref,
    row_ref,
):
    rank, half = rank_ref[0], rank_ref[1]
    block = up_ref.shape[0] // n
    unit = first_ref.shape[2]
    for j in range(n):
        for c, got_ref in enumerate((first_ref, second_ref)):
            units = pl.ds(c * unit, unit)
            up_ref[j * block : (j + 1) * block, units] = got_ref[j, :block]
            down_ref[units, j * 128 : (j + 1) * 128] = got_ref[j, block:]
    dims = (((0,), (0,)), ((), ()))
    row_ref[...] = (
        tokens_ref[...].astype(F32)
        + lax.dot_general(mine_ref[...], out_mine_ref[...], dims, preferred_element_type=F32)
        + lax.dot_general(other_ref[...], out_other_ref[...], dims, preferred_element_type=F32)
    )
    part = residual_ref.shape[0]
    width = residual_ref.shape[1]
    my_cols = pl.ds(pl.multiple_of(half * width, width), width)
    other_cols = pl.ds(pl.multiple_of((1 - half) * width, width), width)
    residual_ref[...] = row_ref[pl.ds(pl.multiple_of(rank * part, part), part), my_cols]
    normed = norm_rows(row_ref[...]).astype(BF16)
    raw = jnp.dot(normed, up_ref[...], preferred_element_type=F32)
    hidden = (0.5 * raw * (1.0 + lax.erf(raw * math.sqrt(0.5)))).astype(BF16)
    keep_ref[...] = jnp.dot(hidden, down_ref[:, my_cols], preferred_element_type=F32)
    send_ref[...] = jnp.dot(hidden, down_ref[:, other_cols], preferred_element_type=F32).astype(BF16)


def mlp(scalars, tokens, mine, other, out_mine, out_other, first, second, n):
    length, depth = tokens.shape
    width = depth // 2
    wide = 2 * first.shape[2]
    return pl.pallas_call(
        functools.partial(mlp_kernel, n),
        in_specs=[sspec()] + [vspec()] * 7,
        out_specs=[vspec()] * 3,
        out_shape=[
            struct((length // n, width), F32),
            struct((length, width), F32),
            struct((length, width)),
        ],
        scratch_shapes=[
            VMEM((depth, wide), BF16),
            VMEM((wide, depth), BF16),
            VMEM((length, depth), F32),
        ],
        compiler_params=params(),
    )(scalars, tokens, mine, other, out_mine, out_other, first, second)


def join_kernel(rank_ref, keep_ref, got_ref, residual_ref, base_ref, out_ref):
    part = residual_ref.shape[0]
    mine = pl.ds(pl.multiple_of(rank_ref[0] * part, part), part)
    base_ref[...] = keep_ref[mine] + got_ref[mine].astype(F32) + residual_ref[...]
    out_ref[...] = (keep_ref[...] + got_ref[...].astype(F32)).astype(BF16)


def join(scalars, keep, got, residual):
    return pl.pallas_call(
        join_kernel,
        in_specs=[sspec()] + [vspec()] * 3,
        out_specs=[vspec()] * 2,
        out_shape=[struct(residual.shape, F32), struct(keep.shape)],
        compiler_params=params(),
    )(scalars, keep, got, residual)


def last_kernel(n, rank_ref, base_ref, terms_ref, out_ref):
    rank = rank_ref[0]
    total = base_ref[...]
    for j in range(1, n):
        total = total + terms_ref[rank ^ j].astype(F32)
    out_ref[...] = total.astype(BF16)


def last(scalars, base, terms):
    return pl.pallas_call(
        functools.partial(last_kernel, terms.shape[0]),
        in_specs=[sspec()] + [vspec()] * 2,
        out_specs=vspec(),
        out_shape=struct(base.shape),
        compiler_params=params(),
    )(scalars, base, terms)


def swap(value, axis, j):
    n = lax.axis_size(axis)
    return lax.ppermute(value, axis, [(i, i ^ j) for i in range(n)])


def exchange(value):
    return lax.all_to_all(value, "seq", split_axis=0, concat_axis=0, tiled=True)


def after(value, *others):
    return lax.optimization_barrier((value, *others))[0]


def local_fast(patches, keep_list, qkv_weight, out_weight, up_weight, down_weight):
    n = lax.axis_size("seq")
    scalars = jnp.stack(
        [lax.axis_index(name).astype(jnp.int32) for name in ("seq", "head", "groups")]
    )
    sup, depth = patches.shape[1], patches.shape[3]
    length = sup * n * 8 // 5
    per_owner = length // n
    half_width = depth // 2
    keep_col = keep_list.reshape(-1, 1)
    flat = patches.reshape(4 * sup, depth)
    out_mine = lax.all_gather(out_weight, "seq", axis=1, tiled=True)
    out_other = swap(out_mine, "head", 1)
    slots = prep(scalars, keep_col, flat, n, sup)
    packed = pack(scalars, up_weight, down_weight, n)
    dealt = exchange(slots)
    qkv_got = exchange(after(qkv_weight.transpose(1, 2, 0), slots))
    owned = pick(scalars, keep_col, dealt, n, sup, per_owner)
    pieces = exchange(owned).reshape(length, half_width)
    first = exchange(after(packed, owned))
    pieces_other = swap(pieces, "head", 1)
    second = swap(first, "groups", 1)
    tokens, attended = attend_fast(scalars, pieces, pieces_other, qkv_got, n)
    gathered = exchange(attended).reshape(half_width, length)
    gathered_other = swap(gathered, "head", 1)
    residual, keep, send = mlp(
        scalars, tokens, gathered, gathered_other, out_mine, out_other, first, second, n
    )
    got = swap(send, "head", 1)
    base, terms = join(scalars, keep, got, residual)
    terms = exchange(terms.reshape(n, per_owner, half_width))
    encoded = last(scalars, base, terms)
    return encoded.reshape(1, per_owner, 1, half_width)


def local(patches, keep_list, qkv_weight, out_weight, up_weight, down_weight):
    n = lax.axis_size("seq")
    one_image = patches.shape[0] == 1 and qkv_weight.shape[1] == n and n & (n - 1) == 0
    one_image = one_image and lax.axis_size("groups") == 2 and up_weight.shape[1] == n * 256
    plan = local_fast if one_image else local_general
    return plan(patches, keep_list, qkv_weight, out_weight, up_weight, down_weight)


def solution(mesh):
    return jax.shard_map(
        local,
        mesh=mesh,
        in_specs=(
            P("groups", "seq", None, None),
            P("groups", None),
            P("seq", "head", None),
            P("head", "seq"),
            P("seq", "head"),
            P("head", "seq"),
        ),
        out_specs=P("groups", None, "seq", "head"),
        check_vma=False,
    )
```

```python
import functools
import math

import jax
import jax.numpy as jnp
from jax import lax
from jax.experimental import pallas as pl
from jax.experimental.pallas import tpu as pltpu
from jax.sharding import PartitionSpec as P

F32 = jnp.float32
BF16 = jnp.bfloat16
VMEM = pltpu.VMEM
SLOT = 32
LIMIT = 32 * 1024 * 1024

def layer_norm(matrix):
    average = jnp.mean(matrix, axis=-1, keepdims=True)
    power = jnp.mean(matrix * matrix, axis=-1, keepdims=True)
    return (matrix - average) * lax.rsqrt(power - average * average + 1e-06)


def attend(queries, keys, values):
    length = queries.shape[0]
    block = math.gcd(length, 512)
    scale = 1.0 / math.sqrt(queries.shape[1])

    def one_block(query_rows):
        scores = (
            lax.dot_general(
                query_rows, keys, (((1,), (1,)), ((), ())), preferred_element_type=jnp.float32
            )
            * scale
        )
        top = jnp.max(scores, axis=1, keepdims=True)
        powers = jnp.exp(scores - top)
        probs = (powers / jnp.sum(powers, axis=1, keepdims=True)).astype(jnp.bfloat16)
        return jnp.dot(probs, values, preferred_element_type=jnp.float32).astype(jnp.bfloat16)

    blocks = lax.map(one_block, queries.reshape(length // block, block, queries.shape[1]))
    return blocks.reshape(length, values.shape[1])


def local_general(patches, keep_list, qkv_weight, out_weight, up_weight, down_weight):
    seq_count = lax.axis_size("seq")
    seq_rank = lax.axis_index("seq")
    head_rank = lax.axis_index("head")
    images = patches.shape[0]
    sup_local = patches.shape[1]
    depth = patches.shape[3]
    half_width = depth // lax.axis_size("head")
    head_count = qkv_weight.shape[1]
    seq_length = sup_local * seq_count * 8 // 5
    per_owner = seq_length // seq_count
    capacity = (4 * sup_local + seq_count - 1) // seq_count
    slot_count = 4 * sup_local
    image_index = jnp.arange(images, dtype=jnp.int32)
    bounds = jnp.arange(seq_count + 1, dtype=jnp.int32) * sup_local
    before = jnp.sum((keep_list[:, :, None] < bounds[None, None, :]).astype(jnp.int32), axis=1)
    starts = bounds[None, :seq_count] + 3 * before[:, :seq_count]
    lengths = sup_local + 3 * (before[:, 1:] - before[:, :seq_count])
    my_start = lax.dynamic_index_in_dim(starts, seq_rank, 1, keepdims=False)
    my_length = lax.dynamic_index_in_dim(lengths, seq_rank, 1, keepdims=False)
    local_ids = seq_rank * sup_local + jnp.arange(sup_local, dtype=jnp.int32)
    kept_flag = jnp.any(keep_list[:, None, :] == local_ids[None, :, None], axis=2).astype(jnp.int32)
    offsets = jnp.arange(sup_local, dtype=jnp.int32)[None, :] + 3 * (
        jnp.cumsum(kept_flag, axis=1) - kept_flag
    )
    slot_ids = jnp.arange(slot_count, dtype=jnp.int32)
    owner_patch = (
        jnp.sum((offsets[:, None, :] <= slot_ids[None, :, None]).astype(jnp.int32), axis=2) - 1
    )
    start_of = jnp.take_along_axis(offsets, owner_patch, axis=1)
    sub_index = jnp.minimum(slot_ids[None, :] - start_of, 3)
    kept_of = jnp.take_along_axis(kept_flag, owner_patch, axis=1)
    flat_patches = patches.reshape(images, sup_local * 4, depth)
    fine_rows = flat_patches[
        image_index[:, None], owner_patch * 4 + jnp.where(kept_of == 1, sub_index, 0)
    ]
    mean_rows = jnp.mean(patches.astype(jnp.float32), axis=2).astype(jnp.bfloat16)
    shared_rows = mean_rows[image_index[:, None], owner_patch]
    local_tokens = jnp.where((kept_of == 1)[:, :, None], fine_rows, shared_rows)
    destinations = jnp.arange(seq_count, dtype=jnp.int32)[:, None, None]
    depth_slots = jnp.arange(capacity, dtype=jnp.int32)[None, None, :]
    positions = (destinations - my_start[None, :, None]) % seq_count + depth_slots * seq_count
    valid = positions < my_length[None, :, None]
    outgoing = local_tokens[image_index[None, :, None], jnp.minimum(positions, slot_count - 1)]
    outgoing = jnp.where(valid[:, :, :, None], outgoing, jnp.zeros((), jnp.bfloat16))
    incoming = lax.all_to_all(outgoing, "seq", split_axis=0, concat_axis=0, tiled=True)
    owned = jnp.arange(per_owner, dtype=jnp.int32) * seq_count + seq_rank
    source = jnp.sum((starts[:, None, :] <= owned[None, :, None]).astype(jnp.int32), axis=2) - 1
    first_of = jnp.take_along_axis(starts, source, axis=1)
    depth_of = (owned[None, :] - first_of) // seq_count
    resident = incoming[source, image_index[:, None], depth_of]
    start_rows = resident.reshape(images * per_owner, depth)
    start_float = start_rows.astype(jnp.float32)
    qkv_full, out_full, up_full, down_full = (
        lax.all_gather(qkv_weight, "seq", axis=0, tiled=True),
        lax.all_gather(out_weight, "seq", axis=1, tiled=True),
        lax.all_gather(up_weight, "seq", axis=0, tiled=True),
        lax.all_gather(down_weight, "seq", axis=1, tiled=True),
    )
    normed = layer_norm(start_float).astype(jnp.bfloat16).reshape(images, per_owner, depth)
    projected = jnp.einsum("ipd,dhc->ihpc", normed, qkv_full, preferred_element_type=jnp.float32)
    head_size = qkv_weight.shape[2] // 3
    sending = projected.astype(jnp.bfloat16).reshape(seq_count, per_owner, 3 * head_size)
    gathered = lax.all_to_all(sending, "seq", split_axis=0, concat_axis=0, tiled=True).reshape(
        seq_length, 3 * head_size
    )
    attended = attend(
        gathered[:, :head_size],
        gathered[:, head_size : 2 * head_size],
        gathered[:, 2 * head_size :],
    )
    returned = lax.all_to_all(
        attended.reshape(seq_count, per_owner, head_size),
        "seq",
        split_axis=0,
        concat_axis=0,
        tiled=True,
    )
    returned = returned.reshape(images, head_count, per_owner, head_size)
    partial_sum = jnp.einsum(
        "ihpc,hcd->ipd",
        returned,
        out_full.reshape(head_count, head_size, depth),
        preferred_element_type=jnp.float32,
    ).reshape(images * per_owner, depth)
    attn_total = lax.psum(partial_sum, "head")
    residual = start_float + attn_total
    residual_half = lax.dynamic_slice_in_dim(residual, head_rank * half_width, half_width, 1)
    normed_two = layer_norm(residual).astype(jnp.bfloat16)
    hidden = jax.nn.gelu(
        jnp.dot(normed_two, up_full, preferred_element_type=jnp.float32), approximate=False
    ).astype(jnp.bfloat16)
    mlp_terms = jnp.dot(hidden, down_full, preferred_element_type=jnp.float32)
    mlp_part = lax.psum_scatter(mlp_terms, "head", scatter_dimension=1, tiled=True)
    encoded = (residual_half + mlp_part).astype(jnp.bfloat16)
    return encoded.reshape(images, per_owner, 1, half_width)


def vspec():
    return pl.BlockSpec(memory_space=VMEM)


def aspec():
    return pl.BlockSpec(memory_space=pl.ANY)


def sspec():
    return pl.BlockSpec(memory_space=pltpu.SMEM)


def params():
    return pltpu.CompilerParams(vmem_limit_bytes=LIMIT)


def cost(micros):
    return pl.CostEstimate(flops=micros * 10**9, bytes_accessed=1 << 20, transcendentals=0)


def struct(shape, dtype=BF16):
    return jax.ShapeDtypeStruct(shape, dtype)


def prep_kernel(n, sup, rank_ref, keep_ref, patches_ref, qkv_ref, out_ref):
    rank = rank_ref[0]
    first = rank * sup
    keep = keep_ref[...]
    rows = 4 * sup
    count = keep.shape[0]
    lane = lax.broadcasted_iota(jnp.int32, (count, rows), 1)
    ids = first + (lane >> 2)
    kept = jnp.sum((keep == ids).astype(jnp.int32), axis=0, keepdims=True)
    below = jnp.sum(
        jnp.logical_and(keep >= first, keep < ids).astype(jnp.int32), axis=0, keepdims=True
    )
    lane_row = lax.broadcasted_iota(jnp.int32, (1, rows), 1)
    fine_pos = jnp.where(kept == 1, (lane_row >> 2) + 3 * below + (lane_row & 3), -1)
    lane_s = lax.broadcasted_iota(jnp.int32, (count, sup), 1)
    ids_s = first + lane_s
    kept_s = jnp.sum((keep == ids_s).astype(jnp.int32), axis=0, keepdims=True)
    below_s = jnp.sum(
        jnp.logical_and(keep >= first, keep < ids_s).astype(jnp.int32), axis=0, keepdims=True
    )
    lane_row_s = lax.broadcasted_iota(jnp.int32, (1, sup), 1)
    mean_pos = jnp.where(kept_s == 1, -1, lane_row_s + 3 * below_s)
    start = first + 3 * jnp.sum((keep < first).astype(jnp.int32), axis=0, keepdims=True)
    flat = patches_ref[...]
    sup_col = lax.broadcasted_iota(jnp.int32, (sup, rows), 0)
    sup_lane = lax.broadcasted_iota(jnp.int32, (sup, rows), 1) >> 2
    averaging = jnp.where(sup_col == sup_lane, 0.25, 0.0).astype(BF16)
    means = jnp.dot(averaging, flat, preferred_element_type=F32).astype(BF16)
    slot = lax.broadcasted_iota(jnp.int32, (SLOT, 1), 0)
    for j in range(n):
        pos = ((j - start) & (n - 1)) + slot * n
        fine = (pos == fine_pos).astype(F32).astype(BF16)
        mean = (pos == mean_pos).astype(F32).astype(BF16)
        dealt = (
            jnp.dot(fine, flat, preferred_element_type=F32)
            + jnp.dot(mean, means, preferred_element_type=F32)
        ).astype(BF16)
        cuts = dealt.shape[1] // 128
        for c in range(cuts):
            out_ref[j, c * SLOT : (c + 1) * SLOT] = dealt[:, c * 128 : (c + 1) * 128]
        out_ref[j, cuts * SLOT :] = qkv_ref[j]


def prep(scalars, keep_col, flat, qkv, n, sup):
    width = flat.shape[1] // 2
    shape = (n, SLOT * width // 128 + qkv.shape[1], 128)
    return pl.pallas_call(
        functools.partial(prep_kernel, n, sup),
        grid_spec=pltpu.PrefetchScalarGridSpec(
            num_scalar_prefetch=1,
            grid=(1,),
            in_specs=[
                pl.BlockSpec(keep_col.shape, lambda i, ref: (0, 0)),
                pl.BlockSpec((flat.shape[0], width), lambda i, ref: (0, ref[1])),
                pl.BlockSpec(qkv.shape, lambda i, ref: (0, 0, 0)),
            ],
            out_specs=pl.BlockSpec(shape, lambda i, ref: (0, 0, 0)),
        ),
        out_shape=struct(shape),
        compiler_params=params(),
    )(scalars, keep_col, flat, qkv)


def pick_kernel(n, sup, per_owner, cuts, rank_ref, keep_ref, got_ref, up_ref, down_ref, out_ref, sem):
    rank, part = rank_ref[0], rank_ref[2]
    rows = up_ref.shape[0]
    wide = up_ref.shape[1] // n
    units = wide // 2
    top = cuts * per_owner
    copies = []
    for j in range(n):
        at = pl.ds(pl.multiple_of(j * wide + part * units, 128), units)
        copies.append((up_ref.at[:, at], out_ref.at[j, pl.ds(top, rows)]))
        copies.append((down_ref.at[at], out_ref.at[j, pl.ds(top + rows, units)]))
    started = []
    for i, (src, dst) in enumerate(copies):
        copy = pltpu.make_async_copy(src, dst, sem.at[i])
        copy.start()
        started.append(copy)
    keep = keep_ref[...]
    count = keep.shape[0]
    lanes = n * SLOT
    shift = SLOT.bit_length() - 1
    source = (lax.broadcasted_iota(jnp.int32, (count, lanes), 1) >> shift)
    low = jnp.sum((keep < source * sup).astype(jnp.int32), axis=0, keepdims=True)
    high = jnp.sum((keep < source * sup + sup).astype(jnp.int32), axis=0, keepdims=True)
    lane = lax.broadcasted_iota(jnp.int32, (1, lanes), 1)
    source_row = lane >> shift
    start = source_row * sup + 3 * low
    stop = source_row * sup + sup + 3 * high
    token = start + ((rank - start) & (n - 1)) + (lane & (SLOT - 1)) * n
    row = jnp.where(token < stop, token >> (n.bit_length() - 1), -1)
    own = lax.broadcasted_iota(jnp.int32, (per_owner, lanes), 0)
    choose = (own == row).astype(F32).astype(BF16)
    for c in range(cuts):
        stacked = jnp.concatenate(
            [got_ref[j, c * SLOT : (c + 1) * SLOT] for j in range(n)], axis=0
        )
        owned = jnp.dot(choose, stacked, preferred_element_type=F32).astype(BF16)
        for j in range(n):
            out_ref[j, c * per_owner : (c + 1) * per_owner] = owned
    for copy in started:
        copy.wait()


def pick(scalars, keep_col, got, up, down, head_rows, n, sup, per_owner):
    cuts = (got.shape[1] - head_rows) // SLOT
    rows = cuts * per_owner + up.shape[0] + up.shape[1] // n // 2
    return pl.pallas_call(
        functools.partial(pick_kernel, n, sup, per_owner, cuts),
        in_specs=[sspec(), vspec(), vspec(), aspec(), aspec()],
        out_specs=vspec(),
        out_shape=struct((n, rows, 128)),
        scratch_shapes=[pltpu.SemaphoreType.DMA((2 * n,))],
        compiler_params=params(),
    )(scalars, keep_col, got, up, down)


def norm_rows(x):
    average = jnp.mean(x, axis=-1, keepdims=True)
    power = jnp.mean(x * x, axis=-1, keepdims=True)
    return (x - average) * lax.rsqrt(power - average * average + 1e-06)


def attend_kernel(n, part, rank_ref, mine_ref, other_ref, got_ref, tokens_ref, out_ref, weight_ref):
    half = rank_ref[1]
    cuts = other_ref.shape[1] // part
    width = cuts * 128
    depth = got_ref.shape[2]
    for j in range(n):
        rows = slice(j * part, (j + 1) * part)
        for c in range(cuts):
            cut = slice(c * part, (c + 1) * part)
            at = pl.ds(pl.multiple_of(half * width + c * 128, 128), 128)
            tokens_ref[rows, at] = mine_ref[j, cut]
            at = pl.ds(pl.multiple_of((1 - half) * width + c * 128, 128), 128)
            tokens_ref[rows, at] = other_ref[j, cut]
        weight_ref[:, j * depth : (j + 1) * depth] = got_ref[j, got_ref.shape[1] - weight_ref.shape[0] :]
    normed = norm_rows(tokens_ref[...].astype(F32)).astype(BF16)
    projected = lax.dot_general(
        normed, weight_ref[...], (((1,), (1,)), ((), ())), preferred_element_type=F32
    ).astype(BF16)
    size = projected.shape[1] // 3
    queries = projected[:, :size]
    keys = projected[:, size : 2 * size]
    values = projected[:, 2 * size :]
    scores = lax.dot_general(
        queries, keys, (((1,), (1,)), ((), ())), preferred_element_type=F32
    ) * (1.0 / math.sqrt(size))
    powers = jnp.exp(scores - jnp.max(scores, axis=1, keepdims=True))
    probs = (powers / jnp.sum(powers, axis=1, keepdims=True)).astype(BF16)
    attended = lax.dot_general(
        values, probs, (((0,), (1,)), ((), ())), preferred_element_type=F32
    ).astype(BF16)
    for j in range(n):
        out_ref[j] = attended


def attend_fast(scalars, mine, other, got, head_rows, per_owner, n):
    length = n * per_owner
    depth = other.shape[1] // per_owner * 256
    size = head_rows // 3
    return pl.pallas_call(
        functools.partial(attend_kernel, n, per_owner),
        in_specs=[sspec()] + [vspec()] * 3,
        out_specs=[vspec()] * 2,
        out_shape=[struct((length, depth)), struct((n, size, length))],
        scratch_shapes=[VMEM((head_rows, n * 128), BF16)],
        compiler_params=params(),
        cost_estimate=cost(30),
    )(scalars, mine, other, got)


def mlp_kernel(
    n,
    rank_ref,
    tokens_ref,
    mine_ref,
    other_ref,
    out_mine_ref,
    out_other_ref,
    first_ref,
    second_ref,
    residual_ref,
    keep_ref,
    send_ref,
    up_ref,
    down_ref,
    row_ref,
    whole_ref,
):
    rank, half = rank_ref[0], rank_ref[1]
    block = up_ref.shape[0] // n
    unit = first_ref.shape[2]
    for j in range(n):
        for c, got_ref in enumerate((first_ref, second_ref)):
            units = pl.ds(c * unit, unit)
            up_ref[j * block : (j + 1) * block, units] = got_ref[j, :block]
            down_ref[units, j * 128 : (j + 1) * 128] = got_ref[j, block:]
    for j in range(n):
        at = pl.ds(pl.multiple_of((rank ^ j) * 128, 128), 128)
        whole_ref[0, :, at] = out_mine_ref[j]
        whole_ref[1, :, at] = out_other_ref[j]
    dims = (((0,), (0,)), ((), ()))
    row_ref[...] = (
        tokens_ref[...].astype(F32)
        + lax.dot_general(mine_ref[...], whole_ref[0], dims, preferred_element_type=F32)
        + lax.dot_general(other_ref[...], whole_ref[1], dims, preferred_element_type=F32)
    )
    part = residual_ref.shape[0]
    width = residual_ref.shape[1]
    my_cols = pl.ds(pl.multiple_of(half * width, width), width)
    other_cols = pl.ds(pl.multiple_of((1 - half) * width, width), width)
    residual_ref[...] = row_ref[pl.ds(pl.multiple_of(rank * part, part), part), my_cols]
    normed = norm_rows(row_ref[...]).astype(BF16)
    raw = jnp.dot(normed, up_ref[...], preferred_element_type=F32)
    hidden = (0.5 * raw * (1.0 + lax.erf(raw * math.sqrt(0.5)))).astype(BF16)
    keep_ref[...] = jnp.dot(hidden, down_ref[:, my_cols], preferred_element_type=F32)
    send_ref[...] = jnp.dot(hidden, down_ref[:, other_cols], preferred_element_type=F32).astype(BF16)


def mlp(scalars, tokens, mine, other, out_mine, out_other, first, second, n):
    length, depth = tokens.shape
    width = depth // 2
    wide = 2 * first.shape[2]
    return pl.pallas_call(
        functools.partial(mlp_kernel, n),
        in_specs=[sspec()] + [vspec()] * 7,
        out_specs=[vspec()] * 3,
        out_shape=[
            struct((length // n, width), F32),
            struct((length, width), F32),
            struct((length, width)),
        ],
        scratch_shapes=[
            VMEM((depth, wide), BF16),
            VMEM((wide, depth), BF16),
            VMEM((length, depth), F32),
            VMEM((2, out_mine.shape[1], depth), BF16),
        ],
        compiler_params=params(),
    )(scalars, tokens, mine, other, out_mine, out_other, first, second)


def join_kernel(rank_ref, keep_ref, got_ref, residual_ref, base_ref, out_ref):
    part = residual_ref.shape[0]
    mine = pl.ds(pl.multiple_of(rank_ref[0] * part, part), part)
    base_ref[...] = keep_ref[mine] + got_ref[mine].astype(F32) + residual_ref[...]
    out_ref[...] = (keep_ref[...] + got_ref[...].astype(F32)).astype(BF16)


def join(scalars, keep, got, residual):
    return pl.pallas_call(
        join_kernel,
        in_specs=[sspec()] + [vspec()] * 3,
        out_specs=[vspec()] * 2,
        out_shape=[struct(residual.shape, F32), struct(keep.shape)],
        compiler_params=params(),
    )(scalars, keep, got, residual)


def last_kernel(n, rank_ref, base_ref, terms_ref, out_ref):
    rank = rank_ref[0]
    total = base_ref[...]
    for j in range(1, n):
        total = total + terms_ref[rank ^ j].astype(F32)
    out_ref[...] = total.astype(BF16)


def last(scalars, base, terms):
    return pl.pallas_call(
        functools.partial(last_kernel, terms.shape[0]),
        in_specs=[sspec()] + [vspec()] * 2,
        out_specs=vspec(),
        out_shape=struct(base.shape),
        compiler_params=params(),
    )(scalars, base, terms)


def swap(value, axis, j):
    n = lax.axis_size(axis)
    return lax.ppermute(value, axis, [(i, i ^ j) for i in range(n)])


def exchange(value):
    return lax.all_to_all(value, "seq", split_axis=0, concat_axis=0, tiled=True)


def after(value, *others):
    return lax.optimization_barrier((value, *others))[0]


def local_fast(patches, keep_list, qkv_weight, out_weight, up_weight, down_weight):
    n = lax.axis_size("seq")
    scalars = jnp.stack(
        [lax.axis_index(name).astype(jnp.int32) for name in ("seq", "head", "groups")]
    )
    sup, depth = patches.shape[1], patches.shape[3]
    length = sup * n * 8 // 5
    per_owner = length // n
    half_width = depth // 2
    head_rows = qkv_weight.shape[2]
    keep_col = keep_list.reshape(-1, 1)
    flat = patches.reshape(4 * sup, depth)
    slots = prep(scalars, keep_col, flat, qkv_weight.transpose(1, 2, 0), n, sup)
    dealt = exchange(slots)
    across = swap(after(out_weight, slots), "seq", n // 2)
    dealt, across = lax.optimization_barrier((dealt, across))
    sent = pick(scalars, keep_col, dealt, up_weight, down_weight, head_rows, n, sup, per_owner)
    pair = jnp.stack([out_weight, across])
    pair = after(pair, sent)
    got = exchange(sent)
    quads = [pair] + [swap(pair, "seq", j) for j in range(1, n // 2)]
    got, *quads = lax.optimization_barrier((got, *quads))
    top = half_width // 128 * per_owner
    pieces = got[:, :top]
    pieces_other = swap(pieces, "head", 1)
    first = got[:, top:]
    second = swap(first, "groups", 1)
    tokens, attended = attend_fast(scalars, pieces, pieces_other, dealt, head_rows, per_owner, n)
    out_mine = jnp.stack([quad[k] for k in range(2) for quad in quads])
    out_other = swap(out_mine, "head", 1)
    gathered = exchange(attended).reshape(half_width, length)
    gathered_other = swap(gathered, "head", 1)
    residual, keep, send = mlp(
        scalars, tokens, gathered, gathered_other, out_mine, out_other, first, second, n
    )
    got = swap(send, "head", 1)
    base, terms = join(scalars, keep, got, residual)
    terms = exchange(terms.reshape(n, per_owner, half_width))
    encoded = last(scalars, base, terms)
    return encoded.reshape(1, per_owner, 1, half_width)


def local(patches, keep_list, qkv_weight, out_weight, up_weight, down_weight):
    n = lax.axis_size("seq")
    one_image = patches.shape[0] == 1 and qkv_weight.shape[1] == n and n & (n - 1) == 0
    one_image = one_image and lax.axis_size("groups") == 2 and up_weight.shape[1] == n * 256
    plan = local_fast if one_image else local_general
    return plan(patches, keep_list, qkv_weight, out_weight, up_weight, down_weight)


def solution(mesh):
    return jax.shard_map(
        local,
        mesh=mesh,
        in_specs=(
            P("groups", "seq", None, None),
            P("groups", None),
            P("seq", "head", None),
            P("head", "seq"),
            P("seq", "head"),
            P("head", "seq"),
        ),
        out_specs=P("groups", None, "seq", "head"),
        check_vma=False,
    )
```

```python
import functools
import math

import jax
import jax.numpy as jnp
from jax import lax
from jax.experimental import pallas as pl
from jax.experimental.pallas import tpu as pltpu
from jax.sharding import PartitionSpec as P

F32 = jnp.float32
BF16 = jnp.bfloat16
VMEM = pltpu.VMEM
SLOT = 32
LIMIT = 32 * 1024 * 1024

def layer_norm(matrix):
    average = jnp.mean(matrix, axis=-1, keepdims=True)
    power = jnp.mean(matrix * matrix, axis=-1, keepdims=True)
    return (matrix - average) * lax.rsqrt(power - average * average + 1e-06)


def attend(queries, keys, values):
    length = queries.shape[0]
    block = math.gcd(length, 512)
    scale = 1.0 / math.sqrt(queries.shape[1])

    def one_block(query_rows):
        scores = (
            lax.dot_general(
                query_rows, keys, (((1,), (1,)), ((), ())), preferred_element_type=jnp.float32
            )
            * scale
        )
        top = jnp.max(scores, axis=1, keepdims=True)
        powers = jnp.exp(scores - top)
        probs = (powers / jnp.sum(powers, axis=1, keepdims=True)).astype(jnp.bfloat16)
        return jnp.dot(probs, values, preferred_element_type=jnp.float32).astype(jnp.bfloat16)

    blocks = lax.map(one_block, queries.reshape(length // block, block, queries.shape[1]))
    return blocks.reshape(length, values.shape[1])


def local_general(patches, keep_list, qkv_weight, out_weight, up_weight, down_weight):
    seq_count = lax.axis_size("seq")
    seq_rank = lax.axis_index("seq")
    head_rank = lax.axis_index("head")
    images = patches.shape[0]
    sup_local = patches.shape[1]
    depth = patches.shape[3]
    half_width = depth // lax.axis_size("head")
    head_count = qkv_weight.shape[1]
    seq_length = sup_local * seq_count * 8 // 5
    per_owner = seq_length // seq_count
    capacity = (4 * sup_local + seq_count - 1) // seq_count
    slot_count = 4 * sup_local
    image_index = jnp.arange(images, dtype=jnp.int32)
    bounds = jnp.arange(seq_count + 1, dtype=jnp.int32) * sup_local
    before = jnp.sum((keep_list[:, :, None] < bounds[None, None, :]).astype(jnp.int32), axis=1)
    starts = bounds[None, :seq_count] + 3 * before[:, :seq_count]
    lengths = sup_local + 3 * (before[:, 1:] - before[:, :seq_count])
    my_start = lax.dynamic_index_in_dim(starts, seq_rank, 1, keepdims=False)
    my_length = lax.dynamic_index_in_dim(lengths, seq_rank, 1, keepdims=False)
    local_ids = seq_rank * sup_local + jnp.arange(sup_local, dtype=jnp.int32)
    kept_flag = jnp.any(keep_list[:, None, :] == local_ids[None, :, None], axis=2).astype(jnp.int32)
    offsets = jnp.arange(sup_local, dtype=jnp.int32)[None, :] + 3 * (
        jnp.cumsum(kept_flag, axis=1) - kept_flag
    )
    slot_ids = jnp.arange(slot_count, dtype=jnp.int32)
    owner_patch = (
        jnp.sum((offsets[:, None, :] <= slot_ids[None, :, None]).astype(jnp.int32), axis=2) - 1
    )
    start_of = jnp.take_along_axis(offsets, owner_patch, axis=1)
    sub_index = jnp.minimum(slot_ids[None, :] - start_of, 3)
    kept_of = jnp.take_along_axis(kept_flag, owner_patch, axis=1)
    flat_patches = patches.reshape(images, sup_local * 4, depth)
    fine_rows = flat_patches[
        image_index[:, None], owner_patch * 4 + jnp.where(kept_of == 1, sub_index, 0)
    ]
    mean_rows = jnp.mean(patches.astype(jnp.float32), axis=2).astype(jnp.bfloat16)
    shared_rows = mean_rows[image_index[:, None], owner_patch]
    local_tokens = jnp.where((kept_of == 1)[:, :, None], fine_rows, shared_rows)
    destinations = jnp.arange(seq_count, dtype=jnp.int32)[:, None, None]
    depth_slots = jnp.arange(capacity, dtype=jnp.int32)[None, None, :]
    positions = (destinations - my_start[None, :, None]) % seq_count + depth_slots * seq_count
    valid = positions < my_length[None, :, None]
    outgoing = local_tokens[image_index[None, :, None], jnp.minimum(positions, slot_count - 1)]
    outgoing = jnp.where(valid[:, :, :, None], outgoing, jnp.zeros((), jnp.bfloat16))
    incoming = lax.all_to_all(outgoing, "seq", split_axis=0, concat_axis=0, tiled=True)
    owned = jnp.arange(per_owner, dtype=jnp.int32) * seq_count + seq_rank
    source = jnp.sum((starts[:, None, :] <= owned[None, :, None]).astype(jnp.int32), axis=2) - 1
    first_of = jnp.take_along_axis(starts, source, axis=1)
    depth_of = (owned[None, :] - first_of) // seq_count
    resident = incoming[source, image_index[:, None], depth_of]
    start_rows = resident.reshape(images * per_owner, depth)
    start_float = start_rows.astype(jnp.float32)
    qkv_full, out_full, up_full, down_full = (
        lax.all_gather(qkv_weight, "seq", axis=0, tiled=True),
        lax.all_gather(out_weight, "seq", axis=1, tiled=True),
        lax.all_gather(up_weight, "seq", axis=0, tiled=True),
        lax.all_gather(down_weight, "seq", axis=1, tiled=True),
    )
    normed = layer_norm(start_float).astype(jnp.bfloat16).reshape(images, per_owner, depth)
    projected = jnp.einsum("ipd,dhc->ihpc", normed, qkv_full, preferred_element_type=jnp.float32)
    head_size = qkv_weight.shape[2] // 3
    sending = projected.astype(jnp.bfloat16).reshape(seq_count, per_owner, 3 * head_size)
    gathered = lax.all_to_all(sending, "seq", split_axis=0, concat_axis=0, tiled=True).reshape(
        seq_length, 3 * head_size
    )
    attended = attend(
        gathered[:, :head_size],
        gathered[:, head_size : 2 * head_size],
        gathered[:, 2 * head_size :],
    )
    returned = lax.all_to_all(
        attended.reshape(seq_count, per_owner, head_size),
        "seq",
        split_axis=0,
        concat_axis=0,
        tiled=True,
    )
    returned = returned.reshape(images, head_count, per_owner, head_size)
    partial_sum = jnp.einsum(
        "ihpc,hcd->ipd",
        returned,
        out_full.reshape(head_count, head_size, depth),
        preferred_element_type=jnp.float32,
    ).reshape(images * per_owner, depth)
    attn_total = lax.psum(partial_sum, "head")
    residual = start_float + attn_total
    residual_half = lax.dynamic_slice_in_dim(residual, head_rank * half_width, half_width, 1)
    normed_two = layer_norm(residual).astype(jnp.bfloat16)
    hidden = jax.nn.gelu(
        jnp.dot(normed_two, up_full, preferred_element_type=jnp.float32), approximate=False
    ).astype(jnp.bfloat16)
    mlp_terms = jnp.dot(hidden, down_full, preferred_element_type=jnp.float32)
    mlp_part = lax.psum_scatter(mlp_terms, "head", scatter_dimension=1, tiled=True)
    encoded = (residual_half + mlp_part).astype(jnp.bfloat16)
    return encoded.reshape(images, per_owner, 1, half_width)


def vspec():
    return pl.BlockSpec(memory_space=VMEM)


def aspec():
    return pl.BlockSpec(memory_space=pl.ANY)


def sspec():
    return pl.BlockSpec(memory_space=pltpu.SMEM)


def params():
    return pltpu.CompilerParams(vmem_limit_bytes=LIMIT)


def cost(micros):
    return pl.CostEstimate(flops=micros * 10**9, bytes_accessed=1 << 20, transcendentals=0)


def struct(shape, dtype=BF16):
    return jax.ShapeDtypeStruct(shape, dtype)


def prep_kernel(n, sup, rank_ref, keep_ref, patches_ref, out_ref):
    rank = rank_ref[0]
    first = rank * sup
    keep = keep_ref[...]
    rows = 4 * sup
    count = keep.shape[0]
    lane = lax.broadcasted_iota(jnp.int32, (count, rows), 1)
    ids = first + (lane >> 2)
    kept = jnp.sum((keep == ids).astype(jnp.int32), axis=0, keepdims=True)
    below = jnp.sum(
        jnp.logical_and(keep >= first, keep < ids).astype(jnp.int32), axis=0, keepdims=True
    )
    lane_row = lax.broadcasted_iota(jnp.int32, (1, rows), 1)
    fine_pos = jnp.where(kept == 1, (lane_row >> 2) + 3 * below + (lane_row & 3), -1)
    lane_s = lax.broadcasted_iota(jnp.int32, (count, sup), 1)
    ids_s = first + lane_s
    kept_s = jnp.sum((keep == ids_s).astype(jnp.int32), axis=0, keepdims=True)
    below_s = jnp.sum(
        jnp.logical_and(keep >= first, keep < ids_s).astype(jnp.int32), axis=0, keepdims=True
    )
    lane_row_s = lax.broadcasted_iota(jnp.int32, (1, sup), 1)
    mean_pos = jnp.where(kept_s == 1, -1, lane_row_s + 3 * below_s)
    start = first + 3 * jnp.sum((keep < first).astype(jnp.int32), axis=0, keepdims=True)
    flat = patches_ref[...]
    sup_col = lax.broadcasted_iota(jnp.int32, (sup, rows), 0)
    sup_lane = lax.broadcasted_iota(jnp.int32, (sup, rows), 1) >> 2
    averaging = jnp.where(sup_col == sup_lane, 0.25, 0.0).astype(BF16)
    means = jnp.dot(averaging, flat, preferred_element_type=F32).astype(BF16)
    slot = lax.broadcasted_iota(jnp.int32, (SLOT, 1), 0)
    for j in range(n):
        pos = ((j - start) & (n - 1)) + slot * n
        fine = (pos == fine_pos).astype(F32).astype(BF16)
        mean = (pos == mean_pos).astype(F32).astype(BF16)
        dealt = (
            jnp.dot(fine, flat, preferred_element_type=F32)
            + jnp.dot(mean, means, preferred_element_type=F32)
        ).astype(BF16)
        cuts = dealt.shape[1] // 128
        for c in range(cuts):
            out_ref[j, c * SLOT : (c + 1) * SLOT] = dealt[:, c * 128 : (c + 1) * 128]


def prep(scalars, keep_col, flat, n, sup):
    width = flat.shape[1] // 2
    shape = (n, SLOT * width // 128, 128)
    return pl.pallas_call(
        functools.partial(prep_kernel, n, sup),
        grid_spec=pltpu.PrefetchScalarGridSpec(
            num_scalar_prefetch=1,
            grid=(1,),
            in_specs=[
                pl.BlockSpec(keep_col.shape, lambda i, ref: (0, 0)),
                pl.BlockSpec((flat.shape[0], width), lambda i, ref: (0, ref[1])),
            ],
            out_specs=pl.BlockSpec(shape, lambda i, ref: (0, 0, 0)),
        ),
        out_shape=struct(shape),
        compiler_params=params(),
    )(scalars, keep_col, flat)


def pick_kernel(n, sup, per_owner, rank_ref, keep_ref, got_ref, out_ref):
    rank = rank_ref[0]
    cuts = got_ref.shape[1] // SLOT
    keep = keep_ref[...]
    count = keep.shape[0]
    lanes = n * SLOT
    shift = SLOT.bit_length() - 1
    source = (lax.broadcasted_iota(jnp.int32, (count, lanes), 1) >> shift)
    low = jnp.sum((keep < source * sup).astype(jnp.int32), axis=0, keepdims=True)
    high = jnp.sum((keep < source * sup + sup).astype(jnp.int32), axis=0, keepdims=True)
    lane = lax.broadcasted_iota(jnp.int32, (1, lanes), 1)
    source_row = lane >> shift
    start = source_row * sup + 3 * low
    stop = source_row * sup + sup + 3 * high
    token = start + ((rank - start) & (n - 1)) + (lane & (SLOT - 1)) * n
    row = jnp.where(token < stop, token >> (n.bit_length() - 1), -1)
    own = lax.broadcasted_iota(jnp.int32, (per_owner, lanes), 0)
    choose = (own == row).astype(F32).astype(BF16)
    for c in range(cuts):
        stacked = jnp.concatenate(
            [got_ref[j, c * SLOT : (c + 1) * SLOT] for j in range(n)], axis=0
        )
        owned = jnp.dot(choose, stacked, preferred_element_type=F32).astype(BF16)
        out_ref[c * per_owner : (c + 1) * per_owner] = owned


def pick(scalars, keep_col, got, n, sup, per_owner):
    return pl.pallas_call(
        functools.partial(pick_kernel, n, sup, per_owner),
        in_specs=[sspec(), vspec(), vspec()],
        out_specs=vspec(),
        out_shape=struct((got.shape[1] // SLOT * per_owner, 128)),
        compiler_params=params(),
    )(scalars, keep_col, got)


def pack_kernel(n, rank_ref, up_ref, down_ref, home_ref, away_ref, sem):
    side, part = rank_ref[0] // (n // 2), rank_ref[2]
    rows = up_ref.shape[0]
    wide = up_ref.shape[1] // n
    units = wide // 2
    copies = []
    for k, out_ref in enumerate((home_ref, away_ref)):
        for d in range(n // 2):
            dest = (side ^ k) * (n // 2) + d
            at = pl.ds(pl.multiple_of(dest * wide + part * units, 128), units)
            copies.append((up_ref.at[:, at], out_ref.at[d, pl.ds(0, rows)]))
            copies.append((down_ref.at[at], out_ref.at[d, pl.ds(rows, units)]))
    started = []
    for i, (src, dst) in enumerate(copies):
        copy = pltpu.make_async_copy(src, dst, sem.at[i])
        copy.start()
        started.append(copy)
    for copy in started:
        copy.wait()


def pack(scalars, up, down, n):
    units = up.shape[1] // n // 2
    shape = struct((n // 2, up.shape[0] + units, units))
    return pl.pallas_call(
        functools.partial(pack_kernel, n),
        in_specs=[sspec(), aspec(), aspec()],
        out_specs=[aspec()] * 2,
        out_shape=[shape, shape],
        scratch_shapes=[pltpu.SemaphoreType.DMA((2 * n,))],
        compiler_params=params(),
    )(scalars, up, down)


def fan_kernel(owned_ref, across_ref, home_ref, away_ref, out_ref):
    rows, depth = owned_ref.shape[0], home_ref.shape[1]
    for d in range(out_ref.shape[0]):
        out_ref[d, :rows] = owned_ref[...]
        out_ref[d, rows : 2 * rows] = across_ref[...]
        out_ref[d, 2 * rows : 2 * rows + depth] = home_ref[d]
        out_ref[d, 2 * rows + depth :] = away_ref[d]


def fan(owned, across, home, away):
    shape = struct((home.shape[0], 2 * owned.shape[0] + 2 * home.shape[1], 128))
    return pl.pallas_call(
        fan_kernel,
        in_specs=[vspec()] * 4,
        out_specs=vspec(),
        out_shape=shape,
        compiler_params=params(),
    )(owned, across, home, away)


def source_of(rank, n, q, k):
    return (rank // (n // 2) ^ k) * (n // 2) + q


def norm_rows(x):
    average = jnp.mean(x, axis=-1, keepdims=True)
    power = jnp.mean(x * x, axis=-1, keepdims=True)
    return (x - average) * lax.rsqrt(power - average * average + 1e-06)


def attend_kernel(n, part, rank_ref, mine_ref, other_ref, tokens_ref, out_ref, weight_ref):
    rank, half = rank_ref[0], rank_ref[1]
    rows = other_ref.shape[1] // 2
    cuts = rows // part
    width = cuts * 128
    depth = weight_ref.shape[0]
    for q in range(n // 2):
        for k in range(2):
            source = source_of(rank, n, q, k)
            at = pl.ds(pl.multiple_of(source * part, part), part)
            for c in range(cuts):
                cut = slice(k * rows + c * part, k * rows + (c + 1) * part)
                to = pl.ds(pl.multiple_of(half * width + c * 128, 128), 128)
                tokens_ref[at, to] = mine_ref[q, cut]
                to = pl.ds(pl.multiple_of((1 - half) * width + c * 128, 128), 128)
                tokens_ref[at, to] = other_ref[q, cut]
            weight_ref[:, pl.ds(pl.multiple_of(source * 128, 128), 128)] = mine_ref[
                q, 2 * rows + k * depth : 2 * rows + (k + 1) * depth
            ]
    normed = norm_rows(tokens_ref[...].astype(F32)).astype(BF16)
    projected = lax.dot_general(
        normed, weight_ref[...], (((1,), (1,)), ((), ())), preferred_element_type=F32
    ).astype(BF16)
    size = projected.shape[1] // 3
    queries = projected[:, :size]
    keys = projected[:, size : 2 * size]
    values = projected[:, 2 * size :]
    scores = lax.dot_general(
        queries, keys, (((1,), (1,)), ((), ())), preferred_element_type=F32
    ) * (1.0 / math.sqrt(size))
    powers = jnp.exp(scores - jnp.max(scores, axis=1, keepdims=True))
    probs = (powers / jnp.sum(powers, axis=1, keepdims=True)).astype(BF16)
    attended = lax.dot_general(
        values, probs, (((0,), (1,)), ((), ())), preferred_element_type=F32
    ).astype(BF16)
    out_ref[...] = attended


def attend_fast(scalars, mine, other, head_rows, per_owner, n):
    length = n * per_owner
    depth = other.shape[1] // (2 * per_owner) * 256
    size = head_rows // 3
    return pl.pallas_call(
        functools.partial(attend_kernel, n, per_owner),
        in_specs=[sspec()] + [vspec()] * 2,
        out_specs=[vspec()] * 2,
        out_shape=[struct((length, depth)), struct((size, length))],
        scratch_shapes=[VMEM((head_rows, n * 128), BF16)],
        compiler_params=params(),
        cost_estimate=cost(30),
    )(scalars, mine, other)


def mlp_kernel(
    n,
    rank_ref,
    tokens_ref,
    mine_ref,
    other_ref,
    out_refs,
    first_ref,
    second_ref,
    residual_ref,
    keep_ref,
    send_ref,
    up_ref,
    down_ref,
    row_ref,
    whole_ref,
    joined_ref,
):
    rank, half, group = rank_ref[0], rank_ref[1], rank_ref[2]
    block = up_ref.shape[0] // n
    unit = first_ref.shape[2]
    size = mine_ref.shape[2]
    rows = out_refs[0][0].shape[1]
    for q in range(n // 2):
        for k in range(2):
            source = source_of(rank, n, q, k)
            at = pl.ds(pl.multiple_of(source * block, block), block)
            to = pl.ds(pl.multiple_of(source * 128, 128), 128)
            for c, got_ref in enumerate((first_ref, second_ref)):
                units = pl.ds(c * unit, unit)
                high = k * (block + unit)
                up_ref[at, units] = got_ref[q, high : high + block]
                down_ref[units, to] = got_ref[q, high + block : high + block + unit]
            at = pl.ds(pl.multiple_of(source * size, size), size)
            joined_ref[0, at] = mine_ref[q, k]
            joined_ref[1, at] = other_ref[q, k]
            source = rank ^ (k * (n // 2) + q)
            to = pl.ds(pl.multiple_of(source * 128, 128), 128)
            for core in range(2):
                for c in range(2):
                    at = pl.ds(pl.multiple_of((group ^ c) * rows, rows), rows)
                    whole_ref[core, at, to] = out_refs[core][c][q * 2 + k]
    dims = (((0,), (0,)), ((), ()))
    row_ref[...] = (
        tokens_ref[...].astype(F32)
        + lax.dot_general(joined_ref[0], whole_ref[0], dims, preferred_element_type=F32)
        + lax.dot_general(joined_ref[1], whole_ref[1], dims, preferred_element_type=F32)
    )
    part = residual_ref.shape[0]
    width = residual_ref.shape[1]
    my_cols = pl.ds(pl.multiple_of(half * width, width), width)
    other_cols = pl.ds(pl.multiple_of((1 - half) * width, width), width)
    residual_ref[...] = row_ref[pl.ds(pl.multiple_of(rank * part, part), part), my_cols]
    normed = norm_rows(row_ref[...]).astype(BF16)
    raw = jnp.dot(normed, up_ref[...], preferred_element_type=F32)
    hidden = (0.5 * raw * (1.0 + lax.erf(raw * math.sqrt(0.5)))).astype(BF16)
    keep_ref[...] = jnp.dot(hidden, down_ref[:, my_cols], preferred_element_type=F32)
    send_ref[...] = jnp.dot(hidden, down_ref[:, other_cols], preferred_element_type=F32).astype(BF16)


def mlp(scalars, tokens, mine, other, outs, first, second, n):
    length, depth = tokens.shape
    width = depth // 2
    wide = 2 * first.shape[2]
    inner = n * mine.shape[2]

    def kernel(scalars, tokens, mine, other, out_a, out_b, out_c, out_d, *refs):
        mlp_kernel(n, scalars, tokens, mine, other, ((out_a, out_b), (out_c, out_d)), *refs)

    return pl.pallas_call(
        kernel,
        in_specs=[sspec()] + [vspec()] * 9,
        out_specs=[vspec()] * 3,
        out_shape=[
            struct((length // n, width), F32),
            struct((length, width), F32),
            struct((length, width)),
        ],
        scratch_shapes=[
            VMEM((depth, wide), BF16),
            VMEM((wide, depth), BF16),
            VMEM((length, depth), F32),
            VMEM((2, inner, depth), BF16),
            VMEM((2, inner, length), BF16),
        ],
        compiler_params=params(),
    )(scalars, tokens, mine, other, *outs, first, second)


def join_kernel(rank_ref, keep_ref, got_ref, residual_ref, base_ref, out_ref):
    part = residual_ref.shape[0]
    mine = pl.ds(pl.multiple_of(rank_ref[0] * part, part), part)
    base_ref[...] = keep_ref[mine] + got_ref[mine].astype(F32) + residual_ref[...]
    out_ref[...] = (keep_ref[...] + got_ref[...].astype(F32)).astype(BF16)


def join(scalars, keep, got, residual):
    return pl.pallas_call(
        join_kernel,
        in_specs=[sspec()] + [vspec()] * 3,
        out_specs=[vspec()] * 2,
        out_shape=[struct(residual.shape, F32), struct(keep.shape)],
        compiler_params=params(),
    )(scalars, keep, got, residual)


def last_kernel(n, rank_ref, base_ref, terms_ref, out_ref):
    rank = rank_ref[0]
    total = base_ref[...]
    for j in range(1, n):
        total = total + terms_ref[rank ^ j].astype(F32)
    out_ref[...] = total.astype(BF16)


def last(scalars, base, terms):
    return pl.pallas_call(
        functools.partial(last_kernel, terms.shape[0]),
        in_specs=[sspec()] + [vspec()] * 2,
        out_specs=vspec(),
        out_shape=struct(base.shape),
        compiler_params=params(),
    )(scalars, base, terms)


def swap(value, axis, j):
    n = lax.axis_size(axis)
    return lax.ppermute(value, axis, [(i, i ^ j) for i in range(n)])


def exchange(value):
    return lax.all_to_all(value, "seq", split_axis=0, concat_axis=0, tiled=True)


def exchange_half(value):
    n = lax.axis_size("seq")
    groups = [list(range(n // 2)), list(range(n // 2, n))]
    return lax.all_to_all(
        value, "seq", split_axis=0, concat_axis=0, axis_index_groups=groups, tiled=True
    )


def after(value, *others):
    return lax.optimization_barrier((value, *others))[0]


def local_fast(patches, keep_list, qkv_weight, out_weight, up_weight, down_weight):
    n = lax.axis_size("seq")
    rank, half, group = (
        lax.axis_index(name).astype(jnp.int32) for name in ("seq", "head", "groups")
    )
    scalars = jnp.stack([rank, half, group])
    side = rank // (n // 2)
    sup, depth = patches.shape[1], patches.shape[3]
    length = sup * n * 8 // 5
    per_owner = length // n
    half_width = depth // 2
    head_rows = qkv_weight.shape[2]
    keep_col = keep_list.reshape(-1, 1)
    flat = patches.reshape(4 * sup, depth)
    heads = qkv_weight.transpose(1, 2, 0)
    qkv_home = lax.dynamic_slice_in_dim(heads, side * (n // 2), n // 2, 0)
    qkv_away = lax.dynamic_slice_in_dim(heads, (1 - side) * (n // 2), n // 2, 0)
    out_rows = out_weight.shape[0] // 2
    out_half = lax.dynamic_slice_in_dim(out_weight, group * out_rows, out_rows, 0)

    slots = prep(scalars, keep_col, flat, n, sup)
    dealt = exchange(slots)
    qkv_across = swap(qkv_away, "seq", n // 2)
    out_across = swap(out_half, "seq", n // 2)
    mlp_home, mlp_away = pack(scalars, up_weight, down_weight, n)
    dealt, out_across = lax.optimization_barrier((dealt, out_across))
    owned = pick(scalars, keep_col, dealt, n, sup, per_owner)

    across = swap(owned, "seq", n // 2)
    out_pair = after(jnp.stack([out_half, out_across]), owned)
    mlp_across = swap(after(mlp_away, owned), "seq", n // 2)
    out_mine = jnp.concatenate(
        [out_pair] + [swap(out_pair, "seq", j) for j in range(1, n // 2)], axis=0
    )

    got = exchange_half(fan(owned, across, qkv_home, qkv_across))
    out_second = swap(out_mine, "groups", 1)
    pieces = got[:, : got.shape[1] - 2 * head_rows]
    pieces_other = swap(pieces, "head", 1)
    tokens, attended = attend_fast(scalars, got, pieces_other, head_rows, per_owner, n)

    mlp_pair = jnp.concatenate([mlp_home, mlp_across], axis=1)
    first = exchange_half(mlp_pair)
    att_across = swap(attended, "seq", n // 2)
    pair = jnp.stack([attended, att_across])
    pair, first = lax.optimization_barrier((pair, first))
    gathered = exchange_half(jnp.broadcast_to(pair[None], (n // 2,) + pair.shape))
    second = swap(first, "groups", 1)
    outs = (out_mine, out_second, swap(out_mine, "head", 1), swap(out_second, "head", 1))
    gathered_other = swap(gathered, "head", 1)
    residual, keep, send = mlp(
        scalars, tokens, gathered, gathered_other, outs, first, second, n
    )
    got = swap(send, "head", 1)
    base, terms = join(scalars, keep, got, residual)
    terms = exchange(terms.reshape(n, per_owner, half_width))
    encoded = last(scalars, base, terms)
    return encoded.reshape(1, per_owner, 1, half_width)


def local(patches, keep_list, qkv_weight, out_weight, up_weight, down_weight):
    n = lax.axis_size("seq")
    one_image = patches.shape[0] == 1 and qkv_weight.shape[1] == n and n & (n - 1) == 0
    one_image = one_image and lax.axis_size("groups") == 2 and up_weight.shape[1] == n * 256
    plan = local_fast if one_image else local_general
    return plan(patches, keep_list, qkv_weight, out_weight, up_weight, down_weight)


def solution(mesh):
    return jax.shard_map(
        local,
        mesh=mesh,
        in_specs=(
            P("groups", "seq", None, None),
            P("groups", None),
            P("seq", "head", None),
            P("head", "seq"),
            P("seq", "head"),
            P("head", "seq"),
        ),
        out_specs=P("groups", None, "seq", "head"),
        check_vma=False,
    )
```

```python
import functools
import math

import jax
import jax.numpy as jnp
from jax import lax
from jax.experimental import pallas as pl
from jax.experimental.pallas import tpu as pltpu
from jax.sharding import PartitionSpec as P

F32 = jnp.float32
BF16 = jnp.bfloat16
VMEM = pltpu.VMEM
LIMIT = 32 * 1024 * 1024

def layer_norm(matrix):
    average = jnp.mean(matrix, axis=-1, keepdims=True)
    power = jnp.mean(matrix * matrix, axis=-1, keepdims=True)
    return (matrix - average) * lax.rsqrt(power - average * average + 1e-06)


def attend(queries, keys, values):
    length = queries.shape[0]
    block = math.gcd(length, 512)
    scale = 1.0 / math.sqrt(queries.shape[1])

    def one_block(query_rows):
        scores = (
            lax.dot_general(
                query_rows, keys, (((1,), (1,)), ((), ())), preferred_element_type=jnp.float32
            )
            * scale
        )
        top = jnp.max(scores, axis=1, keepdims=True)
        powers = jnp.exp(scores - top)
        probs = (powers / jnp.sum(powers, axis=1, keepdims=True)).astype(jnp.bfloat16)
        return jnp.dot(probs, values, preferred_element_type=jnp.float32).astype(jnp.bfloat16)

    blocks = lax.map(one_block, queries.reshape(length // block, block, queries.shape[1]))
    return blocks.reshape(length, values.shape[1])


def local_general(patches, keep_list, qkv_weight, out_weight, up_weight, down_weight):
    seq_count = lax.axis_size("seq")
    seq_rank = lax.axis_index("seq")
    head_rank = lax.axis_index("head")
    images = patches.shape[0]
    sup_local = patches.shape[1]
    depth = patches.shape[3]
    half_width = depth // lax.axis_size("head")
    head_count = qkv_weight.shape[1]
    seq_length = sup_local * seq_count * 8 // 5
    per_owner = seq_length // seq_count
    capacity = (4 * sup_local + seq_count - 1) // seq_count
    slot_count = 4 * sup_local
    image_index = jnp.arange(images, dtype=jnp.int32)
    bounds = jnp.arange(seq_count + 1, dtype=jnp.int32) * sup_local
    before = jnp.sum((keep_list[:, :, None] < bounds[None, None, :]).astype(jnp.int32), axis=1)
    starts = bounds[None, :seq_count] + 3 * before[:, :seq_count]
    lengths = sup_local + 3 * (before[:, 1:] - before[:, :seq_count])
    my_start = lax.dynamic_index_in_dim(starts, seq_rank, 1, keepdims=False)
    my_length = lax.dynamic_index_in_dim(lengths, seq_rank, 1, keepdims=False)
    local_ids = seq_rank * sup_local + jnp.arange(sup_local, dtype=jnp.int32)
    kept_flag = jnp.any(keep_list[:, None, :] == local_ids[None, :, None], axis=2).astype(jnp.int32)
    offsets = jnp.arange(sup_local, dtype=jnp.int32)[None, :] + 3 * (
        jnp.cumsum(kept_flag, axis=1) - kept_flag
    )
    slot_ids = jnp.arange(slot_count, dtype=jnp.int32)
    owner_patch = (
        jnp.sum((offsets[:, None, :] <= slot_ids[None, :, None]).astype(jnp.int32), axis=2) - 1
    )
    start_of = jnp.take_along_axis(offsets, owner_patch, axis=1)
    sub_index = jnp.minimum(slot_ids[None, :] - start_of, 3)
    kept_of = jnp.take_along_axis(kept_flag, owner_patch, axis=1)
    flat_patches = patches.reshape(images, sup_local * 4, depth)
    fine_rows = flat_patches[
        image_index[:, None], owner_patch * 4 + jnp.where(kept_of == 1, sub_index, 0)
    ]
    mean_rows = jnp.mean(patches.astype(jnp.float32), axis=2).astype(jnp.bfloat16)
    shared_rows = mean_rows[image_index[:, None], owner_patch]
    local_tokens = jnp.where((kept_of == 1)[:, :, None], fine_rows, shared_rows)
    destinations = jnp.arange(seq_count, dtype=jnp.int32)[:, None, None]
    depth_slots = jnp.arange(capacity, dtype=jnp.int32)[None, None, :]
    positions = (destinations - my_start[None, :, None]) % seq_count + depth_slots * seq_count
    valid = positions < my_length[None, :, None]
    outgoing = local_tokens[image_index[None, :, None], jnp.minimum(positions, slot_count - 1)]
    outgoing = jnp.where(valid[:, :, :, None], outgoing, jnp.zeros((), jnp.bfloat16))
    incoming = lax.all_to_all(outgoing, "seq", split_axis=0, concat_axis=0, tiled=True)
    owned = jnp.arange(per_owner, dtype=jnp.int32) * seq_count + seq_rank
    source = jnp.sum((starts[:, None, :] <= owned[None, :, None]).astype(jnp.int32), axis=2) - 1
    first_of = jnp.take_along_axis(starts, source, axis=1)
    depth_of = (owned[None, :] - first_of) // seq_count
    resident = incoming[source, image_index[:, None], depth_of]
    start_rows = resident.reshape(images * per_owner, depth)
    start_float = start_rows.astype(jnp.float32)
    qkv_full, out_full, up_full, down_full = (
        lax.all_gather(qkv_weight, "seq", axis=0, tiled=True),
        lax.all_gather(out_weight, "seq", axis=1, tiled=True),
        lax.all_gather(up_weight, "seq", axis=0, tiled=True),
        lax.all_gather(down_weight, "seq", axis=1, tiled=True),
    )
    normed = layer_norm(start_float).astype(jnp.bfloat16).reshape(images, per_owner, depth)
    projected = jnp.einsum("ipd,dhc->ihpc", normed, qkv_full, preferred_element_type=jnp.float32)
    head_size = qkv_weight.shape[2] // 3
    sending = projected.astype(jnp.bfloat16).reshape(seq_count, per_owner, 3 * head_size)
    gathered = lax.all_to_all(sending, "seq", split_axis=0, concat_axis=0, tiled=True).reshape(
        seq_length, 3 * head_size
    )
    attended = attend(
        gathered[:, :head_size],
        gathered[:, head_size : 2 * head_size],
        gathered[:, 2 * head_size :],
    )
    returned = lax.all_to_all(
        attended.reshape(seq_count, per_owner, head_size),
        "seq",
        split_axis=0,
        concat_axis=0,
        tiled=True,
    )
    returned = returned.reshape(images, head_count, per_owner, head_size)
    partial_sum = jnp.einsum(
        "ihpc,hcd->ipd",
        returned,
        out_full.reshape(head_count, head_size, depth),
        preferred_element_type=jnp.float32,
    ).reshape(images * per_owner, depth)
    attn_total = lax.psum(partial_sum, "head")
    residual = start_float + attn_total
    residual_half = lax.dynamic_slice_in_dim(residual, head_rank * half_width, half_width, 1)
    normed_two = layer_norm(residual).astype(jnp.bfloat16)
    hidden = jax.nn.gelu(
        jnp.dot(normed_two, up_full, preferred_element_type=jnp.float32), approximate=False
    ).astype(jnp.bfloat16)
    mlp_terms = jnp.dot(hidden, down_full, preferred_element_type=jnp.float32)
    mlp_part = lax.psum_scatter(mlp_terms, "head", scatter_dimension=1, tiled=True)
    encoded = (residual_half + mlp_part).astype(jnp.bfloat16)
    return encoded.reshape(images, per_owner, 1, half_width)


def vspec():
    return pl.BlockSpec(memory_space=VMEM)


def aspec():
    return pl.BlockSpec(memory_space=pl.ANY)


def sspec():
    return pl.BlockSpec(memory_space=pltpu.SMEM)


def params():
    return pltpu.CompilerParams(vmem_limit_bytes=LIMIT)


def cost(micros):
    return pl.CostEstimate(flops=micros * 10**9, bytes_accessed=1 << 20, transcendentals=0)


def struct(shape, dtype=BF16):
    return jax.ShapeDtypeStruct(shape, dtype)


def slot_of(index, n, capacity, cuts):
    device = sum(((index >= j * cuts * capacity).astype(jnp.int32) for j in range(1, n)), 0 * index)
    inner = index - device * (cuts * capacity)
    cut = sum(((inner >= c * capacity).astype(jnp.int32) for c in range(1, cuts)), 0 * index)
    return device, cut, inner - cut * capacity


def one_hot(mask):
    return mask.astype(F32).astype(BF16)


def prep_kernel(n, sup, capacity, rank_ref, keep_ref, patches_ref, out_ref):
    rank = rank_ref[0]
    first = rank * sup
    keep = keep_ref[...]
    rows = 4 * sup
    count = keep.shape[0]

    def places(width, shift):
        ids = lax.broadcasted_iota(jnp.int32, (count, width), 1) >> shift
        kept = jnp.sum((keep == first + ids).astype(jnp.int32), axis=0, keepdims=True)
        below = jnp.sum(
            jnp.logical_and(keep >= first, keep < first + ids).astype(jnp.int32),
            axis=0,
            keepdims=True,
        )
        return kept, below, lax.broadcasted_iota(jnp.int32, (1, width), 1)

    kept, below, lane = places(rows, 2)
    fine_pos = jnp.where(kept == 1, (lane >> 2) + 3 * below + (lane & 3), -1)
    kept, below, lane = places(sup, 0)
    mean_pos = jnp.where(kept == 1, -1, lane + 3 * below)
    start = first + 3 * jnp.sum((keep < first).astype(jnp.int32), axis=0, keepdims=True)
    flat = patches_ref[...]
    cuts = flat.shape[1] // 128
    sup_col = lax.broadcasted_iota(jnp.int32, (sup, rows), 0)
    sup_lane = lax.broadcasted_iota(jnp.int32, (sup, rows), 1) >> 2
    averaging = jnp.where(sup_col == sup_lane, 0.25, 0.0).astype(BF16)
    means = jnp.dot(averaging, flat, preferred_element_type=F32).astype(BF16)
    index = lax.broadcasted_iota(jnp.int32, (n * cuts * capacity, 1), 0)
    device, cut, slot = slot_of(index, n, capacity, cuts)
    pos = ((device - start) & (n - 1)) + slot * n
    total = jnp.zeros((n * cuts * capacity, 128), F32)
    for c in range(cuts):
        at = jnp.where(cut == c, pos, -2)
        features = slice(c * 128, (c + 1) * 128)
        total = (
            total
            + jnp.dot(one_hot(at == fine_pos), flat[:, features], preferred_element_type=F32)
            + jnp.dot(one_hot(at == mean_pos), means[:, features], preferred_element_type=F32)
        )
    out_ref[...] = total.astype(BF16)


def prep(scalars, keep_col, flat, n, sup, capacity):
    width = flat.shape[1] // 2
    shape = (n * capacity * width // 128, 128)
    return pl.pallas_call(
        functools.partial(prep_kernel, n, sup, capacity),
        grid_spec=pltpu.PrefetchScalarGridSpec(
            num_scalar_prefetch=1,
            grid=(1,),
            in_specs=[
                pl.BlockSpec(keep_col.shape, lambda i, ref: (0, 0)),
                pl.BlockSpec((flat.shape[0], width), lambda i, ref: (0, ref[1])),
            ],
            out_specs=pl.BlockSpec(shape, lambda i, ref: (0, 0)),
        ),
        out_shape=struct(shape),
        compiler_params=params(),
    )(scalars, keep_col, flat)


def pick_kernel(n, sup, per_owner, capacity, rank_ref, keep_ref, got_ref, out_ref):
    rank = rank_ref[0]
    keep = keep_ref[...]
    count = keep.shape[0]
    lanes = got_ref.shape[0]
    cuts = lanes // (n * capacity)
    source, _, _ = slot_of(
        lax.broadcasted_iota(jnp.int32, (count, lanes), 1), n, capacity, cuts
    )
    low = jnp.sum((keep < source * sup).astype(jnp.int32), axis=0, keepdims=True)
    high = jnp.sum((keep < source * sup + sup).astype(jnp.int32), axis=0, keepdims=True)
    source, cut, slot = slot_of(
        lax.broadcasted_iota(jnp.int32, (1, lanes), 1), n, capacity, cuts
    )
    start = source * sup + 3 * low
    stop = source * sup + sup + 3 * high
    token = start + ((rank - start) & (n - 1)) + slot * n
    row = jnp.where(token < stop, token >> (n.bit_length() - 1), -1)
    own = lax.broadcasted_iota(jnp.int32, (per_owner, lanes), 0)
    got = got_ref[...]
    for c in range(cuts):
        choose = one_hot(own == jnp.where(cut == c, row, -1))
        owned = jnp.dot(choose, got, preferred_element_type=F32).astype(BF16)
        out_ref[c * per_owner : (c + 1) * per_owner] = owned


def pick(scalars, keep_col, got, n, sup, per_owner, capacity):
    cuts = got.shape[0] // (n * capacity)
    return pl.pallas_call(
        functools.partial(pick_kernel, n, sup, per_owner, capacity),
        in_specs=[sspec(), vspec(), vspec()],
        out_specs=vspec(),
        out_shape=struct((cuts * per_owner, 128)),
        compiler_params=params(),
    )(scalars, keep_col, got)


def pack_kernel(n, rank_ref, qkv_ref, out_weight_ref, up_ref, down_ref, *refs):
    near, away_ref, sem = refs[: n // 2], refs[n // 2], refs[n // 2 + 1]
    rank, part = rank_ref[0], rank_ref[2]
    half = n // 2
    rows = up_ref.shape[0]
    wide = up_ref.shape[1] // n
    units = wide // 2
    long = out_weight_ref.shape[0]
    copies = []
    for j in range(half):
        dest = rank ^ j
        for c in range(2):
            at = pl.ds(pl.multiple_of(dest * wide + c * units, 128), units)
            copies.append((up_ref.at[:, at], near[j].at[pl.ds(c * rows, rows)]))
        at = pl.ds(pl.multiple_of(dest * wide, 128), wide)
        copies.append((down_ref.at[at], near[j].at[pl.ds(2 * rows, wide)]))
        copies.append((out_weight_ref, near[j].at[pl.ds(2 * rows + wide, long)]))
        copies.append(
            (qkv_ref.at[dest], near[j].at[pl.ds(2 * rows + wide + long, qkv_ref.shape[1])])
        )
        dest = (rank // half ^ 1) * half + j
        at = pl.ds(pl.multiple_of(dest * wide + part * units, 128), units)
        copies.append((up_ref.at[:, at], away_ref.at[j, pl.ds(0, rows)]))
        copies.append((down_ref.at[at], away_ref.at[j, pl.ds(rows, units)]))
    started = []
    for i, (src, dst) in enumerate(copies):
        copy = pltpu.make_async_copy(src, dst, sem.at[i])
        copy.start()
        started.append(copy)
    for copy in started:
        copy.wait()


def pack(scalars, qkv, out_weight, up, down, n):
    wide = up.shape[1] // n
    near = struct((2 * up.shape[0] + wide + out_weight.shape[0] + qkv.shape[1], 128))
    away = struct((n // 2, up.shape[0] + wide // 2, 128))
    outs = pl.pallas_call(
        functools.partial(pack_kernel, n),
        in_specs=[sspec()] + [aspec()] * 4,
        out_specs=[aspec()] * (n // 2 + 1),
        out_shape=[near] * (n // 2) + [away],
        scratch_shapes=[pltpu.SemaphoreType.DMA((7 * n // 2,))],
        compiler_params=params(),
    )(scalars, qkv, out_weight, up, down)
    return list(outs[:-1]), outs[-1]


def fan_kernel(rank_ref, owned_ref, across_ref, mine_ref, other_ref, out_ref):
    part = rank_ref[2]
    rows = owned_ref.shape[0]
    count = out_ref.shape[0]
    depth = (out_ref.shape[1] - 2 * rows) // 2
    for d in range(count):
        out_ref[d, :rows] = owned_ref[...]
        out_ref[d, rows : 2 * rows] = across_ref[...]
        at = pl.ds(pl.multiple_of(2 * rows + part * depth, 32), depth)
        out_ref[d, at] = mine_ref[d * depth : (d + 1) * depth]
        at = pl.ds(pl.multiple_of(2 * rows + (1 - part) * depth, 32), depth)
        out_ref[d, at] = other_ref[d * depth : (d + 1) * depth]


def fan(scalars, owned, across, mine, other, head_rows, n):
    shape = struct((n // 2, 2 * owned.shape[0] + head_rows, 128))
    return pl.pallas_call(
        fan_kernel,
        in_specs=[sspec()] + [vspec()] * 4,
        out_specs=vspec(),
        out_shape=shape,
        compiler_params=params(),
    )(scalars, owned, across, mine, other)


def source_of(rank, n, q, k):
    return (rank // (n // 2) ^ k) * (n // 2) + q


def norm_rows(x):
    average = jnp.mean(x, axis=-1, keepdims=True)
    power = jnp.mean(x * x, axis=-1, keepdims=True)
    return (x - average) * lax.rsqrt(power - average * average + 1e-06)


def attend_kernel(n, part, rank_ref, mine_ref, other_ref, *refs):
    near, (tokens_ref, out_ref, weight_ref) = refs[: n // 2], refs[n // 2 :]
    rank, half = rank_ref[0], rank_ref[1]
    rows = other_ref.shape[1] // 2
    cuts = rows // part
    width = cuts * 128
    depth = weight_ref.shape[0]
    for q in range(n // 2):
        for k in range(2):
            source = source_of(rank, n, q, k)
            at = pl.ds(pl.multiple_of(source * part, part), part)
            for c in range(cuts):
                cut = slice(k * rows + c * part, k * rows + (c + 1) * part)
                to = pl.ds(pl.multiple_of(half * width + c * 128, 128), 128)
                tokens_ref[at, to] = mine_ref[q, cut]
                to = pl.ds(pl.multiple_of((1 - half) * width + c * 128, 128), 128)
                tokens_ref[at, to] = other_ref[q, cut]
        source = source_of(rank, n, q, 1)
        to = pl.ds(pl.multiple_of(source * 128, 128), 128)
        weight_ref[:, to] = mine_ref[q, 2 * rows :]
        to = pl.ds(pl.multiple_of((rank ^ q) * 128, 128), 128)
        weight_ref[:, to] = near[q][near[q].shape[0] - depth :]
    normed = norm_rows(tokens_ref[...].astype(F32)).astype(BF16)
    projected = lax.dot_general(
        normed, weight_ref[...], (((1,), (1,)), ((), ())), preferred_element_type=F32
    ).astype(BF16)
    size = projected.shape[1] // 3
    queries = projected[:, :size]
    keys = projected[:, size : 2 * size]
    values = projected[:, 2 * size :]
    scores = lax.dot_general(
        queries, keys, (((1,), (1,)), ((), ())), preferred_element_type=F32
    ) * (1.0 / math.sqrt(size))
    powers = jnp.exp(scores - jnp.max(scores, axis=1, keepdims=True))
    probs = (powers / jnp.sum(powers, axis=1, keepdims=True)).astype(BF16)
    attended = lax.dot_general(
        values, probs, (((0,), (1,)), ((), ())), preferred_element_type=F32
    ).astype(BF16)
    out_ref[...] = attended


def attend_fast(scalars, mine, other, near, head_rows, per_owner, n):
    length = n * per_owner
    depth = other.shape[1] // (2 * per_owner) * 256
    size = head_rows // 3
    return pl.pallas_call(
        functools.partial(attend_kernel, n, per_owner),
        in_specs=[sspec()] + [vspec()] * (2 + n // 2),
        out_specs=[vspec()] * 2,
        out_shape=[struct((length, depth)), struct((size, length))],
        scratch_shapes=[VMEM((head_rows, n * 128), BF16)],
        compiler_params=params(),
        cost_estimate=cost(30),
    )(scalars, mine, other, *near)


def mlp_kernel(
    n,
    rank_ref,
    tokens_ref,
    pieces,
    outs_near,
    outs_far,
    near,
    far_ref,
    residual_ref,
    keep_ref,
    send_ref,
    up_ref,
    down_ref,
    row_ref,
    whole_ref,
    joined_ref,
):
    rank, half, group = rank_ref[0], rank_ref[1], rank_ref[2]
    block = up_ref.shape[0] // n
    wide = down_ref.shape[0]
    unit = wide // 2
    size = pieces[0].shape[2]
    long = outs_near[0].shape[1]
    rows = long // 2
    for j in range(n // 2):
        source = rank ^ j
        at = pl.ds(pl.multiple_of(source * block, block), block)
        to = pl.ds(pl.multiple_of(source * 128, 128), 128)
        for c in range(2):
            up_ref[at, c * unit : (c + 1) * unit] = near[j][c * block : (c + 1) * block]
        down_ref[:, to] = near[j][2 * block : 2 * block + wide]
        for core in range(2):
            whole_ref[core, :, to] = outs_near[core][j]
        source = source_of(rank, n, j, 1)
        at = pl.ds(pl.multiple_of(source * block, block), block)
        to = pl.ds(pl.multiple_of(source * 128, 128), 128)
        for c in range(2):
            units = pl.ds(pl.multiple_of((group ^ c) * unit, unit), unit)
            high = c * (block + unit)
            up_ref[at, units] = far_ref[j, high : high + block]
            down_ref[units, to] = far_ref[j, high + block : high + block + unit]
        source = rank ^ j ^ (n // 2)
        to = pl.ds(pl.multiple_of(source * 128, 128), 128)
        for core in range(2):
            for c in range(2):
                at = pl.ds(pl.multiple_of((group ^ c) * rows, rows), rows)
                whole_ref[core, at, to] = outs_far[core][j, c * rows : (c + 1) * rows]
            for k in range(2):
                at = pl.ds(pl.multiple_of((rank ^ j ^ (k * n // 2)) * size, size), size)
                joined_ref[core, at] = pieces[core][j, k]
    dims = (((0,), (0,)), ((), ()))
    row_ref[...] = (
        tokens_ref[...].astype(F32)
        + lax.dot_general(joined_ref[0], whole_ref[0], dims, preferred_element_type=F32)
        + lax.dot_general(joined_ref[1], whole_ref[1], dims, preferred_element_type=F32)
    )
    part = residual_ref.shape[0]
    width = residual_ref.shape[1]
    my_cols = pl.ds(pl.multiple_of(half * width, width), width)
    other_cols = pl.ds(pl.multiple_of((1 - half) * width, width), width)
    residual_ref[...] = row_ref[pl.ds(pl.multiple_of(rank * part, part), part), my_cols]
    normed = norm_rows(row_ref[...]).astype(BF16)
    raw = jnp.dot(normed, up_ref[...], preferred_element_type=F32)
    hidden = (0.5 * raw * (1.0 + lax.erf(raw * math.sqrt(0.5)))).astype(BF16)
    keep_ref[...] = jnp.dot(hidden, down_ref[:, my_cols], preferred_element_type=F32)
    send_ref[...] = jnp.dot(hidden, down_ref[:, other_cols], preferred_element_type=F32).astype(BF16)


def mlp(scalars, tokens, pieces, outs_near, outs_far, near, far, n):
    length, depth = tokens.shape
    width = depth // 2
    wide = 2 * (far.shape[1] // 2 - depth // n)
    inner = n * pieces[0].shape[2]

    def kernel(scalars, tokens, a, b, c, d, e, f, *refs):
        near, (far, *refs) = refs[: n // 2], refs[n // 2 :]
        mlp_kernel(n, scalars, tokens, (a, b), (c, d), (e, f), near, far, *refs)

    return pl.pallas_call(
        kernel,
        in_specs=[sspec()] + [vspec()] * (8 + n // 2),
        out_specs=[vspec()] * 3,
        out_shape=[
            struct((length // n, width), F32),
            struct((length, width), F32),
            struct((length, width)),
        ],
        scratch_shapes=[
            VMEM((depth, wide), BF16),
            VMEM((wide, depth), BF16),
            VMEM((length, depth), F32),
            VMEM((2, inner, depth), BF16),
            VMEM((2, inner, length), BF16),
        ],
        compiler_params=params(),
    )(scalars, tokens, *pieces, *outs_near, *outs_far, *near, far)


def join_kernel(rank_ref, keep_ref, got_ref, residual_ref, base_ref, out_ref):
    part = residual_ref.shape[0]
    mine = pl.ds(pl.multiple_of(rank_ref[0] * part, part), part)
    base_ref[...] = keep_ref[mine] + got_ref[mine].astype(F32) + residual_ref[...]
    out_ref[...] = (keep_ref[...] + got_ref[...].astype(F32)).astype(BF16)


def join(scalars, keep, got, residual):
    return pl.pallas_call(
        join_kernel,
        in_specs=[sspec()] + [vspec()] * 3,
        out_specs=[vspec()] * 2,
        out_shape=[struct(residual.shape, F32), struct(keep.shape)],
        compiler_params=params(),
    )(scalars, keep, got, residual)


def last_kernel(n, rank_ref, base_ref, terms_ref, out_ref):
    rank = rank_ref[0]
    total = base_ref[...]
    for j in range(1, n):
        total = total + terms_ref[rank ^ j].astype(F32)
    out_ref[...] = total.astype(BF16)


def last(scalars, base, terms):
    return pl.pallas_call(
        functools.partial(last_kernel, terms.shape[0]),
        in_specs=[sspec()] + [vspec()] * 2,
        out_specs=vspec(),
        out_shape=struct(base.shape),
        compiler_params=params(),
    )(scalars, base, terms)


def swap(value, axis, j):
    n = lax.axis_size(axis)
    return lax.ppermute(value, axis, [(i, i ^ j) for i in range(n)])


def exchange(value):
    return lax.all_to_all(value, "seq", split_axis=0, concat_axis=0, tiled=True)


def exchange_half(value):
    n = lax.axis_size("seq")
    groups = [list(range(n // 2)), list(range(n // 2, n))]
    return lax.all_to_all(
        value, "seq", split_axis=0, concat_axis=0, axis_index_groups=groups, tiled=True
    )


def after(value, *others):
    return lax.optimization_barrier((value, *others))[0]


def local_fast(patches, keep_list, qkv_weight, out_weight, up_weight, down_weight):
    n = lax.axis_size("seq")
    rank, head, group = (
        lax.axis_index(name).astype(jnp.int32) for name in ("seq", "head", "groups")
    )
    scalars = jnp.stack([rank, head, group])
    half = n // 2
    side = rank // half
    sup, depth = patches.shape[1], patches.shape[3]
    length = sup * n * 8 // 5
    per_owner = length // n
    half_width = depth // 2
    head_rows = qkv_weight.shape[2]
    part_rows = head_rows // 2
    out_rows = out_weight.shape[0] // 2
    capacity = (4 * sup + n - 1) // n
    keep_col = keep_list.reshape(-1, 1)
    flat = patches.reshape(4 * sup, depth)
    heads = qkv_weight.transpose(1, 2, 0)

    qkv_away = lax.dynamic_slice(
        heads, ((1 - side) * half, group * part_rows, 0), (half, part_rows, 128)
    ).reshape(half * part_rows, 128)
    out_away = lax.dynamic_slice_in_dim(out_weight, group * out_rows, out_rows, 0)
    early = swap(jnp.concatenate([qkv_away, out_away]), "seq", half)
    slots = prep(scalars, keep_col, flat, n, sup, capacity)
    slots, early = lax.optimization_barrier((slots, early))
    near, mlp_away = pack(scalars, heads, out_weight, up_weight, down_weight, n)
    dealt = exchange(slots)
    near = [near[0]] + [swap(near[j], "seq", j) for j in range(1, half)]
    early_other = swap(early, "groups", 1)
    dealt, early_other, *near = lax.optimization_barrier((dealt, early_other, *near))
    owned = pick(scalars, keep_col, dealt, n, sup, per_owner, capacity)

    across = swap(owned, "seq", half)
    mlp_mine = swap(after(mlp_away, across), "seq", half)
    got = exchange_half(fan(scalars, owned, across, early, early_other, head_rows, n))
    got, mlp_mine = lax.optimization_barrier((got, mlp_mine))

    pieces = got[:, : got.shape[1] - head_rows]
    pieces_other = swap(pieces, "head", 1)
    mlp_other = swap(mlp_mine, "groups", 1)
    out_far = jnp.concatenate([early[half * part_rows :], early_other[half * part_rows :]])
    out_far = after(out_far, got)
    tokens, attended = attend_fast(scalars, got, pieces_other, near, head_rows, per_owner, n)

    outs_far = [out_far] + [swap(out_far, "seq", j) for j in range(1, half)]
    att_across = swap(attended, "seq", half)
    mlp_far = exchange_half(jnp.concatenate([mlp_mine, mlp_other], axis=1))
    att_across, *outs_far = lax.optimization_barrier((att_across, *outs_far))
    pair = jnp.stack([attended, att_across])
    gathered = jnp.stack([pair] + [swap(pair, "seq", j) for j in range(1, half)])
    outs_far = jnp.stack(outs_far)
    top = near[0].shape[0] - head_rows - 2 * out_rows
    outs_near = jnp.stack([block[top : top + 2 * out_rows] for block in near])
    residual, keep, send = mlp(
        scalars,
        tokens,
        (gathered, swap(gathered, "head", 1)),
        (outs_near, swap(outs_near, "head", 1)),
        (outs_far, swap(outs_far, "head", 1)),
        near,
        mlp_far,
        n,
    )
    sent = swap(send, "head", 1)
    base, terms = join(scalars, keep, sent, residual)
    terms = exchange(terms.reshape(n, per_owner, half_width))
    encoded = last(scalars, base, terms)
    return encoded.reshape(1, per_owner, 1, half_width)


def local(patches, keep_list, qkv_weight, out_weight, up_weight, down_weight):
    n = lax.axis_size("seq")
    one_image = patches.shape[0] == 1 and qkv_weight.shape[1] == n and n & (n - 1) == 0
    one_image = one_image and lax.axis_size("groups") == 2 and up_weight.shape[1] == n * 256
    plan = local_fast if one_image else local_general
    return plan(patches, keep_list, qkv_weight, out_weight, up_weight, down_weight)


def solution(mesh):
    return jax.shard_map(
        local,
        mesh=mesh,
        in_specs=(
            P("groups", "seq", None, None),
            P("groups", None),
            P("seq", "head", None),
            P("head", "seq"),
            P("seq", "head"),
            P("head", "seq"),
        ),
        out_specs=P("groups", None, "seq", "head"),
        check_vma=False,
    )
```

```python
import functools
import math

import jax
import jax.numpy as jnp
from jax import lax
from jax.experimental import pallas as pl
from jax.experimental.pallas import tpu as pltpu
from jax.sharding import PartitionSpec as P

F32 = jnp.float32
BF16 = jnp.bfloat16
VMEM = pltpu.VMEM
LIMIT = 24 * 1024 * 1024

def layer_norm(matrix):
    average = jnp.mean(matrix, axis=-1, keepdims=True)
    power = jnp.mean(matrix * matrix, axis=-1, keepdims=True)
    return (matrix - average) * lax.rsqrt(power - average * average + 1e-06)


def attend(queries, keys, values):
    length = queries.shape[0]
    block = math.gcd(length, 512)
    scale = 1.0 / math.sqrt(queries.shape[1])

    def one_block(query_rows):
        scores = (
            lax.dot_general(
                query_rows, keys, (((1,), (1,)), ((), ())), preferred_element_type=jnp.float32
            )
            * scale
        )
        top = jnp.max(scores, axis=1, keepdims=True)
        powers = jnp.exp(scores - top)
        probs = (powers / jnp.sum(powers, axis=1, keepdims=True)).astype(jnp.bfloat16)
        return jnp.dot(probs, values, preferred_element_type=jnp.float32).astype(jnp.bfloat16)

    blocks = lax.map(one_block, queries.reshape(length // block, block, queries.shape[1]))
    return blocks.reshape(length, values.shape[1])


def local_general(patches, keep_list, qkv_weight, out_weight, up_weight, down_weight):
    seq_count = lax.axis_size("seq")
    seq_rank = lax.axis_index("seq")
    head_rank = lax.axis_index("head")
    images = patches.shape[0]
    sup_local = patches.shape[1]
    depth = patches.shape[3]
    half_width = depth // lax.axis_size("head")
    head_count = qkv_weight.shape[1]
    seq_length = sup_local * seq_count * 8 // 5
    per_owner = seq_length // seq_count
    capacity = (4 * sup_local + seq_count - 1) // seq_count
    slot_count = 4 * sup_local
    image_index = jnp.arange(images, dtype=jnp.int32)
    bounds = jnp.arange(seq_count + 1, dtype=jnp.int32) * sup_local
    before = jnp.sum((keep_list[:, :, None] < bounds[None, None, :]).astype(jnp.int32), axis=1)
    starts = bounds[None, :seq_count] + 3 * before[:, :seq_count]
    lengths = sup_local + 3 * (before[:, 1:] - before[:, :seq_count])
    my_start = lax.dynamic_index_in_dim(starts, seq_rank, 1, keepdims=False)
    my_length = lax.dynamic_index_in_dim(lengths, seq_rank, 1, keepdims=False)
    local_ids = seq_rank * sup_local + jnp.arange(sup_local, dtype=jnp.int32)
    kept_flag = jnp.any(keep_list[:, None, :] == local_ids[None, :, None], axis=2).astype(jnp.int32)
    offsets = jnp.arange(sup_local, dtype=jnp.int32)[None, :] + 3 * (
        jnp.cumsum(kept_flag, axis=1) - kept_flag
    )
    slot_ids = jnp.arange(slot_count, dtype=jnp.int32)
    owner_patch = (
        jnp.sum((offsets[:, None, :] <= slot_ids[None, :, None]).astype(jnp.int32), axis=2) - 1
    )
    start_of = jnp.take_along_axis(offsets, owner_patch, axis=1)
    sub_index = jnp.minimum(slot_ids[None, :] - start_of, 3)
    kept_of = jnp.take_along_axis(kept_flag, owner_patch, axis=1)
    flat_patches = patches.reshape(images, sup_local * 4, depth)
    fine_rows = flat_patches[
        image_index[:, None], owner_patch * 4 + jnp.where(kept_of == 1, sub_index, 0)
    ]
    mean_rows = jnp.mean(patches.astype(jnp.float32), axis=2).astype(jnp.bfloat16)
    shared_rows = mean_rows[image_index[:, None], owner_patch]
    local_tokens = jnp.where((kept_of == 1)[:, :, None], fine_rows, shared_rows)
    destinations = jnp.arange(seq_count, dtype=jnp.int32)[:, None, None]
    depth_slots = jnp.arange(capacity, dtype=jnp.int32)[None, None, :]
    positions = (destinations - my_start[None, :, None]) % seq_count + depth_slots * seq_count
    valid = positions < my_length[None, :, None]
    outgoing = local_tokens[image_index[None, :, None], jnp.minimum(positions, slot_count - 1)]
    outgoing = jnp.where(valid[:, :, :, None], outgoing, jnp.zeros((), jnp.bfloat16))
    incoming = lax.all_to_all(outgoing, "seq", split_axis=0, concat_axis=0, tiled=True)
    owned = jnp.arange(per_owner, dtype=jnp.int32) * seq_count + seq_rank
    source = jnp.sum((starts[:, None, :] <= owned[None, :, None]).astype(jnp.int32), axis=2) - 1
    first_of = jnp.take_along_axis(starts, source, axis=1)
    depth_of = (owned[None, :] - first_of) // seq_count
    resident = incoming[source, image_index[:, None], depth_of]
    start_rows = resident.reshape(images * per_owner, depth)
    start_float = start_rows.astype(jnp.float32)
    qkv_full, out_full, up_full, down_full = (
        lax.all_gather(qkv_weight, "seq", axis=0, tiled=True),
        lax.all_gather(out_weight, "seq", axis=1, tiled=True),
        lax.all_gather(up_weight, "seq", axis=0, tiled=True),
        lax.all_gather(down_weight, "seq", axis=1, tiled=True),
    )
    normed = layer_norm(start_float).astype(jnp.bfloat16).reshape(images, per_owner, depth)
    projected = jnp.einsum("ipd,dhc->ihpc", normed, qkv_full, preferred_element_type=jnp.float32)
    head_size = qkv_weight.shape[2] // 3
    sending = projected.astype(jnp.bfloat16).reshape(seq_count, per_owner, 3 * head_size)
    gathered = lax.all_to_all(sending, "seq", split_axis=0, concat_axis=0, tiled=True).reshape(
        seq_length, 3 * head_size
    )
    attended = attend(
        gathered[:, :head_size],
        gathered[:, head_size : 2 * head_size],
        gathered[:, 2 * head_size :],
    )
    returned = lax.all_to_all(
        attended.reshape(seq_count, per_owner, head_size),
        "seq",
        split_axis=0,
        concat_axis=0,
        tiled=True,
    )
    returned = returned.reshape(images, head_count, per_owner, head_size)
    partial_sum = jnp.einsum(
        "ihpc,hcd->ipd",
        returned,
        out_full.reshape(head_count, head_size, depth),
        preferred_element_type=jnp.float32,
    ).reshape(images * per_owner, depth)
    attn_total = lax.psum(partial_sum, "head")
    residual = start_float + attn_total
    residual_half = lax.dynamic_slice_in_dim(residual, head_rank * half_width, half_width, 1)
    normed_two = layer_norm(residual).astype(jnp.bfloat16)
    hidden = jax.nn.gelu(
        jnp.dot(normed_two, up_full, preferred_element_type=jnp.float32), approximate=False
    ).astype(jnp.bfloat16)
    mlp_terms = jnp.dot(hidden, down_full, preferred_element_type=jnp.float32)
    mlp_part = lax.psum_scatter(mlp_terms, "head", scatter_dimension=1, tiled=True)
    encoded = (residual_half + mlp_part).astype(jnp.bfloat16)
    return encoded.reshape(images, per_owner, 1, half_width)


def vspec():
    return pl.BlockSpec(memory_space=VMEM)


def aspec():
    return pl.BlockSpec(memory_space=pl.ANY)


def sspec():
    return pl.BlockSpec(memory_space=pltpu.SMEM)


def hspec():
    return pl.BlockSpec(memory_space=pltpu.HBM)


def run_copies(copies, sem, base=0):
    started = [
        pltpu.make_async_copy(src, dst, sem.at[base + i]) for i, (src, dst) in enumerate(copies)
    ]
    for copy in started:
        copy.start()

    def wait():
        for copy in started:
            copy.wait()

    return wait


def params():
    return pltpu.CompilerParams(vmem_limit_bytes=LIMIT)


def cost(micros):
    return pl.CostEstimate(flops=micros * 10**9, bytes_accessed=1 << 20, transcendentals=0)


def struct(shape, dtype=BF16):
    return jax.ShapeDtypeStruct(shape, dtype)


def slot_of(index, n, capacity, cuts):
    device = sum(((index >= j * cuts * capacity).astype(jnp.int32) for j in range(1, n)), 0 * index)
    inner = index - device * (cuts * capacity)
    cut = sum(((inner >= c * capacity).astype(jnp.int32) for c in range(1, cuts)), 0 * index)
    return device, cut, inner - cut * capacity


def one_hot(mask):
    return mask.astype(F32).astype(BF16)


def prep_kernel(n, sup, capacity, rank_ref, keep_ref, patches_ref, out_ref):
    rank = rank_ref[0]
    first = rank * sup
    keep = keep_ref[...]
    rows = 4 * sup
    count = keep.shape[0]

    def places(width, shift):
        ids = lax.broadcasted_iota(jnp.int32, (count, width), 1) >> shift
        kept = jnp.sum((keep == first + ids).astype(jnp.int32), axis=0, keepdims=True)
        below = jnp.sum(
            jnp.logical_and(keep >= first, keep < first + ids).astype(jnp.int32),
            axis=0,
            keepdims=True,
        )
        return kept, below, lax.broadcasted_iota(jnp.int32, (1, width), 1)

    kept, below, lane = places(rows, 2)
    fine_pos = jnp.where(kept == 1, (lane >> 2) + 3 * below + (lane & 3), -1)
    kept, below, lane = places(sup, 0)
    mean_pos = jnp.where(kept == 1, -1, lane + 3 * below)
    start = first + 3 * jnp.sum((keep < first).astype(jnp.int32), axis=0, keepdims=True)
    flat = patches_ref[...]
    cuts = flat.shape[1] // 128
    sup_col = lax.broadcasted_iota(jnp.int32, (sup, rows), 0)
    sup_lane = lax.broadcasted_iota(jnp.int32, (sup, rows), 1) >> 2
    averaging = jnp.where(sup_col == sup_lane, 0.25, 0.0).astype(BF16)
    means = jnp.dot(averaging, flat, preferred_element_type=F32).astype(BF16)
    index = lax.broadcasted_iota(jnp.int32, (n * cuts * capacity, 1), 0)
    device, cut, slot = slot_of(index, n, capacity, cuts)
    pos = ((device - start) & (n - 1)) + slot * n
    total = jnp.zeros((n * cuts * capacity, 128), F32)
    for c in range(cuts):
        at = jnp.where(cut == c, pos, -2)
        features = slice(c * 128, (c + 1) * 128)
        total = (
            total
            + jnp.dot(one_hot(at == fine_pos), flat[:, features], preferred_element_type=F32)
            + jnp.dot(one_hot(at == mean_pos), means[:, features], preferred_element_type=F32)
        )
    out_ref[...] = total.astype(BF16)


def prep(scalars, keep_col, flat, n, sup, capacity):
    width = flat.shape[1] // 2
    shape = (n * capacity * width // 128, 128)
    return pl.pallas_call(
        functools.partial(prep_kernel, n, sup, capacity),
        grid_spec=pltpu.PrefetchScalarGridSpec(
            num_scalar_prefetch=1,
            grid=(1,),
            in_specs=[
                pl.BlockSpec(keep_col.shape, lambda i, ref: (0, 0)),
                pl.BlockSpec((flat.shape[0], width), lambda i, ref: (0, ref[1])),
            ],
            out_specs=pl.BlockSpec(shape, lambda i, ref: (0, 0)),
        ),
        out_shape=struct(shape),
        compiler_params=params(),
    )(scalars, keep_col, flat)


def pick_kernel(n, sup, per_owner, capacity, rank_ref, keep_ref, got_ref, out_ref):
    rank = rank_ref[0]
    keep = keep_ref[...]
    count = keep.shape[0]
    lanes = got_ref.shape[0]
    cuts = lanes // (n * capacity)
    source, _, _ = slot_of(
        lax.broadcasted_iota(jnp.int32, (count, lanes), 1), n, capacity, cuts
    )
    low = jnp.sum((keep < source * sup).astype(jnp.int32), axis=0, keepdims=True)
    high = jnp.sum((keep < source * sup + sup).astype(jnp.int32), axis=0, keepdims=True)
    source, cut, slot = slot_of(
        lax.broadcasted_iota(jnp.int32, (1, lanes), 1), n, capacity, cuts
    )
    start = source * sup + 3 * low
    stop = source * sup + sup + 3 * high
    token = start + ((rank - start) & (n - 1)) + slot * n
    row = jnp.where(token < stop, token >> (n.bit_length() - 1), -1)
    own = lax.broadcasted_iota(jnp.int32, (per_owner, lanes), 0)
    got = got_ref[...]
    for c in range(cuts):
        choose = one_hot(own == jnp.where(cut == c, row, -1))
        owned = jnp.dot(choose, got, preferred_element_type=F32).astype(BF16)
        out_ref[c * per_owner : (c + 1) * per_owner] = owned


def pick(scalars, keep_col, got, n, sup, per_owner, capacity):
    cuts = got.shape[0] // (n * capacity)
    return pl.pallas_call(
        functools.partial(pick_kernel, n, sup, per_owner, capacity),
        in_specs=[sspec(), vspec(), vspec()],
        out_specs=vspec(),
        out_shape=struct((cuts * per_owner, 128)),
        compiler_params=params(),
    )(scalars, keep_col, got)


def pack_kernel(n, rank_ref, qkv_ref, out_weight_ref, up_ref, down_ref, *refs):
    near, away_ref, sem = refs[: n // 2], refs[n // 2], refs[n // 2 + 1]
    rank, part = rank_ref[0], rank_ref[2]
    half = n // 2
    rows = up_ref.shape[0]
    wide = up_ref.shape[1] // n
    units = wide // 2
    long = out_weight_ref.shape[0]
    copies = []
    for j in range(half):
        dest = rank ^ j
        for c in range(2):
            at = pl.ds(pl.multiple_of(dest * wide + c * units, 128), units)
            copies.append((up_ref.at[:, at], near[j].at[pl.ds(c * rows, rows)]))
        at = pl.ds(pl.multiple_of(dest * wide, 128), wide)
        copies.append((down_ref.at[at], near[j].at[pl.ds(2 * rows, wide)]))
        copies.append((out_weight_ref, near[j].at[pl.ds(2 * rows + wide, long)]))
        copies.append(
            (qkv_ref.at[dest], near[j].at[pl.ds(2 * rows + wide + long, qkv_ref.shape[1])])
        )
        dest = (rank // half ^ 1) * half + j
        at = pl.ds(pl.multiple_of(dest * wide + part * units, 128), units)
        copies.append((up_ref.at[:, at], away_ref.at[j, pl.ds(0, rows)]))
        copies.append((down_ref.at[at], away_ref.at[j, pl.ds(rows, units)]))
    run_copies(copies, sem)()


def pack(scalars, qkv, out_weight, up, down, n):
    wide = up.shape[1] // n
    near = struct((2 * up.shape[0] + wide + out_weight.shape[0] + qkv.shape[1], 128))
    away = struct((n // 2, up.shape[0] + wide // 2, 128))
    outs = pl.pallas_call(
        functools.partial(pack_kernel, n),
        in_specs=[sspec()] + [hspec()] * 4,
        out_specs=[hspec()] * (n // 2 + 1),
        out_shape=[near] * (n // 2) + [away],
        scratch_shapes=[pltpu.SemaphoreType.DMA((7 * n // 2,))],
        compiler_params=params(),
    )(scalars, qkv, out_weight, up, down)
    return list(outs[:-1]), outs[-1]


def early_kernel(n, rank_ref, qkv_ref, out_weight_ref, heads_ref, rows_ref, sem):
    rank, part = rank_ref[0], rank_ref[2]
    half = n // 2
    depth = heads_ref.shape[0] // half
    long = rows_ref.shape[0]
    copies = []
    for d in range(half):
        dest = (rank // half ^ 1) * half + d
        at = pl.ds(pl.multiple_of(part * depth, 32), depth)
        copies.append((qkv_ref.at[dest, at], heads_ref.at[pl.ds(d * depth, depth)]))
    at = pl.ds(pl.multiple_of(part * long, 128), long)
    copies.append((out_weight_ref.at[at], rows_ref))
    run_copies(copies, sem)()


def early_blocks(scalars, qkv, out_weight, n):
    return pl.pallas_call(
        functools.partial(early_kernel, n),
        in_specs=[sspec()] + [hspec()] * 2,
        out_specs=[aspec()] * 2,
        out_shape=[
            struct((n // 2 * qkv.shape[1] // 2, 128)),
            struct((out_weight.shape[0] // 2, 128)),
        ],
        scratch_shapes=[pltpu.SemaphoreType.DMA((n // 2 + 1,))],
        compiler_params=params(),
    )(scalars, qkv, out_weight)


def fan_kernel(rank_ref, owned_ref, across_ref, mine_ref, other_ref, out_ref):
    part = rank_ref[2]
    rows = owned_ref.shape[0]
    count = out_ref.shape[0]
    depth = (out_ref.shape[1] - 2 * rows) // 2
    for d in range(count):
        out_ref[d, :rows] = owned_ref[...]
        out_ref[d, rows : 2 * rows] = across_ref[...]
        at = pl.ds(pl.multiple_of(2 * rows + part * depth, 32), depth)
        out_ref[d, at] = mine_ref[d * depth : (d + 1) * depth]
        at = pl.ds(pl.multiple_of(2 * rows + (1 - part) * depth, 32), depth)
        out_ref[d, at] = other_ref[d * depth : (d + 1) * depth]


def fan(scalars, owned, across, mine, other, head_rows, n):
    shape = struct((n // 2, 2 * owned.shape[0] + head_rows, 128))
    return pl.pallas_call(
        fan_kernel,
        in_specs=[sspec()] + [vspec()] * 4,
        out_specs=vspec(),
        out_shape=shape,
        compiler_params=params(),
    )(scalars, owned, across, mine, other)


def source_of(rank, n, q, k):
    return (rank // (n // 2) ^ k) * (n // 2) + q


def norm_rows(x):
    average = jnp.mean(x, axis=-1, keepdims=True)
    power = jnp.mean(x * x, axis=-1, keepdims=True)
    return (x - average) * lax.rsqrt(power - average * average + 1e-06)


def attend_kernel(n, part, rank_ref, mine_ref, other_ref, *refs):
    near, (tokens_ref, out_ref, weight_ref, sem) = refs[: n // 2], refs[n // 2 :]
    rank, half = rank_ref[0], rank_ref[1]
    depth = weight_ref.shape[0]
    copies = []
    for j in range(n // 2):
        to = pl.ds(pl.multiple_of((rank ^ j) * 128, 128), 128)
        at = pl.ds(near[j].shape[0] - depth, depth)
        copies.append((near[j].at[at], weight_ref.at[:, to]))
    wait = run_copies(copies, sem)
    rows = other_ref.shape[1] // 2
    cuts = rows // part
    width = cuts * 128
    for q in range(n // 2):
        for k in range(2):
            source = source_of(rank, n, q, k)
            at = pl.ds(pl.multiple_of(source * part, part), part)
            for c in range(cuts):
                cut = slice(k * rows + c * part, k * rows + (c + 1) * part)
                to = pl.ds(pl.multiple_of(half * width + c * 128, 128), 128)
                tokens_ref[at, to] = mine_ref[q, cut]
                to = pl.ds(pl.multiple_of((1 - half) * width + c * 128, 128), 128)
                tokens_ref[at, to] = other_ref[q, cut]
        source = source_of(rank, n, q, 1)
        to = pl.ds(pl.multiple_of(source * 128, 128), 128)
        weight_ref[:, to] = mine_ref[q, 2 * rows :]
    normed = norm_rows(tokens_ref[...].astype(F32)).astype(BF16)
    wait()
    projected = lax.dot_general(
        normed, weight_ref[...], (((1,), (1,)), ((), ())), preferred_element_type=F32
    ).astype(BF16)
    size = projected.shape[1] // 3
    queries = projected[:, :size]
    keys = projected[:, size : 2 * size]
    values = projected[:, 2 * size :]
    scores = lax.dot_general(
        queries, keys, (((1,), (1,)), ((), ())), preferred_element_type=F32
    ) * (1.0 / math.sqrt(size))
    powers = jnp.exp(scores - jnp.max(scores, axis=1, keepdims=True))
    probs = (powers / jnp.sum(powers, axis=1, keepdims=True)).astype(BF16)
    attended = lax.dot_general(
        values, probs, (((0,), (1,)), ((), ())), preferred_element_type=F32
    ).astype(BF16)
    out_ref[...] = attended


def attend_fast(scalars, mine, other, near, head_rows, per_owner, n):
    length = n * per_owner
    depth = other.shape[1] // (2 * per_owner) * 256
    size = head_rows // 3
    return pl.pallas_call(
        functools.partial(attend_kernel, n, per_owner),
        in_specs=[sspec()] + [vspec()] * 2 + [aspec()] * (n // 2),
        out_specs=[vspec()] * 2,
        out_shape=[struct((length, depth)), struct((size, length))],
        scratch_shapes=[
            VMEM((head_rows, n * 128), BF16),
            pltpu.SemaphoreType.DMA((n // 2,)),
        ],
        compiler_params=params(),
        cost_estimate=cost(30),
    )(scalars, mine, other, *near)


def mlp_kernel(n, rank_ref, tokens_ref, pieces, far, outs_far, near, near_other, outs, scratch):
    residual_ref, keep_ref, send_ref = outs
    up_ref, down_ref, row_ref, whole_ref, joined_ref, sem = scratch
    rank, half, group = rank_ref[0], rank_ref[1], rank_ref[2]
    block = up_ref.shape[0] // n
    wide = down_ref.shape[0]
    unit = wide // 2
    size = pieces[0].shape[2]
    rows = outs_far[0][0].shape[1]
    first, later = [], []
    for j in range(n // 2):
        source = rank ^ j
        at = pl.ds(pl.multiple_of(source * block, block), block)
        to = pl.ds(pl.multiple_of(source * 128, 128), 128)
        for c in range(2):
            later.append(
                (near[j].at[pl.ds(c * block, block)], up_ref.at[at, pl.ds(c * unit, unit)])
            )
        later.append((near[j].at[pl.ds(2 * block, wide)], down_ref.at[:, to]))
        for core, refs in enumerate((near, near_other)):
            first.append((refs[j].at[pl.ds(2 * block + wide, 2 * rows)], whole_ref.at[core, :, to]))
        source = source_of(rank, n, j, 1)
        at = pl.ds(pl.multiple_of(source * block, block), block)
        to = pl.ds(pl.multiple_of(source * 128, 128), 128)
        for c in range(2):
            units = pl.ds(pl.multiple_of((group ^ c) * unit, unit), unit)
            later.append((far[c].at[j, pl.ds(0, block)], up_ref.at[at, units]))
            later.append((far[c].at[j, pl.ds(block, unit)], down_ref.at[units, to]))
        source = rank ^ j ^ (n // 2)
        to = pl.ds(pl.multiple_of(source * 128, 128), 128)
        for core in range(2):
            for c in range(2):
                at = pl.ds(pl.multiple_of((group ^ c) * rows, rows), rows)
                first.append((outs_far[core][c].at[j], whole_ref.at[core, at, to]))
    wait_first = run_copies(first, sem)
    wait_later = run_copies(later, sem, len(first))
    for j in range(n // 2):
        for core in range(2):
            for k in range(2):
                at = pl.ds(pl.multiple_of((rank ^ j ^ (k * n // 2)) * size, size), size)
                joined_ref[core, at] = pieces[core][j, k]
    wait_first()
    dims = (((0,), (0,)), ((), ()))
    row_ref[...] = (
        tokens_ref[...].astype(F32)
        + lax.dot_general(joined_ref[0], whole_ref[0], dims, preferred_element_type=F32)
        + lax.dot_general(joined_ref[1], whole_ref[1], dims, preferred_element_type=F32)
    )
    part = residual_ref.shape[0]
    width = residual_ref.shape[1]
    my_cols = pl.ds(pl.multiple_of(half * width, width), width)
    other_cols = pl.ds(pl.multiple_of((1 - half) * width, width), width)
    residual_ref[...] = row_ref[pl.ds(pl.multiple_of(rank * part, part), part), my_cols]
    normed = norm_rows(row_ref[...]).astype(BF16)
    wait_later()
    raw = jnp.dot(normed, up_ref[...], preferred_element_type=F32)
    hidden = (0.5 * raw * (1.0 + lax.erf(raw * math.sqrt(0.5)))).astype(BF16)
    keep_ref[...] = jnp.dot(hidden, down_ref[:, my_cols], preferred_element_type=F32)
    send_ref[...] = jnp.dot(hidden, down_ref[:, other_cols], preferred_element_type=F32).astype(BF16)


def mlp(scalars, tokens, pieces, far, outs_far, near, near_other, n):
    length, depth = tokens.shape
    width = depth // 2
    wide = 2 * (far[0].shape[1] - depth // n)
    inner = n * pieces[0].shape[2]
    half = n // 2

    def kernel(scalars, tokens, a, b, c, d, e, f, g, h, *refs):
        near, near_other = refs[:half], refs[half : 2 * half]
        outs, scratch = refs[2 * half : 2 * half + 3], refs[2 * half + 3 :]
        mlp_kernel(
            n, scalars, tokens, (a, b), (c, d), ((e, f), (g, h)), near, near_other, outs, scratch
        )

    return pl.pallas_call(
        kernel,
        in_specs=[sspec()] + [vspec()] * 3 + [aspec()] * (6 + n),
        out_specs=[vspec()] * 3,
        out_shape=[
            struct((length // n, width), F32),
            struct((length, width), F32),
            struct((length, width)),
        ],
        scratch_shapes=[
            VMEM((depth, wide), BF16),
            VMEM((wide, depth), BF16),
            VMEM((length, depth), F32),
            VMEM((2, inner, depth), BF16),
            VMEM((2, inner, length), BF16),
            pltpu.SemaphoreType.DMA((13 * half,)),
        ],
        compiler_params=params(),
    )(scalars, tokens, *pieces, *far, *outs_far[0], *outs_far[1], *near, *near_other)


def join_kernel(rank_ref, keep_ref, got_ref, residual_ref, base_ref, out_ref):
    part = residual_ref.shape[0]
    mine = pl.ds(pl.multiple_of(rank_ref[0] * part, part), part)
    base_ref[...] = keep_ref[mine] + got_ref[mine].astype(F32) + residual_ref[...]
    out_ref[...] = (keep_ref[...] + got_ref[...].astype(F32)).astype(BF16)


def join(scalars, keep, got, residual):
    return pl.pallas_call(
        join_kernel,
        in_specs=[sspec()] + [vspec()] * 3,
        out_specs=[vspec()] * 2,
        out_shape=[struct(residual.shape, F32), struct(keep.shape)],
        compiler_params=params(),
    )(scalars, keep, got, residual)


def last_kernel(n, rank_ref, base_ref, terms_ref, out_ref):
    rank = rank_ref[0]
    total = base_ref[...]
    for j in range(1, n):
        total = total + terms_ref[rank ^ j].astype(F32)
    out_ref[...] = total.astype(BF16)


def last(scalars, base, terms):
    return pl.pallas_call(
        functools.partial(last_kernel, terms.shape[0]),
        in_specs=[sspec()] + [vspec()] * 2,
        out_specs=vspec(),
        out_shape=struct(base.shape),
        compiler_params=params(),
    )(scalars, base, terms)


def swap(value, axis, j):
    n = lax.axis_size(axis)
    return lax.ppermute(value, axis, [(i, i ^ j) for i in range(n)])


def exchange(value):
    return lax.all_to_all(value, "seq", split_axis=0, concat_axis=0, tiled=True)


def exchange_half(value):
    n = lax.axis_size("seq")
    groups = [list(range(n // 2)), list(range(n // 2, n))]
    return lax.all_to_all(
        value, "seq", split_axis=0, concat_axis=0, axis_index_groups=groups, tiled=True
    )


def after(value, *others):
    return lax.optimization_barrier((value, *others))[0]


def local_fast(patches, keep_list, qkv_weight, out_weight, up_weight, down_weight):
    n = lax.axis_size("seq")
    rank, head, group = (
        lax.axis_index(name).astype(jnp.int32) for name in ("seq", "head", "groups")
    )
    scalars = jnp.stack([rank, head, group])
    half = n // 2
    sup, depth = patches.shape[1], patches.shape[3]
    length = sup * n * 8 // 5
    per_owner = length // n
    half_width = depth // 2
    head_rows = qkv_weight.shape[2]
    capacity = (4 * sup + n - 1) // n
    keep_col = keep_list.reshape(-1, 1)
    flat = patches.reshape(4 * sup, depth)
    heads = qkv_weight.transpose(1, 2, 0)

    qkv_away, out_away = early_blocks(scalars, heads, out_weight, n)
    qkv_mine = swap(qkv_away, "seq", half)
    slots = prep(scalars, keep_col, flat, n, sup, capacity)
    slots, qkv_mine = lax.optimization_barrier((slots, qkv_mine))
    dealt = exchange(slots)
    out_far = swap(after(out_away, slots), "seq", half)
    qkv_other = swap(qkv_mine, "groups", 1)
    blocks = lax.optimization_barrier((heads, out_weight, up_weight, down_weight, slots))[:4]
    near, mlp_away = pack(scalars, *blocks, n)
    near = [near[0]] + [swap(near[j], "seq", j) for j in range(1, half)]
    dealt, out_far, qkv_other = lax.optimization_barrier((dealt, out_far, qkv_other))
    owned = pick(scalars, keep_col, dealt, n, sup, per_owner, capacity)

    across = swap(owned, "seq", half)
    out_far = after(out_far, owned)
    outs_far = [out_far] + [swap(out_far, "seq", j) for j in range(1, half)]
    across, *rest = lax.optimization_barrier((across, *outs_far, *near))
    outs_far, near = rest[:half], rest[half:]

    mlp_far = swap(after(mlp_away, across), "seq", half)
    got = exchange_half(fan(scalars, owned, across, qkv_mine, qkv_other, head_rows, n))
    far_mine = jnp.stack(outs_far)
    far_other = swap(far_mine, "groups", 1)
    got, mlp_far, far_other = lax.optimization_barrier((got, mlp_far, far_other))

    pieces = got[:, : got.shape[1] - head_rows]
    pieces_other = swap(pieces, "head", 1)
    tokens, attended = attend_fast(scalars, got, pieces_other, near, head_rows, per_owner, n)

    att_across = swap(attended, "seq", half)
    mlp_mine = exchange_half(after(mlp_far, attended))
    pair = jnp.stack([attended, att_across])
    gathered = jnp.stack([pair] + [swap(pair, "seq", j) for j in range(1, half)])
    mlp_other = swap(mlp_mine, "groups", 1)
    near_other = [swap(block, "head", 1) for block in after(tuple(near), attended)]
    far_mine, far_other = after((far_mine, far_other), attended)
    residual, keep, send = mlp(
        scalars,
        tokens,
        (gathered, swap(gathered, "head", 1)),
        (mlp_mine, mlp_other),
        ((far_mine, far_other), (swap(far_mine, "head", 1), swap(far_other, "head", 1))),
        near,
        near_other,
        n,
    )
    sent = swap(send, "head", 1)
    base, terms = join(scalars, keep, sent, residual)
    terms = exchange(terms.reshape(n, per_owner, half_width))
    encoded = last(scalars, base, terms)
    return encoded.reshape(1, per_owner, 1, half_width)


def local(patches, keep_list, qkv_weight, out_weight, up_weight, down_weight):
    n = lax.axis_size("seq")
    one_image = patches.shape[0] == 1 and qkv_weight.shape[1] == n and n & (n - 1) == 0
    one_image = one_image and lax.axis_size("groups") == 2 and up_weight.shape[1] == n * 256
    plan = local_fast if one_image else local_general
    return plan(patches, keep_list, qkv_weight, out_weight, up_weight, down_weight)


def solution(mesh):
    return jax.shard_map(
        local,
        mesh=mesh,
        in_specs=(
            P("groups", "seq", None, None),
            P("groups", None),
            P("seq", "head", None),
            P("head", "seq"),
            P("seq", "head"),
            P("head", "seq"),
        ),
        out_specs=P("groups", None, "seq", "head"),
        check_vma=False,
    )
```

```python
import functools
import math

import jax
import jax.numpy as jnp
from jax import lax
from jax.experimental import pallas as pl
from jax.experimental.pallas import tpu as pltpu
from jax.sharding import PartitionSpec as P

F32 = jnp.float32
BF16 = jnp.bfloat16
VMEM = pltpu.VMEM
LIMIT = 24 * 1024 * 1024

def layer_norm(matrix):
    average = jnp.mean(matrix, axis=-1, keepdims=True)
    power = jnp.mean(matrix * matrix, axis=-1, keepdims=True)
    return (matrix - average) * lax.rsqrt(power - average * average + 1e-06)


def attend(queries, keys, values):
    length = queries.shape[0]
    block = math.gcd(length, 512)
    scale = 1.0 / math.sqrt(queries.shape[1])

    def one_block(query_rows):
        scores = (
            lax.dot_general(
                query_rows, keys, (((1,), (1,)), ((), ())), preferred_element_type=jnp.float32
            )
            * scale
        )
        top = jnp.max(scores, axis=1, keepdims=True)
        powers = jnp.exp(scores - top)
        probs = (powers / jnp.sum(powers, axis=1, keepdims=True)).astype(jnp.bfloat16)
        return jnp.dot(probs, values, preferred_element_type=jnp.float32).astype(jnp.bfloat16)

    blocks = lax.map(one_block, queries.reshape(length // block, block, queries.shape[1]))
    return blocks.reshape(length, values.shape[1])


def local_general(patches, keep_list, qkv_weight, out_weight, up_weight, down_weight):
    seq_count = lax.axis_size("seq")
    seq_rank = lax.axis_index("seq")
    head_rank = lax.axis_index("head")
    images = patches.shape[0]
    sup_local = patches.shape[1]
    depth = patches.shape[3]
    half_width = depth // lax.axis_size("head")
    head_count = qkv_weight.shape[1]
    seq_length = sup_local * seq_count * 8 // 5
    per_owner = seq_length // seq_count
    capacity = (4 * sup_local + seq_count - 1) // seq_count
    slot_count = 4 * sup_local
    image_index = jnp.arange(images, dtype=jnp.int32)
    bounds = jnp.arange(seq_count + 1, dtype=jnp.int32) * sup_local
    before = jnp.sum((keep_list[:, :, None] < bounds[None, None, :]).astype(jnp.int32), axis=1)
    starts = bounds[None, :seq_count] + 3 * before[:, :seq_count]
    lengths = sup_local + 3 * (before[:, 1:] - before[:, :seq_count])
    my_start = lax.dynamic_index_in_dim(starts, seq_rank, 1, keepdims=False)
    my_length = lax.dynamic_index_in_dim(lengths, seq_rank, 1, keepdims=False)
    local_ids = seq_rank * sup_local + jnp.arange(sup_local, dtype=jnp.int32)
    kept_flag = jnp.any(keep_list[:, None, :] == local_ids[None, :, None], axis=2).astype(jnp.int32)
    offsets = jnp.arange(sup_local, dtype=jnp.int32)[None, :] + 3 * (
        jnp.cumsum(kept_flag, axis=1) - kept_flag
    )
    slot_ids = jnp.arange(slot_count, dtype=jnp.int32)
    owner_patch = (
        jnp.sum((offsets[:, None, :] <= slot_ids[None, :, None]).astype(jnp.int32), axis=2) - 1
    )
    start_of = jnp.take_along_axis(offsets, owner_patch, axis=1)
    sub_index = jnp.minimum(slot_ids[None, :] - start_of, 3)
    kept_of = jnp.take_along_axis(kept_flag, owner_patch, axis=1)
    flat_patches = patches.reshape(images, sup_local * 4, depth)
    fine_rows = flat_patches[
        image_index[:, None], owner_patch * 4 + jnp.where(kept_of == 1, sub_index, 0)
    ]
    mean_rows = jnp.mean(patches.astype(jnp.float32), axis=2).astype(jnp.bfloat16)
    shared_rows = mean_rows[image_index[:, None], owner_patch]
    local_tokens = jnp.where((kept_of == 1)[:, :, None], fine_rows, shared_rows)
    destinations = jnp.arange(seq_count, dtype=jnp.int32)[:, None, None]
    depth_slots = jnp.arange(capacity, dtype=jnp.int32)[None, None, :]
    positions = (destinations - my_start[None, :, None]) % seq_count + depth_slots * seq_count
    valid = positions < my_length[None, :, None]
    outgoing = local_tokens[image_index[None, :, None], jnp.minimum(positions, slot_count - 1)]
    outgoing = jnp.where(valid[:, :, :, None], outgoing, jnp.zeros((), jnp.bfloat16))
    incoming = lax.all_to_all(outgoing, "seq", split_axis=0, concat_axis=0, tiled=True)
    owned = jnp.arange(per_owner, dtype=jnp.int32) * seq_count + seq_rank
    source = jnp.sum((starts[:, None, :] <= owned[None, :, None]).astype(jnp.int32), axis=2) - 1
    first_of = jnp.take_along_axis(starts, source, axis=1)
    depth_of = (owned[None, :] - first_of) // seq_count
    resident = incoming[source, image_index[:, None], depth_of]
    start_rows = resident.reshape(images * per_owner, depth)
    start_float = start_rows.astype(jnp.float32)
    qkv_full, out_full, up_full, down_full = (
        lax.all_gather(qkv_weight, "seq", axis=0, tiled=True),
        lax.all_gather(out_weight, "seq", axis=1, tiled=True),
        lax.all_gather(up_weight, "seq", axis=0, tiled=True),
        lax.all_gather(down_weight, "seq", axis=1, tiled=True),
    )
    normed = layer_norm(start_float).astype(jnp.bfloat16).reshape(images, per_owner, depth)
    projected = jnp.einsum("ipd,dhc->ihpc", normed, qkv_full, preferred_element_type=jnp.float32)
    head_size = qkv_weight.shape[2] // 3
    sending = projected.astype(jnp.bfloat16).reshape(seq_count, per_owner, 3 * head_size)
    gathered = lax.all_to_all(sending, "seq", split_axis=0, concat_axis=0, tiled=True).reshape(
        seq_length, 3 * head_size
    )
    attended = attend(
        gathered[:, :head_size],
        gathered[:, head_size : 2 * head_size],
        gathered[:, 2 * head_size :],
    )
    returned = lax.all_to_all(
        attended.reshape(seq_count, per_owner, head_size),
        "seq",
        split_axis=0,
        concat_axis=0,
        tiled=True,
    )
    returned = returned.reshape(images, head_count, per_owner, head_size)
    partial_sum = jnp.einsum(
        "ihpc,hcd->ipd",
        returned,
        out_full.reshape(head_count, head_size, depth),
        preferred_element_type=jnp.float32,
    ).reshape(images * per_owner, depth)
    attn_total = lax.psum(partial_sum, "head")
    residual = start_float + attn_total
    residual_half = lax.dynamic_slice_in_dim(residual, head_rank * half_width, half_width, 1)
    normed_two = layer_norm(residual).astype(jnp.bfloat16)
    hidden = jax.nn.gelu(
        jnp.dot(normed_two, up_full, preferred_element_type=jnp.float32), approximate=False
    ).astype(jnp.bfloat16)
    mlp_terms = jnp.dot(hidden, down_full, preferred_element_type=jnp.float32)
    mlp_part = lax.psum_scatter(mlp_terms, "head", scatter_dimension=1, tiled=True)
    encoded = (residual_half + mlp_part).astype(jnp.bfloat16)
    return encoded.reshape(images, per_owner, 1, half_width)


def vspec():
    return pl.BlockSpec(memory_space=VMEM)


def aspec():
    return pl.BlockSpec(memory_space=pl.ANY)


def sspec():
    return pl.BlockSpec(memory_space=pltpu.SMEM)


def hspec():
    return pl.BlockSpec(memory_space=pltpu.HBM)


def run_copies(copies, sem, base=0):
    started = [
        pltpu.make_async_copy(src, dst, sem.at[base + i]) for i, (src, dst) in enumerate(copies)
    ]
    for copy in started:
        copy.start()

    def wait():
        for copy in started:
            copy.wait()

    return wait


def params():
    return pltpu.CompilerParams(vmem_limit_bytes=LIMIT)


def cost(micros):
    return pl.CostEstimate(flops=micros * 10**9, bytes_accessed=1 << 20, transcendentals=0)


def struct(shape, dtype=BF16):
    return jax.ShapeDtypeStruct(shape, dtype)


def slot_of(index, n, capacity, cuts):
    device = sum(((index >= j * cuts * capacity).astype(jnp.int32) for j in range(1, n)), 0 * index)
    inner = index - device * (cuts * capacity)
    cut = sum(((inner >= c * capacity).astype(jnp.int32) for c in range(1, cuts)), 0 * index)
    return device, cut, inner - cut * capacity


def one_hot(mask):
    return mask.astype(F32).astype(BF16)


def prep_kernel(n, sup, capacity, rank_ref, keep_ref, patches_ref, out_ref):
    rank = rank_ref[0]
    first = rank * sup
    keep = keep_ref[...]
    rows = 4 * sup
    count = keep.shape[0]

    def places(width, shift):
        ids = lax.broadcasted_iota(jnp.int32, (count, width), 1) >> shift
        kept = jnp.sum((keep == first + ids).astype(jnp.int32), axis=0, keepdims=True)
        below = jnp.sum(
            jnp.logical_and(keep >= first, keep < first + ids).astype(jnp.int32),
            axis=0,
            keepdims=True,
        )
        return kept, below, lax.broadcasted_iota(jnp.int32, (1, width), 1)

    kept, below, lane = places(rows, 2)
    fine_pos = jnp.where(kept == 1, (lane >> 2) + 3 * below + (lane & 3), -1)
    kept, below, lane = places(sup, 0)
    mean_pos = jnp.where(kept == 1, -1, lane + 3 * below)
    start = first + 3 * jnp.sum((keep < first).astype(jnp.int32), axis=0, keepdims=True)
    flat = patches_ref[...]
    cuts = flat.shape[1] // 128
    sup_col = lax.broadcasted_iota(jnp.int32, (sup, rows), 0)
    sup_lane = lax.broadcasted_iota(jnp.int32, (sup, rows), 1) >> 2
    averaging = jnp.where(sup_col == sup_lane, 0.25, 0.0).astype(BF16)
    means = jnp.dot(averaging, flat, preferred_element_type=F32).astype(BF16)
    index = lax.broadcasted_iota(jnp.int32, (n * cuts * capacity, 1), 0)
    device, cut, slot = slot_of(index, n, capacity, cuts)
    pos = ((device - start) & (n - 1)) + slot * n
    total = jnp.zeros((n * cuts * capacity, 128), F32)
    for c in range(cuts):
        at = jnp.where(cut == c, pos, -2)
        features = slice(c * 128, (c + 1) * 128)
        total = (
            total
            + jnp.dot(one_hot(at == fine_pos), flat[:, features], preferred_element_type=F32)
            + jnp.dot(one_hot(at == mean_pos), means[:, features], preferred_element_type=F32)
        )
    out_ref[...] = total.astype(BF16)


def prep(scalars, keep_col, flat, n, sup, capacity):
    width = flat.shape[1] // 2
    shape = (n * capacity * width // 128, 128)
    return pl.pallas_call(
        functools.partial(prep_kernel, n, sup, capacity),
        grid_spec=pltpu.PrefetchScalarGridSpec(
            num_scalar_prefetch=1,
            grid=(1,),
            in_specs=[
                pl.BlockSpec(keep_col.shape, lambda i, ref: (0, 0)),
                pl.BlockSpec((flat.shape[0], width), lambda i, ref: (0, ref[1])),
            ],
            out_specs=pl.BlockSpec(shape, lambda i, ref: (0, 0)),
        ),
        out_shape=struct(shape),
        compiler_params=params(),
    )(scalars, keep_col, flat)


def pick_kernel(n, sup, per_owner, capacity, rank_ref, keep_ref, got_ref, out_ref):
    rank = rank_ref[0]
    keep = keep_ref[...]
    count = keep.shape[0]
    lanes = got_ref.shape[0]
    cuts = lanes // (n * capacity)
    source, _, _ = slot_of(
        lax.broadcasted_iota(jnp.int32, (count, lanes), 1), n, capacity, cuts
    )
    low = jnp.sum((keep < source * sup).astype(jnp.int32), axis=0, keepdims=True)
    high = jnp.sum((keep < source * sup + sup).astype(jnp.int32), axis=0, keepdims=True)
    source, cut, slot = slot_of(
        lax.broadcasted_iota(jnp.int32, (1, lanes), 1), n, capacity, cuts
    )
    start = source * sup + 3 * low
    stop = source * sup + sup + 3 * high
    token = start + ((rank - start) & (n - 1)) + slot * n
    row = jnp.where(token < stop, token >> (n.bit_length() - 1), -1)
    own = lax.broadcasted_iota(jnp.int32, (per_owner, lanes), 0)
    got = got_ref[...]
    for c in range(cuts):
        choose = one_hot(own == jnp.where(cut == c, row, -1))
        owned = jnp.dot(choose, got, preferred_element_type=F32).astype(BF16)
        out_ref[c * per_owner : (c + 1) * per_owner] = owned


def pick(scalars, keep_col, got, n, sup, per_owner, capacity):
    cuts = got.shape[0] // (n * capacity)
    return pl.pallas_call(
        functools.partial(pick_kernel, n, sup, per_owner, capacity),
        in_specs=[sspec(), vspec(), vspec()],
        out_specs=vspec(),
        out_shape=struct((cuts * per_owner, 128)),
        compiler_params=params(),
    )(scalars, keep_col, got)


def pack_kernel(n, rank_ref, up_ref, down_ref, *refs):
    near, away_ref, sem = refs[: n // 2], refs[n // 2], refs[n // 2 + 1]
    rank, part = rank_ref[0], rank_ref[2]
    half = n // 2
    rows = up_ref.shape[0]
    wide = up_ref.shape[1] // n
    units = wide // 2
    copies = []
    for j in range(half):
        dest = rank ^ j
        for c in range(2):
            at = pl.ds(pl.multiple_of(dest * wide + c * units, 128), units)
            copies.append((up_ref.at[:, at], near[j].at[pl.ds(c * rows, rows)]))
        at = pl.ds(pl.multiple_of(dest * wide, 128), wide)
        copies.append((down_ref.at[at], near[j].at[pl.ds(2 * rows, wide)]))
        dest = (rank // half ^ 1) * half + j
        at = pl.ds(pl.multiple_of(dest * wide + part * units, 128), units)
        copies.append((up_ref.at[:, at], away_ref.at[j, pl.ds(0, rows)]))
        copies.append((down_ref.at[at], away_ref.at[j, pl.ds(rows, units)]))
    run_copies(copies, sem)()


def pack(scalars, up, down, n):
    wide = up.shape[1] // n
    near = struct((2 * up.shape[0] + wide, 128))
    away = struct((n // 2, up.shape[0] + wide // 2, 128))
    outs = pl.pallas_call(
        functools.partial(pack_kernel, n),
        in_specs=[sspec()] + [hspec()] * 2,
        out_specs=[hspec()] * (n // 2) + [aspec()],
        out_shape=[near] * (n // 2) + [away],
        scratch_shapes=[pltpu.SemaphoreType.DMA((5 * n // 2,))],
        compiler_params=params(),
    )(scalars, up, down)
    return list(outs[:-1]), outs[-1]


def early_kernel(n, rank_ref, qkv_ref, out_weight_ref, heads_ref, near_ref, rows_ref, sem):
    rank, part = rank_ref[0], rank_ref[2]
    half = n // 2
    depth = heads_ref.shape[0] // half
    long = rows_ref.shape[0]
    copies = []
    for d in range(half):
        dest = (rank // half ^ 1) * half + d
        at = pl.ds(pl.multiple_of(part * depth, 32), depth)
        copies.append((qkv_ref.at[dest, at], heads_ref.at[pl.ds(d * depth, depth)]))
    copies.append((qkv_ref.at[pl.ds(rank // half * half, half)], near_ref))
    at = pl.ds(pl.multiple_of(part * long, 128), long)
    copies.append((out_weight_ref.at[at], rows_ref))
    run_copies(copies, sem)()


def early_blocks(scalars, qkv, out_weight, n):
    return pl.pallas_call(
        functools.partial(early_kernel, n),
        in_specs=[sspec()] + [hspec()] * 2,
        out_specs=[aspec()] * 3,
        out_shape=[
            struct((n // 2 * qkv.shape[1] // 2, 128)),
            struct((n // 2,) + qkv.shape[1:]),
            struct((out_weight.shape[0] // 2, 128)),
        ],
        scratch_shapes=[pltpu.SemaphoreType.DMA((n // 2 + 2,))],
        compiler_params=params(),
    )(scalars, qkv, out_weight)


def fan_kernel(rank_ref, owned_ref, across_ref, mine_ref, other_ref, near_ref, rows_ref, out_ref):
    part = rank_ref[2]
    rows = owned_ref.shape[0]
    count, head_rows = near_ref.shape[:2]
    depth = head_rows // 2
    top = 2 * rows
    for d in range(count):
        out_ref[d, :rows] = owned_ref[...]
        out_ref[d, rows:top] = across_ref[...]
        out_ref[d, top : top + head_rows] = near_ref[d]
        at = pl.ds(pl.multiple_of(top + head_rows + part * depth, 32), depth)
        out_ref[d, at] = mine_ref[d * depth : (d + 1) * depth]
        at = pl.ds(pl.multiple_of(top + head_rows + (1 - part) * depth, 32), depth)
        out_ref[d, at] = other_ref[d * depth : (d + 1) * depth]
        out_ref[d, top + 2 * head_rows :] = rows_ref[...]


def fan(scalars, owned, across, mine, other, near, rows):
    count = near.shape[0]
    shape = struct((count, 2 * owned.shape[0] + 2 * near.shape[1] + rows.shape[0], 128))
    return pl.pallas_call(
        fan_kernel,
        in_specs=[sspec()] + [vspec()] * 6,
        out_specs=vspec(),
        out_shape=shape,
        compiler_params=params(),
    )(scalars, owned, across, mine, other, near, rows)


def source_of(rank, n, q, k):
    return (rank // (n // 2) ^ k) * (n // 2) + q


def norm_rows(x):
    average = jnp.mean(x, axis=-1, keepdims=True)
    power = jnp.mean(x * x, axis=-1, keepdims=True)
    return (x - average) * lax.rsqrt(power - average * average + 1e-06)


def attend_kernel(n, part, rank_ref, mine_ref, other_ref, tokens_ref, out_ref, weight_ref):
    rank, half = rank_ref[0], rank_ref[1]
    rows = other_ref.shape[1] // 2
    cuts = rows // part
    width = cuts * 128
    depth = weight_ref.shape[0]
    for q in range(n // 2):
        for k in range(2):
            source = source_of(rank, n, q, k)
            at = pl.ds(pl.multiple_of(source * part, part), part)
            for c in range(cuts):
                cut = slice(k * rows + c * part, k * rows + (c + 1) * part)
                to = pl.ds(pl.multiple_of(half * width + c * 128, 128), 128)
                tokens_ref[at, to] = mine_ref[q, cut]
                to = pl.ds(pl.multiple_of((1 - half) * width + c * 128, 128), 128)
                tokens_ref[at, to] = other_ref[q, cut]
            to = pl.ds(pl.multiple_of(source * 128, 128), 128)
            high = 2 * rows + k * depth
            weight_ref[:, to] = mine_ref[q, high : high + depth]
    normed = norm_rows(tokens_ref[...].astype(F32)).astype(BF16)
    projected = lax.dot_general(
        normed, weight_ref[...], (((1,), (1,)), ((), ())), preferred_element_type=F32
    ).astype(BF16)
    size = projected.shape[1] // 3
    queries = projected[:, :size]
    keys = projected[:, size : 2 * size]
    values = projected[:, 2 * size :]
    scores = lax.dot_general(
        queries, keys, (((1,), (1,)), ((), ())), preferred_element_type=F32
    ) * (1.0 / math.sqrt(size))
    powers = jnp.exp(scores - jnp.max(scores, axis=1, keepdims=True))
    probs = (powers / jnp.sum(powers, axis=1, keepdims=True)).astype(BF16)
    attended = lax.dot_general(
        values, probs, (((0,), (1,)), ((), ())), preferred_element_type=F32
    ).astype(BF16)
    out_ref[...] = attended


def attend_fast(scalars, mine, other, head_rows, per_owner, n):
    length = n * per_owner
    depth = other.shape[1] // (2 * per_owner) * 256
    size = head_rows // 3
    return pl.pallas_call(
        functools.partial(attend_kernel, n, per_owner),
        in_specs=[sspec()] + [vspec()] * 2,
        out_specs=[vspec()] * 2,
        out_shape=[struct((length, depth)), struct((size, length))],
        scratch_shapes=[VMEM((head_rows, n * 128), BF16)],
        compiler_params=params(),
        cost_estimate=cost(30),
    )(scalars, mine, other)


def mlp_kernel(n, rank_ref, tokens_ref, pieces, far, outs_far, near, outs_near, outs, scratch):
    residual_ref, keep_ref, send_ref = outs
    up_ref, down_ref, row_ref, whole_ref, joined_ref, sem = scratch
    rank, half, group = rank_ref[0], rank_ref[1], rank_ref[2]
    block = up_ref.shape[0] // n
    wide = down_ref.shape[0]
    unit = wide // 2
    size = pieces[0].shape[2]
    rows = outs_far[0][0].shape[1]
    first, later = [], []
    for j in range(n // 2):
        source = rank ^ j
        at = pl.ds(pl.multiple_of(source * block, block), block)
        to = pl.ds(pl.multiple_of(source * 128, 128), 128)
        for c in range(2):
            later.append(
                (near[j].at[pl.ds(c * block, block)], up_ref.at[at, pl.ds(c * unit, unit)])
            )
        later.append((near[j].at[pl.ds(2 * block, wide)], down_ref.at[:, to]))
        for core in range(2):
            first.append((outs_near[core][j], whole_ref.at[core, :, to]))
        source = source_of(rank, n, j, 1)
        at = pl.ds(pl.multiple_of(source * block, block), block)
        to = pl.ds(pl.multiple_of(source * 128, 128), 128)
        for c in range(2):
            units = pl.ds(pl.multiple_of((group ^ c) * unit, unit), unit)
            later.append((far[c].at[j, pl.ds(0, block)], up_ref.at[at, units]))
            later.append((far[c].at[j, pl.ds(block, unit)], down_ref.at[units, to]))
        for core in range(2):
            for c in range(2):
                at = pl.ds(pl.multiple_of((group ^ c) * rows, rows), rows)
                first.append((outs_far[core][c].at[j], whole_ref.at[core, at, to]))
    wait_first = run_copies(first, sem)
    wait_later = run_copies(later, sem, len(first))
    for j in range(n // 2):
        for core in range(2):
            for k in range(2):
                at = pl.ds(pl.multiple_of((rank ^ j ^ (k * n // 2)) * size, size), size)
                joined_ref[core, at] = pieces[core][j, k]
    wait_first()
    dims = (((0,), (0,)), ((), ()))
    row_ref[...] = (
        tokens_ref[...].astype(F32)
        + lax.dot_general(joined_ref[0], whole_ref[0], dims, preferred_element_type=F32)
        + lax.dot_general(joined_ref[1], whole_ref[1], dims, preferred_element_type=F32)
    )
    part = residual_ref.shape[0]
    width = residual_ref.shape[1]
    my_cols = pl.ds(pl.multiple_of(half * width, width), width)
    other_cols = pl.ds(pl.multiple_of((1 - half) * width, width), width)
    residual_ref[...] = row_ref[pl.ds(pl.multiple_of(rank * part, part), part), my_cols]
    normed = norm_rows(row_ref[...]).astype(BF16)
    wait_later()
    raw = jnp.dot(normed, up_ref[...], preferred_element_type=F32)
    hidden = (0.5 * raw * (1.0 + lax.erf(raw * math.sqrt(0.5)))).astype(BF16)
    keep_ref[...] = jnp.dot(hidden, down_ref[:, my_cols], preferred_element_type=F32)
    send_ref[...] = jnp.dot(hidden, down_ref[:, other_cols], preferred_element_type=F32).astype(BF16)


def mlp(scalars, tokens, pieces, far, outs_far, near, outs_near, n):
    length, depth = tokens.shape
    width = depth // 2
    wide = 2 * (far[0].shape[1] - depth // n)
    inner = n * pieces[0].shape[2]
    half = n // 2

    def kernel(scalars, tokens, a, b, c, d, e, f, g, h, *refs):
        near, mine, other = refs[:half], refs[half : 2 * half], refs[2 * half : 3 * half]
        outs, scratch = refs[3 * half : 3 * half + 3], refs[3 * half + 3 :]
        far, outs_far, outs_near = (c, d), ((e, f), (g, h)), (mine, other)
        mlp_kernel(n, scalars, tokens, (a, b), far, outs_far, near, outs_near, outs, scratch)

    return pl.pallas_call(
        kernel,
        in_specs=[sspec()] + [vspec()] * 3 + [hspec()] * (6 + 3 * half),
        out_specs=[vspec()] * 3,
        out_shape=[
            struct((length // n, width), F32),
            struct((length, width), F32),
            struct((length, width)),
        ],
        scratch_shapes=[
            VMEM((depth, wide), BF16),
            VMEM((wide, depth), BF16),
            VMEM((length, depth), F32),
            VMEM((2, inner, depth), BF16),
            VMEM((2, inner, length), BF16),
            pltpu.SemaphoreType.DMA((13 * half,)),
        ],
        compiler_params=params(),
    )(scalars, tokens, *pieces, *far, *outs_far[0], *outs_far[1], *near, *outs_near[0], *outs_near[1])


def join_kernel(rank_ref, keep_ref, got_ref, residual_ref, base_ref, out_ref):
    part = residual_ref.shape[0]
    mine = pl.ds(pl.multiple_of(rank_ref[0] * part, part), part)
    base_ref[...] = keep_ref[mine] + got_ref[mine].astype(F32) + residual_ref[...]
    out_ref[...] = (keep_ref[...] + got_ref[...].astype(F32)).astype(BF16)


def join(scalars, keep, got, residual):
    return pl.pallas_call(
        join_kernel,
        in_specs=[sspec()] + [vspec()] * 3,
        out_specs=[vspec()] * 2,
        out_shape=[struct(residual.shape, F32), struct(keep.shape)],
        compiler_params=params(),
    )(scalars, keep, got, residual)


def last_kernel(n, rank_ref, base_ref, terms_ref, out_ref):
    rank = rank_ref[0]
    total = base_ref[...]
    for j in range(1, n):
        total = total + terms_ref[rank ^ j].astype(F32)
    out_ref[...] = total.astype(BF16)


def last(scalars, base, terms):
    return pl.pallas_call(
        functools.partial(last_kernel, terms.shape[0]),
        in_specs=[sspec()] + [vspec()] * 2,
        out_specs=vspec(),
        out_shape=struct(base.shape),
        compiler_params=params(),
    )(scalars, base, terms)


def swap(value, axis, j):
    n = lax.axis_size(axis)
    return lax.ppermute(value, axis, [(i, i ^ j) for i in range(n)])


def exchange(value):
    return lax.all_to_all(value, "seq", split_axis=0, concat_axis=0, tiled=True)


def exchange_half(value):
    n = lax.axis_size("seq")
    groups = [list(range(n // 2)), list(range(n // 2, n))]
    return lax.all_to_all(
        value, "seq", split_axis=0, concat_axis=0, axis_index_groups=groups, tiled=True
    )


def after(value, *others):
    return lax.optimization_barrier((value, *others))[0]


def local_fast(patches, keep_list, qkv_weight, out_weight, up_weight, down_weight):
    n = lax.axis_size("seq")
    rank, head, group = (
        lax.axis_index(name).astype(jnp.int32) for name in ("seq", "head", "groups")
    )
    scalars = jnp.stack([rank, head, group])
    half = n // 2
    sup, depth = patches.shape[1], patches.shape[3]
    length = sup * n * 8 // 5
    per_owner = length // n
    half_width = depth // 2
    head_rows = qkv_weight.shape[2]
    capacity = (4 * sup + n - 1) // n
    keep_col = keep_list.reshape(-1, 1)
    flat = patches.reshape(4 * sup, depth)
    heads = qkv_weight.transpose(1, 2, 0)

    qkv_away, qkv_near, out_away = early_blocks(scalars, heads, out_weight, n)
    qkv_mine = swap(qkv_away, "seq", half)
    slots = prep(scalars, keep_col, flat, n, sup, capacity)
    slots, qkv_mine = lax.optimization_barrier((slots, qkv_mine))
    dealt = exchange(slots)
    out_far = swap(after(out_away, slots), "seq", half)
    qkv_other = swap(qkv_mine, "groups", 1)
    own_rows = after(out_weight, slots)
    outs_near = [out_weight] + [swap(own_rows, "seq", j) for j in range(1, half)]
    up, down, qkv_other = lax.optimization_barrier((up_weight, down_weight, qkv_other))
    near, mlp_away = pack(scalars, up, down, n)
    dealt, qkv_other, mlp_away, *rest = lax.optimization_barrier(
        (dealt, qkv_other, mlp_away, *near, *outs_near)
    )
    near, outs_near = rest[:half], rest[half:]
    owned = pick(scalars, keep_col, dealt, n, sup, per_owner, capacity)

    across = swap(owned, "seq", half)
    mlp_far = swap(after(mlp_away, across), "seq", half)
    got = exchange_half(fan(scalars, owned, across, qkv_mine, qkv_other, qkv_near, out_far))
    outs_other = [swap(rows, "head", 1) for rows in lax.optimization_barrier((*outs_near, across))[:half]]
    got, mlp_far, *rest = lax.optimization_barrier((got, mlp_far, *near, *outs_other))
    near, outs_other = rest[:half], rest[half:]

    top = 2 * owned.shape[0]
    pieces_other = swap(got[:, :top], "head", 1)
    near = [near[0]] + [swap(near[j], "seq", j) for j in range(1, half)]
    mlp_mine = exchange_half(mlp_far)
    tokens, attended = attend_fast(scalars, got, pieces_other, head_rows, per_owner, n)

    att_across = swap(attended, "seq", half)
    far_mine = got[:, top + 2 * head_rows :]
    far_other = swap(far_mine, "groups", 1)
    att_across, mlp_mine, far_other, *near = lax.optimization_barrier(
        (att_across, mlp_mine, far_other, *near)
    )
    pair = jnp.stack([attended, att_across])
    mlp_other = swap(mlp_mine, "groups", 1)
    pairs = [swap(pair, "seq", j) for j in range(1, half)]
    mlp_other, *pairs = lax.optimization_barrier((mlp_other, *pairs))
    gathered = jnp.stack([pair] + pairs)
    residual, keep, send = mlp(
        scalars,
        tokens,
        (gathered, swap(gathered, "head", 1)),
        (mlp_mine, mlp_other),
        ((far_mine, far_other), (swap(far_mine, "head", 1), swap(far_other, "head", 1))),
        near,
        (outs_near, outs_other),
        n,
    )
    sent = swap(send, "head", 1)
    base, terms = join(scalars, keep, sent, residual)
    terms = exchange(terms.reshape(n, per_owner, half_width))
    encoded = last(scalars, base, terms)
    return encoded.reshape(1, per_owner, 1, half_width)


def local(patches, keep_list, qkv_weight, out_weight, up_weight, down_weight):
    n = lax.axis_size("seq")
    one_image = patches.shape[0] == 1 and qkv_weight.shape[1] == n and n & (n - 1) == 0
    one_image = one_image and lax.axis_size("groups") == 2 and up_weight.shape[1] == n * 256
    plan = local_fast if one_image else local_general
    return plan(patches, keep_list, qkv_weight, out_weight, up_weight, down_weight)


def solution(mesh):
    return jax.shard_map(
        local,
        mesh=mesh,
        in_specs=(
            P("groups", "seq", None, None),
            P("groups", None),
            P("seq", "head", None),
            P("head", "seq"),
            P("seq", "head"),
            P("head", "seq"),
        ),
        out_specs=P("groups", None, "seq", "head"),
        check_vma=False,
    )
```

```python
import functools
import math

import jax
import jax.numpy as jnp
from jax import lax
from jax.experimental import pallas as pl
from jax.experimental.pallas import tpu as pltpu
from jax.sharding import PartitionSpec as P

F32 = jnp.float32
BF16 = jnp.bfloat16
VMEM = pltpu.VMEM

def layer_norm(matrix):
    average = jnp.mean(matrix, axis=-1, keepdims=True)
    power = jnp.mean(matrix * matrix, axis=-1, keepdims=True)
    return (matrix - average) * lax.rsqrt(power - average * average + 1e-06)


def attend(queries, keys, values):
    length = queries.shape[0]
    block = math.gcd(length, 512)
    scale = 1.0 / math.sqrt(queries.shape[1])

    def one_block(query_rows):
        scores = (
            lax.dot_general(
                query_rows, keys, (((1,), (1,)), ((), ())), preferred_element_type=jnp.float32
            )
            * scale
        )
        top = jnp.max(scores, axis=1, keepdims=True)
        powers = jnp.exp(scores - top)
        probs = (powers / jnp.sum(powers, axis=1, keepdims=True)).astype(jnp.bfloat16)
        return jnp.dot(probs, values, preferred_element_type=jnp.float32).astype(jnp.bfloat16)

    blocks = lax.map(one_block, queries.reshape(length // block, block, queries.shape[1]))
    return blocks.reshape(length, values.shape[1])


def local_general(patches, keep_list, qkv_weight, out_weight, up_weight, down_weight):
    seq_count = lax.axis_size("seq")
    seq_rank = lax.axis_index("seq")
    head_rank = lax.axis_index("head")
    images = patches.shape[0]
    sup_local = patches.shape[1]
    depth = patches.shape[3]
    half_width = depth // lax.axis_size("head")
    head_count = qkv_weight.shape[1]
    seq_length = sup_local * seq_count * 8 // 5
    per_owner = seq_length // seq_count
    capacity = (4 * sup_local + seq_count - 1) // seq_count
    slot_count = 4 * sup_local
    image_index = jnp.arange(images, dtype=jnp.int32)
    bounds = jnp.arange(seq_count + 1, dtype=jnp.int32) * sup_local
    before = jnp.sum((keep_list[:, :, None] < bounds[None, None, :]).astype(jnp.int32), axis=1)
    starts = bounds[None, :seq_count] + 3 * before[:, :seq_count]
    lengths = sup_local + 3 * (before[:, 1:] - before[:, :seq_count])
    my_start = lax.dynamic_index_in_dim(starts, seq_rank, 1, keepdims=False)
    my_length = lax.dynamic_index_in_dim(lengths, seq_rank, 1, keepdims=False)
    local_ids = seq_rank * sup_local + jnp.arange(sup_local, dtype=jnp.int32)
    kept_flag = jnp.any(keep_list[:, None, :] == local_ids[None, :, None], axis=2).astype(jnp.int32)
    offsets = jnp.arange(sup_local, dtype=jnp.int32)[None, :] + 3 * (
        jnp.cumsum(kept_flag, axis=1) - kept_flag
    )
    slot_ids = jnp.arange(slot_count, dtype=jnp.int32)
    owner_patch = (
        jnp.sum((offsets[:, None, :] <= slot_ids[None, :, None]).astype(jnp.int32), axis=2) - 1
    )
    start_of = jnp.take_along_axis(offsets, owner_patch, axis=1)
    sub_index = jnp.minimum(slot_ids[None, :] - start_of, 3)
    kept_of = jnp.take_along_axis(kept_flag, owner_patch, axis=1)
    flat_patches = patches.reshape(images, sup_local * 4, depth)
    fine_rows = flat_patches[
        image_index[:, None], owner_patch * 4 + jnp.where(kept_of == 1, sub_index, 0)
    ]
    mean_rows = jnp.mean(patches.astype(jnp.float32), axis=2).astype(jnp.bfloat16)
    shared_rows = mean_rows[image_index[:, None], owner_patch]
    local_tokens = jnp.where((kept_of == 1)[:, :, None], fine_rows, shared_rows)
    destinations = jnp.arange(seq_count, dtype=jnp.int32)[:, None, None]
    depth_slots = jnp.arange(capacity, dtype=jnp.int32)[None, None, :]
    positions = (destinations - my_start[None, :, None]) % seq_count + depth_slots * seq_count
    valid = positions < my_length[None, :, None]
    outgoing = local_tokens[image_index[None, :, None], jnp.minimum(positions, slot_count - 1)]
    outgoing = jnp.where(valid[:, :, :, None], outgoing, jnp.zeros((), jnp.bfloat16))
    incoming = lax.all_to_all(outgoing, "seq", split_axis=0, concat_axis=0, tiled=True)
    owned = jnp.arange(per_owner, dtype=jnp.int32) * seq_count + seq_rank
    source = jnp.sum((starts[:, None, :] <= owned[None, :, None]).astype(jnp.int32), axis=2) - 1
    first_of = jnp.take_along_axis(starts, source, axis=1)
    depth_of = (owned[None, :] - first_of) // seq_count
    resident = incoming[source, image_index[:, None], depth_of]
    start_rows = resident.reshape(images * per_owner, depth)
    start_float = start_rows.astype(jnp.float32)
    qkv_full, out_full, up_full, down_full = (
        lax.all_gather(qkv_weight, "seq", axis=0, tiled=True),
        lax.all_gather(out_weight, "seq", axis=1, tiled=True),
        lax.all_gather(up_weight, "seq", axis=0, tiled=True),
        lax.all_gather(down_weight, "seq", axis=1, tiled=True),
    )
    normed = layer_norm(start_float).astype(jnp.bfloat16).reshape(images, per_owner, depth)
    projected = jnp.einsum("ipd,dhc->ihpc", normed, qkv_full, preferred_element_type=jnp.float32)
    head_size = qkv_weight.shape[2] // 3
    sending = projected.astype(jnp.bfloat16).reshape(seq_count, per_owner, 3 * head_size)
    gathered = lax.all_to_all(sending, "seq", split_axis=0, concat_axis=0, tiled=True).reshape(
        seq_length, 3 * head_size
    )
    attended = attend(
        gathered[:, :head_size],
        gathered[:, head_size : 2 * head_size],
        gathered[:, 2 * head_size :],
    )
    returned = lax.all_to_all(
        attended.reshape(seq_count, per_owner, head_size),
        "seq",
        split_axis=0,
        concat_axis=0,
        tiled=True,
    )
    returned = returned.reshape(images, head_count, per_owner, head_size)
    partial_sum = jnp.einsum(
        "ihpc,hcd->ipd",
        returned,
        out_full.reshape(head_count, head_size, depth),
        preferred_element_type=jnp.float32,
    ).reshape(images * per_owner, depth)
    attn_total = lax.psum(partial_sum, "head")
    residual = start_float + attn_total
    residual_half = lax.dynamic_slice_in_dim(residual, head_rank * half_width, half_width, 1)
    normed_two = layer_norm(residual).astype(jnp.bfloat16)
    hidden = jax.nn.gelu(
        jnp.dot(normed_two, up_full, preferred_element_type=jnp.float32), approximate=False
    ).astype(jnp.bfloat16)
    mlp_terms = jnp.dot(hidden, down_full, preferred_element_type=jnp.float32)
    mlp_part = lax.psum_scatter(mlp_terms, "head", scatter_dimension=1, tiled=True)
    encoded = (residual_half + mlp_part).astype(jnp.bfloat16)
    return encoded.reshape(images, per_owner, 1, half_width)


def vspec():
    return pl.BlockSpec(memory_space=VMEM)


def aspec():
    return pl.BlockSpec(memory_space=pl.ANY)


def sspec():
    return pl.BlockSpec(memory_space=pltpu.SMEM)


def hspec():
    return pl.BlockSpec(memory_space=pltpu.HBM)


def run_copies(copies, sem, base=0):
    started = [
        pltpu.make_async_copy(src, dst, sem.at[base + i]) for i, (src, dst) in enumerate(copies)
    ]
    for copy in started:
        copy.start()

    def wait():
        for copy in started:
            copy.wait()

    return wait


def params(mebibytes=4):
    return pltpu.CompilerParams(vmem_limit_bytes=mebibytes * 1024 * 1024)


def cost(micros):
    return pl.CostEstimate(flops=micros * 10**9, bytes_accessed=1 << 20, transcendentals=0)


def struct(shape, dtype=BF16):
    return jax.ShapeDtypeStruct(shape, dtype)


def slot_of(index, n, capacity, cuts):
    device = sum(((index >= j * cuts * capacity).astype(jnp.int32) for j in range(1, n)), 0 * index)
    inner = index - device * (cuts * capacity)
    cut = sum(((inner >= c * capacity).astype(jnp.int32) for c in range(1, cuts)), 0 * index)
    return device, cut, inner - cut * capacity


def one_hot(mask):
    return mask.astype(F32).astype(BF16)


def prep_kernel(n, sup, capacity, rank_ref, keep_ref, patches_ref, out_ref):
    rank = rank_ref[0]
    first = rank * sup
    keep = keep_ref[...]
    rows = 4 * sup
    count = keep.shape[0]

    def places(width, shift):
        ids = lax.broadcasted_iota(jnp.int32, (count, width), 1) >> shift
        kept = jnp.sum((keep == first + ids).astype(jnp.int32), axis=0, keepdims=True)
        below = jnp.sum(
            jnp.logical_and(keep >= first, keep < first + ids).astype(jnp.int32),
            axis=0,
            keepdims=True,
        )
        return kept, below, lax.broadcasted_iota(jnp.int32, (1, width), 1)

    kept, below, lane = places(rows, 2)
    fine_pos = jnp.where(kept == 1, (lane >> 2) + 3 * below + (lane & 3), -1)
    kept, below, lane = places(sup, 0)
    mean_pos = jnp.where(kept == 1, -1, lane + 3 * below)
    start = first + 3 * jnp.sum((keep < first).astype(jnp.int32), axis=0, keepdims=True)
    flat = patches_ref[...]
    cuts = flat.shape[1] // 128
    sup_col = lax.broadcasted_iota(jnp.int32, (sup, rows), 0)
    sup_lane = lax.broadcasted_iota(jnp.int32, (sup, rows), 1) >> 2
    averaging = jnp.where(sup_col == sup_lane, 0.25, 0.0).astype(BF16)
    means = jnp.dot(averaging, flat, preferred_element_type=F32).astype(BF16)
    index = lax.broadcasted_iota(jnp.int32, (n * cuts * capacity, 1), 0)
    device, cut, slot = slot_of(index, n, capacity, cuts)
    pos = ((device - start) & (n - 1)) + slot * n
    total = jnp.zeros((n * cuts * capacity, 128), F32)
    for c in range(cuts):
        at = jnp.where(cut == c, pos, -2)
        features = slice(c * 128, (c + 1) * 128)
        total = (
            total
            + jnp.dot(one_hot(at == fine_pos), flat[:, features], preferred_element_type=F32)
            + jnp.dot(one_hot(at == mean_pos), means[:, features], preferred_element_type=F32)
        )
    out_ref[...] = total.astype(BF16)


def prep(scalars, keep_col, flat, n, sup, capacity):
    width = flat.shape[1] // 2
    shape = (n * capacity * width // 128, 128)
    return pl.pallas_call(
        functools.partial(prep_kernel, n, sup, capacity),
        grid_spec=pltpu.PrefetchScalarGridSpec(
            num_scalar_prefetch=1,
            grid=(1,),
            in_specs=[
                pl.BlockSpec(keep_col.shape, lambda i, ref: (0, 0)),
                pl.BlockSpec((flat.shape[0], width), lambda i, ref: (0, ref[1])),
            ],
            out_specs=pl.BlockSpec(shape, lambda i, ref: (0, 0)),
        ),
        out_shape=struct(shape),
        compiler_params=params(),
    )(scalars, keep_col, flat)


def pick_kernel(n, sup, per_owner, capacity, rank_ref, keep_ref, got_ref, out_ref):
    rank = rank_ref[0]
    keep = keep_ref[...]
    count = keep.shape[0]
    lanes = got_ref.shape[0]
    cuts = lanes // (n * capacity)
    source, _, _ = slot_of(
        lax.broadcasted_iota(jnp.int32, (count, lanes), 1), n, capacity, cuts
    )
    low = jnp.sum((keep < source * sup).astype(jnp.int32), axis=0, keepdims=True)
    high = jnp.sum((keep < source * sup + sup).astype(jnp.int32), axis=0, keepdims=True)
    source, cut, slot = slot_of(
        lax.broadcasted_iota(jnp.int32, (1, lanes), 1), n, capacity, cuts
    )
    start = source * sup + 3 * low
    stop = source * sup + sup + 3 * high
    token = start + ((rank - start) & (n - 1)) + slot * n
    row = jnp.where(token < stop, token >> (n.bit_length() - 1), -1)
    own = lax.broadcasted_iota(jnp.int32, (per_owner, lanes), 0)
    got = got_ref[...]
    for c in range(cuts):
        choose = one_hot(own == jnp.where(cut == c, row, -1))
        owned = jnp.dot(choose, got, preferred_element_type=F32).astype(BF16)
        out_ref[c * per_owner : (c + 1) * per_owner] = owned


def pick(scalars, keep_col, got, n, sup, per_owner, capacity):
    cuts = got.shape[0] // (n * capacity)
    return pl.pallas_call(
        functools.partial(pick_kernel, n, sup, per_owner, capacity),
        in_specs=[sspec(), vspec(), vspec()],
        out_specs=vspec(),
        out_shape=struct((cuts * per_owner, 128)),
        compiler_params=params(),
    )(scalars, keep_col, got)


def pack_kernel(n, rank_ref, out_weight_ref, up_ref, down_ref, *refs):
    near, away_ref, sem = refs[: n // 2], refs[n // 2], refs[n // 2 + 1]
    rank, part = rank_ref[0], rank_ref[2]
    half = n // 2
    rows = up_ref.shape[0]
    wide = up_ref.shape[1] // n
    units = wide // 2
    long = out_weight_ref.shape[0]
    copies = []
    for j in range(half):
        dest = rank ^ j
        for c in range(2):
            at = pl.ds(pl.multiple_of(dest * wide + c * units, 128), units)
            copies.append((up_ref.at[:, at], near[j].at[pl.ds(c * rows, rows)]))
        at = pl.ds(pl.multiple_of(dest * wide, 128), wide)
        copies.append((down_ref.at[at], near[j].at[pl.ds(2 * rows, wide)]))
        copies.append((out_weight_ref, near[j].at[pl.ds(2 * rows + wide, long)]))
        dest = (rank // half ^ 1) * half + j
        at = pl.ds(pl.multiple_of(dest * wide + part * units, 128), units)
        copies.append((up_ref.at[:, at], away_ref.at[j, pl.ds(0, rows)]))
        copies.append((down_ref.at[at], away_ref.at[j, pl.ds(rows, units)]))
    run_copies(copies, sem)()


def pack(scalars, out_weight, up, down, n):
    wide = up.shape[1] // n
    near = struct((2 * up.shape[0] + wide + out_weight.shape[0], 128))
    away = struct((n // 2, up.shape[0] + wide // 2, 128))
    outs = pl.pallas_call(
        functools.partial(pack_kernel, n),
        in_specs=[sspec()] + [hspec()] * 3,
        out_specs=[aspec()] * (n // 2 + 1),
        out_shape=[near] * (n // 2) + [away],
        scratch_shapes=[pltpu.SemaphoreType.DMA((6 * n // 2,))],
        compiler_params=params(),
    )(scalars, out_weight, up, down)
    return list(outs[:-1]), outs[-1]


def early_kernel(n, rank_ref, qkv_ref, out_weight_ref, heads_ref, near_ref, rows_ref, sem):
    rank, part = rank_ref[0], rank_ref[2]
    half = n // 2
    depth = heads_ref.shape[0] // half
    long = rows_ref.shape[0]
    copies = []
    for d in range(half):
        dest = (rank // half ^ 1) * half + d
        at = pl.ds(pl.multiple_of(part * depth, 32), depth)
        copies.append((qkv_ref.at[dest, at], heads_ref.at[pl.ds(d * depth, depth)]))
    copies.append((qkv_ref.at[pl.ds(rank // half * half, half)], near_ref))
    at = pl.ds(pl.multiple_of(part * long, 128), long)
    copies.append((out_weight_ref.at[at], rows_ref))
    run_copies(copies, sem)()


def early_blocks(scalars, qkv, out_weight, n):
    return pl.pallas_call(
        functools.partial(early_kernel, n),
        in_specs=[sspec()] + [hspec()] * 2,
        out_specs=[aspec()] * 3,
        out_shape=[
            struct((n // 2 * qkv.shape[1] // 2, 128)),
            struct((n // 2,) + qkv.shape[1:]),
            struct((out_weight.shape[0] // 2, 128)),
        ],
        scratch_shapes=[pltpu.SemaphoreType.DMA((n // 2 + 2,))],
        compiler_params=params(),
    )(scalars, qkv, out_weight)


def fan_kernel(rank_ref, owned_ref, across_ref, mine_ref, other_ref, near_ref, rows_ref, out_ref):
    part = rank_ref[2]
    rows = owned_ref.shape[0]
    count, head_rows = near_ref.shape[:2]
    depth = head_rows // 2
    top = 2 * rows
    for d in range(count):
        out_ref[d, :rows] = owned_ref[...]
        out_ref[d, rows:top] = across_ref[...]
        out_ref[d, top : top + head_rows] = near_ref[d]
        at = pl.ds(pl.multiple_of(top + head_rows + part * depth, 32), depth)
        out_ref[d, at] = mine_ref[d * depth : (d + 1) * depth]
        at = pl.ds(pl.multiple_of(top + head_rows + (1 - part) * depth, 32), depth)
        out_ref[d, at] = other_ref[d * depth : (d + 1) * depth]
        out_ref[d, top + 2 * head_rows :] = rows_ref[...]


def fan(scalars, owned, across, mine, other, near, rows):
    count = near.shape[0]
    shape = struct((count, 2 * owned.shape[0] + 2 * near.shape[1] + rows.shape[0], 128))
    return pl.pallas_call(
        fan_kernel,
        in_specs=[sspec()] + [vspec()] * 6,
        out_specs=vspec(),
        out_shape=shape,
        compiler_params=params(),
    )(scalars, owned, across, mine, other, near, rows)


def source_of(rank, n, q, k):
    return (rank // (n // 2) ^ k) * (n // 2) + q


def norm_rows(x):
    average = jnp.mean(x, axis=-1, keepdims=True)
    power = jnp.mean(x * x, axis=-1, keepdims=True)
    return (x - average) * lax.rsqrt(power - average * average + 1e-06)


def attend_kernel(n, part, rank_ref, mine_ref, other_ref, tokens_ref, out_ref, weight_ref):
    rank, half = rank_ref[0], rank_ref[1]
    rows = other_ref.shape[1] // 2
    cuts = rows // part
    width = cuts * 128
    depth = weight_ref.shape[0]
    for q in range(n // 2):
        for k in range(2):
            source = source_of(rank, n, q, k)
            at = pl.ds(pl.multiple_of(source * part, part), part)
            for c in range(cuts):
                cut = slice(k * rows + c * part, k * rows + (c + 1) * part)
                to = pl.ds(pl.multiple_of(half * width + c * 128, 128), 128)
                tokens_ref[at, to] = mine_ref[q, cut]
                to = pl.ds(pl.multiple_of((1 - half) * width + c * 128, 128), 128)
                tokens_ref[at, to] = other_ref[q, cut]
            to = pl.ds(pl.multiple_of(source * 128, 128), 128)
            high = 2 * rows + k * depth
            weight_ref[:, to] = mine_ref[q, high : high + depth]
    normed = norm_rows(tokens_ref[...].astype(F32)).astype(BF16)
    projected = lax.dot_general(
        normed, weight_ref[...], (((1,), (1,)), ((), ())), preferred_element_type=F32
    ).astype(BF16)
    size = projected.shape[1] // 3
    queries = projected[:, :size]
    keys = projected[:, size : 2 * size]
    values = projected[:, 2 * size :]
    scores = lax.dot_general(
        queries, keys, (((1,), (1,)), ((), ())), preferred_element_type=F32
    ) * (1.0 / math.sqrt(size))
    powers = jnp.exp(scores - jnp.max(scores, axis=1, keepdims=True))
    probs = (powers / jnp.sum(powers, axis=1, keepdims=True)).astype(BF16)
    attended = lax.dot_general(
        values, probs, (((0,), (1,)), ((), ())), preferred_element_type=F32
    ).astype(BF16)
    out_ref[...] = attended


def attend_fast(scalars, mine, other, head_rows, per_owner, n):
    length = n * per_owner
    depth = other.shape[1] // (2 * per_owner) * 256
    size = head_rows // 3
    return pl.pallas_call(
        functools.partial(attend_kernel, n, per_owner),
        in_specs=[sspec()] + [vspec()] * 2,
        out_specs=[vspec()] * 2,
        out_shape=[struct((length, depth)), struct((size, length))],
        scratch_shapes=[VMEM((head_rows, n * 128), BF16)],
        compiler_params=params(12),
        cost_estimate=cost(30),
    )(scalars, mine, other)


def mlp_kernel(n, rank_ref, tokens_ref, pieces, far, outs_far, near, outs_near, outs, scratch):
    residual_ref, keep_ref, send_ref = outs
    up_ref, down_ref, row_ref, whole_ref, joined_ref, sem = scratch
    rank, half, group = rank_ref[0], rank_ref[1], rank_ref[2]
    block = up_ref.shape[0] // n
    wide = down_ref.shape[0]
    unit = wide // 2
    size = pieces[0].shape[2]
    rows = outs_far[0][0].shape[1]
    first, later = [], []
    for j in range(n // 2):
        source = rank ^ j
        at = pl.ds(pl.multiple_of(source * block, block), block)
        to = pl.ds(pl.multiple_of(source * 128, 128), 128)
        for c in range(2):
            later.append(
                (near[j].at[pl.ds(c * block, block)], up_ref.at[at, pl.ds(c * unit, unit)])
            )
        later.append((near[j].at[pl.ds(2 * block, wide)], down_ref.at[:, to]))
        for core in range(2):
            rows_from = outs_near[core][j].at[pl.ds(2 * block + wide, 2 * rows)]
            first.append((rows_from, whole_ref.at[core, :, to]))
        source = source_of(rank, n, j, 1)
        at = pl.ds(pl.multiple_of(source * block, block), block)
        to = pl.ds(pl.multiple_of(source * 128, 128), 128)
        for c in range(2):
            units = pl.ds(pl.multiple_of((group ^ c) * unit, unit), unit)
            later.append((far[c].at[j, pl.ds(0, block)], up_ref.at[at, units]))
            later.append((far[c].at[j, pl.ds(block, unit)], down_ref.at[units, to]))
        for core in range(2):
            for c in range(2):
                at = pl.ds(pl.multiple_of((group ^ c) * rows, rows), rows)
                first.append((outs_far[core][c].at[j], whole_ref.at[core, at, to]))
    wait_first = run_copies(first, sem)
    wait_later = run_copies(later, sem, len(first))
    for j in range(n // 2):
        for core in range(2):
            for k in range(2):
                at = pl.ds(pl.multiple_of((rank ^ j ^ (k * n // 2)) * size, size), size)
                joined_ref[core, at] = pieces[core][j, k]
    wait_first()
    dims = (((0,), (0,)), ((), ()))
    row_ref[...] = (
        tokens_ref[...].astype(F32)
        + lax.dot_general(joined_ref[0], whole_ref[0], dims, preferred_element_type=F32)
        + lax.dot_general(joined_ref[1], whole_ref[1], dims, preferred_element_type=F32)
    )
    part = residual_ref.shape[0]
    width = residual_ref.shape[1]
    my_cols = pl.ds(pl.multiple_of(half * width, width), width)
    other_cols = pl.ds(pl.multiple_of((1 - half) * width, width), width)
    residual_ref[...] = row_ref[pl.ds(pl.multiple_of(rank * part, part), part), my_cols]
    normed = norm_rows(row_ref[...]).astype(BF16)
    wait_later()
    raw = jnp.dot(normed, up_ref[...], preferred_element_type=F32)
    hidden = (0.5 * raw * (1.0 + lax.erf(raw * math.sqrt(0.5)))).astype(BF16)
    keep_ref[...] = jnp.dot(hidden, down_ref[:, my_cols], preferred_element_type=F32)
    send_ref[...] = jnp.dot(hidden, down_ref[:, other_cols], preferred_element_type=F32).astype(BF16)


def mlp(scalars, tokens, pieces, far, outs_far, near, near_other, n):
    length, depth = tokens.shape
    width = depth // 2
    wide = 2 * (far[0].shape[1] - depth // n)
    inner = n * pieces[0].shape[2]
    half = n // 2

    def kernel(scalars, tokens, a, b, c, d, e, f, g, h, *refs):
        near, other = refs[:half], refs[half : 2 * half]
        outs, scratch = refs[2 * half : 2 * half + 3], refs[2 * half + 3 :]
        far, outs_far, outs_near = (c, d), ((e, f), (g, h)), (near, other)
        mlp_kernel(n, scalars, tokens, (a, b), far, outs_far, near, outs_near, outs, scratch)

    return pl.pallas_call(
        kernel,
        in_specs=[sspec()] + [vspec()] * 3 + [aspec()] * (6 + 2 * half),
        out_specs=[vspec()] * 3,
        out_shape=[
            struct((length // n, width), F32),
            struct((length, width), F32),
            struct((length, width)),
        ],
        scratch_shapes=[
            VMEM((depth, wide), BF16),
            VMEM((wide, depth), BF16),
            VMEM((length, depth), F32),
            VMEM((2, inner, depth), BF16),
            VMEM((2, inner, length), BF16),
            pltpu.SemaphoreType.DMA((13 * half,)),
        ],
        compiler_params=params(20),
    )(scalars, tokens, *pieces, *far, *outs_far[0], *outs_far[1], *near, *near_other)


def join_kernel(rank_ref, keep_ref, got_ref, residual_ref, base_ref, out_ref):
    part = residual_ref.shape[0]
    mine = pl.ds(pl.multiple_of(rank_ref[0] * part, part), part)
    base_ref[...] = keep_ref[mine] + got_ref[mine].astype(F32) + residual_ref[...]
    out_ref[...] = (keep_ref[...] + got_ref[...].astype(F32)).astype(BF16)


def join(scalars, keep, got, residual):
    return pl.pallas_call(
        join_kernel,
        in_specs=[sspec()] + [vspec()] * 3,
        out_specs=[vspec()] * 2,
        out_shape=[struct(residual.shape, F32), struct(keep.shape)],
        compiler_params=params(8),
    )(scalars, keep, got, residual)


def last_kernel(n, rank_ref, base_ref, terms_ref, out_ref):
    rank = rank_ref[0]
    total = base_ref[...]
    for j in range(1, n):
        total = total + terms_ref[rank ^ j].astype(F32)
    out_ref[...] = total.astype(BF16)


def last(scalars, base, terms):
    return pl.pallas_call(
        functools.partial(last_kernel, terms.shape[0]),
        in_specs=[sspec()] + [vspec()] * 2,
        out_specs=vspec(),
        out_shape=struct(base.shape),
        compiler_params=params(8),
    )(scalars, base, terms)


def swap(value, axis, j):
    n = lax.axis_size(axis)
    return lax.ppermute(value, axis, [(i, i ^ j) for i in range(n)])


def exchange(value):
    return lax.all_to_all(value, "seq", split_axis=0, concat_axis=0, tiled=True)


def exchange_half(value):
    n = lax.axis_size("seq")
    groups = [list(range(n // 2)), list(range(n // 2, n))]
    return lax.all_to_all(
        value, "seq", split_axis=0, concat_axis=0, axis_index_groups=groups, tiled=True
    )


def after(value, *others):
    return lax.optimization_barrier((value, *others))[0]


def local_fast(patches, keep_list, qkv_weight, out_weight, up_weight, down_weight):
    n = lax.axis_size("seq")
    rank, head, group = (
        lax.axis_index(name).astype(jnp.int32) for name in ("seq", "head", "groups")
    )
    scalars = jnp.stack([rank, head, group])
    half = n // 2
    sup, depth = patches.shape[1], patches.shape[3]
    length = sup * n * 8 // 5
    per_owner = length // n
    half_width = depth // 2
    head_rows = qkv_weight.shape[2]
    capacity = (4 * sup + n - 1) // n
    keep_col = keep_list.reshape(-1, 1)
    flat = patches.reshape(4 * sup, depth)
    heads = qkv_weight.transpose(1, 2, 0)

    slots = prep(scalars, keep_col, flat, n, sup, capacity)
    qkv_away, qkv_near, out_away = early_blocks(scalars, heads, out_weight, n)
    dealt = exchange(slots)
    qkv_mine = swap(after(qkv_away, slots), "seq", half)
    out_far = swap(after(out_away, slots), "seq", half)
    qkv_other = swap(qkv_mine, "groups", 1)
    blocks = lax.optimization_barrier((out_weight, up_weight, down_weight, qkv_mine))[:3]
    near, mlp_away = pack(scalars, *blocks, n)
    near = [near[0]] + [swap(near[j], "seq", j) for j in range(1, half)]
    owned = pick(scalars, keep_col, dealt, n, sup, per_owner, capacity)

    across = swap(owned, "seq", half)
    across, out_far, qkv_other = lax.optimization_barrier((across, out_far, qkv_other))
    mlp_far = swap(after(mlp_away, across), "seq", half)
    got = exchange_half(fan(scalars, owned, across, qkv_mine, qkv_other, qkv_near, out_far))
    near_other = [swap(block, "head", 1) for block in near]
    got, mlp_far, *near_other = lax.optimization_barrier((got, mlp_far, *near_other))

    top = 2 * owned.shape[0]
    pieces_other = swap(got[:, :top], "head", 1)
    tokens, attended = attend_fast(scalars, got, pieces_other, head_rows, per_owner, n)

    att_across = swap(attended, "seq", half)
    mlp_far, got = lax.optimization_barrier((mlp_far, got, attended))[:2]
    mlp_mine = exchange_half(mlp_far)
    far_mine = got[:, top + 2 * head_rows :]
    far_other = swap(far_mine, "groups", 1)
    att_across, mlp_mine = lax.optimization_barrier((att_across, mlp_mine))
    pair = jnp.stack([attended, att_across])
    mlp_other = swap(mlp_mine, "groups", 1)
    pairs = [swap(pair, "seq", j) for j in range(1, half)]
    mlp_other, far_other, *pairs = lax.optimization_barrier((mlp_other, far_other, *pairs))
    gathered = jnp.stack([pair] + pairs)
    residual, keep, send = mlp(
        scalars,
        tokens,
        (gathered, swap(gathered, "head", 1)),
        (mlp_mine, mlp_other),
        ((far_mine, far_other), (swap(far_mine, "head", 1), swap(far_other, "head", 1))),
        near,
        near_other,
        n,
    )
    sent = swap(send, "head", 1)
    base, terms = join(scalars, keep, sent, residual)
    terms = exchange(terms.reshape(n, per_owner, half_width))
    encoded = last(scalars, base, terms)
    return encoded.reshape(1, per_owner, 1, half_width)


def local(patches, keep_list, qkv_weight, out_weight, up_weight, down_weight):
    n = lax.axis_size("seq")
    one_image = patches.shape[0] == 1 and qkv_weight.shape[1] == n and n & (n - 1) == 0
    one_image = one_image and lax.axis_size("groups") == 2 and up_weight.shape[1] == n * 256
    plan = local_fast if one_image else local_general
    return plan(patches, keep_list, qkv_weight, out_weight, up_weight, down_weight)


def solution(mesh):
    return jax.shard_map(
        local,
        mesh=mesh,
        in_specs=(
            P("groups", "seq", None, None),
            P("groups", None),
            P("seq", "head", None),
            P("head", "seq"),
            P("seq", "head"),
            P("head", "seq"),
        ),
        out_specs=P("groups", None, "seq", "head"),
        check_vma=False,
    )
```

```python
import functools
import math

import jax
import jax.numpy as jnp
from jax import lax
from jax.experimental import pallas as pl
from jax.experimental.pallas import tpu as pltpu
from jax.sharding import PartitionSpec as P

F32 = jnp.float32
BF16 = jnp.bfloat16
VMEM = pltpu.VMEM

def layer_norm(matrix):
    average = jnp.mean(matrix, axis=-1, keepdims=True)
    power = jnp.mean(matrix * matrix, axis=-1, keepdims=True)
    return (matrix - average) * lax.rsqrt(power - average * average + 1e-06)


def attend(queries, keys, values):
    length = queries.shape[0]
    block = math.gcd(length, 512)
    scale = 1.0 / math.sqrt(queries.shape[1])

    def one_block(query_rows):
        scores = (
            lax.dot_general(
                query_rows, keys, (((1,), (1,)), ((), ())), preferred_element_type=jnp.float32
            )
            * scale
        )
        top = jnp.max(scores, axis=1, keepdims=True)
        powers = jnp.exp(scores - top)
        probs = (powers / jnp.sum(powers, axis=1, keepdims=True)).astype(jnp.bfloat16)
        return jnp.dot(probs, values, preferred_element_type=jnp.float32).astype(jnp.bfloat16)

    blocks = lax.map(one_block, queries.reshape(length // block, block, queries.shape[1]))
    return blocks.reshape(length, values.shape[1])


def local_general(patches, keep_list, qkv_weight, out_weight, up_weight, down_weight):
    seq_count = lax.axis_size("seq")
    seq_rank = lax.axis_index("seq")
    head_rank = lax.axis_index("head")
    images = patches.shape[0]
    sup_local = patches.shape[1]
    depth = patches.shape[3]
    half_width = depth // lax.axis_size("head")
    head_count = qkv_weight.shape[1]
    seq_length = sup_local * seq_count * 8 // 5
    per_owner = seq_length // seq_count
    capacity = (4 * sup_local + seq_count - 1) // seq_count
    slot_count = 4 * sup_local
    image_index = jnp.arange(images, dtype=jnp.int32)
    bounds = jnp.arange(seq_count + 1, dtype=jnp.int32) * sup_local
    before = jnp.sum((keep_list[:, :, None] < bounds[None, None, :]).astype(jnp.int32), axis=1)
    starts = bounds[None, :seq_count] + 3 * before[:, :seq_count]
    lengths = sup_local + 3 * (before[:, 1:] - before[:, :seq_count])
    my_start = lax.dynamic_index_in_dim(starts, seq_rank, 1, keepdims=False)
    my_length = lax.dynamic_index_in_dim(lengths, seq_rank, 1, keepdims=False)
    local_ids = seq_rank * sup_local + jnp.arange(sup_local, dtype=jnp.int32)
    kept_flag = jnp.any(keep_list[:, None, :] == local_ids[None, :, None], axis=2).astype(jnp.int32)
    offsets = jnp.arange(sup_local, dtype=jnp.int32)[None, :] + 3 * (
        jnp.cumsum(kept_flag, axis=1) - kept_flag
    )
    slot_ids = jnp.arange(slot_count, dtype=jnp.int32)
    owner_patch = (
        jnp.sum((offsets[:, None, :] <= slot_ids[None, :, None]).astype(jnp.int32), axis=2) - 1
    )
    start_of = jnp.take_along_axis(offsets, owner_patch, axis=1)
    sub_index = jnp.minimum(slot_ids[None, :] - start_of, 3)
    kept_of = jnp.take_along_axis(kept_flag, owner_patch, axis=1)
    flat_patches = patches.reshape(images, sup_local * 4, depth)
    fine_rows = flat_patches[
        image_index[:, None], owner_patch * 4 + jnp.where(kept_of == 1, sub_index, 0)
    ]
    mean_rows = jnp.mean(patches.astype(jnp.float32), axis=2).astype(jnp.bfloat16)
    shared_rows = mean_rows[image_index[:, None], owner_patch]
    local_tokens = jnp.where((kept_of == 1)[:, :, None], fine_rows, shared_rows)
    destinations = jnp.arange(seq_count, dtype=jnp.int32)[:, None, None]
    depth_slots = jnp.arange(capacity, dtype=jnp.int32)[None, None, :]
    positions = (destinations - my_start[None, :, None]) % seq_count + depth_slots * seq_count
    valid = positions < my_length[None, :, None]
    outgoing = local_tokens[image_index[None, :, None], jnp.minimum(positions, slot_count - 1)]
    outgoing = jnp.where(valid[:, :, :, None], outgoing, jnp.zeros((), jnp.bfloat16))
    incoming = lax.all_to_all(outgoing, "seq", split_axis=0, concat_axis=0, tiled=True)
    owned = jnp.arange(per_owner, dtype=jnp.int32) * seq_count + seq_rank
    source = jnp.sum((starts[:, None, :] <= owned[None, :, None]).astype(jnp.int32), axis=2) - 1
    first_of = jnp.take_along_axis(starts, source, axis=1)
    depth_of = (owned[None, :] - first_of) // seq_count
    resident = incoming[source, image_index[:, None], depth_of]
    start_rows = resident.reshape(images * per_owner, depth)
    start_float = start_rows.astype(jnp.float32)
    qkv_full, out_full, up_full, down_full = (
        lax.all_gather(qkv_weight, "seq", axis=0, tiled=True),
        lax.all_gather(out_weight, "seq", axis=1, tiled=True),
        lax.all_gather(up_weight, "seq", axis=0, tiled=True),
        lax.all_gather(down_weight, "seq", axis=1, tiled=True),
    )
    normed = layer_norm(start_float).astype(jnp.bfloat16).reshape(images, per_owner, depth)
    projected = jnp.einsum("ipd,dhc->ihpc", normed, qkv_full, preferred_element_type=jnp.float32)
    head_size = qkv_weight.shape[2] // 3
    sending = projected.astype(jnp.bfloat16).reshape(seq_count, per_owner, 3 * head_size)
    gathered = lax.all_to_all(sending, "seq", split_axis=0, concat_axis=0, tiled=True).reshape(
        seq_length, 3 * head_size
    )
    attended = attend(
        gathered[:, :head_size],
        gathered[:, head_size : 2 * head_size],
        gathered[:, 2 * head_size :],
    )
    returned = lax.all_to_all(
        attended.reshape(seq_count, per_owner, head_size),
        "seq",
        split_axis=0,
        concat_axis=0,
        tiled=True,
    )
    returned = returned.reshape(images, head_count, per_owner, head_size)
    partial_sum = jnp.einsum(
        "ihpc,hcd->ipd",
        returned,
        out_full.reshape(head_count, head_size, depth),
        preferred_element_type=jnp.float32,
    ).reshape(images * per_owner, depth)
    attn_total = lax.psum(partial_sum, "head")
    residual = start_float + attn_total
    residual_half = lax.dynamic_slice_in_dim(residual, head_rank * half_width, half_width, 1)
    normed_two = layer_norm(residual).astype(jnp.bfloat16)
    hidden = jax.nn.gelu(
        jnp.dot(normed_two, up_full, preferred_element_type=jnp.float32), approximate=False
    ).astype(jnp.bfloat16)
    mlp_terms = jnp.dot(hidden, down_full, preferred_element_type=jnp.float32)
    mlp_part = lax.psum_scatter(mlp_terms, "head", scatter_dimension=1, tiled=True)
    encoded = (residual_half + mlp_part).astype(jnp.bfloat16)
    return encoded.reshape(images, per_owner, 1, half_width)


def vspec():
    return pl.BlockSpec(memory_space=VMEM)


def aspec():
    return pl.BlockSpec(memory_space=pl.ANY)


def sspec():
    return pl.BlockSpec(memory_space=pltpu.SMEM)


def hspec():
    return pl.BlockSpec(memory_space=pltpu.HBM)


def run_copies(copies, sem, base=0):
    started = [
        pltpu.make_async_copy(src, dst, sem.at[base + i]) for i, (src, dst) in enumerate(copies)
    ]
    for copy in started:
        copy.start()

    def wait():
        for copy in started:
            copy.wait()

    return wait


def params(mebibytes=4):
    return pltpu.CompilerParams(vmem_limit_bytes=mebibytes * 1024 * 1024)


def cost(micros):
    return pl.CostEstimate(flops=micros * 10**9, bytes_accessed=1 << 20, transcendentals=0)


def struct(shape, dtype=BF16):
    return jax.ShapeDtypeStruct(shape, dtype)


def slot_of(index, n, capacity, cuts):
    device = sum(((index >= j * cuts * capacity).astype(jnp.int32) for j in range(1, n)), 0 * index)
    inner = index - device * (cuts * capacity)
    cut = sum(((inner >= c * capacity).astype(jnp.int32) for c in range(1, cuts)), 0 * index)
    return device, cut, inner - cut * capacity


def one_hot(mask):
    return mask.astype(F32).astype(BF16)


def prep_kernel(n, sup, capacity, rank_ref, keep_ref, patches_ref, out_ref):
    rank = rank_ref[0]
    first = rank * sup
    keep = keep_ref[...]
    rows = 4 * sup
    count = keep.shape[0]

    def places(width, shift):
        ids = lax.broadcasted_iota(jnp.int32, (count, width), 1) >> shift
        kept = jnp.sum((keep == first + ids).astype(jnp.int32), axis=0, keepdims=True)
        below = jnp.sum(
            jnp.logical_and(keep >= first, keep < first + ids).astype(jnp.int32),
            axis=0,
            keepdims=True,
        )
        return kept, below, lax.broadcasted_iota(jnp.int32, (1, width), 1)

    kept, below, lane = places(rows, 2)
    fine_pos = jnp.where(kept == 1, (lane >> 2) + 3 * below + (lane & 3), -1)
    kept, below, lane = places(sup, 0)
    mean_pos = jnp.where(kept == 1, -1, lane + 3 * below)
    start = first + 3 * jnp.sum((keep < first).astype(jnp.int32), axis=0, keepdims=True)
    flat = patches_ref[...]
    cuts = flat.shape[1] // 128
    sup_col = lax.broadcasted_iota(jnp.int32, (sup, rows), 0)
    sup_lane = lax.broadcasted_iota(jnp.int32, (sup, rows), 1) >> 2
    averaging = jnp.where(sup_col == sup_lane, 0.25, 0.0).astype(BF16)
    means = jnp.dot(averaging, flat, preferred_element_type=F32).astype(BF16)
    index = lax.broadcasted_iota(jnp.int32, (n * cuts * capacity, 1), 0)
    device, cut, slot = slot_of(index, n, capacity, cuts)
    pos = ((device - start) & (n - 1)) + slot * n
    total = jnp.zeros((n * cuts * capacity, 128), F32)
    for c in range(cuts):
        at = jnp.where(cut == c, pos, -2)
        features = slice(c * 128, (c + 1) * 128)
        total = (
            total
            + jnp.dot(one_hot(at == fine_pos), flat[:, features], preferred_element_type=F32)
            + jnp.dot(one_hot(at == mean_pos), means[:, features], preferred_element_type=F32)
        )
    out_ref[...] = total.astype(BF16)


def prep(scalars, keep_col, flat, n, sup, capacity):
    width = flat.shape[1] // 2
    shape = (n * capacity * width // 128, 128)
    return pl.pallas_call(
        functools.partial(prep_kernel, n, sup, capacity),
        grid_spec=pltpu.PrefetchScalarGridSpec(
            num_scalar_prefetch=1,
            grid=(1,),
            in_specs=[
                pl.BlockSpec(keep_col.shape, lambda i, ref: (0, 0)),
                pl.BlockSpec((flat.shape[0], width), lambda i, ref: (0, ref[1])),
            ],
            out_specs=pl.BlockSpec(shape, lambda i, ref: (0, 0)),
        ),
        out_shape=struct(shape),
        compiler_params=params(),
    )(scalars, keep_col, flat)


def pick_kernel(n, sup, per_owner, capacity, rank_ref, keep_ref, got_ref, out_ref):
    rank = rank_ref[0]
    keep = keep_ref[...]
    count = keep.shape[0]
    lanes = got_ref.shape[0]
    cuts = lanes // (n * capacity)
    source, _, _ = slot_of(
        lax.broadcasted_iota(jnp.int32, (count, lanes), 1), n, capacity, cuts
    )
    low = jnp.sum((keep < source * sup).astype(jnp.int32), axis=0, keepdims=True)
    high = jnp.sum((keep < source * sup + sup).astype(jnp.int32), axis=0, keepdims=True)
    source, cut, slot = slot_of(
        lax.broadcasted_iota(jnp.int32, (1, lanes), 1), n, capacity, cuts
    )
    start = source * sup + 3 * low
    stop = source * sup + sup + 3 * high
    token = start + ((rank - start) & (n - 1)) + slot * n
    row = jnp.where(token < stop, token >> (n.bit_length() - 1), -1)
    own = lax.broadcasted_iota(jnp.int32, (per_owner, lanes), 0)
    got = got_ref[...]
    for c in range(cuts):
        choose = one_hot(own == jnp.where(cut == c, row, -1))
        owned = jnp.dot(choose, got, preferred_element_type=F32).astype(BF16)
        out_ref[c * per_owner : (c + 1) * per_owner] = owned


def pick(scalars, keep_col, got, n, sup, per_owner, capacity):
    cuts = got.shape[0] // (n * capacity)
    return pl.pallas_call(
        functools.partial(pick_kernel, n, sup, per_owner, capacity),
        in_specs=[sspec(), vspec(), vspec()],
        out_specs=vspec(),
        out_shape=struct((cuts * per_owner, 128)),
        compiler_params=params(),
    )(scalars, keep_col, got)


def pack_kernel(n, rank_ref, qkv_ref, out_weight_ref, up_ref, down_ref, *refs):
    near, (heads_ref, away_ref, sem) = refs[: n // 2], refs[n // 2 :]
    rank, part = rank_ref[0], rank_ref[2]
    half = n // 2
    rows = up_ref.shape[0]
    wide = up_ref.shape[1] // n
    units = wide // 2
    long = out_weight_ref.shape[0]
    depth = qkv_ref.shape[1] // 2
    each = depth + rows + units
    copies = []
    for d in range(half):
        dest = (rank // half ^ 1) * half + d
        low = d * each
        at = pl.ds(pl.multiple_of(part * depth, 32), depth)
        copies.append((qkv_ref.at[dest, at], away_ref.at[pl.ds(low, depth)]))
        at = pl.ds(pl.multiple_of(dest * wide + part * units, 128), units)
        copies.append((up_ref.at[:, at], away_ref.at[pl.ds(low + depth, rows)]))
        copies.append((down_ref.at[at], away_ref.at[pl.ds(low + depth + rows, units)]))
    at = pl.ds(pl.multiple_of(part * (long // 2), 128), long // 2)
    copies.append((out_weight_ref.at[at], away_ref.at[pl.ds(half * each, long // 2)]))
    copies.append((qkv_ref.at[pl.ds(rank // half * half, half)], heads_ref))
    for j in range(half):
        dest = rank ^ j
        for c in range(2):
            at = pl.ds(pl.multiple_of(dest * wide + c * units, 128), units)
            copies.append((up_ref.at[:, at], near[j].at[pl.ds(c * rows, rows)]))
        at = pl.ds(pl.multiple_of(dest * wide, 128), wide)
        copies.append((down_ref.at[at], near[j].at[pl.ds(2 * rows, wide)]))
        copies.append((out_weight_ref, near[j].at[pl.ds(2 * rows + wide, long)]))
    run_copies(copies, sem)()


def pack(scalars, qkv, out_weight, up, down, n):
    half = n // 2
    wide = up.shape[1] // n
    near = struct((2 * up.shape[0] + wide + out_weight.shape[0], 128))
    each = qkv.shape[1] // 2 + up.shape[0] + wide // 2
    away = struct((half * each + out_weight.shape[0] // 2, 128))
    outs = pl.pallas_call(
        functools.partial(pack_kernel, n),
        in_specs=[sspec()] + [hspec()] * 4,
        out_specs=[aspec()] * (half + 2),
        out_shape=[near] * half + [struct((half,) + qkv.shape[1:]), away],
        scratch_shapes=[pltpu.SemaphoreType.DMA((7 * half + 2,))],
        compiler_params=params(),
    )(scalars, qkv, out_weight, up, down)
    return list(outs[:half]), outs[half], outs[half + 1]


def fan_kernel(owned_ref, across_ref, heads_ref, far_ref, out_ref):
    rows = owned_ref.shape[0]
    count, head_rows = heads_ref.shape[:2]
    top = 2 * rows + head_rows
    rest = out_ref.shape[1] - top
    each = (far_ref.shape[0] - rest) // (count - 1)
    for d in range(count):
        out_ref[d, :rows] = owned_ref[...]
        out_ref[d, rows : 2 * rows] = across_ref[...]
        out_ref[d, 2 * rows : top] = heads_ref[d]
        out_ref[d, top : top + each] = far_ref[d * each : (d + 1) * each]
        out_ref[d, top + each :] = far_ref[count * each :]


def fan(owned, across, heads, far, out_rows):
    count = heads.shape[0]
    each = (far.shape[0] - out_rows) // count
    shape = struct((count, 2 * owned.shape[0] + heads.shape[1] + each + out_rows, 128))
    return pl.pallas_call(
        fan_kernel,
        in_specs=[vspec()] * 4,
        out_specs=vspec(),
        out_shape=shape,
        compiler_params=params(8),
    )(owned, across, heads, far)


def source_of(rank, n, q, k):
    return (rank // (n // 2) ^ k) * (n // 2) + q


def norm_rows(x):
    average = jnp.mean(x, axis=-1, keepdims=True)
    power = jnp.mean(x * x, axis=-1, keepdims=True)
    return (x - average) * lax.rsqrt(power - average * average + 1e-06)


def attend_kernel(n, part, rank_ref, mine_ref, other_ref, far_ref, tokens_ref, out_ref, weight_ref):
    rank, half, group = rank_ref[0], rank_ref[1], rank_ref[2]
    rows = other_ref.shape[1] // 2
    cuts = rows // part
    width = cuts * 128
    depth = weight_ref.shape[0]
    piece = far_ref.shape[1]
    for q in range(n // 2):
        for k in range(2):
            source = source_of(rank, n, q, k)
            at = pl.ds(pl.multiple_of(source * part, part), part)
            for c in range(cuts):
                cut = slice(k * rows + c * part, k * rows + (c + 1) * part)
                to = pl.ds(pl.multiple_of(half * width + c * 128, 128), 128)
                tokens_ref[at, to] = mine_ref[q, cut]
                to = pl.ds(pl.multiple_of((1 - half) * width + c * 128, 128), 128)
                tokens_ref[at, to] = other_ref[q, cut]
        to = pl.ds(pl.multiple_of(source_of(rank, n, q, 0) * 128, 128), 128)
        weight_ref[:, to] = mine_ref[q, 2 * rows : 2 * rows + depth]
        to = pl.ds(pl.multiple_of(source_of(rank, n, q, 1) * 128, 128), 128)
        at = pl.ds(pl.multiple_of(group * piece, 32), piece)
        weight_ref[at, to] = mine_ref[q, 2 * rows + depth : 2 * rows + depth + piece]
        at = pl.ds(pl.multiple_of((1 - group) * piece, 32), piece)
        weight_ref[at, to] = far_ref[q]
    normed = norm_rows(tokens_ref[...].astype(F32)).astype(BF16)
    projected = lax.dot_general(
        normed, weight_ref[...], (((1,), (1,)), ((), ())), preferred_element_type=F32
    ).astype(BF16)
    size = projected.shape[1] // 3
    queries = projected[:, :size]
    keys = projected[:, size : 2 * size]
    values = projected[:, 2 * size :]
    scores = lax.dot_general(
        queries, keys, (((1,), (1,)), ((), ())), preferred_element_type=F32
    ) * (1.0 / math.sqrt(size))
    powers = jnp.exp(scores - jnp.max(scores, axis=1, keepdims=True))
    probs = (powers / jnp.sum(powers, axis=1, keepdims=True)).astype(BF16)
    attended = lax.dot_general(
        values, probs, (((0,), (1,)), ((), ())), preferred_element_type=F32
    ).astype(BF16)
    out_ref[...] = attended


def attend_fast(scalars, mine, other, far, head_rows, per_owner, n):
    length = n * per_owner
    depth = other.shape[1] // (2 * per_owner) * 256
    size = head_rows // 3
    return pl.pallas_call(
        functools.partial(attend_kernel, n, per_owner),
        in_specs=[sspec()] + [vspec()] * 3,
        out_specs=[vspec()] * 2,
        out_shape=[struct((length, depth)), struct((size, length))],
        scratch_shapes=[VMEM((head_rows, n * 128), BF16)],
        compiler_params=params(12),
        cost_estimate=cost(30),
    )(scalars, mine, other, far)


def mlp_kernel(n, rank_ref, tokens_ref, pieces, far, outs_far, near, outs_near, outs, scratch):
    residual_ref, keep_ref, send_ref = outs
    up_ref, down_ref, row_ref, whole_ref, joined_ref, sem = scratch
    rank, half, group = rank_ref[0], rank_ref[1], rank_ref[2]
    block = up_ref.shape[0] // n
    wide = down_ref.shape[0]
    unit = wide // 2
    size = pieces[0].shape[2]
    rows = outs_far[0][0].shape[1]
    first, later = [], []
    for j in range(n // 2):
        source = rank ^ j
        at = pl.ds(pl.multiple_of(source * block, block), block)
        to = pl.ds(pl.multiple_of(source * 128, 128), 128)
        for c in range(2):
            later.append(
                (near[j].at[pl.ds(c * block, block)], up_ref.at[at, pl.ds(c * unit, unit)])
            )
        later.append((near[j].at[pl.ds(2 * block, wide)], down_ref.at[:, to]))
        for core in range(2):
            rows_from = outs_near[core][j].at[pl.ds(2 * block + wide, 2 * rows)]
            first.append((rows_from, whole_ref.at[core, :, to]))
        source = source_of(rank, n, j, 1)
        at = pl.ds(pl.multiple_of(source * block, block), block)
        to = pl.ds(pl.multiple_of(source * 128, 128), 128)
        for c in range(2):
            units = pl.ds(pl.multiple_of((group ^ c) * unit, unit), unit)
            later.append((far[c].at[j, pl.ds(0, block)], up_ref.at[at, units]))
            later.append((far[c].at[j, pl.ds(block, unit)], down_ref.at[units, to]))
        for core in range(2):
            for c in range(2):
                at = pl.ds(pl.multiple_of((group ^ c) * rows, rows), rows)
                first.append((outs_far[core][c].at[j], whole_ref.at[core, at, to]))
    wait_first = run_copies(first, sem)
    wait_later = run_copies(later, sem, len(first))
    for j in range(n // 2):
        for core in range(2):
            for k in range(2):
                at = pl.ds(pl.multiple_of((rank ^ j ^ (k * n // 2)) * size, size), size)
                joined_ref[core, at] = pieces[core][j, k]
    wait_first()
    dims = (((0,), (0,)), ((), ()))
    row_ref[...] = (
        tokens_ref[...].astype(F32)
        + lax.dot_general(joined_ref[0], whole_ref[0], dims, preferred_element_type=F32)
        + lax.dot_general(joined_ref[1], whole_ref[1], dims, preferred_element_type=F32)
    )
    part = residual_ref.shape[0]
    width = residual_ref.shape[1]
    my_cols = pl.ds(pl.multiple_of(half * width, width), width)
    other_cols = pl.ds(pl.multiple_of((1 - half) * width, width), width)
    residual_ref[...] = row_ref[pl.ds(pl.multiple_of(rank * part, part), part), my_cols]
    normed = norm_rows(row_ref[...]).astype(BF16)
    wait_later()
    raw = jnp.dot(normed, up_ref[...], preferred_element_type=F32)
    hidden = (0.5 * raw * (1.0 + lax.erf(raw * math.sqrt(0.5)))).astype(BF16)
    keep_ref[...] = jnp.dot(hidden, down_ref[:, my_cols], preferred_element_type=F32)
    send_ref[...] = jnp.dot(hidden, down_ref[:, other_cols], preferred_element_type=F32).astype(BF16)


def mlp(scalars, tokens, pieces, far, outs_far, near, near_other, n):
    length, depth = tokens.shape
    width = depth // 2
    wide = 2 * (far[0].shape[1] - depth // n)
    inner = n * pieces[0].shape[2]
    half = n // 2

    def kernel(scalars, tokens, a, b, c, d, e, f, g, h, *refs):
        near, other = refs[:half], refs[half : 2 * half]
        outs, scratch = refs[2 * half : 2 * half + 3], refs[2 * half + 3 :]
        far, outs_far, outs_near = (c, d), ((e, f), (g, h)), (near, other)
        mlp_kernel(n, scalars, tokens, (a, b), far, outs_far, near, outs_near, outs, scratch)

    return pl.pallas_call(
        kernel,
        in_specs=[sspec()] + [vspec()] * 3 + [aspec()] * (6 + 2 * half),
        out_specs=[vspec()] * 3,
        out_shape=[
            struct((length // n, width), F32),
            struct((length, width), F32),
            struct((length, width)),
        ],
        scratch_shapes=[
            VMEM((depth, wide), BF16),
            VMEM((wide, depth), BF16),
            VMEM((length, depth), F32),
            VMEM((2, inner, depth), BF16),
            VMEM((2, inner, length), BF16),
            pltpu.SemaphoreType.DMA((13 * half,)),
        ],
        compiler_params=params(20),
    )(scalars, tokens, *pieces, *far, *outs_far[0], *outs_far[1], *near, *near_other)


def join_kernel(rank_ref, keep_ref, got_ref, residual_ref, base_ref, out_ref):
    part = residual_ref.shape[0]
    mine = pl.ds(pl.multiple_of(rank_ref[0] * part, part), part)
    base_ref[...] = keep_ref[mine] + got_ref[mine].astype(F32) + residual_ref[...]
    out_ref[...] = (keep_ref[...] + got_ref[...].astype(F32)).astype(BF16)


def join(scalars, keep, got, residual):
    return pl.pallas_call(
        join_kernel,
        in_specs=[sspec()] + [vspec()] * 3,
        out_specs=[vspec()] * 2,
        out_shape=[struct(residual.shape, F32), struct(keep.shape)],
        compiler_params=params(8),
    )(scalars, keep, got, residual)


def last_kernel(n, rank_ref, base_ref, terms_ref, out_ref):
    rank = rank_ref[0]
    total = base_ref[...]
    for j in range(1, n):
        total = total + terms_ref[rank ^ j].astype(F32)
    out_ref[...] = total.astype(BF16)


def last(scalars, base, terms):
    return pl.pallas_call(
        functools.partial(last_kernel, terms.shape[0]),
        in_specs=[sspec()] + [vspec()] * 2,
        out_specs=vspec(),
        out_shape=struct(base.shape),
        compiler_params=params(8),
    )(scalars, base, terms)


def swap(value, axis, j):
    n = lax.axis_size(axis)
    return lax.ppermute(value, axis, [(i, i ^ j) for i in range(n)])


def exchange(value):
    return lax.all_to_all(value, "seq", split_axis=0, concat_axis=0, tiled=True)


def exchange_half(value):
    n = lax.axis_size("seq")
    groups = [list(range(n // 2)), list(range(n // 2, n))]
    return lax.all_to_all(
        value, "seq", split_axis=0, concat_axis=0, axis_index_groups=groups, tiled=True
    )


def after(value, *others):
    return lax.optimization_barrier((value, *others))[0]


def local_fast(patches, keep_list, qkv_weight, out_weight, up_weight, down_weight):
    n = lax.axis_size("seq")
    rank, head, group = (
        lax.axis_index(name).astype(jnp.int32) for name in ("seq", "head", "groups")
    )
    scalars = jnp.stack([rank, head, group])
    half = n // 2
    sup, depth = patches.shape[1], patches.shape[3]
    length = sup * n * 8 // 5
    per_owner = length // n
    half_width = depth // 2
    head_rows = qkv_weight.shape[2]
    capacity = (4 * sup + n - 1) // n
    keep_col = keep_list.reshape(-1, 1)
    flat = patches.reshape(4 * sup, depth)
    heads = qkv_weight.transpose(1, 2, 0)

    near, qkv_near, away = pack(scalars, heads, out_weight, up_weight, down_weight, n)
    far = swap(away, "seq", half)
    slots = prep(scalars, keep_col, after(flat, away), n, sup, capacity)
    dealt = exchange(slots)
    near = lax.optimization_barrier((*near, slots))[:half]
    near = [near[0]] + [swap(near[j], "seq", j) for j in range(1, half)]
    owned = pick(scalars, keep_col, dealt, n, sup, per_owner, capacity)
    across = swap(owned, "seq", half)
    across, far, *near = lax.optimization_barrier((across, far, *near))

    out_rows = out_weight.shape[0] // 2
    got = exchange_half(fan(owned, across, qkv_near, far, out_rows))
    near_other = [swap(block, "head", 1) for block in near]
    got, *near_other = lax.optimization_barrier((got, *near_other))

    top = 2 * owned.shape[0]
    pieces_other = swap(got[:, :top], "head", 1)
    top = top + head_rows
    qkv_far = swap(got[:, top : top + head_rows // 2], "groups", 1)
    tokens, attended = attend_fast(
        scalars, got, pieces_other, qkv_far, head_rows, per_owner, n
    )

    att_across = swap(attended, "seq", half)
    got = after(got, attended)
    mlp_mine = got[:, top + head_rows // 2 : got.shape[1] - out_rows]
    far_mine = got[:, got.shape[1] - out_rows :]
    far_other = swap(far_mine, "groups", 1)
    mlp_other = swap(mlp_mine, "groups", 1)
    pair = jnp.stack([attended, att_across])
    pairs = [swap(pair, "seq", j) for j in range(1, half)]
    mlp_other, far_other, *pairs = lax.optimization_barrier((mlp_other, far_other, *pairs))
    gathered = jnp.stack([pair] + pairs)
    residual, keep, send = mlp(
        scalars,
        tokens,
        (gathered, swap(gathered, "head", 1)),
        (mlp_mine, mlp_other),
        ((far_mine, far_other), (swap(far_mine, "head", 1), swap(far_other, "head", 1))),
        near,
        near_other,
        n,
    )
    sent = swap(send, "head", 1)
    base, terms = join(scalars, keep, sent, residual)
    terms = exchange(terms.reshape(n, per_owner, half_width))
    encoded = last(scalars, base, terms)
    return encoded.reshape(1, per_owner, 1, half_width)


def local(patches, keep_list, qkv_weight, out_weight, up_weight, down_weight):
    n = lax.axis_size("seq")
    one_image = patches.shape[0] == 1 and qkv_weight.shape[1] == n and n & (n - 1) == 0
    one_image = one_image and lax.axis_size("groups") == 2 and up_weight.shape[1] == n * 256
    plan = local_fast if one_image else local_general
    return plan(patches, keep_list, qkv_weight, out_weight, up_weight, down_weight)


def solution(mesh):
    return jax.shard_map(
        local,
        mesh=mesh,
        in_specs=(
            P("groups", "seq", None, None),
            P("groups", None),
            P("seq", "head", None),
            P("head", "seq"),
            P("seq", "head"),
            P("head", "seq"),
        ),
        out_specs=P("groups", None, "seq", "head"),
        check_vma=False,
    )
```

```python
import functools
import math

import jax
import jax.numpy as jnp
from jax import lax
from jax.experimental import pallas as pl
from jax.experimental.pallas import tpu as pltpu
from jax.sharding import PartitionSpec as P

F32 = jnp.float32
BF16 = jnp.bfloat16
VMEM = pltpu.VMEM

def layer_norm(matrix):
    average = jnp.mean(matrix, axis=-1, keepdims=True)
    power = jnp.mean(matrix * matrix, axis=-1, keepdims=True)
    return (matrix - average) * lax.rsqrt(power - average * average + 1e-06)


def attend(queries, keys, values):
    length = queries.shape[0]
    block = math.gcd(length, 512)
    scale = 1.0 / math.sqrt(queries.shape[1])

    def one_block(query_rows):
        scores = (
            lax.dot_general(
                query_rows, keys, (((1,), (1,)), ((), ())), preferred_element_type=jnp.float32
            )
            * scale
        )
        top = jnp.max(scores, axis=1, keepdims=True)
        powers = jnp.exp(scores - top)
        probs = (powers / jnp.sum(powers, axis=1, keepdims=True)).astype(jnp.bfloat16)
        return jnp.dot(probs, values, preferred_element_type=jnp.float32).astype(jnp.bfloat16)

    blocks = lax.map(one_block, queries.reshape(length // block, block, queries.shape[1]))
    return blocks.reshape(length, values.shape[1])


def local_general(patches, keep_list, qkv_weight, out_weight, up_weight, down_weight):
    seq_count = lax.axis_size("seq")
    seq_rank = lax.axis_index("seq")
    head_rank = lax.axis_index("head")
    images = patches.shape[0]
    sup_local = patches.shape[1]
    depth = patches.shape[3]
    half_width = depth // lax.axis_size("head")
    head_count = qkv_weight.shape[1]
    seq_length = sup_local * seq_count * 8 // 5
    per_owner = seq_length // seq_count
    capacity = (4 * sup_local + seq_count - 1) // seq_count
    slot_count = 4 * sup_local
    image_index = jnp.arange(images, dtype=jnp.int32)
    bounds = jnp.arange(seq_count + 1, dtype=jnp.int32) * sup_local
    before = jnp.sum((keep_list[:, :, None] < bounds[None, None, :]).astype(jnp.int32), axis=1)
    starts = bounds[None, :seq_count] + 3 * before[:, :seq_count]
    lengths = sup_local + 3 * (before[:, 1:] - before[:, :seq_count])
    my_start = lax.dynamic_index_in_dim(starts, seq_rank, 1, keepdims=False)
    my_length = lax.dynamic_index_in_dim(lengths, seq_rank, 1, keepdims=False)
    local_ids = seq_rank * sup_local + jnp.arange(sup_local, dtype=jnp.int32)
    kept_flag = jnp.any(keep_list[:, None, :] == local_ids[None, :, None], axis=2).astype(jnp.int32)
    offsets = jnp.arange(sup_local, dtype=jnp.int32)[None, :] + 3 * (
        jnp.cumsum(kept_flag, axis=1) - kept_flag
    )
    slot_ids = jnp.arange(slot_count, dtype=jnp.int32)
    owner_patch = (
        jnp.sum((offsets[:, None, :] <= slot_ids[None, :, None]).astype(jnp.int32), axis=2) - 1
    )
    start_of = jnp.take_along_axis(offsets, owner_patch, axis=1)
    sub_index = jnp.minimum(slot_ids[None, :] - start_of, 3)
    kept_of = jnp.take_along_axis(kept_flag, owner_patch, axis=1)
    flat_patches = patches.reshape(images, sup_local * 4, depth)
    fine_rows = flat_patches[
        image_index[:, None], owner_patch * 4 + jnp.where(kept_of == 1, sub_index, 0)
    ]
    mean_rows = jnp.mean(patches.astype(jnp.float32), axis=2).astype(jnp.bfloat16)
    shared_rows = mean_rows[image_index[:, None], owner_patch]
    local_tokens = jnp.where((kept_of == 1)[:, :, None], fine_rows, shared_rows)
    destinations = jnp.arange(seq_count, dtype=jnp.int32)[:, None, None]
    depth_slots = jnp.arange(capacity, dtype=jnp.int32)[None, None, :]
    positions = (destinations - my_start[None, :, None]) % seq_count + depth_slots * seq_count
    valid = positions < my_length[None, :, None]
    outgoing = local_tokens[image_index[None, :, None], jnp.minimum(positions, slot_count - 1)]
    outgoing = jnp.where(valid[:, :, :, None], outgoing, jnp.zeros((), jnp.bfloat16))
    incoming = lax.all_to_all(outgoing, "seq", split_axis=0, concat_axis=0, tiled=True)
    owned = jnp.arange(per_owner, dtype=jnp.int32) * seq_count + seq_rank
    source = jnp.sum((starts[:, None, :] <= owned[None, :, None]).astype(jnp.int32), axis=2) - 1
    first_of = jnp.take_along_axis(starts, source, axis=1)
    depth_of = (owned[None, :] - first_of) // seq_count
    resident = incoming[source, image_index[:, None], depth_of]
    start_rows = resident.reshape(images * per_owner, depth)
    start_float = start_rows.astype(jnp.float32)
    qkv_full, out_full, up_full, down_full = (
        lax.all_gather(qkv_weight, "seq", axis=0, tiled=True),
        lax.all_gather(out_weight, "seq", axis=1, tiled=True),
        lax.all_gather(up_weight, "seq", axis=0, tiled=True),
        lax.all_gather(down_weight, "seq", axis=1, tiled=True),
    )
    normed = layer_norm(start_float).astype(jnp.bfloat16).reshape(images, per_owner, depth)
    projected = jnp.einsum("ipd,dhc->ihpc", normed, qkv_full, preferred_element_type=jnp.float32)
    head_size = qkv_weight.shape[2] // 3
    sending = projected.astype(jnp.bfloat16).reshape(seq_count, per_owner, 3 * head_size)
    gathered = lax.all_to_all(sending, "seq", split_axis=0, concat_axis=0, tiled=True).reshape(
        seq_length, 3 * head_size
    )
    attended = attend(
        gathered[:, :head_size],
        gathered[:, head_size : 2 * head_size],
        gathered[:, 2 * head_size :],
    )
    returned = lax.all_to_all(
        attended.reshape(seq_count, per_owner, head_size),
        "seq",
        split_axis=0,
        concat_axis=0,
        tiled=True,
    )
    returned = returned.reshape(images, head_count, per_owner, head_size)
    partial_sum = jnp.einsum(
        "ihpc,hcd->ipd",
        returned,
        out_full.reshape(head_count, head_size, depth),
        preferred_element_type=jnp.float32,
    ).reshape(images * per_owner, depth)
    attn_total = lax.psum(partial_sum, "head")
    residual = start_float + attn_total
    residual_half = lax.dynamic_slice_in_dim(residual, head_rank * half_width, half_width, 1)
    normed_two = layer_norm(residual).astype(jnp.bfloat16)
    hidden = jax.nn.gelu(
        jnp.dot(normed_two, up_full, preferred_element_type=jnp.float32), approximate=False
    ).astype(jnp.bfloat16)
    mlp_terms = jnp.dot(hidden, down_full, preferred_element_type=jnp.float32)
    mlp_part = lax.psum_scatter(mlp_terms, "head", scatter_dimension=1, tiled=True)
    encoded = (residual_half + mlp_part).astype(jnp.bfloat16)
    return encoded.reshape(images, per_owner, 1, half_width)


def vspec():
    return pl.BlockSpec(memory_space=VMEM)


def aspec():
    return pl.BlockSpec(memory_space=pl.ANY)


def sspec():
    return pl.BlockSpec(memory_space=pltpu.SMEM)


def hspec():
    return pl.BlockSpec(memory_space=pltpu.HBM)


def run_copies(copies, sem, base=0):
    started = [
        pltpu.make_async_copy(src, dst, sem.at[base + i]) for i, (src, dst) in enumerate(copies)
    ]
    for copy in started:
        copy.start()

    def wait():
        for copy in started:
            copy.wait()

    return wait


def params(mebibytes=4):
    return pltpu.CompilerParams(vmem_limit_bytes=mebibytes * 1024 * 1024)


def cost(micros):
    return pl.CostEstimate(flops=micros * 10**9, bytes_accessed=1 << 20, transcendentals=0)


def struct(shape, dtype=BF16):
    return jax.ShapeDtypeStruct(shape, dtype)


def slot_of(index, n, capacity, cuts):
    device = sum(((index >= j * cuts * capacity).astype(jnp.int32) for j in range(1, n)), 0 * index)
    inner = index - device * (cuts * capacity)
    cut = sum(((inner >= c * capacity).astype(jnp.int32) for c in range(1, cuts)), 0 * index)
    return device, cut, inner - cut * capacity


def one_hot(mask):
    return mask.astype(F32).astype(BF16)


def prep_kernel(n, sup, capacity, rank_ref, keep_ref, patches_ref, out_ref):
    rank = rank_ref[0]
    first = rank * sup
    keep = keep_ref[...]
    rows = 4 * sup
    count = keep.shape[0]

    def places(width, shift):
        ids = lax.broadcasted_iota(jnp.int32, (count, width), 1) >> shift
        kept = jnp.sum((keep == first + ids).astype(jnp.int32), axis=0, keepdims=True)
        below = jnp.sum(
            jnp.logical_and(keep >= first, keep < first + ids).astype(jnp.int32),
            axis=0,
            keepdims=True,
        )
        return kept, below, lax.broadcasted_iota(jnp.int32, (1, width), 1)

    kept, below, lane = places(rows, 2)
    fine_pos = jnp.where(kept == 1, (lane >> 2) + 3 * below + (lane & 3), -1)
    kept, below, lane = places(sup, 0)
    mean_pos = jnp.where(kept == 1, -1, lane + 3 * below)
    start = first + 3 * jnp.sum((keep < first).astype(jnp.int32), axis=0, keepdims=True)
    flat = patches_ref[...]
    cuts = flat.shape[1] // 128
    sup_col = lax.broadcasted_iota(jnp.int32, (sup, rows), 0)
    sup_lane = lax.broadcasted_iota(jnp.int32, (sup, rows), 1) >> 2
    averaging = jnp.where(sup_col == sup_lane, 0.25, 0.0).astype(BF16)
    means = jnp.dot(averaging, flat, preferred_element_type=F32).astype(BF16)
    index = lax.broadcasted_iota(jnp.int32, (n * cuts * capacity, 1), 0)
    device, cut, slot = slot_of(index, n, capacity, cuts)
    pos = ((device - start) & (n - 1)) + slot * n
    total = jnp.zeros((n * cuts * capacity, 128), F32)
    for c in range(cuts):
        at = jnp.where(cut == c, pos, -2)
        features = slice(c * 128, (c + 1) * 128)
        total = (
            total
            + jnp.dot(one_hot(at == fine_pos), flat[:, features], preferred_element_type=F32)
            + jnp.dot(one_hot(at == mean_pos), means[:, features], preferred_element_type=F32)
        )
    out_ref[...] = total.astype(BF16)


def prep(scalars, keep_col, flat, n, sup, capacity):
    width = flat.shape[1] // 2
    shape = (n * capacity * width // 128, 128)
    return pl.pallas_call(
        functools.partial(prep_kernel, n, sup, capacity),
        grid_spec=pltpu.PrefetchScalarGridSpec(
            num_scalar_prefetch=1,
            grid=(1,),
            in_specs=[
                pl.BlockSpec(keep_col.shape, lambda i, ref: (0, 0)),
                pl.BlockSpec((flat.shape[0], width), lambda i, ref: (0, ref[1])),
            ],
            out_specs=pl.BlockSpec(shape, lambda i, ref: (0, 0)),
        ),
        out_shape=struct(shape),
        compiler_params=params(),
    )(scalars, keep_col, flat)


def pick_kernel(n, sup, per_owner, capacity, rank_ref, keep_ref, got_ref, out_ref):
    rank = rank_ref[0]
    keep = keep_ref[...]
    count = keep.shape[0]
    lanes = got_ref.shape[0]
    cuts = lanes // (n * capacity)
    source, _, _ = slot_of(
        lax.broadcasted_iota(jnp.int32, (count, lanes), 1), n, capacity, cuts
    )
    low = jnp.sum((keep < source * sup).astype(jnp.int32), axis=0, keepdims=True)
    high = jnp.sum((keep < source * sup + sup).astype(jnp.int32), axis=0, keepdims=True)
    source, cut, slot = slot_of(
        lax.broadcasted_iota(jnp.int32, (1, lanes), 1), n, capacity, cuts
    )
    start = source * sup + 3 * low
    stop = source * sup + sup + 3 * high
    token = start + ((rank - start) & (n - 1)) + slot * n
    row = jnp.where(token < stop, token >> (n.bit_length() - 1), -1)
    own = lax.broadcasted_iota(jnp.int32, (per_owner, lanes), 0)
    got = got_ref[...]
    for c in range(cuts):
        choose = one_hot(own == jnp.where(cut == c, row, -1))
        owned = jnp.dot(choose, got, preferred_element_type=F32).astype(BF16)
        out_ref[c * per_owner : (c + 1) * per_owner] = owned


def pick(scalars, keep_col, got, n, sup, per_owner, capacity):
    cuts = got.shape[0] // (n * capacity)
    return pl.pallas_call(
        functools.partial(pick_kernel, n, sup, per_owner, capacity),
        in_specs=[sspec(), vspec(), vspec()],
        out_specs=vspec(),
        out_shape=struct((cuts * per_owner, 128)),
        compiler_params=params(),
    )(scalars, keep_col, got)


def pack_kernel(n, rank_ref, qkv_ref, out_weight_ref, up_ref, down_ref, *refs):
    near, (heads_ref, away_ref, blocks_ref, sem) = refs[: n // 2], refs[n // 2 :]
    rank, part = rank_ref[0], rank_ref[2]
    half = n // 2
    rows = up_ref.shape[0]
    wide = up_ref.shape[1] // n
    units = wide // 2
    long = out_weight_ref.shape[0]
    depth = qkv_ref.shape[1] // 2
    copies = []
    for d in range(half):
        dest = (rank // half ^ 1) * half + d
        at = pl.ds(pl.multiple_of(part * depth, 32), depth)
        copies.append((qkv_ref.at[dest, at], away_ref.at[pl.ds(d * depth, depth)]))
        at = pl.ds(pl.multiple_of(dest * wide + part * units, 128), units)
        copies.append((up_ref.at[:, at], blocks_ref.at[d, pl.ds(0, rows)]))
        copies.append((down_ref.at[at], blocks_ref.at[d, pl.ds(rows, units)]))
    at = pl.ds(pl.multiple_of(part * (long // 2), 128), long // 2)
    copies.append((out_weight_ref.at[at], away_ref.at[pl.ds(half * depth, long // 2)]))
    copies.append((qkv_ref.at[pl.ds(rank // half * half, half)], heads_ref))
    for j in range(half):
        dest = rank ^ j
        for c in range(2):
            at = pl.ds(pl.multiple_of(dest * wide + c * units, 128), units)
            copies.append((up_ref.at[:, at], near[j].at[pl.ds(c * rows, rows)]))
        at = pl.ds(pl.multiple_of(dest * wide, 128), wide)
        copies.append((down_ref.at[at], near[j].at[pl.ds(2 * rows, wide)]))
        copies.append((out_weight_ref, near[j].at[pl.ds(2 * rows + wide, long)]))
    run_copies(copies, sem)()


def pack(scalars, qkv, out_weight, up, down, n):
    half = n // 2
    wide = up.shape[1] // n
    near = struct((2 * up.shape[0] + wide + out_weight.shape[0], 128))
    away = struct((half * qkv.shape[1] // 2 + out_weight.shape[0] // 2, 128))
    blocks = struct((half, up.shape[0] + wide // 2, 128))
    outs = pl.pallas_call(
        functools.partial(pack_kernel, n),
        in_specs=[sspec()] + [hspec()] * 4,
        out_specs=[aspec()] * (half + 3),
        out_shape=[near] * half + [struct((half,) + qkv.shape[1:]), away, blocks],
        scratch_shapes=[pltpu.SemaphoreType.DMA((7 * half + 2,))],
        compiler_params=params(48),
    )(scalars, qkv, out_weight, up, down)
    return list(outs[:half]), *outs[half:]


def fan_kernel(owned_ref, across_ref, heads_ref, far_ref, blocks_ref, out_ref):
    rows = owned_ref.shape[0]
    count, head_rows = heads_ref.shape[:2]
    piece = head_rows // 2
    units = blocks_ref.shape[1]
    for d in range(count):
        parts = (
            owned_ref[...],
            across_ref[...],
            heads_ref[d],
            far_ref[d * piece : (d + 1) * piece],
            blocks_ref[d],
            far_ref[count * piece :],
        )
        low = 0
        for part in parts:
            out_ref[d, low : low + part.shape[0]] = part
            low += part.shape[0]


def fan(owned, across, heads, far, blocks):
    count = heads.shape[0]
    out_rows = far.shape[0] - count * heads.shape[1] // 2
    rows = 2 * owned.shape[0] + 3 * heads.shape[1] // 2 + blocks.shape[1] + out_rows
    return pl.pallas_call(
        fan_kernel,
        in_specs=[vspec()] * 5,
        out_specs=vspec(),
        out_shape=struct((count, rows, 128)),
        compiler_params=params(8),
    )(owned, across, heads, far, blocks)


def source_of(rank, n, q, k):
    return (rank // (n // 2) ^ k) * (n // 2) + q


def norm_rows(x):
    average = jnp.mean(x, axis=-1, keepdims=True)
    power = jnp.mean(x * x, axis=-1, keepdims=True)
    return (x - average) * lax.rsqrt(power - average * average + 1e-06)


def attend_kernel(n, part, rank_ref, mine_ref, other_ref, far_ref, tokens_ref, out_ref, weight_ref):
    rank, half, group = rank_ref[0], rank_ref[1], rank_ref[2]
    rows = other_ref.shape[1] // 2
    cuts = rows // part
    width = cuts * 128
    depth = weight_ref.shape[0]
    piece = far_ref.shape[1]
    for q in range(n // 2):
        for k in range(2):
            source = source_of(rank, n, q, k)
            at = pl.ds(pl.multiple_of(source * part, part), part)
            for c in range(cuts):
                cut = slice(k * rows + c * part, k * rows + (c + 1) * part)
                to = pl.ds(pl.multiple_of(half * width + c * 128, 128), 128)
                tokens_ref[at, to] = mine_ref[q, cut]
                to = pl.ds(pl.multiple_of((1 - half) * width + c * 128, 128), 128)
                tokens_ref[at, to] = other_ref[q, cut]
        to = pl.ds(pl.multiple_of(source_of(rank, n, q, 0) * 128, 128), 128)
        weight_ref[:, to] = mine_ref[q, 2 * rows : 2 * rows + depth]
        to = pl.ds(pl.multiple_of(source_of(rank, n, q, 1) * 128, 128), 128)
        at = pl.ds(pl.multiple_of(group * piece, 32), piece)
        weight_ref[at, to] = mine_ref[q, 2 * rows + depth : 2 * rows + depth + piece]
        at = pl.ds(pl.multiple_of((1 - group) * piece, 32), piece)
        weight_ref[at, to] = far_ref[q]
    normed = norm_rows(tokens_ref[...].astype(F32)).astype(BF16)
    projected = lax.dot_general(
        normed, weight_ref[...], (((1,), (1,)), ((), ())), preferred_element_type=F32
    ).astype(BF16)
    size = projected.shape[1] // 3
    queries = projected[:, :size]
    keys = projected[:, size : 2 * size]
    values = projected[:, 2 * size :]
    scores = lax.dot_general(
        queries, keys, (((1,), (1,)), ((), ())), preferred_element_type=F32
    ) * (1.0 / math.sqrt(size))
    powers = jnp.exp(scores - jnp.max(scores, axis=1, keepdims=True))
    probs = (powers / jnp.sum(powers, axis=1, keepdims=True)).astype(BF16)
    attended = lax.dot_general(
        values, probs, (((0,), (1,)), ((), ())), preferred_element_type=F32
    ).astype(BF16)
    out_ref[...] = attended


def attend_fast(scalars, mine, other, far, head_rows, per_owner, n):
    length = n * per_owner
    depth = other.shape[1] // (2 * per_owner) * 256
    size = head_rows // 3
    return pl.pallas_call(
        functools.partial(attend_kernel, n, per_owner),
        in_specs=[sspec()] + [vspec()] * 3,
        out_specs=[vspec()] * 2,
        out_shape=[struct((length, depth)), struct((size, length))],
        scratch_shapes=[VMEM((head_rows, n * 128), BF16)],
        compiler_params=params(12),
        cost_estimate=cost(30),
    )(scalars, mine, other, far)


def mlp_kernel(n, rank_ref, tokens_ref, pieces, far, outs_far, near, outs_near, outs, scratch):
    residual_ref, keep_ref, send_ref = outs
    up_ref, down_ref, row_ref, whole_ref, joined_ref, sem = scratch
    rank, half, group = rank_ref[0], rank_ref[1], rank_ref[2]
    block = up_ref.shape[0] // n
    wide = down_ref.shape[0]
    unit = wide // 2
    size = pieces[0].shape[2]
    rows = outs_far[0][0].shape[1]
    first, later = [], []
    for j in range(n // 2):
        source = rank ^ j
        at = pl.ds(pl.multiple_of(source * block, block), block)
        to = pl.ds(pl.multiple_of(source * 128, 128), 128)
        for c in range(2):
            later.append(
                (near[j].at[pl.ds(c * block, block)], up_ref.at[at, pl.ds(c * unit, unit)])
            )
        later.append((near[j].at[pl.ds(2 * block, wide)], down_ref.at[:, to]))
        for core in range(2):
            rows_from = outs_near[core][j].at[pl.ds(2 * block + wide, 2 * rows)]
            first.append((rows_from, whole_ref.at[core, :, to]))
        source = source_of(rank, n, j, 1)
        at = pl.ds(pl.multiple_of(source * block, block), block)
        to = pl.ds(pl.multiple_of(source * 128, 128), 128)
        for c in range(2):
            units = pl.ds(pl.multiple_of((group ^ c) * unit, unit), unit)
            later.append((far[c].at[j, pl.ds(0, block)], up_ref.at[at, units]))
            later.append((far[c].at[j, pl.ds(block, unit)], down_ref.at[units, to]))
        for core in range(2):
            for c in range(2):
                at = pl.ds(pl.multiple_of((group ^ c) * rows, rows), rows)
                first.append((outs_far[core][c].at[j], whole_ref.at[core, at, to]))
    wait_first = run_copies(first, sem)
    wait_later = run_copies(later, sem, len(first))
    for j in range(n // 2):
        for core in range(2):
            for k in range(2):
                at = pl.ds(pl.multiple_of((rank ^ j ^ (k * n // 2)) * size, size), size)
                joined_ref[core, at] = pieces[core][j, k]
    wait_first()
    dims = (((0,), (0,)), ((), ()))
    row_ref[...] = (
        tokens_ref[...].astype(F32)
        + lax.dot_general(joined_ref[0], whole_ref[0], dims, preferred_element_type=F32)
        + lax.dot_general(joined_ref[1], whole_ref[1], dims, preferred_element_type=F32)
    )
    part = residual_ref.shape[0]
    width = residual_ref.shape[1]
    my_cols = pl.ds(pl.multiple_of(half * width, width), width)
    other_cols = pl.ds(pl.multiple_of((1 - half) * width, width), width)
    residual_ref[...] = row_ref[pl.ds(pl.multiple_of(rank * part, part), part), my_cols]
    normed = norm_rows(row_ref[...]).astype(BF16)
    wait_later()
    raw = jnp.dot(normed, up_ref[...], preferred_element_type=F32)
    hidden = (0.5 * raw * (1.0 + lax.erf(raw * math.sqrt(0.5)))).astype(BF16)
    keep_ref[...] = jnp.dot(hidden, down_ref[:, my_cols], preferred_element_type=F32)
    send_ref[...] = jnp.dot(hidden, down_ref[:, other_cols], preferred_element_type=F32).astype(BF16)


def mlp(scalars, tokens, pieces, far, outs_far, near, near_other, n):
    length, depth = tokens.shape
    width = depth // 2
    wide = 2 * (far[0].shape[1] - depth // n)
    inner = n * pieces[0].shape[2]
    half = n // 2

    def kernel(scalars, tokens, a, b, c, d, e, f, g, h, *refs):
        near, other = refs[:half], refs[half : 2 * half]
        outs, scratch = refs[2 * half : 2 * half + 3], refs[2 * half + 3 :]
        far, outs_far, outs_near = (c, d), ((e, f), (g, h)), (near, other)
        mlp_kernel(n, scalars, tokens, (a, b), far, outs_far, near, outs_near, outs, scratch)

    return pl.pallas_call(
        kernel,
        in_specs=[sspec()] + [vspec()] * 3 + [aspec()] * (6 + 2 * half),
        out_specs=[vspec()] * 3,
        out_shape=[
            struct((length // n, width), F32),
            struct((length, width), F32),
            struct((length, width)),
        ],
        scratch_shapes=[
            VMEM((depth, wide), BF16),
            VMEM((wide, depth), BF16),
            VMEM((length, depth), F32),
            VMEM((2, inner, depth), BF16),
            VMEM((2, inner, length), BF16),
            pltpu.SemaphoreType.DMA((13 * half,)),
        ],
        compiler_params=params(20),
    )(scalars, tokens, *pieces, *far, *outs_far[0], *outs_far[1], *near, *near_other)


def join_kernel(rank_ref, keep_ref, got_ref, residual_ref, base_ref, out_ref):
    part = residual_ref.shape[0]
    mine = pl.ds(pl.multiple_of(rank_ref[0] * part, part), part)
    base_ref[...] = keep_ref[mine] + got_ref[mine].astype(F32) + residual_ref[...]
    out_ref[...] = (keep_ref[...] + got_ref[...].astype(F32)).astype(BF16)


def join(scalars, keep, got, residual):
    return pl.pallas_call(
        join_kernel,
        in_specs=[sspec()] + [vspec()] * 3,
        out_specs=[vspec()] * 2,
        out_shape=[struct(residual.shape, F32), struct(keep.shape)],
        compiler_params=params(8),
    )(scalars, keep, got, residual)


def last_kernel(n, rank_ref, base_ref, terms_ref, out_ref):
    rank = rank_ref[0]
    total = base_ref[...]
    for j in range(1, n):
        total = total + terms_ref[rank ^ j].astype(F32)
    out_ref[...] = total.astype(BF16)


def last(scalars, base, terms):
    return pl.pallas_call(
        functools.partial(last_kernel, terms.shape[0]),
        in_specs=[sspec()] + [vspec()] * 2,
        out_specs=vspec(),
        out_shape=struct(base.shape),
        compiler_params=params(8),
    )(scalars, base, terms)


def swap(value, axis, j):
    n = lax.axis_size(axis)
    return lax.ppermute(value, axis, [(i, i ^ j) for i in range(n)])


def exchange(value):
    return lax.all_to_all(value, "seq", split_axis=0, concat_axis=0, tiled=True)


def exchange_half(value):
    n = lax.axis_size("seq")
    groups = [list(range(n // 2)), list(range(n // 2, n))]
    return lax.all_to_all(
        value, "seq", split_axis=0, concat_axis=0, axis_index_groups=groups, tiled=True
    )


def after(value, *others):
    return lax.optimization_barrier((value, *others))[0]


def local_fast(patches, keep_list, qkv_weight, out_weight, up_weight, down_weight):
    n = lax.axis_size("seq")
    rank, head, group = (
        lax.axis_index(name).astype(jnp.int32) for name in ("seq", "head", "groups")
    )
    scalars = jnp.stack([rank, head, group])
    half = n // 2
    sup, depth = patches.shape[1], patches.shape[3]
    length = sup * n * 8 // 5
    per_owner = length // n
    half_width = depth // 2
    head_rows = qkv_weight.shape[2]
    capacity = (4 * sup + n - 1) // n
    keep_col = keep_list.reshape(-1, 1)
    flat = patches.reshape(4 * sup, depth)
    heads = qkv_weight.transpose(1, 2, 0)

    near, qkv_near, away, blocks = pack(scalars, heads, out_weight, up_weight, down_weight, n)
    far = swap(away, "seq", half)
    slots = prep(scalars, keep_col, after(flat, away), n, sup, capacity)
    dealt = exchange(slots)
    blocks, *near = lax.optimization_barrier((blocks, *near, slots))[:-1]
    mlp_far = swap(blocks, "seq", half)
    near = [near[0]] + [swap(near[j], "seq", j) for j in range(1, half)]
    owned = pick(scalars, keep_col, dealt, n, sup, per_owner, capacity)
    across = swap(owned, "seq", half)
    across, far, mlp_far, *near = lax.optimization_barrier((across, far, mlp_far, *near))

    out_rows = out_weight.shape[0] // 2
    got = exchange_half(fan(owned, across, qkv_near, far, mlp_far))
    near_other = [swap(block, "head", 1) for block in near]
    got, *near_other = lax.optimization_barrier((got, *near_other))

    top = 2 * owned.shape[0]
    pieces_other = swap(got[:, :top], "head", 1)
    top = top + head_rows
    qkv_far = swap(got[:, top : top + head_rows // 2], "groups", 1)
    tokens, attended = attend_fast(
        scalars, got, pieces_other, qkv_far, head_rows, per_owner, n
    )

    att_across = swap(attended, "seq", half)
    got = after(got, attended)
    mlp_mine = got[:, top + head_rows // 2 : got.shape[1] - out_rows]
    far_mine = got[:, got.shape[1] - out_rows :]
    far_other = swap(far_mine, "groups", 1)
    mlp_other = swap(mlp_mine, "groups", 1)
    pair = jnp.stack([attended, att_across])
    pairs = [swap(pair, "seq", j) for j in range(1, half)]
    mlp_other, far_other, *pairs = lax.optimization_barrier((mlp_other, far_other, *pairs))
    gathered = jnp.stack([pair] + pairs)
    residual, keep, send = mlp(
        scalars,
        tokens,
        (gathered, swap(gathered, "head", 1)),
        (mlp_mine, mlp_other),
        ((far_mine, far_other), (swap(far_mine, "head", 1), swap(far_other, "head", 1))),
        near,
        near_other,
        n,
    )
    sent = swap(send, "head", 1)
    base, terms = join(scalars, keep, sent, residual)
    terms = exchange(terms.reshape(n, per_owner, half_width))
    encoded = last(scalars, base, terms)
    return encoded.reshape(1, per_owner, 1, half_width)


def local(patches, keep_list, qkv_weight, out_weight, up_weight, down_weight):
    n = lax.axis_size("seq")
    one_image = patches.shape[0] == 1 and qkv_weight.shape[1] == n and n & (n - 1) == 0
    one_image = one_image and lax.axis_size("groups") == 2 and up_weight.shape[1] == n * 256
    plan = local_fast if one_image else local_general
    return plan(patches, keep_list, qkv_weight, out_weight, up_weight, down_weight)


def solution(mesh):
    return jax.shard_map(
        local,
        mesh=mesh,
        in_specs=(
            P("groups", "seq", None, None),
            P("groups", None),
            P("seq", "head", None),
            P("head", "seq"),
            P("seq", "head"),
            P("head", "seq"),
        ),
        out_specs=P("groups", None, "seq", "head"),
        check_vma=False,
    )
```

```python
import functools
import math

import jax
import jax.numpy as jnp
from jax import lax
from jax.experimental import pallas as pl
from jax.experimental.pallas import tpu as pltpu
from jax.sharding import PartitionSpec as P

F32 = jnp.float32
BF16 = jnp.bfloat16
VMEM = pltpu.VMEM

def layer_norm(matrix):
    average = jnp.mean(matrix, axis=-1, keepdims=True)
    power = jnp.mean(matrix * matrix, axis=-1, keepdims=True)
    return (matrix - average) * lax.rsqrt(power - average * average + 1e-06)


def attend(queries, keys, values):
    length = queries.shape[0]
    block = math.gcd(length, 512)
    scale = 1.0 / math.sqrt(queries.shape[1])

    def one_block(query_rows):
        scores = (
            lax.dot_general(
                query_rows, keys, (((1,), (1,)), ((), ())), preferred_element_type=jnp.float32
            )
            * scale
        )
        top = jnp.max(scores, axis=1, keepdims=True)
        powers = jnp.exp(scores - top)
        probs = (powers / jnp.sum(powers, axis=1, keepdims=True)).astype(jnp.bfloat16)
        return jnp.dot(probs, values, preferred_element_type=jnp.float32).astype(jnp.bfloat16)

    blocks = lax.map(one_block, queries.reshape(length // block, block, queries.shape[1]))
    return blocks.reshape(length, values.shape[1])


def local_general(patches, keep_list, qkv_weight, out_weight, up_weight, down_weight):
    seq_count = lax.axis_size("seq")
    seq_rank = lax.axis_index("seq")
    head_rank = lax.axis_index("head")
    images = patches.shape[0]
    sup_local = patches.shape[1]
    depth = patches.shape[3]
    half_width = depth // lax.axis_size("head")
    head_count = qkv_weight.shape[1]
    seq_length = sup_local * seq_count * 8 // 5
    per_owner = seq_length // seq_count
    capacity = (4 * sup_local + seq_count - 1) // seq_count
    slot_count = 4 * sup_local
    image_index = jnp.arange(images, dtype=jnp.int32)
    bounds = jnp.arange(seq_count + 1, dtype=jnp.int32) * sup_local
    before = jnp.sum((keep_list[:, :, None] < bounds[None, None, :]).astype(jnp.int32), axis=1)
    starts = bounds[None, :seq_count] + 3 * before[:, :seq_count]
    lengths = sup_local + 3 * (before[:, 1:] - before[:, :seq_count])
    my_start = lax.dynamic_index_in_dim(starts, seq_rank, 1, keepdims=False)
    my_length = lax.dynamic_index_in_dim(lengths, seq_rank, 1, keepdims=False)
    local_ids = seq_rank * sup_local + jnp.arange(sup_local, dtype=jnp.int32)
    kept_flag = jnp.any(keep_list[:, None, :] == local_ids[None, :, None], axis=2).astype(jnp.int32)
    offsets = jnp.arange(sup_local, dtype=jnp.int32)[None, :] + 3 * (
        jnp.cumsum(kept_flag, axis=1) - kept_flag
    )
    slot_ids = jnp.arange(slot_count, dtype=jnp.int32)
    owner_patch = (
        jnp.sum((offsets[:, None, :] <= slot_ids[None, :, None]).astype(jnp.int32), axis=2) - 1
    )
    start_of = jnp.take_along_axis(offsets, owner_patch, axis=1)
    sub_index = jnp.minimum(slot_ids[None, :] - start_of, 3)
    kept_of = jnp.take_along_axis(kept_flag, owner_patch, axis=1)
    flat_patches = patches.reshape(images, sup_local * 4, depth)
    fine_rows = flat_patches[
        image_index[:, None], owner_patch * 4 + jnp.where(kept_of == 1, sub_index, 0)
    ]
    mean_rows = jnp.mean(patches.astype(jnp.float32), axis=2).astype(jnp.bfloat16)
    shared_rows = mean_rows[image_index[:, None], owner_patch]
    local_tokens = jnp.where((kept_of == 1)[:, :, None], fine_rows, shared_rows)
    destinations = jnp.arange(seq_count, dtype=jnp.int32)[:, None, None]
    depth_slots = jnp.arange(capacity, dtype=jnp.int32)[None, None, :]
    positions = (destinations - my_start[None, :, None]) % seq_count + depth_slots * seq_count
    valid = positions < my_length[None, :, None]
    outgoing = local_tokens[image_index[None, :, None], jnp.minimum(positions, slot_count - 1)]
    outgoing = jnp.where(valid[:, :, :, None], outgoing, jnp.zeros((), jnp.bfloat16))
    incoming = lax.all_to_all(outgoing, "seq", split_axis=0, concat_axis=0, tiled=True)
    owned = jnp.arange(per_owner, dtype=jnp.int32) * seq_count + seq_rank
    source = jnp.sum((starts[:, None, :] <= owned[None, :, None]).astype(jnp.int32), axis=2) - 1
    first_of = jnp.take_along_axis(starts, source, axis=1)
    depth_of = (owned[None, :] - first_of) // seq_count
    resident = incoming[source, image_index[:, None], depth_of]
    start_rows = resident.reshape(images * per_owner, depth)
    start_float = start_rows.astype(jnp.float32)
    qkv_full, out_full, up_full, down_full = (
        lax.all_gather(qkv_weight, "seq", axis=0, tiled=True),
        lax.all_gather(out_weight, "seq", axis=1, tiled=True),
        lax.all_gather(up_weight, "seq", axis=0, tiled=True),
        lax.all_gather(down_weight, "seq", axis=1, tiled=True),
    )
    normed = layer_norm(start_float).astype(jnp.bfloat16).reshape(images, per_owner, depth)
    projected = jnp.einsum("ipd,dhc->ihpc", normed, qkv_full, preferred_element_type=jnp.float32)
    head_size = qkv_weight.shape[2] // 3
    sending = projected.astype(jnp.bfloat16).reshape(seq_count, per_owner, 3 * head_size)
    gathered = lax.all_to_all(sending, "seq", split_axis=0, concat_axis=0, tiled=True).reshape(
        seq_length, 3 * head_size
    )
    attended = attend(
        gathered[:, :head_size],
        gathered[:, head_size : 2 * head_size],
        gathered[:, 2 * head_size :],
    )
    returned = lax.all_to_all(
        attended.reshape(seq_count, per_owner, head_size),
        "seq",
        split_axis=0,
        concat_axis=0,
        tiled=True,
    )
    returned = returned.reshape(images, head_count, per_owner, head_size)
    partial_sum = jnp.einsum(
        "ihpc,hcd->ipd",
        returned,
        out_full.reshape(head_count, head_size, depth),
        preferred_element_type=jnp.float32,
    ).reshape(images * per_owner, depth)
    attn_total = lax.psum(partial_sum, "head")
    residual = start_float + attn_total
    residual_half = lax.dynamic_slice_in_dim(residual, head_rank * half_width, half_width, 1)
    normed_two = layer_norm(residual).astype(jnp.bfloat16)
    hidden = jax.nn.gelu(
        jnp.dot(normed_two, up_full, preferred_element_type=jnp.float32), approximate=False
    ).astype(jnp.bfloat16)
    mlp_terms = jnp.dot(hidden, down_full, preferred_element_type=jnp.float32)
    mlp_part = lax.psum_scatter(mlp_terms, "head", scatter_dimension=1, tiled=True)
    encoded = (residual_half + mlp_part).astype(jnp.bfloat16)
    return encoded.reshape(images, per_owner, 1, half_width)


def vspec():
    return pl.BlockSpec(memory_space=VMEM)


def aspec():
    return pl.BlockSpec(memory_space=pl.ANY)


def sspec():
    return pl.BlockSpec(memory_space=pltpu.SMEM)


def hspec():
    return pl.BlockSpec(memory_space=pltpu.HBM)


def run_copies(copies, sem, base=0):
    started = [
        pltpu.make_async_copy(src, dst, sem.at[base + i]) for i, (src, dst) in enumerate(copies)
    ]
    for copy in started:
        copy.start()

    def wait():
        for copy in started:
            copy.wait()

    return wait


def params(mebibytes=4):
    return pltpu.CompilerParams(vmem_limit_bytes=mebibytes * 1024 * 1024)


def cost(micros):
    return pl.CostEstimate(flops=micros * 10**9, bytes_accessed=1 << 20, transcendentals=0)


def struct(shape, dtype=BF16):
    return jax.ShapeDtypeStruct(shape, dtype)


def slot_of(index, n, capacity, cuts):
    device = sum(((index >= j * cuts * capacity).astype(jnp.int32) for j in range(1, n)), 0 * index)
    inner = index - device * (cuts * capacity)
    cut = sum(((inner >= c * capacity).astype(jnp.int32) for c in range(1, cuts)), 0 * index)
    return device, cut, inner - cut * capacity


def as_column(row):
    count = row.shape[1]
    same = lax.broadcasted_iota(jnp.int32, (count, count), 0) == lax.broadcasted_iota(
        jnp.int32, (count, count), 1
    )
    return jnp.sum(jnp.where(same, row, 0), axis=1, keepdims=True)


def one_hot(mask):
    return mask.astype(F32).astype(BF16)


def prep_kernel(n, sup, capacity, rank_ref, keep_ref, patches_ref, out_ref):
    rank = rank_ref[0]
    first = rank * sup
    keep = as_column(keep_ref[...])
    rows = 4 * sup
    count = keep.shape[0]

    def places(width, shift):
        ids = lax.broadcasted_iota(jnp.int32, (count, width), 1) >> shift
        kept = jnp.sum((keep == first + ids).astype(jnp.int32), axis=0, keepdims=True)
        below = jnp.sum(
            jnp.logical_and(keep >= first, keep < first + ids).astype(jnp.int32),
            axis=0,
            keepdims=True,
        )
        return kept, below, lax.broadcasted_iota(jnp.int32, (1, width), 1)

    kept, below, lane = places(rows, 2)
    fine_pos = jnp.where(kept == 1, (lane >> 2) + 3 * below + (lane & 3), -1)
    kept, below, lane = places(sup, 0)
    mean_pos = jnp.where(kept == 1, -1, lane + 3 * below)
    start = first + 3 * jnp.sum((keep < first).astype(jnp.int32), axis=0, keepdims=True)
    flat = patches_ref[...]
    cuts = flat.shape[1] // 128
    sup_col = lax.broadcasted_iota(jnp.int32, (sup, rows), 0)
    sup_lane = lax.broadcasted_iota(jnp.int32, (sup, rows), 1) >> 2
    averaging = jnp.where(sup_col == sup_lane, 0.25, 0.0).astype(BF16)
    means = jnp.dot(averaging, flat, preferred_element_type=F32).astype(BF16)
    index = lax.broadcasted_iota(jnp.int32, (n * cuts * capacity, 1), 0)
    device, cut, slot = slot_of(index, n, capacity, cuts)
    pos = ((device - start) & (n - 1)) + slot * n
    total = jnp.zeros((n * cuts * capacity, 128), F32)
    for c in range(cuts):
        at = jnp.where(cut == c, pos, -2)
        features = slice(c * 128, (c + 1) * 128)
        total = (
            total
            + jnp.dot(one_hot(at == fine_pos), flat[:, features], preferred_element_type=F32)
            + jnp.dot(one_hot(at == mean_pos), means[:, features], preferred_element_type=F32)
        )
    out_ref[...] = total.astype(BF16)


def prep(scalars, keep_list, flat, n, sup, capacity):
    width = flat.shape[1] // 2
    shape = (n * capacity * width // 128, 128)
    return pl.pallas_call(
        functools.partial(prep_kernel, n, sup, capacity),
        grid_spec=pltpu.PrefetchScalarGridSpec(
            num_scalar_prefetch=1,
            grid=(1,),
            in_specs=[
                pl.BlockSpec(keep_list.shape, lambda i, ref: (0, 0)),
                pl.BlockSpec((flat.shape[0], width), lambda i, ref: (0, ref[1])),
            ],
            out_specs=pl.BlockSpec(shape, lambda i, ref: (0, 0)),
        ),
        out_shape=struct(shape),
        compiler_params=params(),
    )(scalars, keep_list, flat)


def pick_kernel(n, sup, per_owner, capacity, rank_ref, keep_ref, got_ref, out_ref):
    rank = rank_ref[0]
    keep = as_column(keep_ref[...])
    count = keep.shape[0]
    lanes = got_ref.shape[0]
    cuts = lanes // (n * capacity)
    source, _, _ = slot_of(
        lax.broadcasted_iota(jnp.int32, (count, lanes), 1), n, capacity, cuts
    )
    low = jnp.sum((keep < source * sup).astype(jnp.int32), axis=0, keepdims=True)
    high = jnp.sum((keep < source * sup + sup).astype(jnp.int32), axis=0, keepdims=True)
    source, cut, slot = slot_of(
        lax.broadcasted_iota(jnp.int32, (1, lanes), 1), n, capacity, cuts
    )
    start = source * sup + 3 * low
    stop = source * sup + sup + 3 * high
    token = start + ((rank - start) & (n - 1)) + slot * n
    row = jnp.where(token < stop, token >> (n.bit_length() - 1), -1)
    own = lax.broadcasted_iota(jnp.int32, (per_owner, lanes), 0)
    got = got_ref[...]
    for c in range(cuts):
        choose = one_hot(own == jnp.where(cut == c, row, -1))
        owned = jnp.dot(choose, got, preferred_element_type=F32).astype(BF16)
        out_ref[c * per_owner : (c + 1) * per_owner] = owned


def pick(scalars, keep_list, got, n, sup, per_owner, capacity):
    cuts = got.shape[0] // (n * capacity)
    return pl.pallas_call(
        functools.partial(pick_kernel, n, sup, per_owner, capacity),
        in_specs=[sspec(), vspec(), vspec()],
        out_specs=vspec(),
        out_shape=struct((cuts * per_owner, 128)),
        compiler_params=params(),
    )(scalars, keep_list, got)


def pack_kernel(n, rank_ref, qkv_ref, out_weight_ref, up_ref, down_ref, *refs):
    near, (heads_ref, away_ref, sem) = refs[: n // 2], refs[n // 2 :]
    rank, part = rank_ref[0], rank_ref[2]
    half = n // 2
    rows = up_ref.shape[0]
    wide = up_ref.shape[1] // n
    units = wide // 2
    long = out_weight_ref.shape[0]
    depth = qkv_ref.shape[1] // 2
    each = depth + rows + units
    copies = []
    for d in range(half):
        dest = (rank // half ^ 1) * half + d
        low = d * each
        at = pl.ds(pl.multiple_of(part * depth, 32), depth)
        copies.append((qkv_ref.at[dest, at], away_ref.at[pl.ds(low, depth)]))
        at = pl.ds(pl.multiple_of(dest * wide + part * units, 128), units)
        copies.append((up_ref.at[:, at], away_ref.at[pl.ds(low + depth, rows)]))
        copies.append((down_ref.at[at], away_ref.at[pl.ds(low + depth + rows, units)]))
    at = pl.ds(pl.multiple_of(part * (long // 2), 128), long // 2)
    copies.append((out_weight_ref.at[at], away_ref.at[pl.ds(half * each, long // 2)]))
    copies.append((qkv_ref.at[pl.ds(rank // half * half, half)], heads_ref))
    for j in range(half):
        dest = rank ^ j
        for c in range(2):
            at = pl.ds(pl.multiple_of(dest * wide + c * units, 128), units)
            copies.append((up_ref.at[:, at], near[j].at[pl.ds(c * rows, rows)]))
        at = pl.ds(pl.multiple_of(dest * wide, 128), wide)
        copies.append((down_ref.at[at], near[j].at[pl.ds(2 * rows, wide)]))
        copies.append((out_weight_ref, near[j].at[pl.ds(2 * rows + wide, long)]))
    run_copies(copies, sem)()


def pack(scalars, qkv, out_weight, up, down, n):
    half = n // 2
    wide = up.shape[1] // n
    near = struct((2 * up.shape[0] + wide + out_weight.shape[0], 128))
    each = qkv.shape[1] // 2 + up.shape[0] + wide // 2
    away = struct((half * each + out_weight.shape[0] // 2, 128))
    outs = pl.pallas_call(
        functools.partial(pack_kernel, n),
        in_specs=[sspec()] + [hspec()] * 4,
        out_specs=[aspec()] * (half + 2),
        out_shape=[near] * half + [struct((half,) + qkv.shape[1:]), away],
        scratch_shapes=[pltpu.SemaphoreType.DMA((7 * half + 2,))],
        compiler_params=params(),
    )(scalars, qkv, out_weight, up, down)
    return list(outs[:half]), outs[half], outs[half + 1]


def fan_kernel(owned_ref, across_ref, heads_ref, far_ref, out_ref):
    rows = owned_ref.shape[0]
    count, head_rows = heads_ref.shape[:2]
    top = 2 * rows + head_rows
    rest = out_ref.shape[1] - top
    each = (far_ref.shape[0] - rest) // (count - 1)
    for d in range(count):
        out_ref[d, :rows] = owned_ref[...]
        out_ref[d, rows : 2 * rows] = across_ref[...]
        out_ref[d, 2 * rows : top] = heads_ref[d]
        out_ref[d, top : top + each] = far_ref[d * each : (d + 1) * each]
        out_ref[d, top + each :] = far_ref[count * each :]


def fan(owned, across, heads, far, out_rows):
    count = heads.shape[0]
    each = (far.shape[0] - out_rows) // count
    shape = struct((count, 2 * owned.shape[0] + heads.shape[1] + each + out_rows, 128))
    return pl.pallas_call(
        fan_kernel,
        in_specs=[vspec()] * 4,
        out_specs=vspec(),
        out_shape=shape,
        compiler_params=params(8),
    )(owned, across, heads, far)


def source_of(rank, n, q, k):
    return (rank // (n // 2) ^ k) * (n // 2) + q


def norm_rows(x):
    average = jnp.mean(x, axis=-1, keepdims=True)
    power = jnp.mean(x * x, axis=-1, keepdims=True)
    return (x - average) * lax.rsqrt(power - average * average + 1e-06)


def attend_kernel(n, part, rank_ref, mine_ref, other_ref, far_ref, tokens_ref, out_ref, weight_ref):
    rank, half, group = rank_ref[0], rank_ref[1], rank_ref[2]
    rows = other_ref.shape[1] // 2
    cuts = rows // part
    width = cuts * 128
    depth = weight_ref.shape[0]
    piece = far_ref.shape[1]
    for q in range(n // 2):
        for k in range(2):
            source = source_of(rank, n, q, k)
            at = pl.ds(pl.multiple_of(source * part, part), part)
            for c in range(cuts):
                cut = slice(k * rows + c * part, k * rows + (c + 1) * part)
                to = pl.ds(pl.multiple_of(half * width + c * 128, 128), 128)
                tokens_ref[at, to] = mine_ref[q, cut]
                to = pl.ds(pl.multiple_of((1 - half) * width + c * 128, 128), 128)
                tokens_ref[at, to] = other_ref[q, cut]
        to = pl.ds(pl.multiple_of(source_of(rank, n, q, 0) * 128, 128), 128)
        weight_ref[:, to] = mine_ref[q, 2 * rows : 2 * rows + depth]
        to = pl.ds(pl.multiple_of(source_of(rank, n, q, 1) * 128, 128), 128)
        at = pl.ds(pl.multiple_of(group * piece, 32), piece)
        weight_ref[at, to] = mine_ref[q, 2 * rows + depth : 2 * rows + depth + piece]
        at = pl.ds(pl.multiple_of((1 - group) * piece, 32), piece)
        weight_ref[at, to] = far_ref[q]
    normed = norm_rows(tokens_ref[...].astype(F32)).astype(BF16)
    projected = lax.dot_general(
        normed, weight_ref[...], (((1,), (1,)), ((), ())), preferred_element_type=F32
    ).astype(BF16)
    size = projected.shape[1] // 3
    queries = projected[:, :size]
    keys = projected[:, size : 2 * size]
    values = projected[:, 2 * size :]
    scores = lax.dot_general(
        queries, keys, (((1,), (1,)), ((), ())), preferred_element_type=F32
    ) * (1.0 / math.sqrt(size))
    powers = jnp.exp(scores - jnp.max(scores, axis=1, keepdims=True))
    probs = (powers / jnp.sum(powers, axis=1, keepdims=True)).astype(BF16)
    attended = lax.dot_general(
        values, probs, (((0,), (1,)), ((), ())), preferred_element_type=F32
    ).astype(BF16)
    out_ref[...] = attended


def attend_fast(scalars, mine, other, far, head_rows, per_owner, n):
    length = n * per_owner
    depth = other.shape[1] // (2 * per_owner) * 256
    size = head_rows // 3
    return pl.pallas_call(
        functools.partial(attend_kernel, n, per_owner),
        in_specs=[sspec()] + [vspec()] * 3,
        out_specs=[vspec()] * 2,
        out_shape=[struct((length, depth)), struct((size, length))],
        scratch_shapes=[VMEM((head_rows, n * 128), BF16)],
        compiler_params=params(12),
        cost_estimate=cost(30),
    )(scalars, mine, other, far)


def mlp_kernel(n, rank_ref, tokens_ref, pieces, far, outs_far, near, outs, scratch):
    base_ref, terms_ref = outs
    up_ref, down_ref, row_ref, whole_ref, joined_ref, sem = scratch
    rank, half, group = rank_ref[0], rank_ref[1], rank_ref[2]
    block = up_ref.shape[0] // n
    wide = down_ref.shape[0] // 2
    unit = wide // 2
    size = pieces[0].shape[2]
    rows = outs_far[0][0].shape[1]
    first, later = [], []
    for j in range(n // 2):
        source = rank ^ j
        at = pl.ds(pl.multiple_of(source * block, block), block)
        to = pl.ds(pl.multiple_of(source * 128, 128), 128)
        for core in range(2):
            ref = near[core][j]
            for c in range(2):
                units = pl.ds(core * wide + c * unit, unit)
                later.append((ref.at[pl.ds(c * block, block)], up_ref.at[at, units]))
            units = pl.ds(core * wide, wide)
            later.append((ref.at[pl.ds(2 * block, wide)], down_ref.at[units, to]))
            rows_from = ref.at[pl.ds(2 * block + wide, 2 * rows)]
            first.append((rows_from, whole_ref.at[core, :, to]))
        source = source_of(rank, n, j, 1)
        at = pl.ds(pl.multiple_of(source * block, block), block)
        to = pl.ds(pl.multiple_of(source * 128, 128), 128)
        for core in range(2):
            for c in range(2):
                units = pl.ds(pl.multiple_of(core * wide + (group ^ c) * unit, unit), unit)
                later.append((far[core][c].at[j, pl.ds(0, block)], up_ref.at[at, units]))
                later.append((far[core][c].at[j, pl.ds(block, unit)], down_ref.at[units, to]))
                rows_to = pl.ds(pl.multiple_of((group ^ c) * rows, rows), rows)
                first.append((outs_far[core][c].at[j], whole_ref.at[core, rows_to, to]))
    wait_first = run_copies(first, sem)
    wait_later = run_copies(later, sem, len(first))
    for j in range(n // 2):
        for core in range(2):
            for k in range(2):
                at = pl.ds(pl.multiple_of((rank ^ j ^ (k * n // 2)) * size, size), size)
                joined_ref[core, at] = pieces[core][j, k]
    wait_first()
    dims = (((0,), (0,)), ((), ()))
    row_ref[...] = (
        tokens_ref[...].astype(F32)
        + lax.dot_general(joined_ref[0], whole_ref[0], dims, preferred_element_type=F32)
        + lax.dot_general(joined_ref[1], whole_ref[1], dims, preferred_element_type=F32)
    )
    part, width = base_ref.shape
    my_cols = pl.ds(pl.multiple_of(half * width, width), width)
    my_rows = pl.ds(pl.multiple_of(rank * part, part), part)
    normed = norm_rows(row_ref[...]).astype(BF16)
    base_ref[...] = row_ref[my_rows, my_cols]
    wait_later()
    raw = jnp.dot(normed, up_ref[...], preferred_element_type=F32)
    hidden = (0.5 * raw * (1.0 + lax.erf(raw * math.sqrt(0.5)))).astype(BF16)
    row_ref[:, :width] = jnp.dot(hidden, down_ref[:, my_cols], preferred_element_type=F32)
    base_ref[...] = base_ref[...] + row_ref[my_rows, :width]
    terms_ref[...] = row_ref[:, :width].astype(BF16)


def mlp(scalars, tokens, pieces, far, outs_far, near, n):
    length, depth = tokens.shape
    width = depth // 2
    wide = 2 * (far[0][0].shape[1] - depth // n)
    inner = n * pieces[0].shape[2]
    half = n // 2

    def kernel(scalars, tokens, a, b, *refs):
        far, refs = (refs[:2], refs[2:4]), refs[4:]
        outs_far, refs = (refs[:2], refs[2:4]), refs[4:]
        near, refs = (refs[:half], refs[half:n]), refs[n:]
        mlp_kernel(n, scalars, tokens, (a, b), far, outs_far, near, refs[:2], refs[2:])

    return pl.pallas_call(
        kernel,
        in_specs=[sspec()] + [vspec()] * 3 + [aspec()] * (8 + n),
        out_specs=[vspec()] * 2,
        out_shape=[struct((length // n, width), F32), struct((length, width))],
        scratch_shapes=[
            VMEM((depth, 2 * wide), BF16),
            VMEM((2 * wide, depth), BF16),
            VMEM((length, depth), F32),
            VMEM((2, inner, depth), BF16),
            VMEM((2, inner, length), BF16),
            pltpu.SemaphoreType.DMA((20 * half,)),
        ],
        compiler_params=params(24),
    )(scalars, tokens, *pieces, *far[0], *far[1], *outs_far[0], *outs_far[1], *near[0], *near[1])


def last_kernel(n, rank_ref, base_ref, terms_ref, out_ref):
    rank = rank_ref[0]
    total = base_ref[...]
    for j in range(1, n):
        total = total + terms_ref[rank ^ j].astype(F32)
    out_ref[...] = total.astype(BF16)


def last(scalars, base, terms):
    return pl.pallas_call(
        functools.partial(last_kernel, terms.shape[0]),
        in_specs=[sspec()] + [vspec()] * 2,
        out_specs=vspec(),
        out_shape=struct(base.shape),
        compiler_params=params(8),
    )(scalars, base, terms)


def swap(value, axis, j):
    n = lax.axis_size(axis)
    return lax.ppermute(value, axis, [(i, i ^ j) for i in range(n)])


def exchange(value):
    return lax.all_to_all(value, "seq", split_axis=0, concat_axis=0, tiled=True)


def exchange_half(value):
    n = lax.axis_size("seq")
    groups = [list(range(n // 2)), list(range(n // 2, n))]
    return lax.all_to_all(
        value, "seq", split_axis=0, concat_axis=0, axis_index_groups=groups, tiled=True
    )


def after(value, *others):
    return lax.optimization_barrier((value, *others))[0]


def local_fast(patches, keep_list, qkv_weight, out_weight, up_weight, down_weight):
    n = lax.axis_size("seq")
    rank, head, group = (
        lax.axis_index(name).astype(jnp.int32) for name in ("seq", "head", "groups")
    )
    scalars = jnp.stack([rank, head, group])
    half = n // 2
    sup, depth = patches.shape[1], patches.shape[3]
    length = sup * n * 8 // 5
    per_owner = length // n
    half_width = depth // 2
    head_rows = qkv_weight.shape[2]
    capacity = (4 * sup + n - 1) // n
    flat = patches.reshape(4 * sup, depth)
    heads = qkv_weight.transpose(1, 2, 0)

    near, qkv_near, away = pack(scalars, heads, out_weight, up_weight, down_weight, n)
    slots = prep(scalars, keep_list, flat, n, sup, capacity)
    dealt = exchange(slots)
    away, *near = lax.optimization_barrier((away, *near, slots))[:-1]
    far = swap(away, "seq", half)
    near = [near[0]] + [swap(near[j], "seq", j) for j in range(1, half)]
    owned = pick(scalars, keep_list, dealt, n, sup, per_owner, capacity)
    across = swap(owned, "seq", half)
    across, far, *near = lax.optimization_barrier((across, far, *near))

    out_rows = out_weight.shape[0] // 2
    got = exchange_half(fan(owned, across, qkv_near, far, out_rows))
    near_other = [swap(block, "head", 1) for block in near]
    got, *near_other = lax.optimization_barrier((got, *near_other))

    top = 2 * owned.shape[0]
    pieces_other = swap(got[:, :top], "head", 1)
    top = top + head_rows
    qkv_far = swap(got[:, top : top + head_rows // 2], "groups", 1)
    tokens, attended = attend_fast(
        scalars, got, pieces_other, qkv_far, head_rows, per_owner, n
    )

    att_across = swap(attended, "seq", half)
    got = after(got, attended)
    mlp_mine = got[:, top + head_rows // 2 : got.shape[1] - out_rows]
    far_mine = got[:, got.shape[1] - out_rows :]
    far_other = swap(far_mine, "groups", 1)
    mlp_other = swap(mlp_mine, "groups", 1)
    pair = jnp.stack([attended, att_across])
    pairs = [swap(pair, "seq", j) for j in range(1, half)]
    mlp_other, far_other, *pairs = lax.optimization_barrier((mlp_other, far_other, *pairs))
    gathered = jnp.stack([pair] + pairs)
    mlp_pair = (mlp_mine, mlp_other)
    far_pair = (far_mine, far_other)
    base, terms = mlp(
        scalars,
        tokens,
        (gathered, swap(gathered, "head", 1)),
        (mlp_pair, tuple(swap(value, "head", 1) for value in mlp_pair)),
        (far_pair, tuple(swap(value, "head", 1) for value in far_pair)),
        (near, near_other),
        n,
    )
    terms = exchange(terms.reshape(n, per_owner, half_width))
    encoded = last(scalars, base, terms)
    return encoded.reshape(1, per_owner, 1, half_width)


def local(patches, keep_list, qkv_weight, out_weight, up_weight, down_weight):
    n = lax.axis_size("seq")
    one_image = patches.shape[0] == 1 and qkv_weight.shape[1] == n and n & (n - 1) == 0
    one_image = one_image and lax.axis_size("groups") == 2 and up_weight.shape[1] == n * 256
    plan = local_fast if one_image else local_general
    return plan(patches, keep_list, qkv_weight, out_weight, up_weight, down_weight)


def solution(mesh):
    return jax.shard_map(
        local,
        mesh=mesh,
        in_specs=(
            P("groups", "seq", None, None),
            P("groups", None),
            P("seq", "head", None),
            P("head", "seq"),
            P("seq", "head"),
            P("head", "seq"),
        ),
        out_specs=P("groups", None, "seq", "head"),
        check_vma=False,
    )
```

```python
import functools
import math

import jax
import jax.numpy as jnp
from jax import lax
from jax.experimental import pallas as pl
from jax.experimental.pallas import tpu as pltpu
from jax.sharding import PartitionSpec as P

F32 = jnp.float32
BF16 = jnp.bfloat16
VMEM = pltpu.VMEM

def layer_norm(matrix):
    average = jnp.mean(matrix, axis=-1, keepdims=True)
    power = jnp.mean(matrix * matrix, axis=-1, keepdims=True)
    return (matrix - average) * lax.rsqrt(power - average * average + 1e-06)


def attend(queries, keys, values):
    length = queries.shape[0]
    block = math.gcd(length, 512)
    scale = 1.0 / math.sqrt(queries.shape[1])

    def one_block(query_rows):
        scores = (
            lax.dot_general(
                query_rows, keys, (((1,), (1,)), ((), ())), preferred_element_type=jnp.float32
            )
            * scale
        )
        top = jnp.max(scores, axis=1, keepdims=True)
        powers = jnp.exp(scores - top)
        probs = (powers / jnp.sum(powers, axis=1, keepdims=True)).astype(jnp.bfloat16)
        return jnp.dot(probs, values, preferred_element_type=jnp.float32).astype(jnp.bfloat16)

    blocks = lax.map(one_block, queries.reshape(length // block, block, queries.shape[1]))
    return blocks.reshape(length, values.shape[1])


def local_general(patches, keep_list, qkv_weight, out_weight, up_weight, down_weight):
    seq_count = lax.axis_size("seq")
    seq_rank = lax.axis_index("seq")
    head_rank = lax.axis_index("head")
    images = patches.shape[0]
    sup_local = patches.shape[1]
    depth = patches.shape[3]
    half_width = depth // lax.axis_size("head")
    head_count = qkv_weight.shape[1]
    seq_length = sup_local * seq_count * 8 // 5
    per_owner = seq_length // seq_count
    capacity = (4 * sup_local + seq_count - 1) // seq_count
    slot_count = 4 * sup_local
    image_index = jnp.arange(images, dtype=jnp.int32)
    bounds = jnp.arange(seq_count + 1, dtype=jnp.int32) * sup_local
    before = jnp.sum((keep_list[:, :, None] < bounds[None, None, :]).astype(jnp.int32), axis=1)
    starts = bounds[None, :seq_count] + 3 * before[:, :seq_count]
    lengths = sup_local + 3 * (before[:, 1:] - before[:, :seq_count])
    my_start = lax.dynamic_index_in_dim(starts, seq_rank, 1, keepdims=False)
    my_length = lax.dynamic_index_in_dim(lengths, seq_rank, 1, keepdims=False)
    local_ids = seq_rank * sup_local + jnp.arange(sup_local, dtype=jnp.int32)
    kept_flag = jnp.any(keep_list[:, None, :] == local_ids[None, :, None], axis=2).astype(jnp.int32)
    offsets = jnp.arange(sup_local, dtype=jnp.int32)[None, :] + 3 * (
        jnp.cumsum(kept_flag, axis=1) - kept_flag
    )
    slot_ids = jnp.arange(slot_count, dtype=jnp.int32)
    owner_patch = (
        jnp.sum((offsets[:, None, :] <= slot_ids[None, :, None]).astype(jnp.int32), axis=2) - 1
    )
    start_of = jnp.take_along_axis(offsets, owner_patch, axis=1)
    sub_index = jnp.minimum(slot_ids[None, :] - start_of, 3)
    kept_of = jnp.take_along_axis(kept_flag, owner_patch, axis=1)
    flat_patches = patches.reshape(images, sup_local * 4, depth)
    fine_rows = flat_patches[
        image_index[:, None], owner_patch * 4 + jnp.where(kept_of == 1, sub_index, 0)
    ]
    mean_rows = jnp.mean(patches.astype(jnp.float32), axis=2).astype(jnp.bfloat16)
    shared_rows = mean_rows[image_index[:, None], owner_patch]
    local_tokens = jnp.where((kept_of == 1)[:, :, None], fine_rows, shared_rows)
    destinations = jnp.arange(seq_count, dtype=jnp.int32)[:, None, None]
    depth_slots = jnp.arange(capacity, dtype=jnp.int32)[None, None, :]
    positions = (destinations - my_start[None, :, None]) % seq_count + depth_slots * seq_count
    valid = positions < my_length[None, :, None]
    outgoing = local_tokens[image_index[None, :, None], jnp.minimum(positions, slot_count - 1)]
    outgoing = jnp.where(valid[:, :, :, None], outgoing, jnp.zeros((), jnp.bfloat16))
    incoming = lax.all_to_all(outgoing, "seq", split_axis=0, concat_axis=0, tiled=True)
    owned = jnp.arange(per_owner, dtype=jnp.int32) * seq_count + seq_rank
    source = jnp.sum((starts[:, None, :] <= owned[None, :, None]).astype(jnp.int32), axis=2) - 1
    first_of = jnp.take_along_axis(starts, source, axis=1)
    depth_of = (owned[None, :] - first_of) // seq_count
    resident = incoming[source, image_index[:, None], depth_of]
    start_rows = resident.reshape(images * per_owner, depth)
    start_float = start_rows.astype(jnp.float32)
    qkv_full, out_full, up_full, down_full = (
        lax.all_gather(qkv_weight, "seq", axis=0, tiled=True),
        lax.all_gather(out_weight, "seq", axis=1, tiled=True),
        lax.all_gather(up_weight, "seq", axis=0, tiled=True),
        lax.all_gather(down_weight, "seq", axis=1, tiled=True),
    )
    normed = layer_norm(start_float).astype(jnp.bfloat16).reshape(images, per_owner, depth)
    projected = jnp.einsum("ipd,dhc->ihpc", normed, qkv_full, preferred_element_type=jnp.float32)
    head_size = qkv_weight.shape[2] // 3
    sending = projected.astype(jnp.bfloat16).reshape(seq_count, per_owner, 3 * head_size)
    gathered = lax.all_to_all(sending, "seq", split_axis=0, concat_axis=0, tiled=True).reshape(
        seq_length, 3 * head_size
    )
    attended = attend(
        gathered[:, :head_size],
        gathered[:, head_size : 2 * head_size],
        gathered[:, 2 * head_size :],
    )
    returned = lax.all_to_all(
        attended.reshape(seq_count, per_owner, head_size),
        "seq",
        split_axis=0,
        concat_axis=0,
        tiled=True,
    )
    returned = returned.reshape(images, head_count, per_owner, head_size)
    partial_sum = jnp.einsum(
        "ihpc,hcd->ipd",
        returned,
        out_full.reshape(head_count, head_size, depth),
        preferred_element_type=jnp.float32,
    ).reshape(images * per_owner, depth)
    attn_total = lax.psum(partial_sum, "head")
    residual = start_float + attn_total
    residual_half = lax.dynamic_slice_in_dim(residual, head_rank * half_width, half_width, 1)
    normed_two = layer_norm(residual).astype(jnp.bfloat16)
    hidden = jax.nn.gelu(
        jnp.dot(normed_two, up_full, preferred_element_type=jnp.float32), approximate=False
    ).astype(jnp.bfloat16)
    mlp_terms = jnp.dot(hidden, down_full, preferred_element_type=jnp.float32)
    mlp_part = lax.psum_scatter(mlp_terms, "head", scatter_dimension=1, tiled=True)
    encoded = (residual_half + mlp_part).astype(jnp.bfloat16)
    return encoded.reshape(images, per_owner, 1, half_width)


def vspec():
    return pl.BlockSpec(memory_space=VMEM)


def aspec():
    return pl.BlockSpec(memory_space=pl.ANY)


def sspec():
    return pl.BlockSpec(memory_space=pltpu.SMEM)


def hspec():
    return pl.BlockSpec(memory_space=pltpu.HBM)


def run_copies(copies, sem, base=0):
    started = [
        pltpu.make_async_copy(src, dst, sem.at[base + i]) for i, (src, dst) in enumerate(copies)
    ]
    for copy in started:
        copy.start()

    def wait():
        for copy in started:
            copy.wait()

    return wait


def params(mebibytes=4):
    return pltpu.CompilerParams(vmem_limit_bytes=mebibytes * 1024 * 1024)


def cost(micros):
    return pl.CostEstimate(flops=micros * 10**9, bytes_accessed=1 << 20, transcendentals=0)


def struct(shape, dtype=BF16):
    return jax.ShapeDtypeStruct(shape, dtype)


def slot_of(index, n, capacity, cuts):
    device = sum(((index >= j * cuts * capacity).astype(jnp.int32) for j in range(1, n)), 0 * index)
    inner = index - device * (cuts * capacity)
    cut = sum(((inner >= c * capacity).astype(jnp.int32) for c in range(1, cuts)), 0 * index)
    return device, cut, inner - cut * capacity


def as_column(row):
    count = row.shape[1]
    same = lax.broadcasted_iota(jnp.int32, (count, count), 0) == lax.broadcasted_iota(
        jnp.int32, (count, count), 1
    )
    return jnp.sum(jnp.where(same, row, 0), axis=1, keepdims=True)


def one_hot(mask):
    return mask.astype(F32).astype(BF16)


def prep_kernel(n, sup, capacity, rank_ref, keep_ref, patches_ref, out_ref):
    rank = rank_ref[0]
    first = rank * sup
    keep = as_column(keep_ref[...])
    rows = 4 * sup
    count = keep.shape[0]

    def places(width, shift):
        ids = lax.broadcasted_iota(jnp.int32, (count, width), 1) >> shift
        kept = jnp.sum((keep == first + ids).astype(jnp.int32), axis=0, keepdims=True)
        below = jnp.sum(
            jnp.logical_and(keep >= first, keep < first + ids).astype(jnp.int32),
            axis=0,
            keepdims=True,
        )
        return kept, below, lax.broadcasted_iota(jnp.int32, (1, width), 1)

    kept, below, lane = places(rows, 2)
    fine_pos = jnp.where(kept == 1, (lane >> 2) + 3 * below + (lane & 3), -1)
    kept, below, lane = places(sup, 0)
    mean_pos = jnp.where(kept == 1, -1, lane + 3 * below)
    start = first + 3 * jnp.sum((keep < first).astype(jnp.int32), axis=0, keepdims=True)
    flat = patches_ref[...]
    cuts = flat.shape[1] // 128
    sup_col = lax.broadcasted_iota(jnp.int32, (sup, rows), 0)
    sup_lane = lax.broadcasted_iota(jnp.int32, (sup, rows), 1) >> 2
    averaging = jnp.where(sup_col == sup_lane, 0.25, 0.0).astype(BF16)
    means = jnp.dot(averaging, flat, preferred_element_type=F32).astype(BF16)
    index = lax.broadcasted_iota(jnp.int32, (n * cuts * capacity, 1), 0)
    device, cut, slot = slot_of(index, n, capacity, cuts)
    pos = ((device - start) & (n - 1)) + slot * n
    total = jnp.zeros((n * cuts * capacity, 128), F32)
    for c in range(cuts):
        at = jnp.where(cut == c, pos, -2)
        features = slice(c * 128, (c + 1) * 128)
        total = (
            total
            + jnp.dot(one_hot(at == fine_pos), flat[:, features], preferred_element_type=F32)
            + jnp.dot(one_hot(at == mean_pos), means[:, features], preferred_element_type=F32)
        )
    out_ref[...] = total.astype(BF16)


def prep(scalars, keep_list, flat, n, sup, capacity):
    width = flat.shape[1] // 2
    shape = (n * capacity * width // 128, 128)
    return pl.pallas_call(
        functools.partial(prep_kernel, n, sup, capacity),
        grid_spec=pltpu.PrefetchScalarGridSpec(
            num_scalar_prefetch=1,
            grid=(1,),
            in_specs=[
                pl.BlockSpec(keep_list.shape, lambda i, ref: (0, 0)),
                pl.BlockSpec((flat.shape[0], width), lambda i, ref: (0, ref[1])),
            ],
            out_specs=pl.BlockSpec(shape, lambda i, ref: (0, 0)),
        ),
        out_shape=struct(shape),
        compiler_params=params(),
    )(scalars, keep_list, flat)


def pick_kernel(n, sup, per_owner, capacity, rank_ref, keep_ref, got_ref, out_ref):
    rank = rank_ref[0]
    keep = as_column(keep_ref[...])
    count = keep.shape[0]
    lanes = got_ref.shape[0]
    cuts = lanes // (n * capacity)
    source, _, _ = slot_of(
        lax.broadcasted_iota(jnp.int32, (count, lanes), 1), n, capacity, cuts
    )
    low = jnp.sum((keep < source * sup).astype(jnp.int32), axis=0, keepdims=True)
    high = jnp.sum((keep < source * sup + sup).astype(jnp.int32), axis=0, keepdims=True)
    source, cut, slot = slot_of(
        lax.broadcasted_iota(jnp.int32, (1, lanes), 1), n, capacity, cuts
    )
    start = source * sup + 3 * low
    stop = source * sup + sup + 3 * high
    token = start + ((rank - start) & (n - 1)) + slot * n
    row = jnp.where(token < stop, token >> (n.bit_length() - 1), -1)
    own = lax.broadcasted_iota(jnp.int32, (per_owner, lanes), 0)
    got = got_ref[...]
    for c in range(cuts):
        choose = one_hot(own == jnp.where(cut == c, row, -1))
        owned = jnp.dot(choose, got, preferred_element_type=F32).astype(BF16)
        out_ref[c * per_owner : (c + 1) * per_owner] = owned


def pick(scalars, keep_list, got, n, sup, per_owner, capacity):
    cuts = got.shape[0] // (n * capacity)
    return pl.pallas_call(
        functools.partial(pick_kernel, n, sup, per_owner, capacity),
        in_specs=[sspec(), vspec(), vspec()],
        out_specs=vspec(),
        out_shape=struct((cuts * per_owner, 128)),
        compiler_params=params(),
    )(scalars, keep_list, got)


def far_kernel(n, rank_ref, qkv_ref, out_weight_ref, up_ref, down_ref, away_ref, sem):
    rank, part = rank_ref[0], rank_ref[2]
    half = n // 2
    rows = up_ref.shape[0]
    wide = up_ref.shape[1] // n
    units = wide // 2
    long = out_weight_ref.shape[0] // 2
    depth = qkv_ref.shape[1] // 2
    each = depth + rows + units
    copies = []
    for d in range(half):
        dest = (rank // half ^ 1) * half + d
        low = d * each
        at = pl.ds(pl.multiple_of(part * depth, 32), depth)
        copies.append((qkv_ref.at[dest, at], away_ref.at[pl.ds(low, depth)]))
        at = pl.ds(pl.multiple_of(dest * wide + part * units, 128), units)
        copies.append((up_ref.at[:, at], away_ref.at[pl.ds(low + depth, rows)]))
        copies.append((down_ref.at[at], away_ref.at[pl.ds(low + depth + rows, units)]))
    at = pl.ds(pl.multiple_of(part * long, 128), long)
    copies.append((out_weight_ref.at[at], away_ref.at[pl.ds(half * each, long)]))
    run_copies(copies, sem)()


def near_kernel(n, rank_ref, qkv_ref, out_weight_ref, up_ref, down_ref, *refs):
    near, (heads_ref, sem) = refs[: n // 2], refs[n // 2 :]
    rank = rank_ref[0]
    half = n // 2
    rows = up_ref.shape[0]
    wide = up_ref.shape[1] // n
    units = wide // 2
    long = out_weight_ref.shape[0]
    copies = [(qkv_ref.at[pl.ds(rank // half * half, half)], heads_ref)]
    for j in range(half):
        dest = rank ^ j
        for c in range(2):
            at = pl.ds(pl.multiple_of(dest * wide + c * units, 128), units)
            copies.append((up_ref.at[:, at], near[j].at[pl.ds(c * rows, rows)]))
        at = pl.ds(pl.multiple_of(dest * wide, 128), wide)
        copies.append((down_ref.at[at], near[j].at[pl.ds(2 * rows, wide)]))
        copies.append((out_weight_ref, near[j].at[pl.ds(2 * rows + wide, long)]))
    run_copies(copies, sem)()


def pack(kernel, shapes, count, scalars, *weights):
    return pl.pallas_call(
        kernel,
        in_specs=[sspec()] + [hspec()] * 4,
        out_specs=[aspec()] * len(shapes),
        out_shape=[struct(shape) for shape in shapes],
        scratch_shapes=[pltpu.SemaphoreType.DMA((count,))],
    )(scalars, *weights)


def pack_far(scalars, qkv, out_weight, up, down, n):
    half = n // 2
    each = qkv.shape[1] // 2 + up.shape[0] + up.shape[1] // n // 2
    shapes = [(half * each + out_weight.shape[0] // 2, 128)]
    kernel = functools.partial(far_kernel, n)
    return pack(kernel, shapes, 3 * half + 1, scalars, qkv, out_weight, up, down)[0]


def pack_near(scalars, qkv, out_weight, up, down, n):
    half = n // 2
    near = (2 * up.shape[0] + up.shape[1] // n + out_weight.shape[0], 128)
    shapes = [near] * half + [(half,) + qkv.shape[1:]]
    kernel = functools.partial(near_kernel, n)
    outs = pack(kernel, shapes, 4 * half + 1, scalars, qkv, out_weight, up, down)
    return list(outs[:half]), outs[half]


def fan_kernel(owned_ref, across_ref, heads_ref, far_ref, out_ref):
    rows = owned_ref.shape[0]
    count, head_rows = heads_ref.shape[:2]
    top = 2 * rows + head_rows
    rest = out_ref.shape[1] - top
    each = (far_ref.shape[0] - rest) // (count - 1)
    for d in range(count):
        out_ref[d, :rows] = owned_ref[...]
        out_ref[d, rows : 2 * rows] = across_ref[...]
        out_ref[d, 2 * rows : top] = heads_ref[d]
        out_ref[d, top : top + each] = far_ref[d * each : (d + 1) * each]
        out_ref[d, top + each :] = far_ref[count * each :]


def fan(owned, across, heads, far, out_rows):
    count = heads.shape[0]
    each = (far.shape[0] - out_rows) // count
    shape = struct((count, 2 * owned.shape[0] + heads.shape[1] + each + out_rows, 128))
    return pl.pallas_call(
        fan_kernel,
        in_specs=[vspec()] * 4,
        out_specs=vspec(),
        out_shape=shape,
        compiler_params=params(8),
    )(owned, across, heads, far)


def source_of(rank, n, q, k):
    return (rank // (n // 2) ^ k) * (n // 2) + q


def norm_rows(x):
    average = jnp.mean(x, axis=-1, keepdims=True)
    power = jnp.mean(x * x, axis=-1, keepdims=True)
    return (x - average) * lax.rsqrt(power - average * average + 1e-06)


def attend_kernel(n, part, rank_ref, mine_ref, other_ref, far_ref, tokens_ref, out_ref, weight_ref):
    rank, half, group = rank_ref[0], rank_ref[1], rank_ref[2]
    rows = other_ref.shape[1] // 2
    cuts = rows // part
    width = cuts * 128
    depth = weight_ref.shape[0]
    piece = far_ref.shape[1]
    for q in range(n // 2):
        for k in range(2):
            source = source_of(rank, n, q, k)
            at = pl.ds(pl.multiple_of(source * part, part), part)
            for c in range(cuts):
                cut = slice(k * rows + c * part, k * rows + (c + 1) * part)
                to = pl.ds(pl.multiple_of(half * width + c * 128, 128), 128)
                tokens_ref[at, to] = mine_ref[q, cut]
                to = pl.ds(pl.multiple_of((1 - half) * width + c * 128, 128), 128)
                tokens_ref[at, to] = other_ref[q, cut]
        to = pl.ds(pl.multiple_of(source_of(rank, n, q, 0) * 128, 128), 128)
        weight_ref[:, to] = mine_ref[q, 2 * rows : 2 * rows + depth]
        to = pl.ds(pl.multiple_of(source_of(rank, n, q, 1) * 128, 128), 128)
        at = pl.ds(pl.multiple_of(group * piece, 32), piece)
        weight_ref[at, to] = mine_ref[q, 2 * rows + depth : 2 * rows + depth + piece]
        at = pl.ds(pl.multiple_of((1 - group) * piece, 32), piece)
        weight_ref[at, to] = far_ref[q]
    normed = norm_rows(tokens_ref[...].astype(F32)).astype(BF16)
    projected = lax.dot_general(
        normed, weight_ref[...], (((1,), (1,)), ((), ())), preferred_element_type=F32
    ).astype(BF16)
    size = projected.shape[1] // 3
    queries = projected[:, :size]
    keys = projected[:, size : 2 * size]
    values = projected[:, 2 * size :]
    scores = lax.dot_general(
        queries, keys, (((1,), (1,)), ((), ())), preferred_element_type=F32
    ) * (1.0 / math.sqrt(size))
    powers = jnp.exp(scores - jnp.max(scores, axis=1, keepdims=True))
    probs = (powers / jnp.sum(powers, axis=1, keepdims=True)).astype(BF16)
    attended = lax.dot_general(
        values, probs, (((0,), (1,)), ((), ())), preferred_element_type=F32
    ).astype(BF16)
    out_ref[...] = attended


def attend_fast(scalars, mine, other, far, head_rows, per_owner, n):
    length = n * per_owner
    depth = other.shape[1] // (2 * per_owner) * 256
    size = head_rows // 3
    return pl.pallas_call(
        functools.partial(attend_kernel, n, per_owner),
        in_specs=[sspec()] + [vspec()] * 3,
        out_specs=[vspec()] * 2,
        out_shape=[struct((length, depth)), struct((size, length))],
        scratch_shapes=[VMEM((head_rows, n * 128), BF16)],
        compiler_params=params(12),
        cost_estimate=cost(30),
    )(scalars, mine, other, far)


def mlp_kernel(n, rank_ref, tokens_ref, pieces, far, outs_far, near, outs, scratch):
    base_ref, away_ref, sends = outs[0], outs[1], outs[2:]
    up_ref, down_ref, row_ref, whole_ref, joined_ref, sem = scratch
    rank, half, group = rank_ref[0], rank_ref[1], rank_ref[2]
    block = up_ref.shape[0] // n
    wide = down_ref.shape[0] // 2
    unit = wide // 2
    size = pieces[0].shape[2]
    rows = outs_far[0][0].shape[1]
    first, later = [], []
    for j in range(n // 2):
        source = rank ^ j
        at = pl.ds(pl.multiple_of(source * block, block), block)
        to = pl.ds(pl.multiple_of(source * 128, 128), 128)
        for core in range(2):
            ref = near[core][j]
            for c in range(2):
                units = pl.ds(core * wide + c * unit, unit)
                later.append((ref.at[pl.ds(c * block, block)], up_ref.at[at, units]))
            units = pl.ds(core * wide, wide)
            later.append((ref.at[pl.ds(2 * block, wide)], down_ref.at[units, to]))
            rows_from = ref.at[pl.ds(2 * block + wide, 2 * rows)]
            first.append((rows_from, whole_ref.at[core, :, to]))
        source = source_of(rank, n, j, 1)
        at = pl.ds(pl.multiple_of(source * block, block), block)
        to = pl.ds(pl.multiple_of(source * 128, 128), 128)
        for core in range(2):
            for c in range(2):
                units = pl.ds(pl.multiple_of(core * wide + (group ^ c) * unit, unit), unit)
                later.append((far[core][c].at[j, pl.ds(0, block)], up_ref.at[at, units]))
                later.append((far[core][c].at[j, pl.ds(block, unit)], down_ref.at[units, to]))
                rows_to = pl.ds(pl.multiple_of((group ^ c) * rows, rows), rows)
                first.append((outs_far[core][c].at[j], whole_ref.at[core, rows_to, to]))
    wait_first = run_copies(first, sem)
    wait_later = run_copies(later, sem, len(first))
    for j in range(n // 2):
        for core in range(2):
            for k in range(2):
                at = pl.ds(pl.multiple_of((rank ^ j ^ (k * n // 2)) * size, size), size)
                joined_ref[core, at] = pieces[core][j, k]
    wait_first()
    dims = (((0,), (0,)), ((), ()))
    row_ref[...] = (
        tokens_ref[...].astype(F32)
        + lax.dot_general(joined_ref[0], whole_ref[0], dims, preferred_element_type=F32)
        + lax.dot_general(joined_ref[1], whole_ref[1], dims, preferred_element_type=F32)
    )
    part, width = base_ref.shape
    my_cols = pl.ds(pl.multiple_of(half * width, width), width)
    my_rows = pl.ds(pl.multiple_of(rank * part, part), part)
    normed = norm_rows(row_ref[...]).astype(BF16)
    base_ref[...] = row_ref[my_rows, my_cols]
    wait_later()
    raw = jnp.dot(normed, up_ref[...], preferred_element_type=F32)
    hidden = (0.5 * raw * (1.0 + lax.erf(raw * math.sqrt(0.5)))).astype(BF16)
    row_ref[:, :width] = jnp.dot(hidden, down_ref[:, my_cols], preferred_element_type=F32)
    base_ref[...] = base_ref[...] + row_ref[my_rows, :width]
    for j in range(n // 2):
        for k in range(2):
            owner = rank ^ j ^ (k * n // 2)
            term = row_ref[pl.ds(pl.multiple_of(owner * part, part), part), :width]
            if j > 0:
                sends[j - 1][k] = term.astype(BF16)
            elif k == 1:
                away_ref[...] = term


def mlp(scalars, tokens, pieces, far, outs_far, near, n):
    length, depth = tokens.shape
    width = depth // 2
    wide = 2 * (far[0][0].shape[1] - depth // n)
    inner = n * pieces[0].shape[2]
    half = n // 2

    def kernel(scalars, tokens, a, b, *refs):
        far, refs = (refs[:2], refs[2:4]), refs[4:]
        outs_far, refs = (refs[:2], refs[2:4]), refs[4:]
        near, refs = (refs[:half], refs[half:n]), refs[n:]
        mlp_kernel(n, scalars, tokens, (a, b), far, outs_far, near, refs[: half + 1], refs[half + 1 :])

    return pl.pallas_call(
        kernel,
        in_specs=[sspec()] + [vspec()] * 3 + [aspec()] * (8 + n),
        out_specs=[vspec()] * (half + 1),
        out_shape=[struct((length // n, width), F32)] * 2
        + [struct((2, length // n, width))] * (half - 1),
        scratch_shapes=[
            VMEM((depth, 2 * wide), BF16),
            VMEM((2 * wide, depth), BF16),
            VMEM((length, depth), F32),
            VMEM((2, inner, depth), BF16),
            VMEM((2, inner, length), BF16),
            pltpu.SemaphoreType.DMA((20 * half,)),
        ],
        compiler_params=params(24),
    )(scalars, tokens, *pieces, *far[0], *far[1], *outs_far[0], *outs_far[1], *near[0], *near[1])


def sum_kernel(base_ref, away_ref, *refs):
    terms, (base_out, away_out) = refs[:-2], refs[-2:]
    base, away = base_ref[...], away_ref[...]
    for ref in terms:
        base = base + ref[0].astype(F32)
        away = away + ref[1].astype(F32)
    base_out[...] = base
    away_out[...] = away.astype(BF16)


def sum_terms(base, away, terms):
    return pl.pallas_call(
        sum_kernel,
        in_specs=[vspec()] * (2 + len(terms)),
        out_specs=[vspec()] * 2,
        out_shape=[struct(base.shape, F32), struct(away.shape)],
        compiler_params=params(),
    )(base, away, *terms)


def last_kernel(base_ref, across_ref, out_ref):
    out_ref[...] = (base_ref[...] + across_ref[...].astype(F32)).astype(BF16)


def last(base, across):
    return pl.pallas_call(
        last_kernel,
        in_specs=[vspec()] * 2,
        out_specs=vspec(),
        out_shape=struct(base.shape),
        compiler_params=params(),
    )(base, across)


def swap(value, axis, j):
    n = lax.axis_size(axis)
    return lax.ppermute(value, axis, [(i, i ^ j) for i in range(n)])


def exchange(value):
    return lax.all_to_all(value, "seq", split_axis=0, concat_axis=0, tiled=True)


def exchange_half(value):
    n = lax.axis_size("seq")
    groups = [list(range(n // 2)), list(range(n // 2, n))]
    return lax.all_to_all(
        value, "seq", split_axis=0, concat_axis=0, axis_index_groups=groups, tiled=True
    )


def after(value, *others):
    return lax.optimization_barrier((value, *others))[0]


def local_fast(patches, keep_list, qkv_weight, out_weight, up_weight, down_weight):
    n = lax.axis_size("seq")
    rank, head, group = (
        lax.axis_index(name).astype(jnp.int32) for name in ("seq", "head", "groups")
    )
    scalars = jnp.stack([rank, head, group])
    half = n // 2
    sup, depth = patches.shape[1], patches.shape[3]
    length = sup * n * 8 // 5
    per_owner = length // n
    half_width = depth // 2
    head_rows = qkv_weight.shape[2]
    capacity = (4 * sup + n - 1) // n
    flat = patches.reshape(4 * sup, depth)
    heads = qkv_weight.transpose(1, 2, 0)

    weights = (heads, out_weight, up_weight, down_weight)
    away = pack_far(scalars, *weights, n)
    far = swap(away, "seq", half)
    slots = prep(scalars, keep_list, after(flat, away), n, sup, capacity)
    dealt = exchange(slots)
    weights = lax.optimization_barrier((*weights, slots))[:4]
    near, qkv_near = pack_near(scalars, *weights, n)
    near = [near[0]] + [swap(near[j], "seq", j) for j in range(1, half)]
    owned = pick(scalars, keep_list, dealt, n, sup, per_owner, capacity)
    across = swap(owned, "seq", half)
    across, far, *near = lax.optimization_barrier((across, far, *near))

    out_rows = out_weight.shape[0] // 2
    got = exchange_half(fan(owned, across, qkv_near, far, out_rows))
    near_other = [swap(block, "head", 1) for block in near]
    got, *near_other = lax.optimization_barrier((got, *near_other))

    top = 2 * owned.shape[0]
    pieces_other = swap(got[:, :top], "head", 1)
    top = top + head_rows
    qkv_far = swap(got[:, top : top + head_rows // 2], "groups", 1)
    tokens, attended = attend_fast(
        scalars, got, pieces_other, qkv_far, head_rows, per_owner, n
    )

    att_across = swap(attended, "seq", half)
    got = after(got, attended)
    mlp_mine = got[:, top + head_rows // 2 : got.shape[1] - out_rows]
    far_mine = got[:, got.shape[1] - out_rows :]
    far_other = swap(far_mine, "groups", 1)
    mlp_other = swap(mlp_mine, "groups", 1)
    pair = jnp.stack([attended, att_across])
    pairs = [swap(pair, "seq", j) for j in range(1, half)]
    mlp_other, far_other, *pairs = lax.optimization_barrier((mlp_other, far_other, *pairs))
    gathered = jnp.stack([pair] + pairs)
    mlp_pair = (mlp_mine, mlp_other)
    far_pair = (far_mine, far_other)
    base, term_away, *terms = mlp(
        scalars,
        tokens,
        (gathered, swap(gathered, "head", 1)),
        (mlp_pair, tuple(swap(value, "head", 1) for value in mlp_pair)),
        (far_pair, tuple(swap(value, "head", 1) for value in far_pair)),
        (near, near_other),
        n,
    )
    terms = [swap(terms[j - 1], "seq", j) for j in range(1, half)]
    base, term_away = sum_terms(base, term_away, terms)
    encoded = last(base, swap(term_away, "seq", half))
    return encoded.reshape(1, per_owner, 1, half_width)


def local(patches, keep_list, qkv_weight, out_weight, up_weight, down_weight):
    n = lax.axis_size("seq")
    one_image = patches.shape[0] == 1 and qkv_weight.shape[1] == n and n & (n - 1) == 0
    one_image = one_image and lax.axis_size("groups") == 2 and up_weight.shape[1] == n * 256
    plan = local_fast if one_image else local_general
    return plan(patches, keep_list, qkv_weight, out_weight, up_weight, down_weight)


def solution(mesh):
    return jax.shard_map(
        local,
        mesh=mesh,
        in_specs=(
            P("groups", "seq", None, None),
            P("groups", None),
            P("seq", "head", None),
            P("head", "seq"),
            P("seq", "head"),
            P("head", "seq"),
        ),
        out_specs=P("groups", None, "seq", "head"),
        check_vma=False,
    )
```

```python
import functools
import math

import jax
import jax.numpy as jnp
from jax import lax
from jax.experimental import pallas as pl
from jax.experimental.pallas import tpu as pltpu
from jax.sharding import PartitionSpec as P

F32 = jnp.float32
BF16 = jnp.bfloat16
VMEM = pltpu.VMEM

def layer_norm(matrix):
    average = jnp.mean(matrix, axis=-1, keepdims=True)
    power = jnp.mean(matrix * matrix, axis=-1, keepdims=True)
    return (matrix - average) * lax.rsqrt(power - average * average + 1e-06)


def attend(queries, keys, values):
    length = queries.shape[0]
    block = math.gcd(length, 512)
    scale = 1.0 / math.sqrt(queries.shape[1])

    def one_block(query_rows):
        scores = (
            lax.dot_general(
                query_rows, keys, (((1,), (1,)), ((), ())), preferred_element_type=jnp.float32
            )
            * scale
        )
        top = jnp.max(scores, axis=1, keepdims=True)
        powers = jnp.exp(scores - top)
        probs = (powers / jnp.sum(powers, axis=1, keepdims=True)).astype(jnp.bfloat16)
        return jnp.dot(probs, values, preferred_element_type=jnp.float32).astype(jnp.bfloat16)

    blocks = lax.map(one_block, queries.reshape(length // block, block, queries.shape[1]))
    return blocks.reshape(length, values.shape[1])


def local_general(patches, keep_list, qkv_weight, out_weight, up_weight, down_weight):
    seq_count = lax.axis_size("seq")
    seq_rank = lax.axis_index("seq")
    head_rank = lax.axis_index("head")
    images = patches.shape[0]
    sup_local = patches.shape[1]
    depth = patches.shape[3]
    half_width = depth // lax.axis_size("head")
    head_count = qkv_weight.shape[1]
    seq_length = sup_local * seq_count * 8 // 5
    per_owner = seq_length // seq_count
    capacity = (4 * sup_local + seq_count - 1) // seq_count
    slot_count = 4 * sup_local
    image_index = jnp.arange(images, dtype=jnp.int32)
    bounds = jnp.arange(seq_count + 1, dtype=jnp.int32) * sup_local
    before = jnp.sum((keep_list[:, :, None] < bounds[None, None, :]).astype(jnp.int32), axis=1)
    starts = bounds[None, :seq_count] + 3 * before[:, :seq_count]
    lengths = sup_local + 3 * (before[:, 1:] - before[:, :seq_count])
    my_start = lax.dynamic_index_in_dim(starts, seq_rank, 1, keepdims=False)
    my_length = lax.dynamic_index_in_dim(lengths, seq_rank, 1, keepdims=False)
    local_ids = seq_rank * sup_local + jnp.arange(sup_local, dtype=jnp.int32)
    kept_flag = jnp.any(keep_list[:, None, :] == local_ids[None, :, None], axis=2).astype(jnp.int32)
    offsets = jnp.arange(sup_local, dtype=jnp.int32)[None, :] + 3 * (
        jnp.cumsum(kept_flag, axis=1) - kept_flag
    )
    slot_ids = jnp.arange(slot_count, dtype=jnp.int32)
    owner_patch = (
        jnp.sum((offsets[:, None, :] <= slot_ids[None, :, None]).astype(jnp.int32), axis=2) - 1
    )
    start_of = jnp.take_along_axis(offsets, owner_patch, axis=1)
    sub_index = jnp.minimum(slot_ids[None, :] - start_of, 3)
    kept_of = jnp.take_along_axis(kept_flag, owner_patch, axis=1)
    flat_patches = patches.reshape(images, sup_local * 4, depth)
    fine_rows = flat_patches[
        image_index[:, None], owner_patch * 4 + jnp.where(kept_of == 1, sub_index, 0)
    ]
    mean_rows = jnp.mean(patches.astype(jnp.float32), axis=2).astype(jnp.bfloat16)
    shared_rows = mean_rows[image_index[:, None], owner_patch]
    local_tokens = jnp.where((kept_of == 1)[:, :, None], fine_rows, shared_rows)
    destinations = jnp.arange(seq_count, dtype=jnp.int32)[:, None, None]
    depth_slots = jnp.arange(capacity, dtype=jnp.int32)[None, None, :]
    positions = (destinations - my_start[None, :, None]) % seq_count + depth_slots * seq_count
    valid = positions < my_length[None, :, None]
    outgoing = local_tokens[image_index[None, :, None], jnp.minimum(positions, slot_count - 1)]
    outgoing = jnp.where(valid[:, :, :, None], outgoing, jnp.zeros((), jnp.bfloat16))
    incoming = lax.all_to_all(outgoing, "seq", split_axis=0, concat_axis=0, tiled=True)
    owned = jnp.arange(per_owner, dtype=jnp.int32) * seq_count + seq_rank
    source = jnp.sum((starts[:, None, :] <= owned[None, :, None]).astype(jnp.int32), axis=2) - 1
    first_of = jnp.take_along_axis(starts, source, axis=1)
    depth_of = (owned[None, :] - first_of) // seq_count
    resident = incoming[source, image_index[:, None], depth_of]
    start_rows = resident.reshape(images * per_owner, depth)
    start_float = start_rows.astype(jnp.float32)
    qkv_full, out_full, up_full, down_full = (
        lax.all_gather(qkv_weight, "seq", axis=0, tiled=True),
        lax.all_gather(out_weight, "seq", axis=1, tiled=True),
        lax.all_gather(up_weight, "seq", axis=0, tiled=True),
        lax.all_gather(down_weight, "seq", axis=1, tiled=True),
    )
    normed = layer_norm(start_float).astype(jnp.bfloat16).reshape(images, per_owner, depth)
    projected = jnp.einsum("ipd,dhc->ihpc", normed, qkv_full, preferred_element_type=jnp.float32)
    head_size = qkv_weight.shape[2] // 3
    sending = projected.astype(jnp.bfloat16).reshape(seq_count, per_owner, 3 * head_size)
    gathered = lax.all_to_all(sending, "seq", split_axis=0, concat_axis=0, tiled=True).reshape(
        seq_length, 3 * head_size
    )
    attended = attend(
        gathered[:, :head_size],
        gathered[:, head_size : 2 * head_size],
        gathered[:, 2 * head_size :],
    )
    returned = lax.all_to_all(
        attended.reshape(seq_count, per_owner, head_size),
        "seq",
        split_axis=0,
        concat_axis=0,
        tiled=True,
    )
    returned = returned.reshape(images, head_count, per_owner, head_size)
    partial_sum = jnp.einsum(
        "ihpc,hcd->ipd",
        returned,
        out_full.reshape(head_count, head_size, depth),
        preferred_element_type=jnp.float32,
    ).reshape(images * per_owner, depth)
    attn_total = lax.psum(partial_sum, "head")
    residual = start_float + attn_total
    residual_half = lax.dynamic_slice_in_dim(residual, head_rank * half_width, half_width, 1)
    normed_two = layer_norm(residual).astype(jnp.bfloat16)
    hidden = jax.nn.gelu(
        jnp.dot(normed_two, up_full, preferred_element_type=jnp.float32), approximate=False
    ).astype(jnp.bfloat16)
    mlp_terms = jnp.dot(hidden, down_full, preferred_element_type=jnp.float32)
    mlp_part = lax.psum_scatter(mlp_terms, "head", scatter_dimension=1, tiled=True)
    encoded = (residual_half + mlp_part).astype(jnp.bfloat16)
    return encoded.reshape(images, per_owner, 1, half_width)


def vspec():
    return pl.BlockSpec(memory_space=VMEM)


def aspec():
    return pl.BlockSpec(memory_space=pl.ANY)


def sspec():
    return pl.BlockSpec(memory_space=pltpu.SMEM)


def hspec():
    return pl.BlockSpec(memory_space=pltpu.HBM)


def run_copies(copies, sem, base=0):
    started = [
        pltpu.make_async_copy(src, dst, sem.at[base + i]) for i, (src, dst) in enumerate(copies)
    ]
    for copy in started:
        copy.start()

    def wait():
        for copy in started:
            copy.wait()

    return wait


def params(mebibytes=4):
    return pltpu.CompilerParams(vmem_limit_bytes=mebibytes * 1024 * 1024)


def cost(micros):
    return pl.CostEstimate(flops=micros * 10**9, bytes_accessed=1 << 20, transcendentals=0)


def struct(shape, dtype=BF16):
    return jax.ShapeDtypeStruct(shape, dtype)


def slot_of(index, n, capacity, cuts):
    device = sum(((index >= j * cuts * capacity).astype(jnp.int32) for j in range(1, n)), 0 * index)
    inner = index - device * (cuts * capacity)
    cut = sum(((inner >= c * capacity).astype(jnp.int32) for c in range(1, cuts)), 0 * index)
    return device, cut, inner - cut * capacity


def as_column(row):
    count = row.shape[1]
    same = lax.broadcasted_iota(jnp.int32, (count, count), 0) == lax.broadcasted_iota(
        jnp.int32, (count, count), 1
    )
    return jnp.sum(jnp.where(same, row, 0), axis=1, keepdims=True)


def one_hot(mask):
    return mask.astype(F32).astype(BF16)


def prep_kernel(n, sup, capacity, rank_ref, keep_ref, patches_ref, out_ref):
    rank = rank_ref[0]
    first = rank * sup
    keep = as_column(keep_ref[...])
    rows = 4 * sup
    count = keep.shape[0]

    def places(width, shift):
        ids = lax.broadcasted_iota(jnp.int32, (count, width), 1) >> shift
        kept = jnp.sum((keep == first + ids).astype(jnp.int32), axis=0, keepdims=True)
        below = jnp.sum(
            jnp.logical_and(keep >= first, keep < first + ids).astype(jnp.int32),
            axis=0,
            keepdims=True,
        )
        return kept, below, lax.broadcasted_iota(jnp.int32, (1, width), 1)

    kept, below, lane = places(rows, 2)
    fine_pos = jnp.where(kept == 1, (lane >> 2) + 3 * below + (lane & 3), -1)
    kept, below, lane = places(sup, 0)
    mean_pos = jnp.where(kept == 1, -1, lane + 3 * below)
    start = first + 3 * jnp.sum((keep < first).astype(jnp.int32), axis=0, keepdims=True)
    flat = patches_ref[...]
    cuts = flat.shape[1] // 128
    sup_col = lax.broadcasted_iota(jnp.int32, (sup, rows), 0)
    sup_lane = lax.broadcasted_iota(jnp.int32, (sup, rows), 1) >> 2
    averaging = jnp.where(sup_col == sup_lane, 0.25, 0.0).astype(BF16)
    means = jnp.dot(averaging, flat, preferred_element_type=F32).astype(BF16)
    index = lax.broadcasted_iota(jnp.int32, (n * cuts * capacity, 1), 0)
    device, cut, slot = slot_of(index, n, capacity, cuts)
    pos = ((device - start) & (n - 1)) + slot * n
    total = jnp.zeros((n * cuts * capacity, 128), F32)
    for c in range(cuts):
        at = jnp.where(cut == c, pos, -2)
        features = slice(c * 128, (c + 1) * 128)
        total = (
            total
            + jnp.dot(one_hot(at == fine_pos), flat[:, features], preferred_element_type=F32)
            + jnp.dot(one_hot(at == mean_pos), means[:, features], preferred_element_type=F32)
        )
    out_ref[...] = total.astype(BF16)


def prep(scalars, keep_list, flat, n, sup, capacity):
    width = flat.shape[1] // 2
    shape = (n * capacity * width // 128, 128)
    return pl.pallas_call(
        functools.partial(prep_kernel, n, sup, capacity),
        grid_spec=pltpu.PrefetchScalarGridSpec(
            num_scalar_prefetch=1,
            grid=(1,),
            in_specs=[
                pl.BlockSpec(keep_list.shape, lambda i, ref: (0, 0)),
                pl.BlockSpec((flat.shape[0], width), lambda i, ref: (0, ref[1])),
            ],
            out_specs=pl.BlockSpec(shape, lambda i, ref: (0, 0)),
        ),
        out_shape=struct(shape),
        compiler_params=params(),
    )(scalars, keep_list, flat)


def pick_kernel(n, sup, per_owner, capacity, rank_ref, keep_ref, got_ref, out_ref):
    rank = rank_ref[0]
    keep = as_column(keep_ref[...])
    count = keep.shape[0]
    lanes = got_ref.shape[0]
    cuts = lanes // (n * capacity)
    source, _, _ = slot_of(
        lax.broadcasted_iota(jnp.int32, (count, lanes), 1), n, capacity, cuts
    )
    low = jnp.sum((keep < source * sup).astype(jnp.int32), axis=0, keepdims=True)
    high = jnp.sum((keep < source * sup + sup).astype(jnp.int32), axis=0, keepdims=True)
    source, cut, slot = slot_of(
        lax.broadcasted_iota(jnp.int32, (1, lanes), 1), n, capacity, cuts
    )
    start = source * sup + 3 * low
    stop = source * sup + sup + 3 * high
    token = start + ((rank - start) & (n - 1)) + slot * n
    row = jnp.where(token < stop, token >> (n.bit_length() - 1), -1)
    own = lax.broadcasted_iota(jnp.int32, (per_owner, lanes), 0)
    got = got_ref[...]
    for c in range(cuts):
        choose = one_hot(own == jnp.where(cut == c, row, -1))
        owned = jnp.dot(choose, got, preferred_element_type=F32).astype(BF16)
        out_ref[c * per_owner : (c + 1) * per_owner] = owned


def pick(scalars, keep_list, got, n, sup, per_owner, capacity):
    cuts = got.shape[0] // (n * capacity)
    return pl.pallas_call(
        functools.partial(pick_kernel, n, sup, per_owner, capacity),
        in_specs=[sspec(), vspec(), vspec()],
        out_specs=vspec(),
        out_shape=struct((cuts * per_owner, 128)),
        compiler_params=params(),
    )(scalars, keep_list, got)


def far_kernel(n, rank_ref, qkv_ref, out_weight_ref, up_ref, down_ref, away_ref, sem):
    rank, part = rank_ref[0], rank_ref[2]
    half = n // 2
    rows = up_ref.shape[0]
    wide = up_ref.shape[1] // n
    units = wide // 2
    long = out_weight_ref.shape[0] // 2
    depth = qkv_ref.shape[1] // 2
    each = depth + rows + units
    copies = []
    for d in range(half):
        dest = (rank // half ^ 1) * half + d
        low = d * each
        at = pl.ds(pl.multiple_of(part * depth, 32), depth)
        copies.append((qkv_ref.at[dest, at], away_ref.at[pl.ds(low, depth)]))
        at = pl.ds(pl.multiple_of(dest * wide + part * units, 128), units)
        copies.append((up_ref.at[:, at], away_ref.at[pl.ds(low + depth, rows)]))
        copies.append((down_ref.at[at], away_ref.at[pl.ds(low + depth + rows, units)]))
    at = pl.ds(pl.multiple_of(part * long, 128), long)
    copies.append((out_weight_ref.at[at], away_ref.at[pl.ds(half * each, long)]))
    run_copies(copies, sem)()


def near_kernel(n, rank_ref, qkv_ref, out_weight_ref, up_ref, down_ref, *refs):
    near, (heads_ref, sem) = refs[: n // 2], refs[n // 2 :]
    rank = rank_ref[0]
    half = n // 2
    rows = up_ref.shape[0]
    wide = up_ref.shape[1] // n
    units = wide // 2
    long = out_weight_ref.shape[0]
    copies = [(qkv_ref.at[pl.ds(rank // half * half, half)], heads_ref)]
    for j in range(half):
        dest = rank ^ j
        for c in range(2):
            at = pl.ds(pl.multiple_of(dest * wide + c * units, 128), units)
            copies.append((up_ref.at[:, at], near[j].at[pl.ds(c * rows, rows)]))
        at = pl.ds(pl.multiple_of(dest * wide, 128), wide)
        copies.append((down_ref.at[at], near[j].at[pl.ds(2 * rows, wide)]))
        copies.append((out_weight_ref, near[j].at[pl.ds(2 * rows + wide, long)]))
    run_copies(copies, sem)()


def pack(kernel, shapes, count, scalars, *weights):
    return pl.pallas_call(
        kernel,
        in_specs=[sspec()] + [hspec()] * 4,
        out_specs=[vspec()] * len(shapes),
        out_shape=[struct(shape) for shape in shapes],
        scratch_shapes=[pltpu.SemaphoreType.DMA((count,))],
    )(scalars, *weights)


def pack_far(scalars, qkv, out_weight, up, down, n):
    half = n // 2
    each = qkv.shape[1] // 2 + up.shape[0] + up.shape[1] // n // 2
    shapes = [(half * each + out_weight.shape[0] // 2, 128)]
    kernel = functools.partial(far_kernel, n)
    return pack(kernel, shapes, 3 * half + 1, scalars, qkv, out_weight, up, down)[0]


def pack_near(scalars, qkv, out_weight, up, down, n):
    half = n // 2
    near = (2 * up.shape[0] + up.shape[1] // n + out_weight.shape[0], 128)
    shapes = [near] * half + [(half,) + qkv.shape[1:]]
    kernel = functools.partial(near_kernel, n)
    outs = pack(kernel, shapes, 4 * half + 1, scalars, qkv, out_weight, up, down)
    return list(outs[:half]), outs[half]


def fan_kernel(owned_ref, across_ref, heads_ref, far_ref, out_ref):
    rows = owned_ref.shape[0]
    count, head_rows = heads_ref.shape[:2]
    top = 2 * rows + head_rows
    rest = out_ref.shape[1] - top
    each = (far_ref.shape[0] - rest) // (count - 1)
    for d in range(count):
        out_ref[d, :rows] = owned_ref[...]
        out_ref[d, rows : 2 * rows] = across_ref[...]
        out_ref[d, 2 * rows : top] = heads_ref[d]
        out_ref[d, top : top + each] = far_ref[d * each : (d + 1) * each]
        out_ref[d, top + each :] = far_ref[count * each :]


def fan(owned, across, heads, far, out_rows):
    count = heads.shape[0]
    each = (far.shape[0] - out_rows) // count
    shape = struct((count, 2 * owned.shape[0] + heads.shape[1] + each + out_rows, 128))
    return pl.pallas_call(
        fan_kernel,
        in_specs=[vspec()] * 4,
        out_specs=vspec(),
        out_shape=shape,
        compiler_params=params(8),
    )(owned, across, heads, far)


def source_of(rank, n, q, k):
    return (rank // (n // 2) ^ k) * (n // 2) + q


def norm_rows(x):
    average = jnp.mean(x, axis=-1, keepdims=True)
    power = jnp.mean(x * x, axis=-1, keepdims=True)
    return (x - average) * lax.rsqrt(power - average * average + 1e-06)


def attend_kernel(n, part, rank_ref, mine_ref, other_ref, far_ref, tokens_ref, out_ref, weight_ref):
    rank, half, group = rank_ref[0], rank_ref[1], rank_ref[2]
    rows = other_ref.shape[1] // 2
    cuts = rows // part
    width = cuts * 128
    depth = weight_ref.shape[0]
    piece = far_ref.shape[1]
    for q in range(n // 2):
        for k in range(2):
            source = source_of(rank, n, q, k)
            at = pl.ds(pl.multiple_of(source * part, part), part)
            for c in range(cuts):
                cut = slice(k * rows + c * part, k * rows + (c + 1) * part)
                to = pl.ds(pl.multiple_of(half * width + c * 128, 128), 128)
                tokens_ref[at, to] = mine_ref[q, cut]
                to = pl.ds(pl.multiple_of((1 - half) * width + c * 128, 128), 128)
                tokens_ref[at, to] = other_ref[q, cut]
        to = pl.ds(pl.multiple_of(source_of(rank, n, q, 0) * 128, 128), 128)
        weight_ref[:, to] = mine_ref[q, 2 * rows : 2 * rows + depth]
        to = pl.ds(pl.multiple_of(source_of(rank, n, q, 1) * 128, 128), 128)
        at = pl.ds(pl.multiple_of(group * piece, 32), piece)
        weight_ref[at, to] = mine_ref[q, 2 * rows + depth : 2 * rows + depth + piece]
        at = pl.ds(pl.multiple_of((1 - group) * piece, 32), piece)
        weight_ref[at, to] = far_ref[q]
    normed = norm_rows(tokens_ref[...].astype(F32)).astype(BF16)
    projected = lax.dot_general(
        normed, weight_ref[...], (((1,), (1,)), ((), ())), preferred_element_type=F32
    ).astype(BF16)
    size = projected.shape[1] // 3
    queries = projected[:, :size]
    keys = projected[:, size : 2 * size]
    values = projected[:, 2 * size :]
    scores = lax.dot_general(
        queries, keys, (((1,), (1,)), ((), ())), preferred_element_type=F32
    ) * (1.0 / math.sqrt(size))
    powers = jnp.exp(scores - jnp.max(scores, axis=1, keepdims=True))
    probs = (powers / jnp.sum(powers, axis=1, keepdims=True)).astype(BF16)
    attended = lax.dot_general(
        values, probs, (((0,), (1,)), ((), ())), preferred_element_type=F32
    ).astype(BF16)
    out_ref[...] = attended


def attend_fast(scalars, mine, other, far, head_rows, per_owner, n):
    length = n * per_owner
    depth = other.shape[1] // (2 * per_owner) * 256
    size = head_rows // 3
    return pl.pallas_call(
        functools.partial(attend_kernel, n, per_owner),
        in_specs=[sspec()] + [vspec()] * 3,
        out_specs=[vspec()] * 2,
        out_shape=[struct((length, depth)), struct((size, length))],
        scratch_shapes=[VMEM((head_rows, n * 128), BF16)],
        compiler_params=params(12),
        cost_estimate=cost(30),
    )(scalars, mine, other, far)


def mlp_kernel(n, rank_ref, tokens_ref, pieces, far, outs_far, near, outs, scratch):
    base_ref, away_ref, sends = outs[0], outs[1], outs[2:]
    up_ref, down_ref, row_ref, whole_ref, joined_ref, sem = scratch
    rank, half, group = rank_ref[0], rank_ref[1], rank_ref[2]
    block = up_ref.shape[0] // n
    wide = down_ref.shape[0] // 2
    unit = wide // 2
    size = pieces[0].shape[2]
    rows = outs_far[0][0].shape[1]
    first, later = [], []
    for j in range(n // 2):
        source = rank ^ j
        at = pl.ds(pl.multiple_of(source * block, block), block)
        to = pl.ds(pl.multiple_of(source * 128, 128), 128)
        for core in range(2):
            ref = near[core][j]
            for c in range(2):
                units = pl.ds(core * wide + c * unit, unit)
                later.append((ref.at[pl.ds(c * block, block)], up_ref.at[at, units]))
            units = pl.ds(core * wide, wide)
            later.append((ref.at[pl.ds(2 * block, wide)], down_ref.at[units, to]))
            rows_from = ref.at[pl.ds(2 * block + wide, 2 * rows)]
            first.append((rows_from, whole_ref.at[core, :, to]))
        source = source_of(rank, n, j, 1)
        at = pl.ds(pl.multiple_of(source * block, block), block)
        to = pl.ds(pl.multiple_of(source * 128, 128), 128)
        for core in range(2):
            for c in range(2):
                units = pl.ds(pl.multiple_of(core * wide + (group ^ c) * unit, unit), unit)
                later.append((far[core][c].at[j, pl.ds(0, block)], up_ref.at[at, units]))
                later.append((far[core][c].at[j, pl.ds(block, unit)], down_ref.at[units, to]))
                rows_to = pl.ds(pl.multiple_of((group ^ c) * rows, rows), rows)
                first.append((outs_far[core][c].at[j], whole_ref.at[core, rows_to, to]))
    wait_first = run_copies(first, sem)
    wait_later = run_copies(later, sem, len(first))
    for j in range(n // 2):
        for core in range(2):
            for k in range(2):
                at = pl.ds(pl.multiple_of((rank ^ j ^ (k * n // 2)) * size, size), size)
                joined_ref[core, at] = pieces[core][j, k]
    wait_first()
    dims = (((0,), (0,)), ((), ()))
    row_ref[...] = (
        tokens_ref[...].astype(F32)
        + lax.dot_general(joined_ref[0], whole_ref[0], dims, preferred_element_type=F32)
        + lax.dot_general(joined_ref[1], whole_ref[1], dims, preferred_element_type=F32)
    )
    part, width = base_ref.shape
    my_cols = pl.ds(pl.multiple_of(half * width, width), width)
    my_rows = pl.ds(pl.multiple_of(rank * part, part), part)
    normed = norm_rows(row_ref[...]).astype(BF16)
    base_ref[...] = row_ref[my_rows, my_cols]
    wait_later()
    raw = jnp.dot(normed, up_ref[...], preferred_element_type=F32)
    hidden = (0.5 * raw * (1.0 + lax.erf(raw * math.sqrt(0.5)))).astype(BF16)
    row_ref[:, :width] = jnp.dot(hidden, down_ref[:, my_cols], preferred_element_type=F32)
    base_ref[...] = base_ref[...] + row_ref[my_rows, :width]
    for j in range(n // 2):
        for k in range(2):
            owner = rank ^ j ^ (k * n // 2)
            term = row_ref[pl.ds(pl.multiple_of(owner * part, part), part), :width]
            if j > 0:
                sends[j - 1][k] = term.astype(BF16)
            elif k == 1:
                away_ref[...] = term


def mlp(scalars, tokens, pieces, far, outs_far, near, n):
    length, depth = tokens.shape
    width = depth // 2
    wide = 2 * (far[0][0].shape[1] - depth // n)
    inner = n * pieces[0].shape[2]
    half = n // 2

    def kernel(scalars, tokens, a, b, *refs):
        far, refs = (refs[:2], refs[2:4]), refs[4:]
        outs_far, refs = (refs[:2], refs[2:4]), refs[4:]
        near, refs = (refs[:half], refs[half:n]), refs[n:]
        mlp_kernel(n, scalars, tokens, (a, b), far, outs_far, near, refs[: half + 1], refs[half + 1 :])

    return pl.pallas_call(
        kernel,
        in_specs=[sspec()] + [vspec()] * 3 + [aspec()] * (8 + n),
        out_specs=[vspec()] * (half + 1),
        out_shape=[struct((length // n, width), F32)] * 2
        + [struct((2, length // n, width))] * (half - 1),
        scratch_shapes=[
            VMEM((depth, 2 * wide), BF16),
            VMEM((2 * wide, depth), BF16),
            VMEM((length, depth), F32),
            VMEM((2, inner, depth), BF16),
            VMEM((2, inner, length), BF16),
            pltpu.SemaphoreType.DMA((20 * half,)),
        ],
        compiler_params=params(24),
    )(scalars, tokens, *pieces, *far[0], *far[1], *outs_far[0], *outs_far[1], *near[0], *near[1])


def sum_kernel(base_ref, away_ref, *refs):
    terms, (base_out, away_out) = refs[:-2], refs[-2:]
    base, away = base_ref[...], away_ref[...]
    for ref in terms:
        base = base + ref[0].astype(F32)
        away = away + ref[1].astype(F32)
    base_out[...] = base
    away_out[...] = away.astype(BF16)


def sum_terms(base, away, terms):
    return pl.pallas_call(
        sum_kernel,
        in_specs=[vspec()] * (2 + len(terms)),
        out_specs=[vspec()] * 2,
        out_shape=[struct(base.shape, F32), struct(away.shape)],
        compiler_params=params(),
    )(base, away, *terms)


def last_kernel(base_ref, across_ref, out_ref):
    out_ref[...] = (base_ref[...] + across_ref[...].astype(F32)).astype(BF16)


def last(base, across):
    return pl.pallas_call(
        last_kernel,
        in_specs=[vspec()] * 2,
        out_specs=vspec(),
        out_shape=struct(base.shape),
        compiler_params=params(),
    )(base, across)


def swap(value, axis, j):
    n = lax.axis_size(axis)
    return lax.ppermute(value, axis, [(i, i ^ j) for i in range(n)])


def exchange(value):
    return lax.all_to_all(value, "seq", split_axis=0, concat_axis=0, tiled=True)


def exchange_half(value):
    n = lax.axis_size("seq")
    groups = [list(range(n // 2)), list(range(n // 2, n))]
    return lax.all_to_all(
        value, "seq", split_axis=0, concat_axis=0, axis_index_groups=groups, tiled=True
    )


def after(value, *others):
    return lax.optimization_barrier((value, *others))[0]


def local_fast(patches, keep_list, qkv_weight, out_weight, up_weight, down_weight):
    n = lax.axis_size("seq")
    rank, head, group = (
        lax.axis_index(name).astype(jnp.int32) for name in ("seq", "head", "groups")
    )
    scalars = jnp.stack([rank, head, group])
    half = n // 2
    sup, depth = patches.shape[1], patches.shape[3]
    length = sup * n * 8 // 5
    per_owner = length // n
    half_width = depth // 2
    head_rows = qkv_weight.shape[2]
    capacity = (4 * sup + n - 1) // n
    flat = patches.reshape(4 * sup, depth)
    heads = qkv_weight.transpose(1, 2, 0)

    weights = (heads, out_weight, up_weight, down_weight)
    away = pack_far(scalars, *weights, n)
    far = swap(away, "seq", half)
    slots = prep(scalars, keep_list, after(flat, away), n, sup, capacity)
    dealt = exchange(slots)
    weights = lax.optimization_barrier((*weights, slots))[:4]
    near, qkv_near = pack_near(scalars, *weights, n)
    near = [near[0]] + [swap(near[j], "seq", j) for j in range(1, half)]
    owned = pick(scalars, keep_list, dealt, n, sup, per_owner, capacity)
    across = swap(owned, "seq", half)
    across, far, *near = lax.optimization_barrier((across, far, *near))

    out_rows = out_weight.shape[0] // 2
    got = exchange_half(fan(owned, across, qkv_near, far, out_rows))
    near_other = [swap(block, "head", 1) for block in near]
    got, *near_other = lax.optimization_barrier((got, *near_other))

    top = 2 * owned.shape[0]
    pieces_other = swap(got[:, :top], "head", 1)
    top = top + head_rows
    qkv_far = swap(got[:, top : top + head_rows // 2], "groups", 1)
    tokens, attended = attend_fast(
        scalars, got, pieces_other, qkv_far, head_rows, per_owner, n
    )

    att_across = swap(attended, "seq", half)
    got = after(got, attended)
    mlp_mine = got[:, top + head_rows // 2 : got.shape[1] - out_rows]
    far_mine = got[:, got.shape[1] - out_rows :]
    far_other = swap(far_mine, "groups", 1)
    mlp_other = swap(mlp_mine, "groups", 1)
    pair = jnp.stack([attended, att_across])
    pairs = [swap(pair, "seq", j) for j in range(1, half)]
    mlp_other, far_other, *pairs = lax.optimization_barrier((mlp_other, far_other, *pairs))
    gathered = jnp.stack([pair] + pairs)
    mlp_pair = (mlp_mine, mlp_other)
    far_pair = (far_mine, far_other)
    base, term_away, *terms = mlp(
        scalars,
        tokens,
        (gathered, swap(gathered, "head", 1)),
        (mlp_pair, tuple(swap(value, "head", 1) for value in mlp_pair)),
        (far_pair, tuple(swap(value, "head", 1) for value in far_pair)),
        (near, near_other),
        n,
    )
    terms = [swap(terms[j - 1], "seq", j) for j in range(1, half)]
    base, term_away = sum_terms(base, term_away, terms)
    encoded = last(base, swap(term_away, "seq", half))
    return encoded.reshape(1, per_owner, 1, half_width)


def local(patches, keep_list, qkv_weight, out_weight, up_weight, down_weight):
    n = lax.axis_size("seq")
    one_image = patches.shape[0] == 1 and qkv_weight.shape[1] == n and n & (n - 1) == 0
    one_image = one_image and lax.axis_size("groups") == 2 and up_weight.shape[1] == n * 256
    plan = local_fast if one_image else local_general
    return plan(patches, keep_list, qkv_weight, out_weight, up_weight, down_weight)


def solution(mesh):
    return jax.shard_map(
        local,
        mesh=mesh,
        in_specs=(
            P("groups", "seq", None, None),
            P("groups", None),
            P("seq", "head", None),
            P("head", "seq"),
            P("seq", "head"),
            P("head", "seq"),
        ),
        out_specs=P("groups", None, "seq", "head"),
        check_vma=False,
    )
```

```python
import functools
import math

import jax
import jax.numpy as jnp
from jax import lax
from jax.experimental import pallas as pl
from jax.experimental.pallas import tpu as pltpu
from jax.sharding import PartitionSpec as P

F32 = jnp.float32
BF16 = jnp.bfloat16
VMEM = pltpu.VMEM

def layer_norm(matrix):
    average = jnp.mean(matrix, axis=-1, keepdims=True)
    power = jnp.mean(matrix * matrix, axis=-1, keepdims=True)
    return (matrix - average) * lax.rsqrt(power - average * average + 1e-06)


def attend(queries, keys, values):
    length = queries.shape[0]
    block = math.gcd(length, 512)
    scale = 1.0 / math.sqrt(queries.shape[1])

    def one_block(query_rows):
        scores = (
            lax.dot_general(
                query_rows, keys, (((1,), (1,)), ((), ())), preferred_element_type=jnp.float32
            )
            * scale
        )
        top = jnp.max(scores, axis=1, keepdims=True)
        powers = jnp.exp(scores - top)
        probs = (powers / jnp.sum(powers, axis=1, keepdims=True)).astype(jnp.bfloat16)
        return jnp.dot(probs, values, preferred_element_type=jnp.float32).astype(jnp.bfloat16)

    blocks = lax.map(one_block, queries.reshape(length // block, block, queries.shape[1]))
    return blocks.reshape(length, values.shape[1])


def local_general(patches, keep_list, qkv_weight, out_weight, up_weight, down_weight):
    seq_count = lax.axis_size("seq")
    seq_rank = lax.axis_index("seq")
    head_rank = lax.axis_index("head")
    images = patches.shape[0]
    sup_local = patches.shape[1]
    depth = patches.shape[3]
    half_width = depth // lax.axis_size("head")
    head_count = qkv_weight.shape[1]
    seq_length = sup_local * seq_count * 8 // 5
    per_owner = seq_length // seq_count
    capacity = (4 * sup_local + seq_count - 1) // seq_count
    slot_count = 4 * sup_local
    image_index = jnp.arange(images, dtype=jnp.int32)
    bounds = jnp.arange(seq_count + 1, dtype=jnp.int32) * sup_local
    before = jnp.sum((keep_list[:, :, None] < bounds[None, None, :]).astype(jnp.int32), axis=1)
    starts = bounds[None, :seq_count] + 3 * before[:, :seq_count]
    lengths = sup_local + 3 * (before[:, 1:] - before[:, :seq_count])
    my_start = lax.dynamic_index_in_dim(starts, seq_rank, 1, keepdims=False)
    my_length = lax.dynamic_index_in_dim(lengths, seq_rank, 1, keepdims=False)
    local_ids = seq_rank * sup_local + jnp.arange(sup_local, dtype=jnp.int32)
    kept_flag = jnp.any(keep_list[:, None, :] == local_ids[None, :, None], axis=2).astype(jnp.int32)
    offsets = jnp.arange(sup_local, dtype=jnp.int32)[None, :] + 3 * (
        jnp.cumsum(kept_flag, axis=1) - kept_flag
    )
    slot_ids = jnp.arange(slot_count, dtype=jnp.int32)
    owner_patch = (
        jnp.sum((offsets[:, None, :] <= slot_ids[None, :, None]).astype(jnp.int32), axis=2) - 1
    )
    start_of = jnp.take_along_axis(offsets, owner_patch, axis=1)
    sub_index = jnp.minimum(slot_ids[None, :] - start_of, 3)
    kept_of = jnp.take_along_axis(kept_flag, owner_patch, axis=1)
    flat_patches = patches.reshape(images, sup_local * 4, depth)
    fine_rows = flat_patches[
        image_index[:, None], owner_patch * 4 + jnp.where(kept_of == 1, sub_index, 0)
    ]
    mean_rows = jnp.mean(patches.astype(jnp.float32), axis=2).astype(jnp.bfloat16)
    shared_rows = mean_rows[image_index[:, None], owner_patch]
    local_tokens = jnp.where((kept_of == 1)[:, :, None], fine_rows, shared_rows)
    destinations = jnp.arange(seq_count, dtype=jnp.int32)[:, None, None]
    depth_slots = jnp.arange(capacity, dtype=jnp.int32)[None, None, :]
    positions = (destinations - my_start[None, :, None]) % seq_count + depth_slots * seq_count
    valid = positions < my_length[None, :, None]
    outgoing = local_tokens[image_index[None, :, None], jnp.minimum(positions, slot_count - 1)]
    outgoing = jnp.where(valid[:, :, :, None], outgoing, jnp.zeros((), jnp.bfloat16))
    incoming = lax.all_to_all(outgoing, "seq", split_axis=0, concat_axis=0, tiled=True)
    owned = jnp.arange(per_owner, dtype=jnp.int32) * seq_count + seq_rank
    source = jnp.sum((starts[:, None, :] <= owned[None, :, None]).astype(jnp.int32), axis=2) - 1
    first_of = jnp.take_along_axis(starts, source, axis=1)
    depth_of = (owned[None, :] - first_of) // seq_count
    resident = incoming[source, image_index[:, None], depth_of]
    start_rows = resident.reshape(images * per_owner, depth)
    start_float = start_rows.astype(jnp.float32)
    qkv_full, out_full, up_full, down_full = (
        lax.all_gather(qkv_weight, "seq", axis=0, tiled=True),
        lax.all_gather(out_weight, "seq", axis=1, tiled=True),
        lax.all_gather(up_weight, "seq", axis=0, tiled=True),
        lax.all_gather(down_weight, "seq", axis=1, tiled=True),
    )
    normed = layer_norm(start_float).astype(jnp.bfloat16).reshape(images, per_owner, depth)
    projected = jnp.einsum("ipd,dhc->ihpc", normed, qkv_full, preferred_element_type=jnp.float32)
    head_size = qkv_weight.shape[2] // 3
    sending = projected.astype(jnp.bfloat16).reshape(seq_count, per_owner, 3 * head_size)
    gathered = lax.all_to_all(sending, "seq", split_axis=0, concat_axis=0, tiled=True).reshape(
        seq_length, 3 * head_size
    )
    attended = attend(
        gathered[:, :head_size],
        gathered[:, head_size : 2 * head_size],
        gathered[:, 2 * head_size :],
    )
    returned = lax.all_to_all(
        attended.reshape(seq_count, per_owner, head_size),
        "seq",
        split_axis=0,
        concat_axis=0,
        tiled=True,
    )
    returned = returned.reshape(images, head_count, per_owner, head_size)
    partial_sum = jnp.einsum(
        "ihpc,hcd->ipd",
        returned,
        out_full.reshape(head_count, head_size, depth),
        preferred_element_type=jnp.float32,
    ).reshape(images * per_owner, depth)
    attn_total = lax.psum(partial_sum, "head")
    residual = start_float + attn_total
    residual_half = lax.dynamic_slice_in_dim(residual, head_rank * half_width, half_width, 1)
    normed_two = layer_norm(residual).astype(jnp.bfloat16)
    hidden = jax.nn.gelu(
        jnp.dot(normed_two, up_full, preferred_element_type=jnp.float32), approximate=False
    ).astype(jnp.bfloat16)
    mlp_terms = jnp.dot(hidden, down_full, preferred_element_type=jnp.float32)
    mlp_part = lax.psum_scatter(mlp_terms, "head", scatter_dimension=1, tiled=True)
    encoded = (residual_half + mlp_part).astype(jnp.bfloat16)
    return encoded.reshape(images, per_owner, 1, half_width)


def vspec():
    return pl.BlockSpec(memory_space=VMEM)


def aspec():
    return pl.BlockSpec(memory_space=pl.ANY)


def sspec():
    return pl.BlockSpec(memory_space=pltpu.SMEM)


def hspec():
    return pl.BlockSpec(memory_space=pltpu.HBM)


def run_copies(copies, sem, base=0):
    started = [
        pltpu.make_async_copy(src, dst, sem.at[base + i]) for i, (src, dst) in enumerate(copies)
    ]
    for copy in started:
        copy.start()

    def wait():
        for copy in started:
            copy.wait()

    return wait


def params(mebibytes=4):
    return pltpu.CompilerParams(vmem_limit_bytes=mebibytes * 1024 * 1024)


def cost(micros):
    return pl.CostEstimate(flops=micros * 10**9, bytes_accessed=1 << 20, transcendentals=0)


def struct(shape, dtype=BF16):
    return jax.ShapeDtypeStruct(shape, dtype)


def slot_of(index, n, capacity, cuts):
    device = sum(((index >= j * cuts * capacity).astype(jnp.int32) for j in range(1, n)), 0 * index)
    inner = index - device * (cuts * capacity)
    cut = sum(((inner >= c * capacity).astype(jnp.int32) for c in range(1, cuts)), 0 * index)
    return device, cut, inner - cut * capacity


def as_column(row):
    count = row.shape[1]
    same = lax.broadcasted_iota(jnp.int32, (count, count), 0) == lax.broadcasted_iota(
        jnp.int32, (count, count), 1
    )
    return jnp.sum(jnp.where(same, row, 0), axis=1, keepdims=True)


def one_hot(mask):
    return mask.astype(F32).astype(BF16)


def prep_kernel(n, sup, capacity, rank_ref, keep_ref, patches_ref, out_ref):
    rank = rank_ref[0]
    first = rank * sup
    keep = as_column(keep_ref[...])
    rows = 4 * sup
    count = keep.shape[0]

    def places(width, shift):
        ids = lax.broadcasted_iota(jnp.int32, (count, width), 1) >> shift
        kept = jnp.sum((keep == first + ids).astype(jnp.int32), axis=0, keepdims=True)
        below = jnp.sum(
            jnp.logical_and(keep >= first, keep < first + ids).astype(jnp.int32),
            axis=0,
            keepdims=True,
        )
        return kept, below, lax.broadcasted_iota(jnp.int32, (1, width), 1)

    kept, below, lane = places(rows, 2)
    fine_pos = jnp.where(kept == 1, (lane >> 2) + 3 * below + (lane & 3), -1)
    kept, below, lane = places(sup, 0)
    mean_pos = jnp.where(kept == 1, -1, lane + 3 * below)
    start = first + 3 * jnp.sum((keep < first).astype(jnp.int32), axis=0, keepdims=True)
    flat = patches_ref[...]
    cuts = flat.shape[1] // 128
    sup_col = lax.broadcasted_iota(jnp.int32, (sup, rows), 0)
    sup_lane = lax.broadcasted_iota(jnp.int32, (sup, rows), 1) >> 2
    averaging = jnp.where(sup_col == sup_lane, 0.25, 0.0).astype(BF16)
    means = jnp.dot(averaging, flat, preferred_element_type=F32).astype(BF16)
    index = lax.broadcasted_iota(jnp.int32, (n * cuts * capacity, 1), 0)
    device, cut, slot = slot_of(index, n, capacity, cuts)
    pos = ((device - start) & (n - 1)) + slot * n
    total = jnp.zeros((n * cuts * capacity, 128), F32)
    for c in range(cuts):
        at = jnp.where(cut == c, pos, -2)
        features = slice(c * 128, (c + 1) * 128)
        total = (
            total
            + jnp.dot(one_hot(at == fine_pos), flat[:, features], preferred_element_type=F32)
            + jnp.dot(one_hot(at == mean_pos), means[:, features], preferred_element_type=F32)
        )
    out_ref[...] = total.astype(BF16)


def prep(scalars, keep_list, flat, n, sup, capacity):
    width = flat.shape[1] // 2
    shape = (n * capacity * width // 128, 128)
    return pl.pallas_call(
        functools.partial(prep_kernel, n, sup, capacity),
        grid_spec=pltpu.PrefetchScalarGridSpec(
            num_scalar_prefetch=1,
            grid=(1,),
            in_specs=[
                pl.BlockSpec(keep_list.shape, lambda i, ref: (0, 0)),
                pl.BlockSpec((flat.shape[0], width), lambda i, ref: (0, ref[1])),
            ],
            out_specs=pl.BlockSpec(shape, lambda i, ref: (0, 0)),
        ),
        out_shape=struct(shape),
        compiler_params=params(),
    )(scalars, keep_list, flat)


def pick_kernel(n, sup, per_owner, capacity, rank_ref, keep_ref, got_ref, out_ref):
    rank = rank_ref[0]
    keep = as_column(keep_ref[...])
    count = keep.shape[0]
    lanes = got_ref.shape[0]
    cuts = lanes // (n * capacity)
    source, _, _ = slot_of(
        lax.broadcasted_iota(jnp.int32, (count, lanes), 1), n, capacity, cuts
    )
    low = jnp.sum((keep < source * sup).astype(jnp.int32), axis=0, keepdims=True)
    high = jnp.sum((keep < source * sup + sup).astype(jnp.int32), axis=0, keepdims=True)
    source, cut, slot = slot_of(
        lax.broadcasted_iota(jnp.int32, (1, lanes), 1), n, capacity, cuts
    )
    start = source * sup + 3 * low
    stop = source * sup + sup + 3 * high
    token = start + ((rank - start) & (n - 1)) + slot * n
    row = jnp.where(token < stop, token >> (n.bit_length() - 1), -1)
    own = lax.broadcasted_iota(jnp.int32, (per_owner, lanes), 0)
    got = got_ref[...]
    for c in range(cuts):
        choose = one_hot(own == jnp.where(cut == c, row, -1))
        owned = jnp.dot(choose, got, preferred_element_type=F32).astype(BF16)
        out_ref[c * per_owner : (c + 1) * per_owner] = owned


def pick(scalars, keep_list, got, n, sup, per_owner, capacity):
    cuts = got.shape[0] // (n * capacity)
    return pl.pallas_call(
        functools.partial(pick_kernel, n, sup, per_owner, capacity),
        in_specs=[sspec(), vspec(), vspec()],
        out_specs=vspec(),
        out_shape=struct((cuts * per_owner, 128)),
        compiler_params=params(),
    )(scalars, keep_list, got)


def far_kernel(n, rank_ref, qkv_ref, out_weight_ref, up_ref, down_ref, away_ref, sem):
    rank, part = rank_ref[0], rank_ref[2]
    half = n // 2
    rows = up_ref.shape[0]
    wide = up_ref.shape[1] // n
    units = wide // 2
    long = out_weight_ref.shape[0] // 2
    depth = qkv_ref.shape[1] // 2
    each = depth + rows + units
    copies = []
    for d in range(half):
        dest = (rank // half ^ 1) * half + d
        low = d * each
        at = pl.ds(pl.multiple_of(part * depth, 32), depth)
        copies.append((qkv_ref.at[dest, at], away_ref.at[pl.ds(low, depth)]))
        at = pl.ds(pl.multiple_of(dest * wide + part * units, 128), units)
        copies.append((up_ref.at[:, at], away_ref.at[pl.ds(low + depth, rows)]))
        copies.append((down_ref.at[at], away_ref.at[pl.ds(low + depth + rows, units)]))
    at = pl.ds(pl.multiple_of(part * long, 128), long)
    copies.append((out_weight_ref.at[at], away_ref.at[pl.ds(half * each, long)]))
    run_copies(copies, sem)()


def near_kernel(n, rank_ref, qkv_ref, out_weight_ref, up_ref, down_ref, *refs):
    near, sem = refs[: n // 2], refs[n // 2]
    rank, part = rank_ref[0], rank_ref[2]
    rows = up_ref.shape[0]
    wide = up_ref.shape[1] // n
    units = wide // 2
    long = out_weight_ref.shape[0] // 2
    copies = []
    for j in range(n // 2):
        dest = rank ^ j
        at = pl.ds(pl.multiple_of(dest * wide + part * units, 128), units)
        copies.append((up_ref.at[:, at], near[j].at[pl.ds(0, rows)]))
        copies.append((down_ref.at[at], near[j].at[pl.ds(rows, units)]))
        at = pl.ds(pl.multiple_of(part * long, 128), long)
        copies.append((out_weight_ref.at[at], near[j].at[pl.ds(rows + units, long)]))
        low = rows + units + long
        copies.append((qkv_ref.at[dest], near[j].at[pl.ds(low, qkv_ref.shape[1])]))
    run_copies(copies, sem)()


def pack(kernel, shapes, count, scalars, *weights):
    return pl.pallas_call(
        kernel,
        in_specs=[sspec()] + [hspec()] * 4,
        out_specs=[vspec()] * len(shapes),
        out_shape=[struct(shape) for shape in shapes],
        scratch_shapes=[pltpu.SemaphoreType.DMA((count,))],
    )(scalars, *weights)


def pack_far(scalars, qkv, out_weight, up, down, n):
    half = n // 2
    each = qkv.shape[1] // 2 + up.shape[0] + up.shape[1] // n // 2
    shapes = [(half * each + out_weight.shape[0] // 2, 128)]
    kernel = functools.partial(far_kernel, n)
    return pack(kernel, shapes, 3 * half + 1, scalars, qkv, out_weight, up, down)[0]


def pack_near(scalars, qkv, out_weight, up, down, n):
    half = n // 2
    rows = up.shape[0] + up.shape[1] // n // 2 + out_weight.shape[0] // 2 + qkv.shape[1]
    kernel = functools.partial(near_kernel, n)
    return pack(kernel, [(rows, 128)] * half, 4 * half, scalars, qkv, out_weight, up, down)


def fan_kernel(owned_ref, across_ref, far_ref, out_ref):
    rows = owned_ref.shape[0]
    count = out_ref.shape[0]
    top = 2 * rows
    rest = out_ref.shape[1] - top
    each = (far_ref.shape[0] - rest) // (count - 1)
    for d in range(count):
        out_ref[d, :rows] = owned_ref[...]
        out_ref[d, rows:top] = across_ref[...]
        out_ref[d, top : top + each] = far_ref[d * each : (d + 1) * each]
        out_ref[d, top + each :] = far_ref[count * each :]


def fan(owned, across, far, out_rows, count):
    each = (far.shape[0] - out_rows) // count
    shape = struct((count, 2 * owned.shape[0] + each + out_rows, 128))
    return pl.pallas_call(
        fan_kernel,
        in_specs=[vspec()] * 3,
        out_specs=vspec(),
        out_shape=shape,
        compiler_params=params(8),
    )(owned, across, far)


def source_of(rank, n, q, k):
    return (rank // (n // 2) ^ k) * (n // 2) + q


def norm_rows(x):
    average = jnp.mean(x, axis=-1, keepdims=True)
    power = jnp.mean(x * x, axis=-1, keepdims=True)
    return (x - average) * lax.rsqrt(power - average * average + 1e-06)


def attend_kernel(
    n, part, rank_ref, mine_ref, other_ref, near_ref, far_ref, tokens_ref, out_ref, weight_ref
):
    rank, half, group = rank_ref[0], rank_ref[1], rank_ref[2]
    rows = other_ref.shape[1] // 2
    cuts = rows // part
    width = cuts * 128
    depth = weight_ref.shape[0]
    piece = far_ref.shape[1]
    for q in range(n // 2):
        for k in range(2):
            source = source_of(rank, n, q, k)
            at = pl.ds(pl.multiple_of(source * part, part), part)
            for c in range(cuts):
                cut = slice(k * rows + c * part, k * rows + (c + 1) * part)
                to = pl.ds(pl.multiple_of(half * width + c * 128, 128), 128)
                tokens_ref[at, to] = mine_ref[q, cut]
                to = pl.ds(pl.multiple_of((1 - half) * width + c * 128, 128), 128)
                tokens_ref[at, to] = other_ref[q, cut]
        to = pl.ds(pl.multiple_of((rank ^ q) * 128, 128), 128)
        weight_ref[:, to] = near_ref[q]
        to = pl.ds(pl.multiple_of(source_of(rank, n, q, 1) * 128, 128), 128)
        at = pl.ds(pl.multiple_of(group * piece, 32), piece)
        weight_ref[at, to] = mine_ref[q, 2 * rows : 2 * rows + piece]
        at = pl.ds(pl.multiple_of((1 - group) * piece, 32), piece)
        weight_ref[at, to] = far_ref[q]
    normed = norm_rows(tokens_ref[...].astype(F32)).astype(BF16)
    projected = lax.dot_general(
        normed, weight_ref[...], (((1,), (1,)), ((), ())), preferred_element_type=F32
    ).astype(BF16)
    size = projected.shape[1] // 3
    queries = projected[:, :size]
    keys = projected[:, size : 2 * size]
    values = projected[:, 2 * size :]
    scores = lax.dot_general(
        queries, keys, (((1,), (1,)), ((), ())), preferred_element_type=F32
    ) * (1.0 / math.sqrt(size))
    powers = jnp.exp(scores - jnp.max(scores, axis=1, keepdims=True))
    probs = (powers / jnp.sum(powers, axis=1, keepdims=True)).astype(BF16)
    attended = lax.dot_general(
        values, probs, (((0,), (1,)), ((), ())), preferred_element_type=F32
    ).astype(BF16)
    out_ref[...] = attended


def attend_fast(scalars, mine, other, near, far, head_rows, per_owner, n):
    length = n * per_owner
    depth = other.shape[1] // (2 * per_owner) * 256
    size = head_rows // 3
    return pl.pallas_call(
        functools.partial(attend_kernel, n, per_owner),
        in_specs=[sspec()] + [vspec()] * 4,
        out_specs=[vspec()] * 2,
        out_shape=[struct((length, depth)), struct((size, length))],
        scratch_shapes=[VMEM((head_rows, n * 128), BF16)],
        compiler_params=params(12),
        cost_estimate=cost(30),
    )(scalars, mine, other, near, far)


def mlp_kernel(n, rank_ref, tokens_ref, pieces, far, outs_far, near, outs, scratch):
    base_ref, away_ref, sends = outs[0], outs[1], outs[2:]
    up_ref, down_ref, row_ref, whole_ref, joined_ref, sem = scratch
    rank, half, group = rank_ref[0], rank_ref[1], rank_ref[2]
    block = up_ref.shape[0] // n
    wide = down_ref.shape[0] // 2
    unit = wide // 2
    size = pieces[0].shape[2]
    rows = outs_far[0][0].shape[1]
    first, later = [], []
    for j in range(n // 2):
        source = rank ^ j
        at = pl.ds(pl.multiple_of(source * block, block), block)
        to = pl.ds(pl.multiple_of(source * 128, 128), 128)
        for core in range(2):
            for c in range(2):
                ref = near[core][c]
                units = pl.ds(pl.multiple_of(core * wide + (group ^ c) * unit, unit), unit)
                later.append((ref.at[j, pl.ds(0, block)], up_ref.at[at, units]))
                later.append((ref.at[j, pl.ds(block, unit)], down_ref.at[units, to]))
                rows_to = pl.ds(pl.multiple_of((group ^ c) * rows, rows), rows)
                rows_from = ref.at[j, pl.ds(block + unit, rows)]
                first.append((rows_from, whole_ref.at[core, rows_to, to]))
        source = source_of(rank, n, j, 1)
        at = pl.ds(pl.multiple_of(source * block, block), block)
        to = pl.ds(pl.multiple_of(source * 128, 128), 128)
        for core in range(2):
            for c in range(2):
                units = pl.ds(pl.multiple_of(core * wide + (group ^ c) * unit, unit), unit)
                later.append((far[core][c].at[j, pl.ds(0, block)], up_ref.at[at, units]))
                later.append((far[core][c].at[j, pl.ds(block, unit)], down_ref.at[units, to]))
                rows_to = pl.ds(pl.multiple_of((group ^ c) * rows, rows), rows)
                first.append((outs_far[core][c].at[j], whole_ref.at[core, rows_to, to]))
    wait_first = run_copies(first, sem)
    wait_later = run_copies(later, sem, len(first))
    for j in range(n // 2):
        for core in range(2):
            for k in range(2):
                at = pl.ds(pl.multiple_of((rank ^ j ^ (k * n // 2)) * size, size), size)
                joined_ref[core, at] = pieces[core][j, k]
    wait_first()
    dims = (((0,), (0,)), ((), ()))
    row_ref[...] = (
        tokens_ref[...].astype(F32)
        + lax.dot_general(joined_ref[0], whole_ref[0], dims, preferred_element_type=F32)
        + lax.dot_general(joined_ref[1], whole_ref[1], dims, preferred_element_type=F32)
    )
    part, width = base_ref.shape
    my_cols = pl.ds(pl.multiple_of(half * width, width), width)
    my_rows = pl.ds(pl.multiple_of(rank * part, part), part)
    normed = norm_rows(row_ref[...]).astype(BF16)
    base_ref[...] = row_ref[my_rows, my_cols]
    wait_later()
    raw = jnp.dot(normed, up_ref[...], preferred_element_type=F32)
    hidden = (0.5 * raw * (1.0 + lax.erf(raw * math.sqrt(0.5)))).astype(BF16)
    row_ref[:, :width] = jnp.dot(hidden, down_ref[:, my_cols], preferred_element_type=F32)
    base_ref[...] = base_ref[...] + row_ref[my_rows, :width]
    for j in range(n // 2):
        for k in range(2):
            owner = rank ^ j ^ (k * n // 2)
            term = row_ref[pl.ds(pl.multiple_of(owner * part, part), part), :width]
            if j > 0:
                sends[j - 1][k] = term.astype(BF16)
            elif k == 1:
                away_ref[...] = term


def mlp(scalars, tokens, pieces, far, outs_far, near, n):
    length, depth = tokens.shape
    width = depth // 2
    wide = 2 * (far[0][0].shape[1] - depth // n)
    inner = n * pieces[0].shape[2]
    half = n // 2

    def kernel(scalars, tokens, a, b, *refs):
        far, refs = (refs[:2], refs[2:4]), refs[4:]
        outs_far, refs = (refs[:2], refs[2:4]), refs[4:]
        near, refs = (refs[:2], refs[2:4]), refs[4:]
        mlp_kernel(n, scalars, tokens, (a, b), far, outs_far, near, refs[: half + 1], refs[half + 1 :])

    return pl.pallas_call(
        kernel,
        in_specs=[sspec()] + [vspec()] * 3 + [aspec()] * 12,
        out_specs=[vspec()] * (half + 1),
        out_shape=[struct((length // n, width), F32)] * 2
        + [struct((2, length // n, width))] * (half - 1),
        scratch_shapes=[
            VMEM((depth, 2 * wide), BF16),
            VMEM((2 * wide, depth), BF16),
            VMEM((length, depth), F32),
            VMEM((2, inner, depth), BF16),
            VMEM((2, inner, length), BF16),
            pltpu.SemaphoreType.DMA((24 * half,)),
        ],
        compiler_params=params(24),
    )(scalars, tokens, *pieces, *far[0], *far[1], *outs_far[0], *outs_far[1], *near[0], *near[1])


def sum_kernel(base_ref, away_ref, *refs):
    terms, (base_out, away_out) = refs[:-2], refs[-2:]
    base, away = base_ref[...], away_ref[...]
    for ref in terms:
        base = base + ref[0].astype(F32)
        away = away + ref[1].astype(F32)
    base_out[...] = base
    away_out[...] = away.astype(BF16)


def sum_terms(base, away, terms):
    return pl.pallas_call(
        sum_kernel,
        in_specs=[vspec()] * (2 + len(terms)),
        out_specs=[vspec()] * 2,
        out_shape=[struct(base.shape, F32), struct(away.shape)],
        compiler_params=params(),
    )(base, away, *terms)


def last_kernel(base_ref, across_ref, out_ref):
    out_ref[...] = (base_ref[...] + across_ref[...].astype(F32)).astype(BF16)


def last(base, across):
    return pl.pallas_call(
        last_kernel,
        in_specs=[vspec()] * 2,
        out_specs=vspec(),
        out_shape=struct(base.shape),
        compiler_params=params(),
    )(base, across)


def swap(value, axis, j):
    n = lax.axis_size(axis)
    return lax.ppermute(value, axis, [(i, i ^ j) for i in range(n)])


def exchange(value):
    return lax.all_to_all(value, "seq", split_axis=0, concat_axis=0, tiled=True)


def exchange_half(value):
    n = lax.axis_size("seq")
    groups = [list(range(n // 2)), list(range(n // 2, n))]
    return lax.all_to_all(
        value, "seq", split_axis=0, concat_axis=0, axis_index_groups=groups, tiled=True
    )


def after(value, *others):
    return lax.optimization_barrier((value, *others))[0]


def local_fast(patches, keep_list, qkv_weight, out_weight, up_weight, down_weight):
    n = lax.axis_size("seq")
    rank, head, group = (
        lax.axis_index(name).astype(jnp.int32) for name in ("seq", "head", "groups")
    )
    scalars = jnp.stack([rank, head, group])
    half = n // 2
    sup, depth = patches.shape[1], patches.shape[3]
    length = sup * n * 8 // 5
    per_owner = length // n
    half_width = depth // 2
    head_rows = qkv_weight.shape[2]
    capacity = (4 * sup + n - 1) // n
    flat = patches.reshape(4 * sup, depth)
    heads = qkv_weight.transpose(1, 2, 0)

    weights = (heads, out_weight, up_weight, down_weight)
    away = pack_far(scalars, *weights, n)
    far = swap(away, "seq", half)
    slots = prep(scalars, keep_list, after(flat, away), n, sup, capacity)
    dealt = exchange(slots)
    weights = lax.optimization_barrier((*weights, slots))[:4]
    near = pack_near(scalars, *weights, n)
    near = [near[0]] + [swap(near[j], "seq", j) for j in range(1, half)]
    owned = pick(scalars, keep_list, dealt, n, sup, per_owner, capacity)
    across = swap(owned, "seq", half)
    across, far, *near = lax.optimization_barrier((across, far, *near))

    out_rows = out_weight.shape[0] // 2
    got = exchange_half(fan(owned, across, far, out_rows, half))
    near_qkv = jnp.stack([block[block.shape[0] - head_rows :] for block in near])
    near_mine = jnp.stack([block[: block.shape[0] - head_rows] for block in near])
    near_other = swap(near_mine, "groups", 1)
    near_pair = swap(near_mine, "head", 1)
    got, near_qkv, near_other, near_pair = lax.optimization_barrier(
        (got, near_qkv, near_other, near_pair)
    )

    top = 2 * owned.shape[0]
    pieces_other = swap(got[:, :top], "head", 1)
    qkv_far = swap(got[:, top : top + head_rows // 2], "groups", 1)
    tokens, attended = attend_fast(
        scalars, got, pieces_other, near_qkv, qkv_far, head_rows, per_owner, n
    )

    att_across = swap(attended, "seq", half)
    att_across, near_last = lax.optimization_barrier((att_across, swap(near_other, "head", 1)))
    got = after(got, attended)
    mlp_mine = got[:, top + head_rows // 2 : got.shape[1] - out_rows]
    far_mine = got[:, got.shape[1] - out_rows :]
    far_other = swap(far_mine, "groups", 1)
    mlp_other = swap(mlp_mine, "groups", 1)
    pair = jnp.stack([attended, att_across])
    pairs = [swap(pair, "seq", j) for j in range(1, half)]
    mlp_other, far_other, *pairs = lax.optimization_barrier((mlp_other, far_other, *pairs))
    gathered = jnp.stack([pair] + pairs)
    mlp_pair = (mlp_mine, mlp_other)
    far_pair = (far_mine, far_other)
    base, term_away, *terms = mlp(
        scalars,
        tokens,
        (gathered, swap(gathered, "head", 1)),
        (mlp_pair, tuple(swap(value, "head", 1) for value in mlp_pair)),
        (far_pair, tuple(swap(value, "head", 1) for value in far_pair)),
        ((near_mine, near_other), (near_pair, near_last)),
        n,
    )
    terms = [swap(terms[j - 1], "seq", j) for j in range(1, half)]
    base, term_away = sum_terms(base, term_away, terms)
    encoded = last(base, swap(term_away, "seq", half))
    return encoded.reshape(1, per_owner, 1, half_width)


def local(patches, keep_list, qkv_weight, out_weight, up_weight, down_weight):
    n = lax.axis_size("seq")
    one_image = patches.shape[0] == 1 and qkv_weight.shape[1] == n and n & (n - 1) == 0
    one_image = one_image and lax.axis_size("groups") == 2 and up_weight.shape[1] == n * 256
    plan = local_fast if one_image else local_general
    return plan(patches, keep_list, qkv_weight, out_weight, up_weight, down_weight)


def solution(mesh):
    return jax.shard_map(
        local,
        mesh=mesh,
        in_specs=(
            P("groups", "seq", None, None),
            P("groups", None),
            P("seq", "head", None),
            P("head", "seq"),
            P("seq", "head"),
            P("head", "seq"),
        ),
        out_specs=P("groups", None, "seq", "head"),
        check_vma=False,
    )
```

```python
import functools
import math

import jax
import jax.numpy as jnp
from jax import lax
from jax.experimental import pallas as pl
from jax.experimental.pallas import tpu as pltpu
from jax.sharding import PartitionSpec as P

F32 = jnp.float32
BF16 = jnp.bfloat16
VMEM = pltpu.VMEM

def layer_norm(matrix):
    average = jnp.mean(matrix, axis=-1, keepdims=True)
    power = jnp.mean(matrix * matrix, axis=-1, keepdims=True)
    return (matrix - average) * lax.rsqrt(power - average * average + 1e-06)


def attend(queries, keys, values):
    length = queries.shape[0]
    block = math.gcd(length, 512)
    scale = 1.0 / math.sqrt(queries.shape[1])

    def one_block(query_rows):
        scores = (
            lax.dot_general(
                query_rows, keys, (((1,), (1,)), ((), ())), preferred_element_type=jnp.float32
            )
            * scale
        )
        top = jnp.max(scores, axis=1, keepdims=True)
        powers = jnp.exp(scores - top)
        probs = (powers / jnp.sum(powers, axis=1, keepdims=True)).astype(jnp.bfloat16)
        return jnp.dot(probs, values, preferred_element_type=jnp.float32).astype(jnp.bfloat16)

    blocks = lax.map(one_block, queries.reshape(length // block, block, queries.shape[1]))
    return blocks.reshape(length, values.shape[1])


def local_general(patches, keep_list, qkv_weight, out_weight, up_weight, down_weight):
    seq_count = lax.axis_size("seq")
    seq_rank = lax.axis_index("seq")
    head_rank = lax.axis_index("head")
    images = patches.shape[0]
    sup_local = patches.shape[1]
    depth = patches.shape[3]
    half_width = depth // lax.axis_size("head")
    head_count = qkv_weight.shape[1]
    seq_length = sup_local * seq_count * 8 // 5
    per_owner = seq_length // seq_count
    capacity = (4 * sup_local + seq_count - 1) // seq_count
    slot_count = 4 * sup_local
    image_index = jnp.arange(images, dtype=jnp.int32)
    bounds = jnp.arange(seq_count + 1, dtype=jnp.int32) * sup_local
    before = jnp.sum((keep_list[:, :, None] < bounds[None, None, :]).astype(jnp.int32), axis=1)
    starts = bounds[None, :seq_count] + 3 * before[:, :seq_count]
    lengths = sup_local + 3 * (before[:, 1:] - before[:, :seq_count])
    my_start = lax.dynamic_index_in_dim(starts, seq_rank, 1, keepdims=False)
    my_length = lax.dynamic_index_in_dim(lengths, seq_rank, 1, keepdims=False)
    local_ids = seq_rank * sup_local + jnp.arange(sup_local, dtype=jnp.int32)
    kept_flag = jnp.any(keep_list[:, None, :] == local_ids[None, :, None], axis=2).astype(jnp.int32)
    offsets = jnp.arange(sup_local, dtype=jnp.int32)[None, :] + 3 * (
        jnp.cumsum(kept_flag, axis=1) - kept_flag
    )
    slot_ids = jnp.arange(slot_count, dtype=jnp.int32)
    owner_patch = (
        jnp.sum((offsets[:, None, :] <= slot_ids[None, :, None]).astype(jnp.int32), axis=2) - 1
    )
    start_of = jnp.take_along_axis(offsets, owner_patch, axis=1)
    sub_index = jnp.minimum(slot_ids[None, :] - start_of, 3)
    kept_of = jnp.take_along_axis(kept_flag, owner_patch, axis=1)
    flat_patches = patches.reshape(images, sup_local * 4, depth)
    fine_rows = flat_patches[
        image_index[:, None], owner_patch * 4 + jnp.where(kept_of == 1, sub_index, 0)
    ]
    mean_rows = jnp.mean(patches.astype(jnp.float32), axis=2).astype(jnp.bfloat16)
    shared_rows = mean_rows[image_index[:, None], owner_patch]
    local_tokens = jnp.where((kept_of == 1)[:, :, None], fine_rows, shared_rows)
    destinations = jnp.arange(seq_count, dtype=jnp.int32)[:, None, None]
    depth_slots = jnp.arange(capacity, dtype=jnp.int32)[None, None, :]
    positions = (destinations - my_start[None, :, None]) % seq_count + depth_slots * seq_count
    valid = positions < my_length[None, :, None]
    outgoing = local_tokens[image_index[None, :, None], jnp.minimum(positions, slot_count - 1)]
    outgoing = jnp.where(valid[:, :, :, None], outgoing, jnp.zeros((), jnp.bfloat16))
    incoming = lax.all_to_all(outgoing, "seq", split_axis=0, concat_axis=0, tiled=True)
    owned = jnp.arange(per_owner, dtype=jnp.int32) * seq_count + seq_rank
    source = jnp.sum((starts[:, None, :] <= owned[None, :, None]).astype(jnp.int32), axis=2) - 1
    first_of = jnp.take_along_axis(starts, source, axis=1)
    depth_of = (owned[None, :] - first_of) // seq_count
    resident = incoming[source, image_index[:, None], depth_of]
    start_rows = resident.reshape(images * per_owner, depth)
    start_float = start_rows.astype(jnp.float32)
    qkv_full, out_full, up_full, down_full = (
        lax.all_gather(qkv_weight, "seq", axis=0, tiled=True),
        lax.all_gather(out_weight, "seq", axis=1, tiled=True),
        lax.all_gather(up_weight, "seq", axis=0, tiled=True),
        lax.all_gather(down_weight, "seq", axis=1, tiled=True),
    )
    normed = layer_norm(start_float).astype(jnp.bfloat16).reshape(images, per_owner, depth)
    projected = jnp.einsum("ipd,dhc->ihpc", normed, qkv_full, preferred_element_type=jnp.float32)
    head_size = qkv_weight.shape[2] // 3
    sending = projected.astype(jnp.bfloat16).reshape(seq_count, per_owner, 3 * head_size)
    gathered = lax.all_to_all(sending, "seq", split_axis=0, concat_axis=0, tiled=True).reshape(
        seq_length, 3 * head_size
    )
    attended = attend(
        gathered[:, :head_size],
        gathered[:, head_size : 2 * head_size],
        gathered[:, 2 * head_size :],
    )
    returned = lax.all_to_all(
        attended.reshape(seq_count, per_owner, head_size),
        "seq",
        split_axis=0,
        concat_axis=0,
        tiled=True,
    )
    returned = returned.reshape(images, head_count, per_owner, head_size)
    partial_sum = jnp.einsum(
        "ihpc,hcd->ipd",
        returned,
        out_full.reshape(head_count, head_size, depth),
        preferred_element_type=jnp.float32,
    ).reshape(images * per_owner, depth)
    attn_total = lax.psum(partial_sum, "head")
    residual = start_float + attn_total
    residual_half = lax.dynamic_slice_in_dim(residual, head_rank * half_width, half_width, 1)
    normed_two = layer_norm(residual).astype(jnp.bfloat16)
    hidden = jax.nn.gelu(
        jnp.dot(normed_two, up_full, preferred_element_type=jnp.float32), approximate=False
    ).astype(jnp.bfloat16)
    mlp_terms = jnp.dot(hidden, down_full, preferred_element_type=jnp.float32)
    mlp_part = lax.psum_scatter(mlp_terms, "head", scatter_dimension=1, tiled=True)
    encoded = (residual_half + mlp_part).astype(jnp.bfloat16)
    return encoded.reshape(images, per_owner, 1, half_width)


def vspec():
    return pl.BlockSpec(memory_space=VMEM)


def aspec():
    return pl.BlockSpec(memory_space=pl.ANY)


def sspec():
    return pl.BlockSpec(memory_space=pltpu.SMEM)


def hspec():
    return pl.BlockSpec(memory_space=pltpu.HBM)


def run_copies(copies, sem, base=0):
    started = [
        pltpu.make_async_copy(src, dst, sem.at[base + i]) for i, (src, dst) in enumerate(copies)
    ]
    for copy in started:
        copy.start()

    def wait():
        for copy in started:
            copy.wait()

    return wait


def params(mebibytes=4):
    return pltpu.CompilerParams(vmem_limit_bytes=mebibytes * 1024 * 1024)


def cost(micros):
    return pl.CostEstimate(flops=micros * 10**9, bytes_accessed=1 << 20, transcendentals=0)


def struct(shape, dtype=BF16):
    return jax.ShapeDtypeStruct(shape, dtype)


def slot_of(index, n, capacity, cuts):
    device = sum(((index >= j * cuts * capacity).astype(jnp.int32) for j in range(1, n)), 0 * index)
    inner = index - device * (cuts * capacity)
    cut = sum(((inner >= c * capacity).astype(jnp.int32) for c in range(1, cuts)), 0 * index)
    return device, cut, inner - cut * capacity


def as_column(row):
    count = row.shape[1]
    same = lax.broadcasted_iota(jnp.int32, (count, count), 0) == lax.broadcasted_iota(
        jnp.int32, (count, count), 1
    )
    return jnp.sum(jnp.where(same, row, 0), axis=1, keepdims=True)


def one_hot(mask):
    return mask.astype(F32).astype(BF16)


def prep_kernel(n, sup, capacity, rank_ref, keep_ref, patches_ref, out_ref):
    rank = rank_ref[0]
    first = rank * sup
    keep = as_column(keep_ref[...])
    rows = 4 * sup
    count = keep.shape[0]

    def places(width, shift):
        ids = lax.broadcasted_iota(jnp.int32, (count, width), 1) >> shift
        kept = jnp.sum((keep == first + ids).astype(jnp.int32), axis=0, keepdims=True)
        below = jnp.sum(
            jnp.logical_and(keep >= first, keep < first + ids).astype(jnp.int32),
            axis=0,
            keepdims=True,
        )
        return kept, below, lax.broadcasted_iota(jnp.int32, (1, width), 1)

    kept, below, lane = places(rows, 2)
    fine_pos = jnp.where(kept == 1, (lane >> 2) + 3 * below + (lane & 3), -1)
    kept, below, lane = places(sup, 0)
    mean_pos = jnp.where(kept == 1, -1, lane + 3 * below)
    start = first + 3 * jnp.sum((keep < first).astype(jnp.int32), axis=0, keepdims=True)
    flat = patches_ref[...]
    cuts = flat.shape[1] // 128
    sup_col = lax.broadcasted_iota(jnp.int32, (sup, rows), 0)
    sup_lane = lax.broadcasted_iota(jnp.int32, (sup, rows), 1) >> 2
    averaging = jnp.where(sup_col == sup_lane, 0.25, 0.0).astype(BF16)
    means = jnp.dot(averaging, flat, preferred_element_type=F32).astype(BF16)
    index = lax.broadcasted_iota(jnp.int32, (n * cuts * capacity, 1), 0)
    device, cut, slot = slot_of(index, n, capacity, cuts)
    pos = ((device - start) & (n - 1)) + slot * n
    total = jnp.zeros((n * cuts * capacity, 128), F32)
    for c in range(cuts):
        at = jnp.where(cut == c, pos, -2)
        features = slice(c * 128, (c + 1) * 128)
        total = (
            total
            + jnp.dot(one_hot(at == fine_pos), flat[:, features], preferred_element_type=F32)
            + jnp.dot(one_hot(at == mean_pos), means[:, features], preferred_element_type=F32)
        )
    out_ref[...] = total.astype(BF16)


def prep(scalars, keep_list, flat, n, sup, capacity):
    width = flat.shape[1] // 2
    shape = (n * capacity * width // 128, 128)
    return pl.pallas_call(
        functools.partial(prep_kernel, n, sup, capacity),
        grid_spec=pltpu.PrefetchScalarGridSpec(
            num_scalar_prefetch=1,
            grid=(1,),
            in_specs=[
                pl.BlockSpec(keep_list.shape, lambda i, ref: (0, 0)),
                pl.BlockSpec((flat.shape[0], width), lambda i, ref: (0, ref[1])),
            ],
            out_specs=pl.BlockSpec(shape, lambda i, ref: (0, 0)),
        ),
        out_shape=struct(shape),
        compiler_params=params(),
    )(scalars, keep_list, flat)


def pick_kernel(n, sup, per_owner, capacity, rank_ref, keep_ref, got_ref, out_ref):
    rank = rank_ref[0]
    keep = as_column(keep_ref[...])
    count = keep.shape[0]
    lanes = got_ref.shape[0]
    cuts = lanes // (n * capacity)
    source, _, _ = slot_of(
        lax.broadcasted_iota(jnp.int32, (count, lanes), 1), n, capacity, cuts
    )
    low = jnp.sum((keep < source * sup).astype(jnp.int32), axis=0, keepdims=True)
    high = jnp.sum((keep < source * sup + sup).astype(jnp.int32), axis=0, keepdims=True)
    source, cut, slot = slot_of(
        lax.broadcasted_iota(jnp.int32, (1, lanes), 1), n, capacity, cuts
    )
    start = source * sup + 3 * low
    stop = source * sup + sup + 3 * high
    token = start + ((rank - start) & (n - 1)) + slot * n
    row = jnp.where(token < stop, token >> (n.bit_length() - 1), -1)
    own = lax.broadcasted_iota(jnp.int32, (per_owner, lanes), 0)
    got = got_ref[...]
    for c in range(cuts):
        choose = one_hot(own == jnp.where(cut == c, row, -1))
        owned = jnp.dot(choose, got, preferred_element_type=F32).astype(BF16)
        out_ref[c * per_owner : (c + 1) * per_owner] = owned


def pick(scalars, keep_list, got, n, sup, per_owner, capacity):
    cuts = got.shape[0] // (n * capacity)
    return pl.pallas_call(
        functools.partial(pick_kernel, n, sup, per_owner, capacity),
        in_specs=[sspec(), vspec(), vspec()],
        out_specs=vspec(),
        out_shape=struct((cuts * per_owner, 128)),
        compiler_params=params(),
    )(scalars, keep_list, got)


def far_kernel(n, rank_ref, qkv_ref, out_weight_ref, up_ref, down_ref, away_ref, blocks_ref, sem):
    rank, part = rank_ref[0], rank_ref[2]
    half = n // 2
    rows = up_ref.shape[0]
    wide = up_ref.shape[1] // n
    units = wide // 2
    long = out_weight_ref.shape[0] // 2
    depth = qkv_ref.shape[1] // 2
    copies = []
    for d in range(half):
        dest = (rank // half ^ 1) * half + d
        at = pl.ds(pl.multiple_of(part * depth, 32), depth)
        copies.append((qkv_ref.at[dest, at], away_ref.at[pl.ds(d * depth, depth)]))
        at = pl.ds(pl.multiple_of(dest * wide + part * units, 128), units)
        copies.append((up_ref.at[:, at], blocks_ref.at[d, pl.ds(0, rows)]))
        copies.append((down_ref.at[at], blocks_ref.at[d, pl.ds(rows, units)]))
    at = pl.ds(pl.multiple_of(part * long, 128), long)
    copies.append((out_weight_ref.at[at], away_ref.at[pl.ds(half * depth, long)]))
    run_copies(copies, sem)()


def near_kernel(n, rank_ref, qkv_ref, out_weight_ref, up_ref, down_ref, *refs):
    near, sem = refs[: n // 2], refs[n // 2]
    rank, part = rank_ref[0], rank_ref[2]
    rows = up_ref.shape[0]
    wide = up_ref.shape[1] // n
    units = wide // 2
    long = out_weight_ref.shape[0] // 2
    copies = []
    for j in range(n // 2):
        dest = rank ^ j
        at = pl.ds(pl.multiple_of(dest * wide + part * units, 128), units)
        copies.append((up_ref.at[:, at], near[j].at[pl.ds(0, rows)]))
        copies.append((down_ref.at[at], near[j].at[pl.ds(rows, units)]))
        at = pl.ds(pl.multiple_of(part * long, 128), long)
        copies.append((out_weight_ref.at[at], near[j].at[pl.ds(rows + units, long)]))
        low = rows + units + long
        copies.append((qkv_ref.at[dest], near[j].at[pl.ds(low, qkv_ref.shape[1])]))
    run_copies(copies, sem)()


def pack(kernel, shapes, count, scalars, *weights):
    return pl.pallas_call(
        kernel,
        in_specs=[sspec()] + [hspec()] * 4,
        out_specs=[vspec()] * len(shapes),
        out_shape=[struct(shape) for shape in shapes],
        scratch_shapes=[pltpu.SemaphoreType.DMA((count,))],
    )(scalars, *weights)


def pack_far(scalars, qkv, out_weight, up, down, n):
    half = n // 2
    away = (half * qkv.shape[1] // 2 + out_weight.shape[0] // 2, 128)
    blocks = (half, up.shape[0] + up.shape[1] // n // 2, 128)
    kernel = functools.partial(far_kernel, n)
    return pack(kernel, [away, blocks], 3 * half + 1, scalars, qkv, out_weight, up, down)


def pack_near(scalars, qkv, out_weight, up, down, n):
    half = n // 2
    rows = up.shape[0] + up.shape[1] // n // 2 + out_weight.shape[0] // 2 + qkv.shape[1]
    kernel = functools.partial(near_kernel, n)
    return pack(kernel, [(rows, 128)] * half, 4 * half, scalars, qkv, out_weight, up, down)


def fan_kernel(owned_ref, across_ref, far_ref, out_ref):
    rows = owned_ref.shape[0]
    count = out_ref.shape[0]
    top = 2 * rows
    rest = out_ref.shape[1] - top
    each = (far_ref.shape[0] - rest) // (count - 1)
    for d in range(count):
        out_ref[d, :rows] = owned_ref[...]
        out_ref[d, rows:top] = across_ref[...]
        out_ref[d, top : top + each] = far_ref[d * each : (d + 1) * each]
        out_ref[d, top + each :] = far_ref[count * each :]


def fan(owned, across, far, out_rows, count):
    each = (far.shape[0] - out_rows) // count
    shape = struct((count, 2 * owned.shape[0] + each + out_rows, 128))
    return pl.pallas_call(
        fan_kernel,
        in_specs=[vspec()] * 3,
        out_specs=vspec(),
        out_shape=shape,
        compiler_params=params(8),
    )(owned, across, far)


def source_of(rank, n, q, k):
    return (rank // (n // 2) ^ k) * (n // 2) + q


def norm_rows(x):
    average = jnp.mean(x, axis=-1, keepdims=True)
    power = jnp.mean(x * x, axis=-1, keepdims=True)
    return (x - average) * lax.rsqrt(power - average * average + 1e-06)


def attend_kernel(
    n, part, rank_ref, mine_ref, other_ref, near_ref, far_ref, tokens_ref, out_ref, weight_ref
):
    rank, half, group = rank_ref[0], rank_ref[1], rank_ref[2]
    rows = other_ref.shape[1] // 2
    cuts = rows // part
    width = cuts * 128
    depth = weight_ref.shape[0]
    piece = far_ref.shape[1]
    for q in range(n // 2):
        for k in range(2):
            source = source_of(rank, n, q, k)
            at = pl.ds(pl.multiple_of(source * part, part), part)
            for c in range(cuts):
                cut = slice(k * rows + c * part, k * rows + (c + 1) * part)
                to = pl.ds(pl.multiple_of(half * width + c * 128, 128), 128)
                tokens_ref[at, to] = mine_ref[q, cut]
                to = pl.ds(pl.multiple_of((1 - half) * width + c * 128, 128), 128)
                tokens_ref[at, to] = other_ref[q, cut]
        to = pl.ds(pl.multiple_of((rank ^ q) * 128, 128), 128)
        weight_ref[:, to] = near_ref[q]
        to = pl.ds(pl.multiple_of(source_of(rank, n, q, 1) * 128, 128), 128)
        at = pl.ds(pl.multiple_of(group * piece, 32), piece)
        weight_ref[at, to] = mine_ref[q, 2 * rows : 2 * rows + piece]
        at = pl.ds(pl.multiple_of((1 - group) * piece, 32), piece)
        weight_ref[at, to] = far_ref[q]
    normed = norm_rows(tokens_ref[...].astype(F32)).astype(BF16)
    projected = lax.dot_general(
        normed, weight_ref[...], (((1,), (1,)), ((), ())), preferred_element_type=F32
    ).astype(BF16)
    size = projected.shape[1] // 3
    queries = projected[:, :size]
    keys = projected[:, size : 2 * size]
    values = projected[:, 2 * size :]
    scores = lax.dot_general(
        queries, keys, (((1,), (1,)), ((), ())), preferred_element_type=F32
    ) * (1.0 / math.sqrt(size))
    powers = jnp.exp(scores - jnp.max(scores, axis=1, keepdims=True))
    probs = (powers / jnp.sum(powers, axis=1, keepdims=True)).astype(BF16)
    attended = lax.dot_general(
        values, probs, (((0,), (1,)), ((), ())), preferred_element_type=F32
    ).astype(BF16)
    out_ref[...] = attended


def attend_fast(scalars, mine, other, near, far, head_rows, per_owner, n):
    length = n * per_owner
    depth = other.shape[1] // (2 * per_owner) * 256
    size = head_rows // 3
    return pl.pallas_call(
        functools.partial(attend_kernel, n, per_owner),
        in_specs=[sspec()] + [vspec()] * 4,
        out_specs=[vspec()] * 2,
        out_shape=[struct((length, depth)), struct((size, length))],
        scratch_shapes=[VMEM((head_rows, n * 128), BF16)],
        compiler_params=params(12),
        cost_estimate=cost(30),
    )(scalars, mine, other, near, far)


def mlp_kernel(n, rank_ref, tokens_ref, pieces, far, outs_far, near, outs, scratch):
    base_ref, away_ref, sends = outs[0], outs[1], outs[2:]
    up_ref, down_ref, row_ref, whole_ref, joined_ref, sem = scratch
    rank, half, group = rank_ref[0], rank_ref[1], rank_ref[2]
    block = up_ref.shape[0] // n
    wide = down_ref.shape[0] // 2
    unit = wide // 2
    size = pieces[0].shape[2]
    rows = outs_far[0][0].shape[1]
    first, later = [], []
    for j in range(n // 2):
        source = rank ^ j
        at = pl.ds(pl.multiple_of(source * block, block), block)
        to = pl.ds(pl.multiple_of(source * 128, 128), 128)
        for core in range(2):
            for c in range(2):
                ref = near[core][c]
                units = pl.ds(pl.multiple_of(core * wide + (group ^ c) * unit, unit), unit)
                later.append((ref.at[j, pl.ds(0, block)], up_ref.at[at, units]))
                later.append((ref.at[j, pl.ds(block, unit)], down_ref.at[units, to]))
                rows_to = pl.ds(pl.multiple_of((group ^ c) * rows, rows), rows)
                rows_from = ref.at[j, pl.ds(block + unit, rows)]
                first.append((rows_from, whole_ref.at[core, rows_to, to]))
        source = source_of(rank, n, j, 1)
        at = pl.ds(pl.multiple_of(source * block, block), block)
        to = pl.ds(pl.multiple_of(source * 128, 128), 128)
        for core in range(2):
            for c in range(2):
                units = pl.ds(pl.multiple_of(core * wide + (group ^ c) * unit, unit), unit)
                later.append((far[core][c].at[j, pl.ds(0, block)], up_ref.at[at, units]))
                later.append((far[core][c].at[j, pl.ds(block, unit)], down_ref.at[units, to]))
                rows_to = pl.ds(pl.multiple_of((group ^ c) * rows, rows), rows)
                first.append((outs_far[core][c].at[j], whole_ref.at[core, rows_to, to]))
    wait_first = run_copies(first, sem)
    wait_later = run_copies(later, sem, len(first))
    for j in range(n // 2):
        for core in range(2):
            for k in range(2):
                at = pl.ds(pl.multiple_of((rank ^ j ^ (k * n // 2)) * size, size), size)
                joined_ref[core, at] = pieces[core][j, k]
    wait_first()
    dims = (((0,), (0,)), ((), ()))
    row_ref[...] = (
        tokens_ref[...].astype(F32)
        + lax.dot_general(joined_ref[0], whole_ref[0], dims, preferred_element_type=F32)
        + lax.dot_general(joined_ref[1], whole_ref[1], dims, preferred_element_type=F32)
    )
    part, width = base_ref.shape
    my_cols = pl.ds(pl.multiple_of(half * width, width), width)
    my_rows = pl.ds(pl.multiple_of(rank * part, part), part)
    normed = norm_rows(row_ref[...]).astype(BF16)
    base_ref[...] = row_ref[my_rows, my_cols]
    wait_later()
    raw = jnp.dot(normed, up_ref[...], preferred_element_type=F32)
    hidden = (0.5 * raw * (1.0 + lax.erf(raw * math.sqrt(0.5)))).astype(BF16)
    row_ref[:, :width] = jnp.dot(hidden, down_ref[:, my_cols], preferred_element_type=F32)
    base_ref[...] = base_ref[...] + row_ref[my_rows, :width]
    for j in range(n // 2):
        for k in range(2):
            owner = rank ^ j ^ (k * n // 2)
            term = row_ref[pl.ds(pl.multiple_of(owner * part, part), part), :width]
            if j > 0:
                sends[j - 1][k] = term.astype(BF16)
            elif k == 1:
                away_ref[...] = term


def mlp(scalars, tokens, pieces, far, outs_far, near, n):
    length, depth = tokens.shape
    width = depth // 2
    wide = 2 * (far[0][0].shape[1] - depth // n)
    inner = n * pieces[0].shape[2]
    half = n // 2

    def kernel(scalars, tokens, a, b, *refs):
        far, refs = (refs[:2], refs[2:4]), refs[4:]
        outs_far, refs = (refs[:2], refs[2:4]), refs[4:]
        near, refs = (refs[:2], refs[2:4]), refs[4:]
        mlp_kernel(n, scalars, tokens, (a, b), far, outs_far, near, refs[: half + 1], refs[half + 1 :])

    return pl.pallas_call(
        kernel,
        in_specs=[sspec()] + [vspec()] * 3 + [aspec()] * 12,
        out_specs=[vspec()] * (half + 1),
        out_shape=[struct((length // n, width), F32)] * 2
        + [struct((2, length // n, width))] * (half - 1),
        scratch_shapes=[
            VMEM((depth, 2 * wide), BF16),
            VMEM((2 * wide, depth), BF16),
            VMEM((length, depth), F32),
            VMEM((2, inner, depth), BF16),
            VMEM((2, inner, length), BF16),
            pltpu.SemaphoreType.DMA((24 * half,)),
        ],
        compiler_params=params(24),
    )(scalars, tokens, *pieces, *far[0], *far[1], *outs_far[0], *outs_far[1], *near[0], *near[1])


def sum_kernel(base_ref, away_ref, *refs):
    terms, (base_out, away_out) = refs[:-2], refs[-2:]
    base, away = base_ref[...], away_ref[...]
    for ref in terms:
        base = base + ref[0].astype(F32)
        away = away + ref[1].astype(F32)
    base_out[...] = base
    away_out[...] = away.astype(BF16)


def sum_terms(base, away, terms):
    return pl.pallas_call(
        sum_kernel,
        in_specs=[vspec()] * (2 + len(terms)),
        out_specs=[vspec()] * 2,
        out_shape=[struct(base.shape, F32), struct(away.shape)],
        compiler_params=params(),
    )(base, away, *terms)


def last_kernel(base_ref, across_ref, out_ref):
    out_ref[...] = (base_ref[...] + across_ref[...].astype(F32)).astype(BF16)


def last(base, across):
    return pl.pallas_call(
        last_kernel,
        in_specs=[vspec()] * 2,
        out_specs=vspec(),
        out_shape=struct(base.shape),
        compiler_params=params(),
    )(base, across)


def swap(value, axis, j):
    n = lax.axis_size(axis)
    return lax.ppermute(value, axis, [(i, i ^ j) for i in range(n)])


def exchange(value):
    return lax.all_to_all(value, "seq", split_axis=0, concat_axis=0, tiled=True)


def exchange_half(value):
    n = lax.axis_size("seq")
    groups = [list(range(n // 2)), list(range(n // 2, n))]
    return lax.all_to_all(
        value, "seq", split_axis=0, concat_axis=0, axis_index_groups=groups, tiled=True
    )


def after(value, *others):
    return lax.optimization_barrier((value, *others))[0]


def local_fast(patches, keep_list, qkv_weight, out_weight, up_weight, down_weight):
    n = lax.axis_size("seq")
    rank, head, group = (
        lax.axis_index(name).astype(jnp.int32) for name in ("seq", "head", "groups")
    )
    scalars = jnp.stack([rank, head, group])
    half = n // 2
    sup, depth = patches.shape[1], patches.shape[3]
    length = sup * n * 8 // 5
    per_owner = length // n
    half_width = depth // 2
    head_rows = qkv_weight.shape[2]
    capacity = (4 * sup + n - 1) // n
    flat = patches.reshape(4 * sup, depth)
    heads = qkv_weight.transpose(1, 2, 0)

    weights = (heads, out_weight, up_weight, down_weight)
    away, blocks = pack_far(scalars, *weights, n)
    far = swap(away, "seq", half)
    slots = prep(scalars, keep_list, after(flat, away), n, sup, capacity)
    dealt = exchange(slots)
    weights = lax.optimization_barrier((*weights, slots))[:4]
    near = pack_near(scalars, *weights, n)
    near = [near[0]] + [swap(near[j], "seq", j) for j in range(1, half)]
    owned = pick(scalars, keep_list, dealt, n, sup, per_owner, capacity)
    across = swap(owned, "seq", half)
    across, far, *near = lax.optimization_barrier((across, far, *near))

    out_rows = out_weight.shape[0] // 2
    mlp_far = swap(after(blocks, across), "seq", half)
    got = exchange_half(fan(owned, across, far, out_rows, half))
    near_qkv = jnp.stack([block[block.shape[0] - head_rows :] for block in near])
    near_mine = jnp.stack([block[: block.shape[0] - head_rows] for block in near])
    near_other = swap(near_mine, "groups", 1)
    near_pair = swap(near_mine, "head", 1)
    got, mlp_far, near_qkv, near_other, near_pair = lax.optimization_barrier(
        (got, mlp_far, near_qkv, near_other, near_pair)
    )

    top = 2 * owned.shape[0]
    pieces_other = swap(got[:, :top], "head", 1)
    qkv_far = swap(got[:, top : top + head_rows // 2], "groups", 1)
    mlp_mine = exchange_half(mlp_far)
    tokens, attended = attend_fast(
        scalars, got, pieces_other, near_qkv, qkv_far, head_rows, per_owner, n
    )

    att_across = swap(attended, "seq", half)
    att_across, near_last, mlp_mine = lax.optimization_barrier(
        (att_across, swap(near_other, "head", 1), mlp_mine)
    )
    got = after(got, attended)
    far_mine = got[:, got.shape[1] - out_rows :]
    far_other = swap(far_mine, "groups", 1)
    mlp_other = swap(mlp_mine, "groups", 1)
    pair = jnp.stack([attended, att_across])
    pairs = [swap(pair, "seq", j) for j in range(1, half)]
    mlp_other, far_other, *pairs = lax.optimization_barrier((mlp_other, far_other, *pairs))
    gathered = jnp.stack([pair] + pairs)
    mlp_pair = (mlp_mine, mlp_other)
    far_pair = (far_mine, far_other)
    base, term_away, *terms = mlp(
        scalars,
        tokens,
        (gathered, swap(gathered, "head", 1)),
        (mlp_pair, tuple(swap(value, "head", 1) for value in mlp_pair)),
        (far_pair, tuple(swap(value, "head", 1) for value in far_pair)),
        ((near_mine, near_other), (near_pair, near_last)),
        n,
    )
    terms = [swap(terms[j - 1], "seq", j) for j in range(1, half)]
    base, term_away = sum_terms(base, term_away, terms)
    encoded = last(base, swap(term_away, "seq", half))
    return encoded.reshape(1, per_owner, 1, half_width)


def local(patches, keep_list, qkv_weight, out_weight, up_weight, down_weight):
    n = lax.axis_size("seq")
    one_image = patches.shape[0] == 1 and qkv_weight.shape[1] == n and n & (n - 1) == 0
    one_image = one_image and lax.axis_size("groups") == 2 and up_weight.shape[1] == n * 256
    plan = local_fast if one_image else local_general
    return plan(patches, keep_list, qkv_weight, out_weight, up_weight, down_weight)


def solution(mesh):
    return jax.shard_map(
        local,
        mesh=mesh,
        in_specs=(
            P("groups", "seq", None, None),
            P("groups", None),
            P("seq", "head", None),
            P("head", "seq"),
            P("seq", "head"),
            P("head", "seq"),
        ),
        out_specs=P("groups", None, "seq", "head"),
        check_vma=False,
    )
```

```python
import functools
import math

import jax
import jax.numpy as jnp
from jax import lax
from jax.experimental import pallas as pl
from jax.experimental.pallas import tpu as pltpu
from jax.sharding import PartitionSpec as P

F32 = jnp.float32
BF16 = jnp.bfloat16
VMEM = pltpu.VMEM

def layer_norm(matrix):
    average = jnp.mean(matrix, axis=-1, keepdims=True)
    power = jnp.mean(matrix * matrix, axis=-1, keepdims=True)
    return (matrix - average) * lax.rsqrt(power - average * average + 1e-06)


def attend(queries, keys, values):
    length = queries.shape[0]
    block = math.gcd(length, 512)
    scale = 1.0 / math.sqrt(queries.shape[1])

    def one_block(query_rows):
        scores = (
            lax.dot_general(
                query_rows, keys, (((1,), (1,)), ((), ())), preferred_element_type=jnp.float32
            )
            * scale
        )
        top = jnp.max(scores, axis=1, keepdims=True)
        powers = jnp.exp(scores - top)
        probs = (powers / jnp.sum(powers, axis=1, keepdims=True)).astype(jnp.bfloat16)
        return jnp.dot(probs, values, preferred_element_type=jnp.float32).astype(jnp.bfloat16)

    blocks = lax.map(one_block, queries.reshape(length // block, block, queries.shape[1]))
    return blocks.reshape(length, values.shape[1])


def local_general(patches, keep_list, qkv_weight, out_weight, up_weight, down_weight):
    seq_count = lax.axis_size("seq")
    seq_rank = lax.axis_index("seq")
    head_rank = lax.axis_index("head")
    images = patches.shape[0]
    sup_local = patches.shape[1]
    depth = patches.shape[3]
    half_width = depth // lax.axis_size("head")
    head_count = qkv_weight.shape[1]
    seq_length = sup_local * seq_count * 8 // 5
    per_owner = seq_length // seq_count
    capacity = (4 * sup_local + seq_count - 1) // seq_count
    slot_count = 4 * sup_local
    image_index = jnp.arange(images, dtype=jnp.int32)
    bounds = jnp.arange(seq_count + 1, dtype=jnp.int32) * sup_local
    before = jnp.sum((keep_list[:, :, None] < bounds[None, None, :]).astype(jnp.int32), axis=1)
    starts = bounds[None, :seq_count] + 3 * before[:, :seq_count]
    lengths = sup_local + 3 * (before[:, 1:] - before[:, :seq_count])
    my_start = lax.dynamic_index_in_dim(starts, seq_rank, 1, keepdims=False)
    my_length = lax.dynamic_index_in_dim(lengths, seq_rank, 1, keepdims=False)
    local_ids = seq_rank * sup_local + jnp.arange(sup_local, dtype=jnp.int32)
    kept_flag = jnp.any(keep_list[:, None, :] == local_ids[None, :, None], axis=2).astype(jnp.int32)
    offsets = jnp.arange(sup_local, dtype=jnp.int32)[None, :] + 3 * (
        jnp.cumsum(kept_flag, axis=1) - kept_flag
    )
    slot_ids = jnp.arange(slot_count, dtype=jnp.int32)
    owner_patch = (
        jnp.sum((offsets[:, None, :] <= slot_ids[None, :, None]).astype(jnp.int32), axis=2) - 1
    )
    start_of = jnp.take_along_axis(offsets, owner_patch, axis=1)
    sub_index = jnp.minimum(slot_ids[None, :] - start_of, 3)
    kept_of = jnp.take_along_axis(kept_flag, owner_patch, axis=1)
    flat_patches = patches.reshape(images, sup_local * 4, depth)
    fine_rows = flat_patches[
        image_index[:, None], owner_patch * 4 + jnp.where(kept_of == 1, sub_index, 0)
    ]
    mean_rows = jnp.mean(patches.astype(jnp.float32), axis=2).astype(jnp.bfloat16)
    shared_rows = mean_rows[image_index[:, None], owner_patch]
    local_tokens = jnp.where((kept_of == 1)[:, :, None], fine_rows, shared_rows)
    destinations = jnp.arange(seq_count, dtype=jnp.int32)[:, None, None]
    depth_slots = jnp.arange(capacity, dtype=jnp.int32)[None, None, :]
    positions = (destinations - my_start[None, :, None]) % seq_count + depth_slots * seq_count
    valid = positions < my_length[None, :, None]
    outgoing = local_tokens[image_index[None, :, None], jnp.minimum(positions, slot_count - 1)]
    outgoing = jnp.where(valid[:, :, :, None], outgoing, jnp.zeros((), jnp.bfloat16))
    incoming = lax.all_to_all(outgoing, "seq", split_axis=0, concat_axis=0, tiled=True)
    owned = jnp.arange(per_owner, dtype=jnp.int32) * seq_count + seq_rank
    source = jnp.sum((starts[:, None, :] <= owned[None, :, None]).astype(jnp.int32), axis=2) - 1
    first_of = jnp.take_along_axis(starts, source, axis=1)
    depth_of = (owned[None, :] - first_of) // seq_count
    resident = incoming[source, image_index[:, None], depth_of]
    start_rows = resident.reshape(images * per_owner, depth)
    start_float = start_rows.astype(jnp.float32)
    qkv_full, out_full, up_full, down_full = (
        lax.all_gather(qkv_weight, "seq", axis=0, tiled=True),
        lax.all_gather(out_weight, "seq", axis=1, tiled=True),
        lax.all_gather(up_weight, "seq", axis=0, tiled=True),
        lax.all_gather(down_weight, "seq", axis=1, tiled=True),
    )
    normed = layer_norm(start_float).astype(jnp.bfloat16).reshape(images, per_owner, depth)
    projected = jnp.einsum("ipd,dhc->ihpc", normed, qkv_full, preferred_element_type=jnp.float32)
    head_size = qkv_weight.shape[2] // 3
    sending = projected.astype(jnp.bfloat16).reshape(seq_count, per_owner, 3 * head_size)
    gathered = lax.all_to_all(sending, "seq", split_axis=0, concat_axis=0, tiled=True).reshape(
        seq_length, 3 * head_size
    )
    attended = attend(
        gathered[:, :head_size],
        gathered[:, head_size : 2 * head_size],
        gathered[:, 2 * head_size :],
    )
    returned = lax.all_to_all(
        attended.reshape(seq_count, per_owner, head_size),
        "seq",
        split_axis=0,
        concat_axis=0,
        tiled=True,
    )
    returned = returned.reshape(images, head_count, per_owner, head_size)
    partial_sum = jnp.einsum(
        "ihpc,hcd->ipd",
        returned,
        out_full.reshape(head_count, head_size, depth),
        preferred_element_type=jnp.float32,
    ).reshape(images * per_owner, depth)
    attn_total = lax.psum(partial_sum, "head")
    residual = start_float + attn_total
    residual_half = lax.dynamic_slice_in_dim(residual, head_rank * half_width, half_width, 1)
    normed_two = layer_norm(residual).astype(jnp.bfloat16)
    hidden = jax.nn.gelu(
        jnp.dot(normed_two, up_full, preferred_element_type=jnp.float32), approximate=False
    ).astype(jnp.bfloat16)
    mlp_terms = jnp.dot(hidden, down_full, preferred_element_type=jnp.float32)
    mlp_part = lax.psum_scatter(mlp_terms, "head", scatter_dimension=1, tiled=True)
    encoded = (residual_half + mlp_part).astype(jnp.bfloat16)
    return encoded.reshape(images, per_owner, 1, half_width)


def vspec():
    return pl.BlockSpec(memory_space=VMEM)


def aspec():
    return pl.BlockSpec(memory_space=pl.ANY)


def sspec():
    return pl.BlockSpec(memory_space=pltpu.SMEM)


def hspec():
    return pl.BlockSpec(memory_space=pltpu.HBM)


def run_copies(copies, sem, base=0):
    started = [
        pltpu.make_async_copy(src, dst, sem.at[base + i]) for i, (src, dst) in enumerate(copies)
    ]
    for copy in started:
        copy.start()

    def wait():
        for copy in started:
            copy.wait()

    return wait


def params(mebibytes=4):
    return pltpu.CompilerParams(vmem_limit_bytes=mebibytes * 1024 * 1024)


def cost(micros):
    return pl.CostEstimate(flops=micros * 10**9, bytes_accessed=1 << 20, transcendentals=0)


def struct(shape, dtype=BF16):
    return jax.ShapeDtypeStruct(shape, dtype)


def slot_of(index, n, capacity, cuts):
    device = sum(((index >= j * cuts * capacity).astype(jnp.int32) for j in range(1, n)), 0 * index)
    inner = index - device * (cuts * capacity)
    cut = sum(((inner >= c * capacity).astype(jnp.int32) for c in range(1, cuts)), 0 * index)
    return device, cut, inner - cut * capacity


def as_column(row):
    count = row.shape[1]
    same = lax.broadcasted_iota(jnp.int32, (count, count), 0) == lax.broadcasted_iota(
        jnp.int32, (count, count), 1
    )
    return jnp.sum(jnp.where(same, row, 0), axis=1, keepdims=True)


def one_hot(mask):
    return mask.astype(F32).astype(BF16)


def prep_kernel(n, sup, capacity, rank_ref, keep_ref, patches_ref, out_ref):
    rank = rank_ref[0]
    first = rank * sup
    keep = as_column(keep_ref[...])
    rows = 4 * sup
    count = keep.shape[0]

    def places(width, shift):
        ids = lax.broadcasted_iota(jnp.int32, (count, width), 1) >> shift
        kept = jnp.sum((keep == first + ids).astype(jnp.int32), axis=0, keepdims=True)
        below = jnp.sum(
            jnp.logical_and(keep >= first, keep < first + ids).astype(jnp.int32),
            axis=0,
            keepdims=True,
        )
        return kept, below, lax.broadcasted_iota(jnp.int32, (1, width), 1)

    kept, below, lane = places(rows, 2)
    fine_pos = jnp.where(kept == 1, (lane >> 2) + 3 * below + (lane & 3), -1)
    kept, below, lane = places(sup, 0)
    mean_pos = jnp.where(kept == 1, -1, lane + 3 * below)
    start = first + 3 * jnp.sum((keep < first).astype(jnp.int32), axis=0, keepdims=True)
    flat = patches_ref[...]
    cuts = flat.shape[1] // 128
    sup_col = lax.broadcasted_iota(jnp.int32, (sup, rows), 0)
    sup_lane = lax.broadcasted_iota(jnp.int32, (sup, rows), 1) >> 2
    averaging = jnp.where(sup_col == sup_lane, 0.25, 0.0).astype(BF16)
    means = jnp.dot(averaging, flat, preferred_element_type=F32).astype(BF16)
    index = lax.broadcasted_iota(jnp.int32, (n * cuts * capacity, 1), 0)
    device, cut, slot = slot_of(index, n, capacity, cuts)
    pos = ((device - start) & (n - 1)) + slot * n
    total = jnp.zeros((n * cuts * capacity, 128), F32)
    for c in range(cuts):
        at = jnp.where(cut == c, pos, -2)
        features = slice(c * 128, (c + 1) * 128)
        total = (
            total
            + jnp.dot(one_hot(at == fine_pos), flat[:, features], preferred_element_type=F32)
            + jnp.dot(one_hot(at == mean_pos), means[:, features], preferred_element_type=F32)
        )
    out_ref[...] = total.astype(BF16)


def prep(scalars, keep_list, flat, n, sup, capacity):
    width = flat.shape[1] // 2
    shape = (n * capacity * width // 128, 128)
    return pl.pallas_call(
        functools.partial(prep_kernel, n, sup, capacity),
        grid_spec=pltpu.PrefetchScalarGridSpec(
            num_scalar_prefetch=1,
            grid=(1,),
            in_specs=[
                pl.BlockSpec(keep_list.shape, lambda i, ref: (0, 0)),
                pl.BlockSpec((flat.shape[0], width), lambda i, ref: (0, ref[1])),
            ],
            out_specs=pl.BlockSpec(shape, lambda i, ref: (0, 0)),
        ),
        out_shape=struct(shape),
        compiler_params=params(),
    )(scalars, keep_list, flat)


def pick_kernel(n, sup, per_owner, capacity, rank_ref, keep_ref, got_ref, out_ref):
    rank = rank_ref[0]
    keep = as_column(keep_ref[...])
    count = keep.shape[0]
    lanes = got_ref.shape[0]
    cuts = lanes // (n * capacity)
    source, _, _ = slot_of(
        lax.broadcasted_iota(jnp.int32, (count, lanes), 1), n, capacity, cuts
    )
    low = jnp.sum((keep < source * sup).astype(jnp.int32), axis=0, keepdims=True)
    high = jnp.sum((keep < source * sup + sup).astype(jnp.int32), axis=0, keepdims=True)
    source, cut, slot = slot_of(
        lax.broadcasted_iota(jnp.int32, (1, lanes), 1), n, capacity, cuts
    )
    start = source * sup + 3 * low
    stop = source * sup + sup + 3 * high
    token = start + ((rank - start) & (n - 1)) + slot * n
    row = jnp.where(token < stop, token >> (n.bit_length() - 1), -1)
    own = lax.broadcasted_iota(jnp.int32, (per_owner, lanes), 0)
    got = got_ref[...]
    for c in range(cuts):
        choose = one_hot(own == jnp.where(cut == c, row, -1))
        owned = jnp.dot(choose, got, preferred_element_type=F32).astype(BF16)
        out_ref[c * per_owner : (c + 1) * per_owner] = owned


def pick(scalars, keep_list, got, n, sup, per_owner, capacity):
    cuts = got.shape[0] // (n * capacity)
    return pl.pallas_call(
        functools.partial(pick_kernel, n, sup, per_owner, capacity),
        in_specs=[sspec(), vspec(), vspec()],
        out_specs=vspec(),
        out_shape=struct((cuts * per_owner, 128)),
        compiler_params=params(),
    )(scalars, keep_list, got)


def far_kernel(n, rank_ref, qkv_ref, out_weight_ref, up_ref, down_ref, away_ref, blocks_ref, sem):
    rank, part = rank_ref[0], rank_ref[2]
    half = n // 2
    rows = up_ref.shape[0]
    wide = up_ref.shape[1] // n
    units = wide // 2
    long = out_weight_ref.shape[0] // 2
    depth = qkv_ref.shape[1] // 2
    copies = []
    for d in range(half):
        dest = (rank // half ^ 1) * half + d
        at = pl.ds(pl.multiple_of(part * depth, 32), depth)
        copies.append((qkv_ref.at[dest, at], away_ref.at[pl.ds(d * depth, depth)]))
        at = pl.ds(pl.multiple_of(dest * wide + part * units, 128), units)
        copies.append((up_ref.at[:, at], blocks_ref.at[d, pl.ds(0, rows)]))
        copies.append((down_ref.at[at], blocks_ref.at[d, pl.ds(rows, units)]))
    at = pl.ds(pl.multiple_of(part * long, 128), long)
    copies.append((out_weight_ref.at[at], away_ref.at[pl.ds(half * depth, long)]))
    run_copies(copies, sem)()


def near_kernel(n, rank_ref, qkv_ref, out_weight_ref, up_ref, down_ref, *refs):
    near, sem = refs[: n // 2], refs[n // 2]
    rank, part = rank_ref[0], rank_ref[2]
    rows = up_ref.shape[0]
    wide = up_ref.shape[1] // n
    units = wide // 2
    long = out_weight_ref.shape[0] // 2
    copies = []
    for j in range(n // 2):
        dest = rank ^ j
        at = pl.ds(pl.multiple_of(dest * wide + part * units, 128), units)
        copies.append((up_ref.at[:, at], near[j].at[pl.ds(0, rows)]))
        copies.append((down_ref.at[at], near[j].at[pl.ds(rows, units)]))
        at = pl.ds(pl.multiple_of(part * long, 128), long)
        copies.append((out_weight_ref.at[at], near[j].at[pl.ds(rows + units, long)]))
        low = rows + units + long
        copies.append((qkv_ref.at[dest], near[j].at[pl.ds(low, qkv_ref.shape[1])]))
    run_copies(copies, sem)()


def pack(kernel, shapes, count, scalars, *weights):
    return pl.pallas_call(
        kernel,
        in_specs=[sspec()] + [hspec()] * 4,
        out_specs=[vspec()] * len(shapes),
        out_shape=[struct(shape) for shape in shapes],
        scratch_shapes=[pltpu.SemaphoreType.DMA((count,))],
    )(scalars, *weights)


def pack_far(scalars, qkv, out_weight, up, down, n):
    half = n // 2
    away = (half * qkv.shape[1] // 2 + out_weight.shape[0] // 2, 128)
    blocks = (half, up.shape[0] + up.shape[1] // n // 2, 128)
    kernel = functools.partial(far_kernel, n)
    return pack(kernel, [away, blocks], 3 * half + 1, scalars, qkv, out_weight, up, down)


def pack_near(scalars, qkv, out_weight, up, down, n):
    half = n // 2
    rows = up.shape[0] + up.shape[1] // n // 2 + out_weight.shape[0] // 2 + qkv.shape[1]
    kernel = functools.partial(near_kernel, n)
    return pack(kernel, [(rows, 128)] * half, 4 * half, scalars, qkv, out_weight, up, down)


def fan_kernel(owned_ref, across_ref, far_ref, out_ref):
    rows = owned_ref.shape[0]
    count = out_ref.shape[0]
    top = 2 * rows
    rest = out_ref.shape[1] - top
    each = (far_ref.shape[0] - rest) // (count - 1)
    for d in range(count):
        out_ref[d, :rows] = owned_ref[...]
        out_ref[d, rows:top] = across_ref[...]
        out_ref[d, top : top + each] = far_ref[d * each : (d + 1) * each]
        out_ref[d, top + each :] = far_ref[count * each :]


def fan(owned, across, far, out_rows, count):
    each = (far.shape[0] - out_rows) // count
    shape = struct((count, 2 * owned.shape[0] + each + out_rows, 128))
    return pl.pallas_call(
        fan_kernel,
        in_specs=[vspec()] * 3,
        out_specs=vspec(),
        out_shape=shape,
        compiler_params=params(8),
    )(owned, across, far)


def source_of(rank, n, q, k):
    return (rank // (n // 2) ^ k) * (n // 2) + q


def norm_rows(x):
    average = jnp.mean(x, axis=-1, keepdims=True)
    power = jnp.mean(x * x, axis=-1, keepdims=True)
    return (x - average) * lax.rsqrt(power - average * average + 1e-06)


def attend_kernel(
    n, part, rank_ref, mine_ref, other_ref, near_ref, far_ref, tokens_ref, out_ref, weight_ref
):
    rank, half, group = rank_ref[0], rank_ref[1], rank_ref[2]
    rows = other_ref.shape[1] // 2
    cuts = rows // part
    width = cuts * 128
    depth = weight_ref.shape[0]
    piece = far_ref.shape[1]
    for q in range(n // 2):
        for k in range(2):
            source = source_of(rank, n, q, k)
            at = pl.ds(pl.multiple_of(source * part, part), part)
            for c in range(cuts):
                cut = slice(k * rows + c * part, k * rows + (c + 1) * part)
                to = pl.ds(pl.multiple_of(half * width + c * 128, 128), 128)
                tokens_ref[at, to] = mine_ref[q, cut]
                to = pl.ds(pl.multiple_of((1 - half) * width + c * 128, 128), 128)
                tokens_ref[at, to] = other_ref[q, cut]
        to = pl.ds(pl.multiple_of((rank ^ q) * 128, 128), 128)
        weight_ref[:, to] = near_ref[q]
        to = pl.ds(pl.multiple_of(source_of(rank, n, q, 1) * 128, 128), 128)
        at = pl.ds(pl.multiple_of(group * piece, 32), piece)
        weight_ref[at, to] = mine_ref[q, 2 * rows : 2 * rows + piece]
        at = pl.ds(pl.multiple_of((1 - group) * piece, 32), piece)
        weight_ref[at, to] = far_ref[q]
    normed = norm_rows(tokens_ref[...].astype(F32)).astype(BF16)
    projected = lax.dot_general(
        normed, weight_ref[...], (((1,), (1,)), ((), ())), preferred_element_type=F32
    ).astype(BF16)
    size = projected.shape[1] // 3
    queries = projected[:, :size]
    keys = projected[:, size : 2 * size]
    values = projected[:, 2 * size :]
    scores = lax.dot_general(
        queries, keys, (((1,), (1,)), ((), ())), preferred_element_type=F32
    ) * (1.0 / math.sqrt(size))
    powers = jnp.exp(scores - jnp.max(scores, axis=1, keepdims=True))
    probs = (powers / jnp.sum(powers, axis=1, keepdims=True)).astype(BF16)
    attended = lax.dot_general(
        values, probs, (((0,), (1,)), ((), ())), preferred_element_type=F32
    ).astype(BF16)
    out_ref[...] = attended


def attend_fast(scalars, mine, other, near, far, head_rows, per_owner, n):
    length = n * per_owner
    depth = other.shape[1] // (2 * per_owner) * 256
    size = head_rows // 3
    return pl.pallas_call(
        functools.partial(attend_kernel, n, per_owner),
        in_specs=[sspec()] + [vspec()] * 4,
        out_specs=[vspec()] * 2,
        out_shape=[struct((length, depth)), struct((size, length))],
        scratch_shapes=[VMEM((head_rows, n * 128), BF16)],
        compiler_params=params(8),
        cost_estimate=cost(30),
    )(scalars, mine, other, near, far)


def mlp_kernel(n, rank_ref, tokens_ref, pieces, far, outs_far, near, outs, scratch):
    base_ref, away_ref, sends = outs[0], outs[1], outs[2:]
    up_ref, down_ref, row_ref, whole_ref, joined_ref, sem = scratch
    rank, half, group = rank_ref[0], rank_ref[1], rank_ref[2]
    block = up_ref.shape[0] // n
    wide = down_ref.shape[0] // 2
    unit = wide // 2
    size = pieces[0].shape[2]
    rows = outs_far[0][0].shape[1]
    first, later = [], []
    for j in range(n // 2):
        source = rank ^ j
        at = pl.ds(pl.multiple_of(source * block, block), block)
        to = pl.ds(pl.multiple_of(source * 128, 128), 128)
        for core in range(2):
            for c in range(2):
                ref = near[core][c]
                units = pl.ds(pl.multiple_of(core * wide + (group ^ c) * unit, unit), unit)
                later.append((ref.at[j, pl.ds(0, block)], up_ref.at[at, units]))
                later.append((ref.at[j, pl.ds(block, unit)], down_ref.at[units, to]))
                rows_to = pl.ds(pl.multiple_of((group ^ c) * rows, rows), rows)
                rows_from = ref.at[j, pl.ds(block + unit, rows)]
                first.append((rows_from, whole_ref.at[core, rows_to, to]))
        source = source_of(rank, n, j, 1)
        at = pl.ds(pl.multiple_of(source * block, block), block)
        to = pl.ds(pl.multiple_of(source * 128, 128), 128)
        for core in range(2):
            for c in range(2):
                units = pl.ds(pl.multiple_of(core * wide + (group ^ c) * unit, unit), unit)
                later.append((far[core][c].at[j, pl.ds(0, block)], up_ref.at[at, units]))
                later.append((far[core][c].at[j, pl.ds(block, unit)], down_ref.at[units, to]))
                rows_to = pl.ds(pl.multiple_of((group ^ c) * rows, rows), rows)
                first.append((outs_far[core][c].at[j], whole_ref.at[core, rows_to, to]))
    wait_first = run_copies(first, sem)
    wait_later = run_copies(later, sem, len(first))
    for j in range(n // 2):
        for core in range(2):
            for k in range(2):
                at = pl.ds(pl.multiple_of((rank ^ j ^ (k * n // 2)) * size, size), size)
                joined_ref[core, at] = pieces[core][j, k]
    wait_first()
    dims = (((0,), (0,)), ((), ()))
    row_ref[...] = (
        tokens_ref[...].astype(F32)
        + lax.dot_general(joined_ref[0], whole_ref[0], dims, preferred_element_type=F32)
        + lax.dot_general(joined_ref[1], whole_ref[1], dims, preferred_element_type=F32)
    )
    part, width = base_ref.shape
    my_cols = pl.ds(pl.multiple_of(half * width, width), width)
    my_rows = pl.ds(pl.multiple_of(rank * part, part), part)
    normed = norm_rows(row_ref[...]).astype(BF16)
    base_ref[...] = row_ref[my_rows, my_cols]
    wait_later()
    raw = jnp.dot(normed, up_ref[...], preferred_element_type=F32)
    hidden = (0.5 * raw * (1.0 + lax.erf(raw * math.sqrt(0.5)))).astype(BF16)
    row_ref[:, :width] = jnp.dot(hidden, down_ref[:, my_cols], preferred_element_type=F32)
    base_ref[...] = base_ref[...] + row_ref[my_rows, :width]
    for j in range(n // 2):
        for k in range(2):
            owner = rank ^ j ^ (k * n // 2)
            term = row_ref[pl.ds(pl.multiple_of(owner * part, part), part), :width]
            if j > 0:
                sends[j - 1][k] = term.astype(BF16)
            elif k == 1:
                away_ref[...] = term


def mlp(scalars, tokens, pieces, far, outs_far, near, n):
    length, depth = tokens.shape
    width = depth // 2
    wide = 2 * (far[0][0].shape[1] - depth // n)
    inner = n * pieces[0].shape[2]
    half = n // 2

    def kernel(scalars, tokens, a, b, *refs):
        far, refs = (refs[:2], refs[2:4]), refs[4:]
        outs_far, refs = (refs[:2], refs[2:4]), refs[4:]
        near, refs = (refs[:2], refs[2:4]), refs[4:]
        mlp_kernel(n, scalars, tokens, (a, b), far, outs_far, near, refs[: half + 1], refs[half + 1 :])

    return pl.pallas_call(
        kernel,
        in_specs=[sspec()] + [vspec()] * 3 + [aspec()] * 12,
        out_specs=[vspec()] * (half + 1),
        out_shape=[struct((length // n, width), F32)] * 2
        + [struct((2, length // n, width))] * (half - 1),
        scratch_shapes=[
            VMEM((depth, 2 * wide), BF16),
            VMEM((2 * wide, depth), BF16),
            VMEM((length, depth), F32),
            VMEM((2, inner, depth), BF16),
            VMEM((2, inner, length), BF16),
            pltpu.SemaphoreType.DMA((24 * half,)),
        ],
        compiler_params=params(16),
    )(scalars, tokens, *pieces, *far[0], *far[1], *outs_far[0], *outs_far[1], *near[0], *near[1])


def sum_kernel(base_ref, away_ref, *refs):
    terms, (base_out, away_out) = refs[:-2], refs[-2:]
    base, away = base_ref[...], away_ref[...]
    for ref in terms:
        base = base + ref[0].astype(F32)
        away = away + ref[1].astype(F32)
    base_out[...] = base
    away_out[...] = away.astype(BF16)


def sum_terms(base, away, terms):
    return pl.pallas_call(
        sum_kernel,
        in_specs=[vspec()] * (2 + len(terms)),
        out_specs=[vspec()] * 2,
        out_shape=[struct(base.shape, F32), struct(away.shape)],
        compiler_params=params(),
    )(base, away, *terms)


def last_kernel(base_ref, across_ref, out_ref):
    out_ref[...] = (base_ref[...] + across_ref[...].astype(F32)).astype(BF16)


def last(base, across):
    return pl.pallas_call(
        last_kernel,
        in_specs=[vspec()] * 2,
        out_specs=vspec(),
        out_shape=struct(base.shape),
        compiler_params=params(),
    )(base, across)


def swap(value, axis, j):
    n = lax.axis_size(axis)
    return lax.ppermute(value, axis, [(i, i ^ j) for i in range(n)])


def exchange(value):
    return lax.all_to_all(value, "seq", split_axis=0, concat_axis=0, tiled=True)


def exchange_half(value):
    n = lax.axis_size("seq")
    groups = [list(range(n // 2)), list(range(n // 2, n))]
    return lax.all_to_all(
        value, "seq", split_axis=0, concat_axis=0, axis_index_groups=groups, tiled=True
    )


def after(value, *others):
    return lax.optimization_barrier((value, *others))[0]


def local_fast(patches, keep_list, qkv_weight, out_weight, up_weight, down_weight):
    n = lax.axis_size("seq")
    rank, head, group = (
        lax.axis_index(name).astype(jnp.int32) for name in ("seq", "head", "groups")
    )
    scalars = jnp.stack([rank, head, group])
    half = n // 2
    sup, depth = patches.shape[1], patches.shape[3]
    length = sup * n * 8 // 5
    per_owner = length // n
    half_width = depth // 2
    head_rows = qkv_weight.shape[2]
    capacity = (4 * sup + n - 1) // n
    flat = patches.reshape(4 * sup, depth)
    heads = qkv_weight.transpose(1, 2, 0)

    weights = (heads, out_weight, up_weight, down_weight)
    away, blocks = pack_far(scalars, *weights, n)
    far = swap(away, "seq", half)
    slots = prep(scalars, keep_list, after(flat, away), n, sup, capacity)
    slots, far = lax.optimization_barrier((slots, far))
    dealt = exchange(slots)
    weights = lax.optimization_barrier((*weights, slots))[:4]
    near = pack_near(scalars, *weights, n)
    near = [near[0]] + [swap(near[j], "seq", j) for j in range(1, half)]
    owned = pick(scalars, keep_list, dealt, n, sup, per_owner, capacity)
    across = swap(owned, "seq", half)
    across, far, *near = lax.optimization_barrier((across, far, *near))

    out_rows = out_weight.shape[0] // 2
    mlp_far = swap(after(blocks, across), "seq", half)
    got = exchange_half(fan(owned, across, far, out_rows, half))
    near_qkv = jnp.stack([block[block.shape[0] - head_rows :] for block in near])
    near_mine = jnp.stack([block[: block.shape[0] - head_rows] for block in near])
    near_other = swap(near_mine, "groups", 1)
    near_pair = swap(near_mine, "head", 1)
    got, mlp_far, near_qkv, near_other, near_pair = lax.optimization_barrier(
        (got, mlp_far, near_qkv, near_other, near_pair)
    )

    top = 2 * owned.shape[0]
    pieces_other = swap(got[:, :top], "head", 1)
    qkv_far = swap(got[:, top : top + head_rows // 2], "groups", 1)
    mlp_mine = exchange_half(mlp_far)
    tokens, attended = attend_fast(
        scalars, got, pieces_other, near_qkv, qkv_far, head_rows, per_owner, n
    )

    att_across = swap(attended, "seq", half)
    far_pair = swap(got[:, got.shape[1] - out_rows :], "head", 1)
    att_across, near_last, mlp_mine, far_pair = lax.optimization_barrier(
        (att_across, swap(near_other, "head", 1), mlp_mine, far_pair)
    )
    got = after(got, attended)
    far_mine = got[:, got.shape[1] - out_rows :]
    far_other = swap(far_mine, "groups", 1)
    mlp_other = swap(mlp_mine, "groups", 1)
    pair = jnp.stack([attended, att_across])
    pairs = [swap(pair, "seq", j) for j in range(1, half)]
    mlp_other, far_other, *pairs = lax.optimization_barrier((mlp_other, far_other, *pairs))
    gathered = jnp.stack([pair] + pairs)
    mlp_pair = (mlp_mine, mlp_other)
    base, term_away, *terms = mlp(
        scalars,
        tokens,
        (gathered, swap(gathered, "head", 1)),
        (mlp_pair, tuple(swap(value, "head", 1) for value in mlp_pair)),
        ((far_mine, far_other), (far_pair, swap(far_other, "head", 1))),
        ((near_mine, near_other), (near_pair, near_last)),
        n,
    )
    terms = [swap(terms[j - 1], "seq", j) for j in range(1, half)]
    base, term_away = sum_terms(base, term_away, terms)
    encoded = last(base, swap(term_away, "seq", half))
    return encoded.reshape(1, per_owner, 1, half_width)


def local(patches, keep_list, qkv_weight, out_weight, up_weight, down_weight):
    n = lax.axis_size("seq")
    one_image = patches.shape[0] == 1 and qkv_weight.shape[1] == n and n & (n - 1) == 0
    one_image = one_image and lax.axis_size("groups") == 2 and up_weight.shape[1] == n * 256
    plan = local_fast if one_image else local_general
    return plan(patches, keep_list, qkv_weight, out_weight, up_weight, down_weight)


def solution(mesh):
    return jax.shard_map(
        local,
        mesh=mesh,
        in_specs=(
            P("groups", "seq", None, None),
            P("groups", None),
            P("seq", "head", None),
            P("head", "seq"),
            P("seq", "head"),
            P("head", "seq"),
        ),
        out_specs=P("groups", None, "seq", "head"),
        check_vma=False,
    )
```

```python
import functools
import math

import jax
import jax.numpy as jnp
from jax import lax
from jax.experimental import pallas as pl
from jax.experimental.pallas import tpu as pltpu
from jax.sharding import PartitionSpec as P

F32 = jnp.float32
BF16 = jnp.bfloat16
VMEM = pltpu.VMEM

def layer_norm(matrix):
    average = jnp.mean(matrix, axis=-1, keepdims=True)
    power = jnp.mean(matrix * matrix, axis=-1, keepdims=True)
    return (matrix - average) * lax.rsqrt(power - average * average + 1e-06)


def attend(queries, keys, values):
    length = queries.shape[0]
    block = math.gcd(length, 512)
    scale = 1.0 / math.sqrt(queries.shape[1])

    def one_block(query_rows):
        scores = (
            lax.dot_general(
                query_rows, keys, (((1,), (1,)), ((), ())), preferred_element_type=jnp.float32
            )
            * scale
        )
        top = jnp.max(scores, axis=1, keepdims=True)
        powers = jnp.exp(scores - top)
        probs = (powers / jnp.sum(powers, axis=1, keepdims=True)).astype(jnp.bfloat16)
        return jnp.dot(probs, values, preferred_element_type=jnp.float32).astype(jnp.bfloat16)

    blocks = lax.map(one_block, queries.reshape(length // block, block, queries.shape[1]))
    return blocks.reshape(length, values.shape[1])


def local_general(patches, keep_list, qkv_weight, out_weight, up_weight, down_weight):
    seq_count = lax.axis_size("seq")
    seq_rank = lax.axis_index("seq")
    head_rank = lax.axis_index("head")
    images = patches.shape[0]
    sup_local = patches.shape[1]
    depth = patches.shape[3]
    half_width = depth // lax.axis_size("head")
    head_count = qkv_weight.shape[1]
    seq_length = sup_local * seq_count * 8 // 5
    per_owner = seq_length // seq_count
    capacity = (4 * sup_local + seq_count - 1) // seq_count
    slot_count = 4 * sup_local
    image_index = jnp.arange(images, dtype=jnp.int32)
    bounds = jnp.arange(seq_count + 1, dtype=jnp.int32) * sup_local
    before = jnp.sum((keep_list[:, :, None] < bounds[None, None, :]).astype(jnp.int32), axis=1)
    starts = bounds[None, :seq_count] + 3 * before[:, :seq_count]
    lengths = sup_local + 3 * (before[:, 1:] - before[:, :seq_count])
    my_start = lax.dynamic_index_in_dim(starts, seq_rank, 1, keepdims=False)
    my_length = lax.dynamic_index_in_dim(lengths, seq_rank, 1, keepdims=False)
    local_ids = seq_rank * sup_local + jnp.arange(sup_local, dtype=jnp.int32)
    kept_flag = jnp.any(keep_list[:, None, :] == local_ids[None, :, None], axis=2).astype(jnp.int32)
    offsets = jnp.arange(sup_local, dtype=jnp.int32)[None, :] + 3 * (
        jnp.cumsum(kept_flag, axis=1) - kept_flag
    )
    slot_ids = jnp.arange(slot_count, dtype=jnp.int32)
    owner_patch = (
        jnp.sum((offsets[:, None, :] <= slot_ids[None, :, None]).astype(jnp.int32), axis=2) - 1
    )
    start_of = jnp.take_along_axis(offsets, owner_patch, axis=1)
    sub_index = jnp.minimum(slot_ids[None, :] - start_of, 3)
    kept_of = jnp.take_along_axis(kept_flag, owner_patch, axis=1)
    flat_patches = patches.reshape(images, sup_local * 4, depth)
    fine_rows = flat_patches[
        image_index[:, None], owner_patch * 4 + jnp.where(kept_of == 1, sub_index, 0)
    ]
    mean_rows = jnp.mean(patches.astype(jnp.float32), axis=2).astype(jnp.bfloat16)
    shared_rows = mean_rows[image_index[:, None], owner_patch]
    local_tokens = jnp.where((kept_of == 1)[:, :, None], fine_rows, shared_rows)
    destinations = jnp.arange(seq_count, dtype=jnp.int32)[:, None, None]
    depth_slots = jnp.arange(capacity, dtype=jnp.int32)[None, None, :]
    positions = (destinations - my_start[None, :, None]) % seq_count + depth_slots * seq_count
    valid = positions < my_length[None, :, None]
    outgoing = local_tokens[image_index[None, :, None], jnp.minimum(positions, slot_count - 1)]
    outgoing = jnp.where(valid[:, :, :, None], outgoing, jnp.zeros((), jnp.bfloat16))
    incoming = lax.all_to_all(outgoing, "seq", split_axis=0, concat_axis=0, tiled=True)
    owned = jnp.arange(per_owner, dtype=jnp.int32) * seq_count + seq_rank
    source = jnp.sum((starts[:, None, :] <= owned[None, :, None]).astype(jnp.int32), axis=2) - 1
    first_of = jnp.take_along_axis(starts, source, axis=1)
    depth_of = (owned[None, :] - first_of) // seq_count
    resident = incoming[source, image_index[:, None], depth_of]
    start_rows = resident.reshape(images * per_owner, depth)
    start_float = start_rows.astype(jnp.float32)
    qkv_full, out_full, up_full, down_full = (
        lax.all_gather(qkv_weight, "seq", axis=0, tiled=True),
        lax.all_gather(out_weight, "seq", axis=1, tiled=True),
        lax.all_gather(up_weight, "seq", axis=0, tiled=True),
        lax.all_gather(down_weight, "seq", axis=1, tiled=True),
    )
    normed = layer_norm(start_float).astype(jnp.bfloat16).reshape(images, per_owner, depth)
    projected = jnp.einsum("ipd,dhc->ihpc", normed, qkv_full, preferred_element_type=jnp.float32)
    head_size = qkv_weight.shape[2] // 3
    sending = projected.astype(jnp.bfloat16).reshape(seq_count, per_owner, 3 * head_size)
    gathered = lax.all_to_all(sending, "seq", split_axis=0, concat_axis=0, tiled=True).reshape(
        seq_length, 3 * head_size
    )
    attended = attend(
        gathered[:, :head_size],
        gathered[:, head_size : 2 * head_size],
        gathered[:, 2 * head_size :],
    )
    returned = lax.all_to_all(
        attended.reshape(seq_count, per_owner, head_size),
        "seq",
        split_axis=0,
        concat_axis=0,
        tiled=True,
    )
    returned = returned.reshape(images, head_count, per_owner, head_size)
    partial_sum = jnp.einsum(
        "ihpc,hcd->ipd",
        returned,
        out_full.reshape(head_count, head_size, depth),
        preferred_element_type=jnp.float32,
    ).reshape(images * per_owner, depth)
    attn_total = lax.psum(partial_sum, "head")
    residual = start_float + attn_total
    residual_half = lax.dynamic_slice_in_dim(residual, head_rank * half_width, half_width, 1)
    normed_two = layer_norm(residual).astype(jnp.bfloat16)
    hidden = jax.nn.gelu(
        jnp.dot(normed_two, up_full, preferred_element_type=jnp.float32), approximate=False
    ).astype(jnp.bfloat16)
    mlp_terms = jnp.dot(hidden, down_full, preferred_element_type=jnp.float32)
    mlp_part = lax.psum_scatter(mlp_terms, "head", scatter_dimension=1, tiled=True)
    encoded = (residual_half + mlp_part).astype(jnp.bfloat16)
    return encoded.reshape(images, per_owner, 1, half_width)


def vspec():
    return pl.BlockSpec(memory_space=VMEM)


def aspec():
    return pl.BlockSpec(memory_space=pl.ANY)


def sspec():
    return pl.BlockSpec(memory_space=pltpu.SMEM)


def hspec():
    return pl.BlockSpec(memory_space=pltpu.HBM)


def run_copies(copies, sem, base=0):
    started = [
        pltpu.make_async_copy(src, dst, sem.at[base + i]) for i, (src, dst) in enumerate(copies)
    ]
    for copy in started:
        copy.start()

    def wait():
        for copy in started:
            copy.wait()

    return wait


def params(mebibytes=4):
    return pltpu.CompilerParams(vmem_limit_bytes=mebibytes * 1024 * 1024)


def cost(micros):
    return pl.CostEstimate(flops=micros * 10**9, bytes_accessed=1 << 20, transcendentals=0)


def struct(shape, dtype=BF16):
    return jax.ShapeDtypeStruct(shape, dtype)


def slot_of(index, n, capacity, cuts):
    device = sum(((index >= j * cuts * capacity).astype(jnp.int32) for j in range(1, n)), 0 * index)
    inner = index - device * (cuts * capacity)
    cut = sum(((inner >= c * capacity).astype(jnp.int32) for c in range(1, cuts)), 0 * index)
    return device, cut, inner - cut * capacity


def as_column(row):
    count = row.shape[1]
    same = lax.broadcasted_iota(jnp.int32, (count, count), 0) == lax.broadcasted_iota(
        jnp.int32, (count, count), 1
    )
    return jnp.sum(jnp.where(same, row, 0), axis=1, keepdims=True)


def one_hot(mask):
    return mask.astype(F32).astype(BF16)


def prep_kernel(n, sup, capacity, rank_ref, keep_ref, patches_ref, out_ref):
    rank = rank_ref[0]
    first = rank * sup
    keep = as_column(keep_ref[...])
    rows = 4 * sup
    count = keep.shape[0]

    def places(width, shift):
        ids = lax.broadcasted_iota(jnp.int32, (count, width), 1) >> shift
        kept = jnp.sum((keep == first + ids).astype(jnp.int32), axis=0, keepdims=True)
        below = jnp.sum(
            jnp.logical_and(keep >= first, keep < first + ids).astype(jnp.int32),
            axis=0,
            keepdims=True,
        )
        return kept, below, lax.broadcasted_iota(jnp.int32, (1, width), 1)

    kept, below, lane = places(rows, 2)
    fine_pos = jnp.where(kept == 1, (lane >> 2) + 3 * below + (lane & 3), -1)
    kept, below, lane = places(sup, 0)
    mean_pos = jnp.where(kept == 1, -1, lane + 3 * below)
    start = first + 3 * jnp.sum((keep < first).astype(jnp.int32), axis=0, keepdims=True)
    flat = patches_ref[...]
    cuts = flat.shape[1] // 128
    sup_col = lax.broadcasted_iota(jnp.int32, (sup, rows), 0)
    sup_lane = lax.broadcasted_iota(jnp.int32, (sup, rows), 1) >> 2
    averaging = jnp.where(sup_col == sup_lane, 0.25, 0.0).astype(BF16)
    means = jnp.dot(averaging, flat, preferred_element_type=F32).astype(BF16)
    index = lax.broadcasted_iota(jnp.int32, (n * cuts * capacity, 1), 0)
    device, cut, slot = slot_of(index, n, capacity, cuts)
    pos = ((device - start) & (n - 1)) + slot * n
    total = jnp.zeros((n * cuts * capacity, 128), F32)
    for c in range(cuts):
        at = jnp.where(cut == c, pos, -2)
        features = slice(c * 128, (c + 1) * 128)
        total = (
            total
            + jnp.dot(one_hot(at == fine_pos), flat[:, features], preferred_element_type=F32)
            + jnp.dot(one_hot(at == mean_pos), means[:, features], preferred_element_type=F32)
        )
    out_ref[...] = total.astype(BF16)


def prep(scalars, keep_list, flat, n, sup, capacity):
    width = flat.shape[1] // 2
    shape = (n * capacity * width // 128, 128)
    return pl.pallas_call(
        functools.partial(prep_kernel, n, sup, capacity),
        grid_spec=pltpu.PrefetchScalarGridSpec(
            num_scalar_prefetch=1,
            grid=(1,),
            in_specs=[
                pl.BlockSpec(keep_list.shape, lambda i, ref: (0, 0)),
                pl.BlockSpec((flat.shape[0], width), lambda i, ref: (0, ref[1])),
            ],
            out_specs=pl.BlockSpec(shape, lambda i, ref: (0, 0)),
        ),
        out_shape=struct(shape),
        compiler_params=params(),
    )(scalars, keep_list, flat)


def pick_kernel(n, sup, per_owner, capacity, rank_ref, keep_ref, got_ref, out_ref):
    rank = rank_ref[0]
    keep = as_column(keep_ref[...])
    count = keep.shape[0]
    lanes = got_ref.shape[0]
    cuts = lanes // (n * capacity)
    source, _, _ = slot_of(
        lax.broadcasted_iota(jnp.int32, (count, lanes), 1), n, capacity, cuts
    )
    low = jnp.sum((keep < source * sup).astype(jnp.int32), axis=0, keepdims=True)
    high = jnp.sum((keep < source * sup + sup).astype(jnp.int32), axis=0, keepdims=True)
    source, cut, slot = slot_of(
        lax.broadcasted_iota(jnp.int32, (1, lanes), 1), n, capacity, cuts
    )
    start = source * sup + 3 * low
    stop = source * sup + sup + 3 * high
    token = start + ((rank - start) & (n - 1)) + slot * n
    row = jnp.where(token < stop, token >> (n.bit_length() - 1), -1)
    own = lax.broadcasted_iota(jnp.int32, (per_owner, lanes), 0)
    got = got_ref[...]
    for c in range(cuts):
        choose = one_hot(own == jnp.where(cut == c, row, -1))
        owned = jnp.dot(choose, got, preferred_element_type=F32).astype(BF16)
        out_ref[c * per_owner : (c + 1) * per_owner] = owned


def pick(scalars, keep_list, got, n, sup, per_owner, capacity):
    cuts = got.shape[0] // (n * capacity)
    return pl.pallas_call(
        functools.partial(pick_kernel, n, sup, per_owner, capacity),
        in_specs=[sspec(), vspec(), vspec()],
        out_specs=vspec(),
        out_shape=struct((cuts * per_owner, 128)),
        compiler_params=params(),
    )(scalars, keep_list, got)


def far_kernel(n, rank_ref, qkv_ref, out_weight_ref, up_ref, down_ref, away_ref, sem):
    rank, part = rank_ref[0], rank_ref[2]
    half = n // 2
    rows = up_ref.shape[0]
    wide = up_ref.shape[1] // n
    units = wide // 2
    long = out_weight_ref.shape[0] // 2
    depth = qkv_ref.shape[1] // 2
    each = depth + rows + units
    copies = []
    for d in range(half):
        dest = (rank // half ^ 1) * half + d
        low = d * each
        at = pl.ds(pl.multiple_of(part * depth, 32), depth)
        copies.append((qkv_ref.at[dest, at], away_ref.at[pl.ds(low, depth)]))
        at = pl.ds(pl.multiple_of(dest * wide + part * units, 128), units)
        copies.append((up_ref.at[:, at], away_ref.at[pl.ds(low + depth, rows)]))
        copies.append((down_ref.at[at], away_ref.at[pl.ds(low + depth + rows, units)]))
    at = pl.ds(pl.multiple_of(part * long, 128), long)
    copies.append((out_weight_ref.at[at], away_ref.at[pl.ds(half * each, long)]))
    run_copies(copies, sem)()


def near_kernel(n, rank_ref, qkv_ref, out_weight_ref, up_ref, down_ref, *refs):
    near, sem = refs[: n // 2], refs[n // 2]
    rank, part = rank_ref[0], rank_ref[2]
    rows = up_ref.shape[0]
    wide = up_ref.shape[1] // n
    units = wide // 2
    long = out_weight_ref.shape[0] // 2
    copies = []
    for j in range(n // 2):
        dest = rank ^ j
        at = pl.ds(pl.multiple_of(dest * wide + part * units, 128), units)
        copies.append((up_ref.at[:, at], near[j].at[pl.ds(0, rows)]))
        copies.append((down_ref.at[at], near[j].at[pl.ds(rows, units)]))
        at = pl.ds(pl.multiple_of(part * long, 128), long)
        copies.append((out_weight_ref.at[at], near[j].at[pl.ds(rows + units, long)]))
        low = rows + units + long
        copies.append((qkv_ref.at[dest], near[j].at[pl.ds(low, qkv_ref.shape[1])]))
    run_copies(copies, sem)()


def pack(kernel, shapes, count, scalars, *weights):
    return pl.pallas_call(
        kernel,
        in_specs=[sspec()] + [hspec()] * 4,
        out_specs=[vspec()] * len(shapes),
        out_shape=[struct(shape) for shape in shapes],
        scratch_shapes=[pltpu.SemaphoreType.DMA((count,))],
    )(scalars, *weights)


def pack_far(scalars, qkv, out_weight, up, down, n):
    half = n // 2
    each = qkv.shape[1] // 2 + up.shape[0] + up.shape[1] // n // 2
    shapes = [(half * each + out_weight.shape[0] // 2, 128)]
    kernel = functools.partial(far_kernel, n)
    return pack(kernel, shapes, 3 * half + 1, scalars, qkv, out_weight, up, down)[0]


def pack_near(scalars, qkv, out_weight, up, down, n):
    half = n // 2
    rows = up.shape[0] + up.shape[1] // n // 2 + out_weight.shape[0] // 2 + qkv.shape[1]
    kernel = functools.partial(near_kernel, n)
    return pack(kernel, [(rows, 128)] * half, 4 * half, scalars, qkv, out_weight, up, down)


def fan_kernel(owned_ref, across_ref, far_ref, out_ref):
    rows = owned_ref.shape[0]
    count = out_ref.shape[0]
    top = 2 * rows
    rest = out_ref.shape[1] - top
    each = (far_ref.shape[0] - rest) // (count - 1)
    for d in range(count):
        out_ref[d, :rows] = owned_ref[...]
        out_ref[d, rows:top] = across_ref[...]
        out_ref[d, top : top + each] = far_ref[d * each : (d + 1) * each]
        out_ref[d, top + each :] = far_ref[count * each :]


def fan(owned, across, far, out_rows, count):
    each = (far.shape[0] - out_rows) // count
    shape = struct((count, 2 * owned.shape[0] + each + out_rows, 128))
    return pl.pallas_call(
        fan_kernel,
        in_specs=[vspec()] * 3,
        out_specs=vspec(),
        out_shape=shape,
        compiler_params=params(8),
    )(owned, across, far)


def source_of(rank, n, q, k):
    return (rank // (n // 2) ^ k) * (n // 2) + q


def norm_rows(x):
    average = jnp.mean(x, axis=-1, keepdims=True)
    power = jnp.mean(x * x, axis=-1, keepdims=True)
    return (x - average) * lax.rsqrt(power - average * average + 1e-06)


def attend_kernel(
    n, part, rank_ref, mine_ref, other_ref, near_ref, far_ref, tokens_ref, out_ref, weight_ref
):
    rank, half, group = rank_ref[0], rank_ref[1], rank_ref[2]
    rows = other_ref.shape[1] // 2
    cuts = rows // part
    width = cuts * 128
    depth = weight_ref.shape[0]
    piece = far_ref.shape[1]
    for q in range(n // 2):
        for k in range(2):
            source = source_of(rank, n, q, k)
            at = pl.ds(pl.multiple_of(source * part, part), part)
            for c in range(cuts):
                cut = slice(k * rows + c * part, k * rows + (c + 1) * part)
                to = pl.ds(pl.multiple_of(half * width + c * 128, 128), 128)
                tokens_ref[at, to] = mine_ref[q, cut]
                to = pl.ds(pl.multiple_of((1 - half) * width + c * 128, 128), 128)
                tokens_ref[at, to] = other_ref[q, cut]
        to = pl.ds(pl.multiple_of((rank ^ q) * 128, 128), 128)
        weight_ref[:, to] = near_ref[q]
        to = pl.ds(pl.multiple_of(source_of(rank, n, q, 1) * 128, 128), 128)
        at = pl.ds(pl.multiple_of(group * piece, 32), piece)
        weight_ref[at, to] = mine_ref[q, 2 * rows : 2 * rows + piece]
        at = pl.ds(pl.multiple_of((1 - group) * piece, 32), piece)
        weight_ref[at, to] = far_ref[q]
    normed = norm_rows(tokens_ref[...].astype(F32)).astype(BF16)
    projected = lax.dot_general(
        normed, weight_ref[...], (((1,), (1,)), ((), ())), preferred_element_type=F32
    ).astype(BF16)
    size = projected.shape[1] // 3
    queries = projected[:, :size]
    keys = projected[:, size : 2 * size]
    values = projected[:, 2 * size :]
    scores = lax.dot_general(
        queries, keys, (((1,), (1,)), ((), ())), preferred_element_type=F32
    ) * (1.0 / math.sqrt(size))
    powers = jnp.exp(scores - jnp.max(scores, axis=1, keepdims=True))
    probs = (powers / jnp.sum(powers, axis=1, keepdims=True)).astype(BF16)
    attended = lax.dot_general(
        values, probs, (((0,), (1,)), ((), ())), preferred_element_type=F32
    ).astype(BF16)
    out_ref[...] = attended


def attend_fast(scalars, mine, other, near, far, head_rows, per_owner, n):
    length = n * per_owner
    depth = other.shape[1] // (2 * per_owner) * 256
    size = head_rows // 3
    return pl.pallas_call(
        functools.partial(attend_kernel, n, per_owner),
        in_specs=[sspec()] + [vspec()] * 4,
        out_specs=[vspec()] * 2,
        out_shape=[struct((length, depth)), struct((size, length))],
        scratch_shapes=[VMEM((head_rows, n * 128), BF16)],
        compiler_params=params(12),
        cost_estimate=cost(30),
    )(scalars, mine, other, near, far)


def mlp_kernel(n, rank_ref, tokens_ref, pieces, far, outs_far, near, outs, scratch):
    base_ref, away_ref, sends = outs[0], outs[1], outs[2:]
    up_ref, down_ref, row_ref, whole_ref, joined_ref, sem = scratch
    rank, half, group = rank_ref[0], rank_ref[1], rank_ref[2]
    block = up_ref.shape[0] // n
    wide = down_ref.shape[0] // 2
    unit = wide // 2
    size = pieces[0].shape[2]
    rows = outs_far[0][0].shape[1]
    first, later = [], []
    for j in range(n // 2):
        source = rank ^ j
        at = pl.ds(pl.multiple_of(source * block, block), block)
        to = pl.ds(pl.multiple_of(source * 128, 128), 128)
        for core in range(2):
            for c in range(2):
                ref = near[core][c]
                units = pl.ds(pl.multiple_of(core * wide + (group ^ c) * unit, unit), unit)
                later.append((ref.at[j, pl.ds(0, block)], up_ref.at[at, units]))
                later.append((ref.at[j, pl.ds(block, unit)], down_ref.at[units, to]))
                rows_to = pl.ds(pl.multiple_of((group ^ c) * rows, rows), rows)
                rows_from = ref.at[j, pl.ds(block + unit, rows)]
                first.append((rows_from, whole_ref.at[core, rows_to, to]))
        source = source_of(rank, n, j, 1)
        at = pl.ds(pl.multiple_of(source * block, block), block)
        to = pl.ds(pl.multiple_of(source * 128, 128), 128)
        for core in range(2):
            for c in range(2):
                units = pl.ds(pl.multiple_of(core * wide + (group ^ c) * unit, unit), unit)
                later.append((far[core][c].at[j, pl.ds(0, block)], up_ref.at[at, units]))
                later.append((far[core][c].at[j, pl.ds(block, unit)], down_ref.at[units, to]))
                rows_to = pl.ds(pl.multiple_of((group ^ c) * rows, rows), rows)
                first.append((outs_far[core][c].at[j], whole_ref.at[core, rows_to, to]))
    wait_first = run_copies(first, sem)
    wait_later = run_copies(later, sem, len(first))
    for j in range(n // 2):
        for core in range(2):
            for k in range(2):
                at = pl.ds(pl.multiple_of((rank ^ j ^ (k * n // 2)) * size, size), size)
                joined_ref[core, at] = pieces[core][j, k]
    wait_first()
    dims = (((0,), (0,)), ((), ()))
    row_ref[...] = (
        tokens_ref[...].astype(F32)
        + lax.dot_general(joined_ref[0], whole_ref[0], dims, preferred_element_type=F32)
        + lax.dot_general(joined_ref[1], whole_ref[1], dims, preferred_element_type=F32)
    )
    part, width = base_ref.shape
    my_cols = pl.ds(pl.multiple_of(half * width, width), width)
    my_rows = pl.ds(pl.multiple_of(rank * part, part), part)
    normed = norm_rows(row_ref[...]).astype(BF16)
    base_ref[...] = row_ref[my_rows, my_cols]
    wait_later()
    raw = jnp.dot(normed, up_ref[...], preferred_element_type=F32)
    hidden = (0.5 * raw * (1.0 + lax.erf(raw * math.sqrt(0.5)))).astype(BF16)
    row_ref[:, :width] = jnp.dot(hidden, down_ref[:, my_cols], preferred_element_type=F32)
    base_ref[...] = base_ref[...] + row_ref[my_rows, :width]
    for j in range(n // 2):
        for k in range(2):
            owner = rank ^ j ^ (k * n // 2)
            term = row_ref[pl.ds(pl.multiple_of(owner * part, part), part), :width]
            if j > 0:
                sends[j - 1][k] = term.astype(BF16)
            elif k == 1:
                away_ref[...] = term


def mlp(scalars, tokens, pieces, far, outs_far, near, n):
    length, depth = tokens.shape
    width = depth // 2
    wide = 2 * (far[0][0].shape[1] - depth // n)
    inner = n * pieces[0].shape[2]
    half = n // 2

    def kernel(scalars, tokens, a, b, *refs):
        far, refs = (refs[:2], refs[2:4]), refs[4:]
        outs_far, refs = (refs[:2], refs[2:4]), refs[4:]
        near, refs = (refs[:2], refs[2:4]), refs[4:]
        mlp_kernel(n, scalars, tokens, (a, b), far, outs_far, near, refs[: half + 1], refs[half + 1 :])

    return pl.pallas_call(
        kernel,
        in_specs=[sspec()] + [vspec()] * 3 + [aspec()] * 12,
        out_specs=[vspec()] * (half + 1),
        out_shape=[struct((length // n, width), F32)] * 2
        + [struct((2, length // n, width))] * (half - 1),
        scratch_shapes=[
            VMEM((depth, 2 * wide), BF16),
            VMEM((2 * wide, depth), BF16),
            VMEM((length, depth), F32),
            VMEM((2, inner, depth), BF16),
            VMEM((2, inner, length), BF16),
            pltpu.SemaphoreType.DMA((24 * half,)),
        ],
        compiler_params=params(24),
    )(scalars, tokens, *pieces, *far[0], *far[1], *outs_far[0], *outs_far[1], *near[0], *near[1])


def sum_kernel(base_ref, away_ref, *refs):
    terms, (base_out, away_out) = refs[:-2], refs[-2:]
    base, away = base_ref[...], away_ref[...]
    for ref in terms:
        base = base + ref[0].astype(F32)
        away = away + ref[1].astype(F32)
    base_out[...] = base
    away_out[...] = away.astype(BF16)


def sum_terms(base, away, terms):
    return pl.pallas_call(
        sum_kernel,
        in_specs=[vspec()] * (2 + len(terms)),
        out_specs=[vspec()] * 2,
        out_shape=[struct(base.shape, F32), struct(away.shape)],
        compiler_params=params(),
    )(base, away, *terms)


def last_kernel(base_ref, across_ref, out_ref):
    out_ref[...] = (base_ref[...] + across_ref[...].astype(F32)).astype(BF16)


def last(base, across):
    return pl.pallas_call(
        last_kernel,
        in_specs=[vspec()] * 2,
        out_specs=vspec(),
        out_shape=struct(base.shape),
        compiler_params=params(),
    )(base, across)


def swap(value, axis, j):
    n = lax.axis_size(axis)
    return lax.ppermute(value, axis, [(i, i ^ j) for i in range(n)])


def exchange(value):
    return lax.all_to_all(value, "seq", split_axis=0, concat_axis=0, tiled=True)


def exchange_half(value):
    n = lax.axis_size("seq")
    groups = [list(range(n // 2)), list(range(n // 2, n))]
    return lax.all_to_all(
        value, "seq", split_axis=0, concat_axis=0, axis_index_groups=groups, tiled=True
    )


def after(value, *others):
    return lax.optimization_barrier((value, *others))[0]


def local_fast(patches, keep_list, qkv_weight, out_weight, up_weight, down_weight):
    n = lax.axis_size("seq")
    rank, head, group = (
        lax.axis_index(name).astype(jnp.int32) for name in ("seq", "head", "groups")
    )
    scalars = jnp.stack([rank, head, group])
    half = n // 2
    sup, depth = patches.shape[1], patches.shape[3]
    length = sup * n * 8 // 5
    per_owner = length // n
    half_width = depth // 2
    head_rows = qkv_weight.shape[2]
    capacity = (4 * sup + n - 1) // n
    flat = patches.reshape(4 * sup, depth)
    heads = qkv_weight.transpose(1, 2, 0)

    weights = (heads, out_weight, up_weight, down_weight)
    away = pack_far(scalars, *weights, n)
    far = swap(away, "seq", half)
    slots = prep(scalars, keep_list, after(flat, away), n, sup, capacity)
    dealt = exchange(slots)
    weights = lax.optimization_barrier((*weights, slots))[:4]
    near = pack_near(scalars, *weights, n)
    near = [near[0]] + [swap(near[j], "seq", j) for j in range(1, half)]
    owned = pick(scalars, keep_list, dealt, n, sup, per_owner, capacity)
    across = swap(owned, "seq", half)
    across, far, *near = lax.optimization_barrier((across, far, *near))

    out_rows = out_weight.shape[0] // 2
    got = exchange_half(fan(owned, across, far, out_rows, half))
    near_qkv = jnp.stack([block[block.shape[0] - head_rows :] for block in near])
    near_mine = jnp.stack([block[: block.shape[0] - head_rows] for block in near])
    near_other = swap(near_mine, "groups", 1)
    near_pair = swap(near_mine, "head", 1)
    got, near_qkv, near_other, near_pair = lax.optimization_barrier(
        (got, near_qkv, near_other, near_pair)
    )

    top = 2 * owned.shape[0]
    pieces_other = swap(got[:, :top], "head", 1)
    qkv_far = swap(got[:, top : top + head_rows // 2], "groups", 1)
    tokens, attended = attend_fast(
        scalars, got, pieces_other, near_qkv, qkv_far, head_rows, per_owner, n
    )

    att_across = swap(attended, "seq", half)
    far_last = swap(got[:, top + head_rows // 2 :], "head", 1)
    att_across, near_last, far_last = lax.optimization_barrier(
        (att_across, swap(near_other, "head", 1), far_last)
    )
    units = far_last.shape[1] - out_rows
    got = after(got, attended)
    mlp_mine = got[:, top + head_rows // 2 : got.shape[1] - out_rows]
    far_mine = got[:, got.shape[1] - out_rows :]
    far_other = swap(far_mine, "groups", 1)
    mlp_other = swap(mlp_mine, "groups", 1)
    pair = jnp.stack([attended, att_across])
    pairs = [swap(pair, "seq", j) for j in range(1, half)]
    mlp_other, far_other, *pairs = lax.optimization_barrier((mlp_other, far_other, *pairs))
    gathered = jnp.stack([pair] + pairs)
    mlp_pair = (mlp_mine, mlp_other)
    far_pair = (far_mine, far_other)
    base, term_away, *terms = mlp(
        scalars,
        tokens,
        (gathered, swap(gathered, "head", 1)),
        (mlp_pair, (far_last[:, :units], swap(mlp_other, "head", 1))),
        (far_pair, (far_last[:, units:], swap(far_other, "head", 1))),
        ((near_mine, near_other), (near_pair, near_last)),
        n,
    )
    terms = [swap(terms[j - 1], "seq", j) for j in range(1, half)]
    base, term_away = sum_terms(base, term_away, terms)
    encoded = last(base, swap(term_away, "seq", half))
    return encoded.reshape(1, per_owner, 1, half_width)


def local(patches, keep_list, qkv_weight, out_weight, up_weight, down_weight):
    n = lax.axis_size("seq")
    one_image = patches.shape[0] == 1 and qkv_weight.shape[1] == n and n & (n - 1) == 0
    one_image = one_image and lax.axis_size("groups") == 2 and up_weight.shape[1] == n * 256
    plan = local_fast if one_image else local_general
    return plan(patches, keep_list, qkv_weight, out_weight, up_weight, down_weight)


def solution(mesh):
    return jax.shard_map(
        local,
        mesh=mesh,
        in_specs=(
            P("groups", "seq", None, None),
            P("groups", None),
            P("seq", "head", None),
            P("head", "seq"),
            P("seq", "head"),
            P("head", "seq"),
        ),
        out_specs=P("groups", None, "seq", "head"),
        check_vma=False,
    )
```
